32 devices in a mesh: seq: 16 (over z, y, core), pos: 2 (over x).
Axes of the slice: x: 2, y: 2, z: 4, core: 2. Of those that a mesh axis runs over, the one named last changes fastest.
Arguments:
- block_input: bfloat16 [2, 16, 1024, 768], P(None, 'seq', 'pos'), may hold values from -6 to 6
- out_grad: bfloat16 [2, 16, 1024, 768], P(None, 'seq', 'pos'), may hold values from -6 to 6
- lengths: int32 [2, 16], P(None, 'seq'), may hold values from 256 to 1024, as said below
- decay_rates: float32 [768], replicated, may hold values from 1.5 to 15
- proj_weights: float32 [768, 6144], P('seq'), may hold values from -0.21875 to 0.21875
- proj_moment: float32 [768, 6144], P('seq'), as said below
- proj_average: float32 [768, 6144], P('seq'), may hold values from -0.21875 to 0.21875
- down_weights: float32 [3072, 768], P('seq'), may hold values from -0.109375 to 0.109375
- down_moment: float32 [3072, 768], P('seq'), as said below
- down_average: float32 [3072, 768], P('seq'), may hold values from -0.109375 to 0.109375
- vectors: float32 [26, 768], replicated, may hold values from -3.2 to 3.2, as said below
- vector_moment: float32 [26, 768], replicated, as said below
- vector_average: float32 [26, 768], replicated, may hold values from -3 to 3
- filter_net: float32 [165, 64], replicated, may hold values from -2 to 2, as said below
- net_moment: float32 [165, 64], replicated, as said below
- net_average: float32 [165, 64], replicated, may hold values from -2 to 2
- filter_out: float32 [64, 768], replicated, may hold values from -0.09375 to 0.09375
- final_moment: float32 [64, 768], replicated, as said below
- final_average: float32 [64, 768], replicated, may hold values from -0.09375 to 0.09375
Outputs:
- block_output: bfloat16 [2, 16, 1024, 768], P(None, 'seq', 'pos')
- input_grad: bfloat16 [2, 16, 1024, 768], P(None, 'seq', 'pos')
- proj_grad: float32 [768, 6144], P('seq')
- proj_next: float32 [768, 6144], P('seq')
- proj_moment_next: float32 [768, 6144], P('seq')
- proj_average_next: float32 [768, 6144], P('seq')
- down_grad: float32 [3072, 768], P('seq')
- down_next: float32 [3072, 768], P('seq')
- down_moment_next: float32 [3072, 768], P('seq')
- down_average_next: float32 [3072, 768], P('seq')
- vector_grad: float32 [26, 768], replicated
- vector_next: float32 [26, 768], replicated
- vector_moment_next: float32 [26, 768], replicated
- vector_average_next: float32 [26, 768], replicated
- net_grad: float32 [165, 64], replicated
- net_next: float32 [165, 64], replicated
- net_moment_next: float32 [165, 64], replicated
- net_average_next: float32 [165, 64], replicated
- final_grad: float32 [64, 768], replicated
- final_next: float32 [64, 768], replicated
- final_moment_next: float32 [64, 768], replicated
- final_average_next: float32 [64, 768], replicated
The draws below stay inside these ranges and needn't reach their ends.
Inputs may be any that keep to these rules, and one draw needn't show every extreme that they name: `lengths`: at least 256; in each micro-batch at least one sequence has all 1024 positions valid. `vectors`: gains rows near one, the other rows of both signs. `filter_net`: frequencies between 0.7 and 1.3. `proj_moment`: both signs. `down_moment`: both signs. `vector_moment`: both signs. `net_moment`: both signs. `final_moment`: both signs.
All inputs are finite; a program needn't handle non-finite values.
Results may differ from the reference program's by a relative error of at most 0.018.
Values may be sent and summed in bfloat16 or wider, within the bound.
A program may use at most 256 MiB of HBM per device.

```python
import math
import jax
import jax.numpy as jnp
from jax import lax

D = 768
FF = 3072
HID = 64
EMB = 33
MICRO = 2
VROWS = 26
SEQS = 16
SLOT = 1024
TOKENS = 32768
MCOLS = 6144
NROWS = 165


def scaled_normal(key, shape, scale):
    return jnp.clip(jax.random.normal(key, shape, jnp.float32), -4.0, 4.0) * scale


def draw_lengths(key, part):
    key = jax.random.fold_in(key, 1)
    key_one, key_two = jax.random.split(key)
    drawn = jax.random.randint(key_one, (MICRO, SEQS), SLOT // 4, SLOT + 1)
    chosen = jax.random.randint(key_two, (MICRO, 1), 0, SEQS)
    column = jnp.arange(SEQS, dtype=jnp.int32)[None, :]
    return jnp.where(column == chosen, SLOT, drawn).astype(jnp.int32)


def draw_vectors(key, part):
    key = jax.random.fold_in(key, 2)
    base = scaled_normal(key, (VROWS, D), 1.0)
    row_index = jnp.arange(VROWS)[:, None]
    is_gain = (row_index == 0) | (row_index == 2)
    scale = jnp.where(row_index >= 25, 0.8, jnp.where(row_index >= 22, 0.2, jnp.where(row_index >= 13, 0.5, 0.3)))
    return jnp.where(is_gain, 1.0 + 0.15 * base, scale * base)


def draw_filter_net(key, part):
    key = jax.random.fold_in(key, 3)
    base = scaled_normal(key, (NROWS, HID), 1.0)
    row_index = jnp.arange(NROWS)[:, None]
    is_bias = (row_index == EMB) | (row_index == EMB + 1 + HID) | (row_index == EMB + 2 + 2 * HID)
    is_freq = row_index == EMB + 3 + 2 * HID
    weights = jnp.where(row_index < EMB, 1.5 / math.sqrt(EMB), 1.5 / math.sqrt(HID)) * base
    values = jnp.where(is_bias, 0.5 * base, weights)
    return jnp.where(is_freq, 1.0 + 0.15 * jnp.clip(base, -2.0, 2.0), values)


def draw_proj_moment(key, part):
    key = jax.random.fold_in(key, 4)
    return scaled_normal(key, (D, MCOLS), 0.5 * math.sqrt(TOKENS))


def draw_down_moment(key, part):
    key = jax.random.fold_in(key, 5)
    return scaled_normal(key, (FF, D), 0.5 * math.sqrt(TOKENS))


def draw_vector_moment(key, part):
    key = jax.random.fold_in(key, 6)
    return scaled_normal(key, (VROWS, D), 0.5 * math.sqrt(TOKENS))


def draw_net_moment(key, part):
    key = jax.random.fold_in(key, 7)
    return scaled_normal(key, (NROWS, HID), 0.5 * math.sqrt(TOKENS))


def draw_final_moment(key, part):
    key = jax.random.fold_in(key, 8)
    return scaled_normal(key, (HID, D), 0.05 * math.sqrt(TOKENS * SLOT))


def shard_levels(own_key, dims, shards, smallest, top_value):
    level, own = 1.0, jax.random.fold_in(own_key, 6)
    for axis_at, shards_of in shards:
        heights = jnp.exp(jax.random.uniform(jax.random.fold_in(own, axis_at), (shards_of,), jnp.float32, smallest / len(shards), top_value / len(shards)))
        level = level * jnp.repeat(heights, dims[axis_at] // shards_of).reshape([-1 if axis == axis_at else 1 for axis in range(len(dims))])
    return level


def gaussian(key, extent, spread, bound, pieces=(), kind=jnp.bfloat16):
    values = spread * jax.random.normal(key, extent, jnp.float32)
    if pieces:
        values = values * shard_levels(key, extent, pieces, -0.22, 0.18)
    return jnp.clip(values, -bound, bound).astype(kind)


def setup_inputs(seed: int = 0) -> dict:
    key_list = jax.random.split(jax.random.key(seed), 20)
    return {
        "block_input": gaussian(key_list[0], (MICRO, SEQS, SLOT, D), 1.0, 6.0, ((1, 16), (2, 2))),
        "out_grad": gaussian(key_list[1], (MICRO, SEQS, SLOT, D), 1.0, 6.0, ((1, 16), (2, 2))),
        "lengths": draw_lengths(jax.random.fold_in(key_list[19], 71), 0),
        "decay_rates": jnp.clip(jnp.exp(jax.random.uniform(key_list[3], (D,), jnp.float32, math.log(1.5), math.log(15.0))), 1.5, 15.0),
        "proj_weights": gaussian(key_list[4], (D, MCOLS), D ** -0.5, 0.21875, ((0, 16),), jnp.float32),
        "proj_moment": draw_proj_moment(jax.random.fold_in(key_list[19], 71), 0),
        "proj_average": gaussian(key_list[6], (D, MCOLS), D ** -0.5, 0.21875, ((0, 16),), jnp.float32),
        "down_weights": gaussian(key_list[7], (FF, D), FF ** -0.5, 0.109375, ((0, 16),), jnp.float32),
        "down_moment": draw_down_moment(jax.random.fold_in(key_list[19], 71), 0),
        "down_average": gaussian(key_list[9], (FF, D), FF ** -0.5, 0.109375, ((0, 16),), jnp.float32),
        "vectors": draw_vectors(jax.random.fold_in(key_list[19], 71), 0),
        "vector_moment": draw_vector_moment(jax.random.fold_in(key_list[19], 71), 0),
        "vector_average": gaussian(key_list[12], (VROWS, D), 0.5, 3.0, (), jnp.float32),
        "filter_net": draw_filter_net(jax.random.fold_in(key_list[19], 71), 0),
        "net_moment": draw_net_moment(jax.random.fold_in(key_list[19], 71), 0),
        "net_average": gaussian(key_list[15], (NROWS, HID), 0.3, 2.0, (), jnp.float32),
        "filter_out": gaussian(key_list[16], (HID, D), (4 * SLOT) ** -0.5, 0.09375, (), jnp.float32),
        "final_moment": draw_final_moment(jax.random.fold_in(key_list[19], 71), 0),
        "final_average": gaussian(key_list[18], (HID, D), (4 * SLOT) ** -0.5, 0.09375, (), jnp.float32),
    }


highest = lax.Precision.HIGHEST

@jax.custom_vjp
def low(v):
    return lax.optimization_barrier(v.astype(jnp.bfloat16)).astype(jnp.float32)

@jax.custom_vjp
def low_back(v):
    return v

def low_keep(v):
    return (low(v), None)

def low_pass(kept, grad):
    return (grad,)

def back_keep(v):
    return (v, None)

def back_low(kept, grad):
    return (low(grad),)
low.defvjp(low_keep, low_pass)
low_back.defvjp(back_keep, back_low)

def layer_norm(values, gain, offset):
    center = lax.optimization_barrier(jnp.mean(values, axis=-1, keepdims=True))
    centred = values - center
    variance = lax.optimization_barrier(jnp.mean(centred * centred, axis=-1, keepdims=True))
    return centred * lax.rsqrt(variance + 1e-05) * gain + offset

def features(positions, slot_length):
    band_count = (EMB - 1) // 2
    scaled = positions.astype(jnp.float32) / slot_length
    bands = 0.0001 + jnp.arange(band_count, dtype=jnp.float32) * ((band_count - 1 - 0.0001) / (band_count - 1))
    angles = 2.0 * math.pi * scaled[:, None] * bands[None, :]
    return jnp.concatenate([scaled[:, None], jnp.cos(angles), -jnp.sin(angles)], axis=1)

def filter_fn(net_values, final_values, rates, positions, slot_length):
    embedded = features(positions, slot_length)
    frequency = net_values[EMB + 3 + 2 * HID]
    layer_one = jnp.sin(frequency * (jnp.dot(embedded, net_values[:EMB], precision=highest) + net_values[EMB]))
    layer_two = jnp.sin(frequency * (jnp.dot(layer_one, net_values[EMB + 1:EMB + 1 + HID], precision=highest) + net_values[EMB + 1 + HID]))
    layer_three = jnp.sin(frequency * (jnp.dot(layer_two, net_values[EMB + 2 + HID:EMB + 2 + 2 * HID], precision=highest) + net_values[EMB + 2 + 2 * HID]))
    shaped = jnp.einsum('hc,nh->cn', final_values, layer_three, precision=highest)
    scaled = positions.astype(jnp.float32) / slot_length
    window = jnp.exp(-rates[:, None] * scaled[None, :]) + 0.05
    return shaped * window

def short_conv(columns, previous, taps, offset):
    extended = jnp.concatenate([previous, columns], axis=1)
    return taps[0][:, None] * extended[:, 2:] + taps[1][:, None] * extended[:, 1:-1] + taps[2][:, None] * extended[:, :-2] + offset[:, None]

def long_conv(signal, spectrum, slot_length):
    product = jnp.fft.rfft(signal, n=2 * slot_length, axis=-1) * spectrum
    return jnp.fft.irfft(product, n=2 * slot_length, axis=-1)[..., :slot_length]

def mixer(parts, spectrum, long_bias, valid_mask, slot_length):
    gated = parts[1] * parts[2]
    convolved = long_conv(gated, spectrum, slot_length) + long_bias[:, None] * gated
    return parts[0] * convolved * valid_mask

def nesterov(weight, moment, average, gradient, rate):
    moment_next = 0.9 * moment + gradient
    weight_next = weight - rate * (gradient + 0.9 * moment_next)
    average_next = 0.9 * average + 0.1 * weight_next
    return (gradient, weight_next, moment_next, average_next)

def reference(block_input, out_grad, lengths, decay_rates, proj_weights, proj_moment, proj_average, down_weights, down_moment, down_average, vectors, vector_moment, vector_average, filter_net, net_moment, net_average, filter_out, final_moment, final_average):
    slot_length = block_input.shape[2]
    width = block_input.shape[3]
    positions = jnp.arange(slot_length, dtype=jnp.int32)

    def forward(proj_full, down_full, vector_set, net_values, final_layer, inputs):
        proj_low = low(proj_full)
        down_low = low(down_full)
        filters = filter_fn(net_values, final_layer, decay_rates, positions, slot_length)
        spectrum = jnp.fft.rfft(filters, n=2 * slot_length, axis=-1)

        def sequence(tokens, length):
            normed = low(layer_norm(tokens, vector_set[0], vector_set[1]))
            projected = low_back(jnp.dot(normed, proj_low[:, :3 * width], precision=highest) + vector_set[4:7].reshape(-1))
            shorted = short_conv(projected.T, jnp.zeros((3 * width, 2), jnp.float32), vector_set[13:22].reshape(3, 3 * width), vector_set[22:25].reshape(-1))
            shorted = low_back(low(shorted))
            valid_mask = (positions < length).astype(jnp.float32)
            mixer_out = low_back(low(mixer(shorted.reshape(3, width, slot_length), spectrum, vector_set[25], valid_mask, slot_length)))
            branch = low_back(jnp.dot(mixer_out.T, proj_low[:, 3 * width:4 * width], precision=highest) + vector_set[7])
            residual = tokens + branch
            normed_two = low(layer_norm(residual, vector_set[2], vector_set[3]))
            pre_act = low_back(jnp.dot(normed_two, proj_low[:, 4 * width:], precision=highest) + vector_set[8:12].reshape(-1))
            activated = low(jax.nn.gelu(pre_act))
            mlp_out = low_back(jnp.dot(activated, down_low, precision=highest) + vector_set[12])
            return residual + mlp_out

        def scan_step(carried, item):
            return (carried, jax.checkpoint(sequence)(item[0], item[1]))
        flat_tokens = inputs.reshape(-1, slot_length, width)
        flat_lengths = lengths.reshape(-1)
        carried, results = lax.scan(scan_step, jnp.float32(0.0), (flat_tokens, flat_lengths))
        return results.reshape(inputs.shape)
    result, backward = jax.vjp(forward, proj_weights, down_weights, vectors, filter_net, filter_out, block_input.astype(jnp.float32))
    gradients = backward(out_grad.astype(jnp.float32))
    proj_set = nesterov(proj_weights, proj_moment, proj_average, gradients[0], 0.0001)
    down_set = nesterov(down_weights, down_moment, down_average, gradients[1], 0.0001)
    vector_set_out = nesterov(vectors, vector_moment, vector_average, gradients[2], 0.001)
    net_set = nesterov(filter_net, net_moment, net_average, gradients[3], 0.0001)
    final_set = nesterov(filter_out, final_moment, final_average, gradients[4], 2e-06)
    return (result.astype(jnp.bfloat16), gradients[5].astype(jnp.bfloat16), proj_set[0], proj_set[1], proj_set[2], proj_set[3], down_set[0], down_set[1], down_set[2], down_set[3], vector_set_out[0], vector_set_out[1], vector_set_out[2], vector_set_out[3], net_set[0], net_set[1], net_set[2], net_set[3], final_set[0], final_set[1], final_set[2], final_set[3])
```

```python
import math

import jax
import jax.numpy as jnp
import numpy as np
from jax import lax
from jax.sharding import PartitionSpec as P

HID = 64
EMB = 33

highest = lax.Precision.HIGHEST
f32 = jnp.float32
bf16 = jnp.bfloat16


def passed_along(block, axis, distance):
    devices = range(lax.axis_size(axis))
    route = [(i - distance, i) for i in devices if i - distance in devices]
    return lax.ppermute(block, axis, route)


def dot(a, b):
    return lax.dot_general(a, b, (((1,), (0,)), ((), ())), preferred_element_type=f32)


def dot_tn(a, b):
    return lax.dot_general(a, b, (((0,), (0,)), ((), ())), preferred_element_type=f32)


def dot_nt(a, b):
    return lax.dot_general(a, b, (((1,), (1,)), ((), ())), preferred_element_type=f32)


def features(positions, slot_length):
    band_count = (EMB - 1) // 2
    scaled = positions.astype(f32) / slot_length
    bands = 0.0001 + jnp.arange(band_count, dtype=f32) * (
        (band_count - 1 - 0.0001) / (band_count - 1)
    )
    angles = 2.0 * math.pi * scaled[:, None] * bands[None, :]
    return jnp.concatenate([scaled[:, None], jnp.cos(angles), -jnp.sin(angles)], axis=1)


def filter_fn(net_values, final_values, rates, positions, slot_length):
    embedded = features(positions, slot_length)
    frequency = net_values[EMB + 3 + 2 * HID]
    layer_one = jnp.sin(
        frequency * (jnp.dot(embedded, net_values[:EMB], precision=highest) + net_values[EMB])
    )
    layer_two = jnp.sin(
        frequency
        * (
            jnp.dot(layer_one, net_values[EMB + 1 : EMB + 1 + HID], precision=highest)
            + net_values[EMB + 1 + HID]
        )
    )
    layer_three = jnp.sin(
        frequency
        * (
            jnp.dot(layer_two, net_values[EMB + 2 + HID : EMB + 2 + 2 * HID], precision=highest)
            + net_values[EMB + 2 + 2 * HID]
        )
    )
    shaped = jnp.dot(layer_three, final_values, precision=highest)
    scaled = positions.astype(f32) / slot_length
    window = jnp.exp(-scaled[:, None] * rates[None, :]) + 0.05
    return shaped * window


def transform_table(length):
    product = np.outer(2 * np.arange(length) + 1, np.arange(length)) % (4 * length)
    angle = product.astype(np.float64) * (math.pi / (2 * length))
    return np.concatenate([np.cos(angle), -np.sin(angle)], axis=0).astype(np.float32)


def halves(spectrum):
    half = spectrum.shape[-2] // 2
    return spectrum[..., :half, :], spectrum[..., half:, :]


def turned(spectrum, sign):
    re, im = halves(spectrum)
    parity = (1.0 - 2.0 * (jnp.arange(re.shape[-2]) % 2).astype(f32))[:, None] * sign
    return jnp.concatenate([-parity * im, parity * re], axis=-2)


def product(kernel, signal):
    kr, ki = halves(kernel)
    sr, si = halves(signal)
    return jnp.concatenate([kr * sr - ki * si, kr * si + ki * sr], axis=-2)


def product_conj(kernel, signal):
    kr, ki = halves(kernel)
    sr, si = halves(signal)
    return jnp.concatenate([kr * sr + ki * si, kr * si - ki * sr], axis=-2)


def nesterov(weight, moment, average, gradient, rate):
    moment_next = 0.9 * moment + gradient
    weight_next = weight - rate * (gradient + 0.9 * moment_next)
    average_next = 0.9 * average + 0.1 * weight_next
    return (gradient, weight_next, moment_next, average_next)


def norm_parts(values):
    center = jnp.mean(values, axis=-1, keepdims=True)
    centred = values - center
    variance = jnp.mean(centred * centred, axis=-1, keepdims=True)
    scale = lax.rsqrt(variance + 1e-05)
    return centred * scale, scale


def norm_back(grad, xh, scale, gain):
    q = grad * gain
    return (
        (q - jnp.mean(q, -1, keepdims=True) - xh * jnp.mean(q * xh, -1, keepdims=True)) * scale,
        jnp.sum(grad * xh, axis=0),
        jnp.sum(grad, axis=0),
    )


def on_device(
    block_input,
    out_grad,
    lengths,
    decay_rates,
    proj_weights,
    proj_moment,
    proj_average,
    down_weights,
    down_moment,
    down_average,
    vectors,
    vector_moment,
    vector_average,
    filter_net,
    net_moment,
    net_average,
    filter_out,
    final_moment,
    final_average,
):
    micro = block_input.shape[0]
    count = block_input.shape[2]
    width = block_input.shape[3]
    groups = lax.axis_size("pos")
    slot_length = count * groups
    tokens_all = micro * count
    group = lax.axis_index("pos")
    tap = vectors[13:22].reshape(3, 3 * width)
    short_bias = vectors[22:25].reshape(-1)
    in_bias = vectors[4:7].reshape(-1)
    up_bias = vectors[8:12].reshape(-1)
    skip = vectors[25]

    low_rows = proj_weights.astype(bf16)
    in_weight = lax.all_gather(low_rows[:, : 3 * width], "seq", axis=0, tiled=True)
    out_weight = lax.all_gather(low_rows[:, 3 * width : 4 * width], "seq", axis=0, tiled=True)
    up_weight = lax.all_gather(low_rows[:, 4 * width :], "seq", axis=0, tiled=True)
    down_weight = lax.all_gather(down_weights.astype(bf16), "seq", axis=0, tiled=True)

    table = jnp.asarray(transform_table(count))
    table_low = table.astype(bf16)
    every = jnp.arange(slot_length, dtype=jnp.int32)

    def make_filter(net_values, final_values):
        return filter_fn(net_values, final_values, decay_rates, every, slot_length)

    filters, filter_back = jax.vjp(make_filter, filter_net, filter_out)
    pieces = filters.reshape(groups, count, width)
    spectra = [
        jnp.dot(table, pieces[d], precision=lax.Precision.HIGH, preferred_element_type=f32)
        for d in range(groups)
    ]
    kernels = [spectra[0]] + [spectra[d] + turned(spectra[d - 1], 1.0) for d in range(1, groups)]

    def transform(values):
        return jnp.stack([dot(table_low, values[m]) for m in range(micro)])

    def transform_back(spectrum):
        low = spectrum.astype(bf16)
        return jnp.stack([dot_tn(table_low, low[m]) for m in range(micro)]) * (1.0 / count)

    tokens_low = block_input[:, 0]
    before = passed_along(tokens_low[:, -2:], "pos", 1)
    tokens = tokens_low.astype(f32).reshape(tokens_all, width)
    xh_one, scale_one = norm_parts(tokens)
    normed = (xh_one * vectors[0] + vectors[1]).astype(bf16)
    xh_before, _ = norm_parts(before.astype(f32).reshape(micro * 2, width))
    normed_before = (xh_before * vectors[0] + vectors[1]).astype(bf16)
    z = (dot(normed, in_weight) + in_bias).reshape(micro, count, 3 * width)
    z_before = (dot(normed_before, in_weight) + in_bias).reshape(micro, 2, 3 * width)
    z_before = jnp.where(group > 0, z_before, 0.0)
    z_long = jnp.concatenate([z_before, z], axis=1)
    short = (
        tap[0] * z_long[:, 2:] + tap[1] * z_long[:, 1:-1] + tap[2] * z_long[:, :-2] + short_bias
    ).astype(bf16)
    x0 = short[:, :, :width].astype(f32)
    x1 = short[:, :, width : 2 * width].astype(f32)
    v = short[:, :, 2 * width :].astype(f32)

    u = x1 * v
    u_low = u.astype(bf16)
    u_hat = [transform(u_low)]
    for d in range(1, groups):
        u_hat.append(transform(passed_along(u_low, "pos", d)))
    total = product(kernels[0], u_hat[0])
    for d in range(1, groups):
        total = total + product(kernels[d], u_hat[d])
    conv = transform_back(total) + skip * u
    here = group * count + jnp.arange(count, dtype=jnp.int32)
    mask = (here[None, :] < lengths[:, 0][:, None]).astype(f32)[:, :, None]
    y = (mask * x0 * conv).astype(bf16).reshape(tokens_all, width)
    residual = tokens + dot(y, out_weight) + vectors[7]
    xh_two, scale_two = norm_parts(residual)
    normed_two = (xh_two * vectors[2] + vectors[3]).astype(bf16)

    cot_low = out_grad[:, 0].reshape(tokens_all, width)
    cot = cot_low.astype(f32)
    pre = dot(normed_two, up_weight) + up_bias
    hidden, gelu_back = jax.vjp(jax.nn.gelu, pre)
    hidden_low = hidden.astype(bf16)
    block_output = (residual + dot(hidden_low, down_weight) + vectors[12]).astype(bf16)
    pre_grad = gelu_back(dot_nt(cot_low, down_weight))[0].astype(bf16)
    down_step = dot_tn(hidden_low, cot_low)
    up_step = dot_tn(normed_two, pre_grad)
    normed_two_grad = dot_nt(pre_grad, up_weight)
    part, gain_two, shift_two = norm_back(normed_two_grad, xh_two, scale_two, vectors[2])
    residual_grad = cot + part
    branch_low = residual_grad.astype(bf16)
    out_step = dot_tn(y, branch_low)
    y_grad = dot_nt(branch_low, out_weight).astype(bf16).astype(f32).reshape(micro, count, width)

    gw = mask * y_grad
    gx0 = gw * conv
    gc = gw * x0
    gc_low = gc.astype(bf16)
    skip_grad = jnp.sum(gc * u, axis=(0, 1))
    gc_hat = [transform(gc_low)]
    for d in range(1, groups):
        gc_hat.append(transform(passed_along(gc_low, "pos", -d)))
    back = product_conj(kernels[0], gc_hat[0])
    for d in range(1, groups):
        back = back + product_conj(kernels[d], gc_hat[d])
    gu = transform_back(back) + skip * gc
    kernel_grads = [jnp.sum(product_conj(u_hat[d], gc_hat[0]), axis=0) for d in range(groups)]
    filter_grads = []
    for d in range(groups):
        got = kernel_grads[d]
        if d + 1 < groups:
            got = got + turned(kernel_grads[d + 1], -1.0)
        filter_grads.append(dot_tn(table_low, got.astype(bf16)) * (1.0 / count))
    net_local, final_local = filter_back(jnp.concatenate(filter_grads, axis=0))
    short_grad = jnp.concatenate([gx0, gu * v, gu * x1], axis=-1).astype(bf16)
    after = passed_along(short_grad[:, :2], "pos", -1)
    short_long = jnp.concatenate([short_grad, after], axis=1).astype(f32)
    z_grad = (
        tap[0] * short_long[:, :-2] + tap[1] * short_long[:, 1:-1] + tap[2] * short_long[:, 2:]
    ).astype(bf16)
    here_grad = short_long[:, :-2]
    tap_grads = [
        jnp.sum(here_grad * z_long[:, 2 - k : 2 - k + count], axis=(0, 1)) for k in range(3)
    ]
    short_bias_grad = jnp.sum(here_grad, axis=(0, 1))
    z_grad = z_grad.reshape(tokens_all, 3 * width)
    in_step = dot_tn(normed, z_grad)
    in_bias_grad = jnp.sum(z_grad.astype(f32), axis=0)
    normed_grad = dot_nt(z_grad, in_weight)
    part, gain_one, shift_one = norm_back(normed_grad, xh_one, scale_one, vectors[0])
    input_grad = (residual_grad + part).astype(bf16)

    vector_local = jnp.concatenate(
        [
            gain_one[None],
            shift_one[None],
            gain_two[None],
            shift_two[None],
            in_bias_grad.reshape(3, width),
            jnp.sum(branch_low.astype(f32), axis=0)[None],
            jnp.sum(pre_grad.astype(f32), axis=0).reshape(4, width),
            jnp.sum(cot, axis=0)[None],
            jnp.stack(tap_grads).reshape(9, width),
            short_bias_grad.reshape(3, width),
            skip_grad[None],
        ],
        axis=0,
    )
    proj_local = jnp.concatenate([in_step, out_step, up_step], axis=1).astype(bf16)
    proj_shard = lax.psum_scatter(proj_local, "seq", scatter_dimension=0, tiled=True)
    down_shard = lax.psum_scatter(down_step.astype(bf16), "seq", scatter_dimension=0, tiled=True)
    proj_sum = lax.psum(proj_shard, "pos").astype(f32)
    down_sum = lax.psum(down_shard, "pos").astype(f32)
    vector_sum, net_sum, final_sum = lax.psum(
        (vector_local, net_local, final_local), ("seq", "pos")
    )
    return (
        block_output.reshape(micro, 1, count, width),
        input_grad.reshape(micro, 1, count, width),
        *nesterov(proj_weights, proj_moment, proj_average, proj_sum, 0.0001),
        *nesterov(down_weights, down_moment, down_average, down_sum, 0.0001),
        *nesterov(vectors, vector_moment, vector_average, vector_sum, 0.001),
        *nesterov(filter_net, net_moment, net_average, net_sum, 0.0001),
        *nesterov(filter_out, final_moment, final_average, final_sum, 2e-06),
    )


def solution(mesh):
    tokens = P(None, "seq", "pos", None)
    rows = P("seq", None)
    whole = P()
    return jax.shard_map(
        on_device,
        mesh=mesh,
        in_specs=(tokens, tokens, P(None, "seq"), whole) + (rows,) * 6 + (whole,) * 9,
        out_specs=(tokens, tokens) + (rows,) * 8 + (whole,) * 12,
        check_vma=False,
    )
```

```python
import functools
import math

import jax
import jax.numpy as jnp
import numpy as np
from jax import lax
from jax.experimental import pallas as pl
from jax.experimental.pallas import tpu as pltpu
from jax.sharding import PartitionSpec as P

HID = 64
EMB = 33

highest = lax.Precision.HIGHEST
f32 = jnp.float32
bf16 = jnp.bfloat16


def passed_along(block, axis, distance):
    devices = range(lax.axis_size(axis))
    route = [(i - distance, i) for i in devices if i - distance in devices]
    return lax.ppermute(block, axis, route)


def dot(a, b):
    return lax.dot_general(a, b, (((1,), (0,)), ((), ())), preferred_element_type=f32)


def dot_tn(a, b):
    return lax.dot_general(a, b, (((0,), (0,)), ((), ())), preferred_element_type=f32)


def dot_nt(a, b):
    return lax.dot_general(a, b, (((1,), (1,)), ((), ())), preferred_element_type=f32)


def features(positions, slot_length):
    band_count = (EMB - 1) // 2
    scaled = positions.astype(f32) / slot_length
    bands = 0.0001 + jnp.arange(band_count, dtype=f32) * (
        (band_count - 1 - 0.0001) / (band_count - 1)
    )
    angles = 2.0 * math.pi * scaled[:, None] * bands[None, :]
    return jnp.concatenate([scaled[:, None], jnp.cos(angles), -jnp.sin(angles)], axis=1)


def filter_fn(net_values, final_values, rates, positions, slot_length):
    embedded = features(positions, slot_length)
    frequency = net_values[EMB + 3 + 2 * HID]
    layer_one = jnp.sin(
        frequency * (jnp.dot(embedded, net_values[:EMB], precision=highest) + net_values[EMB])
    )
    layer_two = jnp.sin(
        frequency
        * (
            jnp.dot(layer_one, net_values[EMB + 1 : EMB + 1 + HID], precision=highest)
            + net_values[EMB + 1 + HID]
        )
    )
    layer_three = jnp.sin(
        frequency
        * (
            jnp.dot(layer_two, net_values[EMB + 2 + HID : EMB + 2 + 2 * HID], precision=highest)
            + net_values[EMB + 2 + 2 * HID]
        )
    )
    shaped = jnp.dot(layer_three, final_values, precision=highest)
    scaled = positions.astype(f32) / slot_length
    window = jnp.exp(-scaled[:, None] * rates[None, :]) + 0.05
    return shaped * window


def transform_table(length):
    product = np.outer(2 * np.arange(length) + 1, np.arange(length)) % (4 * length)
    angle = product.astype(np.float64) * (math.pi / (2 * length))
    return np.concatenate([np.cos(angle), -np.sin(angle)], axis=0).astype(np.float32)


def halves(spectrum):
    half = spectrum.shape[-2] // 2
    return spectrum[..., :half, :], spectrum[..., half:, :]


def turned(spectrum, sign):
    re, im = halves(spectrum)
    parity = (1.0 - 2.0 * (jnp.arange(re.shape[-2]) % 2).astype(f32))[:, None] * sign
    return jnp.concatenate([-parity * im, parity * re], axis=-2)


def product(kernel, signal):
    kr, ki = halves(kernel)
    sr, si = halves(signal)
    return jnp.concatenate([kr * sr - ki * si, kr * si + ki * sr], axis=-2)


def product_conj(kernel, signal):
    kr, ki = halves(kernel)
    sr, si = halves(signal)
    return jnp.concatenate([kr * sr + ki * si, kr * si - ki * sr], axis=-2)


def nesterov(weight, moment, average, gradient, rate):
    moment_next = 0.9 * moment + gradient
    weight_next = weight - rate * (gradient + 0.9 * moment_next)
    average_next = 0.9 * average + 0.1 * weight_next
    return (gradient, weight_next, moment_next, average_next)


def norm_parts(values):
    center = jnp.mean(values, axis=-1, keepdims=True)
    centred = values - center
    variance = jnp.mean(centred * centred, axis=-1, keepdims=True)
    scale = lax.rsqrt(variance + 1e-05)
    return centred * scale, scale


def norm_back(grad, xh, scale, gain):
    q = grad * gain
    return (
        (q - jnp.mean(q, -1, keepdims=True) - xh * jnp.mean(q * xh, -1, keepdims=True)) * scale,
        jnp.sum(grad * xh, axis=0),
        jnp.sum(grad, axis=0),
    )


MESH = pl.DeviceIdType.MESH


class Ring:
    def __init__(self, size):
        self.size = size
        self.count = size // 2
        self.seq = lax.axis_index("seq")
        self.pos = lax.axis_index("pos")
        self.core = lax.rem(self.seq, 2)
        chip = self.seq // 2
        odd = lax.rem(chip, 2)
        self.place = (1 - odd) * (chip // 2) + odd * (self.count - 1 - chip // 2)

    def chip(self, shift):
        place = lax.rem(self.place + (shift + self.count), self.count)
        low = jnp.where(place < self.count // 2, 1, 0)
        return low * (2 * place) + (1 - low) * (2 * (self.count - 1 - place) + 1)

    def device(self, shift):
        return {"seq": 2 * self.chip(shift) + self.core}

    @property
    def sibling(self):
        return {"seq": self.seq + 1 - 2 * self.core}

    @property
    def across(self):
        return {"pos": 1 - self.pos}


def greet_all(ring):
    barrier = pltpu.get_barrier_semaphore()
    for step in range(1, ring.size):
        other = lax.rem(ring.seq + step, ring.size)
        pl.semaphore_signal(barrier, inc=1, device_id={"seq": other}, device_id_type=MESH)
    pl.semaphore_signal(barrier, inc=1, device_id=ring.across, device_id_type=MESH)
    pl.semaphore_wait(barrier, ring.size)


def remote(src, dst, send, recv, device):
    return pltpu.make_async_remote_copy(
        src_ref=src, dst_ref=dst, send_sem=send, recv_sem=recv, device_id=device,
        device_id_type=MESH,
    )


class Reduction:
    def __init__(self, ring, grad, twin, up, down, own, other, sums, sems):
        self.ring = ring
        self.grad, self.twin, self.up, self.down = grad, twin, up, down
        self.own, self.other, self.sums = own, other, sums
        self.sems = sems
        self.ups = ring.count // 2
        self.downs = (ring.count - 1) // 2
        self.waiting = []

    def start(self, src, dst, index, device):
        copy = remote(src, dst, self.sems.at[0, index], self.sems.at[1, index], device)
        copy.start()
        self.waiting.append(copy)
        return copy

    def begin(self):
        core = self.ring.core
        self.first = self.start(self.grad.at[:, 1 - core], self.twin, 0, self.ring.sibling)

    def merge(self):
        self.first.wait_recv()
        core = self.ring.core

        @pl.loop(0, self.ring.count)
        def _(chip):
            self.twin[chip] = self.twin[chip] + self.grad[chip, core]

        self.send_up(0)
        self.send_down(0)

    def send_up(self, step):
        owner = self.ring.chip(self.ups - step)
        self.up_copy = self.start(
            self.twin.at[owner], self.up.at[step], 1 + step, self.ring.device(1)
        )

    def send_down(self, step):
        owner = self.ring.chip(step - self.downs)
        self.down_copy = self.start(
            self.twin.at[owner], self.down.at[step], 1 + self.ups + step, self.ring.device(-1)
        )

    def advance(self, step):
        self.up_copy.wait_recv()
        owner = self.ring.chip(self.ups - step)
        self.twin[owner] = self.twin[owner] + self.up[step - 1]
        self.send_up(step)
        if step < self.downs:
            self.down_copy.wait_recv()
            owner = self.ring.chip(step - self.downs)
            self.twin[owner] = self.twin[owner] + self.down[step - 1]
            self.send_down(step)

    def collect(self):
        self.up_copy.wait_recv()
        self.down_copy.wait_recv()
        mine = self.ring.chip(0)
        total = (
            self.twin[mine].astype(f32)
            + self.up[self.ups - 1].astype(f32)
            + self.down[self.downs - 1].astype(f32)
        )
        self.own[...] = total.astype(bf16)
        index = 1 + self.ups + self.downs
        self.last = self.start(self.own, self.other, index, self.ring.across)

    def finish(self):
        self.last.wait_recv()
        self.sums[...] = self.own[...].astype(f32) + self.other[...].astype(f32)
        for copy in self.waiting:
            copy.wait_send()


class SmallSum:
    def __init__(self, ring, values, parts, mine, other, sums, sems):
        self.ring, self.values, self.parts = ring, values, parts
        self.mine, self.other, self.sums = mine, other, sums
        self.sems = sems
        self.rows = parts.shape[1]
        self.waiting = []

    def block(self, index):
        return pl.ds(pl.multiple_of(index * self.rows, 8), self.rows)

    def begin(self):
        ring = self.ring
        self.arriving = []
        for step in range(1, ring.size):
            other = lax.rem(ring.seq + step, ring.size)
            copy = remote(
                self.values.at[self.block(other)], self.parts.at[step],
                self.sems.at[0, step], self.sems.at[1, step], {"seq": other},
            )
            copy.start()
            self.arriving.append(copy)
            self.waiting.append(copy)

    def middle(self):
        for copy in self.arriving:
            copy.wait_recv()
        total = self.values[self.block(self.ring.seq)]
        for step in range(1, self.ring.size):
            total = total + self.parts[step]
        self.mine[...] = total
        copy = remote(
            self.mine, self.other, self.sems.at[0, 0], self.sems.at[1, 0], self.ring.across
        )
        copy.start()
        self.waiting.append(copy)
        copy.wait_recv()
        block = self.block(self.ring.seq)
        self.sums[block] = self.mine[...] + self.other[...]
        self.arriving = []
        for step in range(1, self.ring.size):
            other = lax.rem(self.ring.seq + step, self.ring.size)
            copy = remote(
                self.sums.at[block], self.sums.at[block],
                self.sems.at[2, step], self.sems.at[3, step], {"seq": other},
            )
            copy.start()
            self.waiting.append(copy)
            back = lax.rem(self.ring.seq + (self.ring.size - step), self.ring.size)
            self.arriving.append(
                remote(
                    self.sums.at[self.block(back)], self.sums.at[self.block(back)],
                    self.sems.at[2, step], self.sems.at[3, step], {"seq": other},
                )
            )

    def finish(self):
        for copy in self.arriving:
            copy.wait_recv()
        for copy in self.waiting:
            copy.wait_send()


def reduction_scratch(size, rows, columns):
    chips = size // 2
    ups, downs = chips // 2, (chips - 1) // 2
    return [
        pltpu.VMEM((chips, rows, columns), bf16),
        pltpu.VMEM((ups, rows, columns), bf16),
        pltpu.VMEM((downs, rows, columns), bf16),
        pltpu.VMEM((rows, columns), bf16),
        pltpu.VMEM((rows, columns), bf16),
        pltpu.SemaphoreType.DMA((2, 2 + ups + downs)),
    ]


def small_scratch(size, rows, columns):
    return [
        pltpu.VMEM((size, rows // size, columns), f32),
        pltpu.VMEM((rows // size, columns), f32),
        pltpu.VMEM((rows // size, columns), f32),
        pltpu.SemaphoreType.DMA((4, size)),
    ]


def reduce_kernel(size, large, small, *refs):
    ins, refs = refs[: large + small], refs[large + small :]
    outs, refs = refs[: large + small], refs[large + small :]
    ring = Ring(size)
    greet_all(ring)
    works = []
    for i in range(large):
        twin, up, down, own, other, sems = refs[6 * i : 6 * i + 6]
        works.append(Reduction(ring, ins[i], twin, up, down, own, other, outs[i], sems))
    refs = refs[6 * large :]
    sums = []
    for i in range(small):
        parts, mine, other, sems = refs[4 * i : 4 * i + 4]
        sums.append(SmallSum(ring, ins[large + i], parts, mine, other, outs[large + i], sems))
    for work in sums:
        work.begin()
    for work in works:
        work.begin()
    for work in works:
        work.merge()
    for work in sums:
        work.middle()
    for step in range(1, ring.count // 2):
        for work in works:
            work.advance(step)
    for work in works:
        work.collect()
    for work in works:
        work.finish()
    for work in sums:
        work.finish()


def reduce_all(size, grads, smalls):
    chips = size // 2
    grads = [g.reshape(chips, 2, g.shape[0] // size, g.shape[1]) for g in grads]
    scratch, shapes = [], []
    for g in grads:
        scratch += reduction_scratch(size, g.shape[2], g.shape[3])
        shapes.append(jax.ShapeDtypeStruct((g.shape[2], g.shape[3]), f32))
    for s in smalls:
        scratch += small_scratch(size, s.shape[0], s.shape[1])
        shapes.append(jax.ShapeDtypeStruct(s.shape, f32))
    vmem = pl.BlockSpec(memory_space=pltpu.VMEM)
    return pl.pallas_call(
        functools.partial(reduce_kernel, size, len(grads), len(smalls)),
        out_shape=shapes,
        in_specs=[vmem] * (len(grads) + len(smalls)),
        out_specs=[vmem] * len(shapes),
        scratch_shapes=scratch,
        compiler_params=pltpu.CompilerParams(
            collective_id=1, has_side_effects=True, vmem_limit_bytes=60 * 1024 * 1024
        ),
        name="reduce_all",
    )(*grads, *smalls)


def fits(size, groups, proj_rows, down_rows):
    return groups == 2 and size % 4 == 0 and proj_rows % 16 == 0 and down_rows % 16 == 0


def on_device(
    block_input,
    out_grad,
    lengths,
    decay_rates,
    proj_weights,
    proj_moment,
    proj_average,
    down_weights,
    down_moment,
    down_average,
    vectors,
    vector_moment,
    vector_average,
    filter_net,
    net_moment,
    net_average,
    filter_out,
    final_moment,
    final_average,
):
    micro = block_input.shape[0]
    count = block_input.shape[2]
    width = block_input.shape[3]
    groups = lax.axis_size("pos")
    slot_length = count * groups
    tokens_all = micro * count
    group = lax.axis_index("pos")
    tap = vectors[13:22].reshape(3, 3 * width)
    short_bias = vectors[22:25].reshape(-1)
    in_bias = vectors[4:7].reshape(-1)
    up_bias = vectors[8:12].reshape(-1)
    skip = vectors[25]

    low_rows = proj_weights.astype(bf16)
    in_weight = lax.all_gather(low_rows[:, : 3 * width], "seq", axis=0, tiled=True)
    out_weight = lax.all_gather(low_rows[:, 3 * width : 4 * width], "seq", axis=0, tiled=True)
    up_weight = lax.all_gather(low_rows[:, 4 * width :], "seq", axis=0, tiled=True)
    down_weight = lax.all_gather(down_weights.astype(bf16), "seq", axis=0, tiled=True)

    table = jnp.asarray(transform_table(count))
    table_low = table.astype(bf16)
    every = jnp.arange(slot_length, dtype=jnp.int32)

    def make_filter(net_values, final_values):
        return filter_fn(net_values, final_values, decay_rates, every, slot_length)

    filters, filter_back = jax.vjp(make_filter, filter_net, filter_out)
    pieces = filters.reshape(groups, count, width)
    spectra = [
        jnp.dot(table, pieces[d], precision=lax.Precision.HIGH, preferred_element_type=f32)
        for d in range(groups)
    ]
    kernels = [spectra[0]] + [spectra[d] + turned(spectra[d - 1], 1.0) for d in range(1, groups)]

    def transform(values):
        return jnp.stack([dot(table_low, values[m]) for m in range(micro)])

    def transform_back(spectrum):
        low = spectrum.astype(bf16)
        return jnp.stack([dot_tn(table_low, low[m]) for m in range(micro)]) * (1.0 / count)

    tokens_low = block_input[:, 0]
    before = passed_along(tokens_low[:, -2:], "pos", 1)
    tokens = tokens_low.astype(f32).reshape(tokens_all, width)
    xh_one, scale_one = norm_parts(tokens)
    normed = (xh_one * vectors[0] + vectors[1]).astype(bf16)
    xh_before, _ = norm_parts(before.astype(f32).reshape(micro * 2, width))
    normed_before = (xh_before * vectors[0] + vectors[1]).astype(bf16)
    z = (dot(normed, in_weight) + in_bias).reshape(micro, count, 3 * width)
    z_before = (dot(normed_before, in_weight) + in_bias).reshape(micro, 2, 3 * width)
    z_before = jnp.where(group > 0, z_before, 0.0)
    z_long = jnp.concatenate([z_before, z], axis=1)
    short = (
        tap[0] * z_long[:, 2:] + tap[1] * z_long[:, 1:-1] + tap[2] * z_long[:, :-2] + short_bias
    ).astype(bf16)
    x0 = short[:, :, :width].astype(f32)
    x1 = short[:, :, width : 2 * width].astype(f32)
    v = short[:, :, 2 * width :].astype(f32)

    u = x1 * v
    u_low = u.astype(bf16)
    u_hat = [transform(u_low)]
    for d in range(1, groups):
        u_hat.append(transform(passed_along(u_low, "pos", d)))
    total = product(kernels[0], u_hat[0])
    for d in range(1, groups):
        total = total + product(kernels[d], u_hat[d])
    conv = transform_back(total) + skip * u
    here = group * count + jnp.arange(count, dtype=jnp.int32)
    mask = (here[None, :] < lengths[:, 0][:, None]).astype(f32)[:, :, None]
    y = (mask * x0 * conv).astype(bf16).reshape(tokens_all, width)
    residual = tokens + dot(y, out_weight) + vectors[7]
    xh_two, scale_two = norm_parts(residual)
    normed_two = (xh_two * vectors[2] + vectors[3]).astype(bf16)

    cot_low = out_grad[:, 0].reshape(tokens_all, width)
    cot = cot_low.astype(f32)
    pre = dot(normed_two, up_weight) + up_bias
    hidden, gelu_back = jax.vjp(jax.nn.gelu, pre)
    hidden_low = hidden.astype(bf16)
    block_output = (residual + dot(hidden_low, down_weight) + vectors[12]).astype(bf16)
    pre_grad = gelu_back(dot_nt(cot_low, down_weight))[0].astype(bf16)
    down_step = dot_tn(hidden_low, cot_low)
    up_step = dot_tn(normed_two, pre_grad)
    normed_two_grad = dot_nt(pre_grad, up_weight)
    part, gain_two, shift_two = norm_back(normed_two_grad, xh_two, scale_two, vectors[2])
    residual_grad = cot + part
    branch_low = residual_grad.astype(bf16)
    out_step = dot_tn(y, branch_low)
    y_grad = dot_nt(branch_low, out_weight).astype(bf16).astype(f32).reshape(micro, count, width)

    gw = mask * y_grad
    gx0 = gw * conv
    gc = gw * x0
    gc_low = gc.astype(bf16)
    skip_grad = jnp.sum(gc * u, axis=(0, 1))
    gc_hat = [transform(gc_low)]
    for d in range(1, groups):
        gc_hat.append(transform(passed_along(gc_low, "pos", -d)))
    back = product_conj(kernels[0], gc_hat[0])
    for d in range(1, groups):
        back = back + product_conj(kernels[d], gc_hat[d])
    gu = transform_back(back) + skip * gc
    kernel_grads = [jnp.sum(product_conj(u_hat[d], gc_hat[0]), axis=0) for d in range(groups)]
    filter_grads = []
    for d in range(groups):
        got = kernel_grads[d]
        if d + 1 < groups:
            got = got + turned(kernel_grads[d + 1], -1.0)
        filter_grads.append(dot_tn(table_low, got.astype(bf16)) * (1.0 / count))
    net_local, final_local = filter_back(jnp.concatenate(filter_grads, axis=0))
    short_grad = jnp.concatenate([gx0, gu * v, gu * x1], axis=-1).astype(bf16)
    after = passed_along(short_grad[:, :2], "pos", -1)
    short_long = jnp.concatenate([short_grad, after], axis=1).astype(f32)
    z_grad = (
        tap[0] * short_long[:, :-2] + tap[1] * short_long[:, 1:-1] + tap[2] * short_long[:, 2:]
    ).astype(bf16)
    here_grad = short_long[:, :-2]
    tap_grads = [
        jnp.sum(here_grad * z_long[:, 2 - k : 2 - k + count], axis=(0, 1)) for k in range(3)
    ]
    short_bias_grad = jnp.sum(here_grad, axis=(0, 1))
    z_grad = z_grad.reshape(tokens_all, 3 * width)
    in_step = dot_tn(normed, z_grad)
    in_bias_grad = jnp.sum(z_grad.astype(f32), axis=0)
    normed_grad = dot_nt(z_grad, in_weight)
    part, gain_one, shift_one = norm_back(normed_grad, xh_one, scale_one, vectors[0])
    input_grad = (residual_grad + part).astype(bf16)

    vector_local = jnp.concatenate(
        [
            gain_one[None],
            shift_one[None],
            gain_two[None],
            shift_two[None],
            in_bias_grad.reshape(3, width),
            jnp.sum(branch_low.astype(f32), axis=0)[None],
            jnp.sum(pre_grad.astype(f32), axis=0).reshape(4, width),
            jnp.sum(cot, axis=0)[None],
            jnp.stack(tap_grads).reshape(9, width),
            short_bias_grad.reshape(3, width),
            skip_grad[None],
        ],
        axis=0,
    )
    size = lax.axis_size("seq")
    if fits(size, groups, proj_weights.shape[0], down_weights.shape[0]):
        net_flat = jnp.pad(net_local, ((0, 256 - net_local.shape[0]), (0, 128 - HID)))
        rest = jnp.concatenate([vector_local, final_local], axis=0)
        rest_rows = rest.shape[0]
        rest = jnp.pad(rest, ((0, -rest_rows % (8 * size)), (0, 0)))
        down_sum, up_sum, out_sum, in_sum, rest, net_sum = reduce_all(
            size,
            [down_step.astype(bf16), up_step.astype(bf16), out_step.astype(bf16), in_step.astype(bf16)],
            [rest, net_flat],
        )
        proj_sum = jnp.concatenate([in_sum, out_sum, up_sum], axis=1)
        vector_sum = rest[: vectors.shape[0]]
        final_sum = rest[vectors.shape[0] : rest_rows]
        net_sum = net_sum[: net_local.shape[0], :HID]
    else:
        proj_local = jnp.concatenate([in_step, out_step, up_step], axis=1).astype(bf16)
        proj_shard = lax.psum_scatter(proj_local, "seq", scatter_dimension=0, tiled=True)
        down_shard = lax.psum_scatter(
            down_step.astype(bf16), "seq", scatter_dimension=0, tiled=True
        )
        proj_sum = lax.psum(proj_shard, "pos").astype(f32)
        down_sum = lax.psum(down_shard, "pos").astype(f32)
        vector_sum, net_sum, final_sum = lax.psum(
            (vector_local, net_local, final_local), ("seq", "pos")
        )
    return (
        block_output.reshape(micro, 1, count, width),
        input_grad.reshape(micro, 1, count, width),
        *nesterov(proj_weights, proj_moment, proj_average, proj_sum, 0.0001),
        *nesterov(down_weights, down_moment, down_average, down_sum, 0.0001),
        *nesterov(vectors, vector_moment, vector_average, vector_sum, 0.001),
        *nesterov(filter_net, net_moment, net_average, net_sum, 0.0001),
        *nesterov(filter_out, final_moment, final_average, final_sum, 2e-06),
    )


def solution(mesh):
    tokens = P(None, "seq", "pos", None)
    rows = P("seq", None)
    whole = P()
    return jax.shard_map(
        on_device,
        mesh=mesh,
        in_specs=(tokens, tokens, P(None, "seq"), whole) + (rows,) * 6 + (whole,) * 9,
        out_specs=(tokens, tokens) + (rows,) * 8 + (whole,) * 12,
        check_vma=False,
    )
```

```python
import functools
import math

import jax
import jax.numpy as jnp
import numpy as np
from jax import lax
from jax.experimental import pallas as pl
from jax.experimental.pallas import tpu as pltpu
from jax.sharding import PartitionSpec as P

HID = 64
EMB = 33

highest = lax.Precision.HIGHEST
f32 = jnp.float32
bf16 = jnp.bfloat16


def passed_along(block, axis, distance):
    devices = range(lax.axis_size(axis))
    route = [(i - distance, i) for i in devices if i - distance in devices]
    return lax.ppermute(block, axis, route)


def dot(a, b):
    return lax.dot_general(a, b, (((1,), (0,)), ((), ())), preferred_element_type=f32)


def dot_tn(a, b):
    return lax.dot_general(a, b, (((0,), (0,)), ((), ())), preferred_element_type=f32)


def dot_nt(a, b):
    return lax.dot_general(a, b, (((1,), (1,)), ((), ())), preferred_element_type=f32)


def features(positions, slot_length):
    band_count = (EMB - 1) // 2
    scaled = positions.astype(f32) / slot_length
    bands = 0.0001 + jnp.arange(band_count, dtype=f32) * (
        (band_count - 1 - 0.0001) / (band_count - 1)
    )
    angles = 2.0 * math.pi * scaled[:, None] * bands[None, :]
    return jnp.concatenate([scaled[:, None], jnp.cos(angles), -jnp.sin(angles)], axis=1)


def filter_fn(net_values, final_values, rates, positions, slot_length):
    embedded = features(positions, slot_length)
    frequency = net_values[EMB + 3 + 2 * HID]
    layer_one = jnp.sin(
        frequency * (jnp.dot(embedded, net_values[:EMB], precision=highest) + net_values[EMB])
    )
    layer_two = jnp.sin(
        frequency
        * (
            jnp.dot(layer_one, net_values[EMB + 1 : EMB + 1 + HID], precision=highest)
            + net_values[EMB + 1 + HID]
        )
    )
    layer_three = jnp.sin(
        frequency
        * (
            jnp.dot(layer_two, net_values[EMB + 2 + HID : EMB + 2 + 2 * HID], precision=highest)
            + net_values[EMB + 2 + 2 * HID]
        )
    )
    shaped = jnp.dot(layer_three, final_values, precision=highest)
    scaled = positions.astype(f32) / slot_length
    window = jnp.exp(-scaled[:, None] * rates[None, :]) + 0.05
    return shaped * window


def transform_table(length):
    product = np.outer(2 * np.arange(length) + 1, np.arange(length)) % (4 * length)
    angle = product.astype(np.float64) * (math.pi / (2 * length))
    return np.concatenate([np.cos(angle), -np.sin(angle)], axis=0).astype(np.float32)


def feature_table(slot_length):
    scaled = np.arange(slot_length, dtype=np.float32) / np.float32(slot_length)
    band_count = (EMB - 1) // 2
    bands = (
        np.float32(0.0001)
        + np.arange(band_count, dtype=np.float32) * np.float32((band_count - 1 - 0.0001) / (band_count - 1))
    )
    angles = (np.float32(2.0 * math.pi) * scaled[:, None]) * bands[None, :]
    table = np.zeros((slot_length, EMB + 4 + 2 * HID), np.float32)
    table[:, 0] = scaled
    table[:, 1 : 1 + band_count] = np.cos(angles)
    table[:, 1 + band_count : EMB] = -np.sin(angles)
    table[:, EMB] = 1.0
    return jnp.asarray(table)


def halves(spectrum):
    half = spectrum.shape[-2] // 2
    return spectrum[..., :half, :], spectrum[..., half:, :]


def turned(spectrum, sign):
    re, im = halves(spectrum)
    parity = (1.0 - 2.0 * (jnp.arange(re.shape[-2]) % 2).astype(f32))[:, None] * sign
    return jnp.concatenate([-parity * im, parity * re], axis=-2)


def product(kernel, signal):
    kr, ki = halves(kernel)
    sr, si = halves(signal)
    return jnp.concatenate([kr * sr - ki * si, kr * si + ki * sr], axis=-2)


def product_conj(kernel, signal):
    kr, ki = halves(kernel)
    sr, si = halves(signal)
    return jnp.concatenate([kr * sr + ki * si, kr * si - ki * sr], axis=-2)


def nesterov(weight, moment, average, gradient, rate):
    moment_next = 0.9 * moment + gradient
    weight_next = weight - rate * (gradient + 0.9 * moment_next)
    average_next = 0.9 * average + 0.1 * weight_next
    return (gradient, weight_next, moment_next, average_next)


def norm_parts(values):
    center = jnp.mean(values, axis=-1, keepdims=True)
    centred = values - center
    variance = jnp.mean(centred * centred, axis=-1, keepdims=True)
    scale = lax.rsqrt(variance + 1e-05)
    return centred * scale, scale


def norm_back(grad, xh, scale, gain):
    q = grad * gain
    return (
        (q - jnp.mean(q, -1, keepdims=True) - xh * jnp.mean(q * xh, -1, keepdims=True)) * scale,
        jnp.sum(grad * xh, axis=0),
        jnp.sum(grad, axis=0),
    )


MESH = pl.DeviceIdType.MESH


class Ring:
    def __init__(self, size):
        self.size = size
        self.count = size // 2
        self.seq = lax.axis_index("seq")
        self.pos = lax.axis_index("pos")
        self.core = lax.rem(self.seq, 2)
        chip = self.seq // 2
        odd = lax.rem(chip, 2)
        self.place = (1 - odd) * (chip // 2) + odd * (self.count - 1 - chip // 2)

    def chip(self, shift):
        place = lax.rem(self.place + (shift + self.count), self.count)
        low = jnp.where(place < self.count // 2, 1, 0)
        return low * (2 * place) + (1 - low) * (2 * (self.count - 1 - place) + 1)

    def device(self, shift):
        return {"seq": 2 * self.chip(shift) + self.core}

    @property
    def sibling(self):
        return {"seq": self.seq + 1 - 2 * self.core}

    @property
    def across(self):
        return {"pos": 1 - self.pos}


def greet_all(ring):
    barrier = pltpu.get_barrier_semaphore()
    for step in range(1, ring.size):
        other = lax.rem(ring.seq + step, ring.size)
        pl.semaphore_signal(barrier, inc=1, device_id={"seq": other}, device_id_type=MESH)
    pl.semaphore_signal(barrier, inc=1, device_id=ring.across, device_id_type=MESH)
    pl.semaphore_wait(barrier, ring.size)


def remote(src, dst, send, recv, device):
    return pltpu.make_async_remote_copy(
        src_ref=src, dst_ref=dst, send_sem=send, recv_sem=recv, device_id=device,
        device_id_type=MESH,
    )


class Reduction:
    def __init__(self, ring, grad, twin, up, down, own, other, sums, sems):
        self.ring = ring
        self.grad, self.twin, self.up, self.down = grad, twin, up, down
        self.own, self.other, self.sums = own, other, sums
        self.sems = sems
        self.ups = ring.count // 2
        self.downs = (ring.count - 1) // 2
        self.waiting = []

    def start(self, src, dst, index, device):
        copy = remote(src, dst, self.sems.at[0, index], self.sems.at[1, index], device)
        copy.start()
        self.waiting.append(copy)
        return copy

    def begin(self):
        core = self.ring.core
        self.first = self.start(self.grad.at[:, 1 - core], self.twin, 0, self.ring.sibling)

    def merge(self):
        self.first.wait_recv()
        core = self.ring.core

        @pl.loop(0, self.ring.count)
        def _(chip):
            self.twin[chip] = self.twin[chip] + self.grad[chip, core]

        self.send_up(0)
        self.send_down(0)

    def send_up(self, step):
        owner = self.ring.chip(self.ups - step)
        self.up_copy = self.start(
            self.twin.at[owner], self.up.at[step], 1 + step, self.ring.device(1)
        )

    def send_down(self, step):
        owner = self.ring.chip(step - self.downs)
        self.down_copy = self.start(
            self.twin.at[owner], self.down.at[step], 1 + self.ups + step, self.ring.device(-1)
        )

    def advance(self, step):
        self.up_copy.wait_recv()
        owner = self.ring.chip(self.ups - step)
        self.twin[owner] = self.twin[owner] + self.up[step - 1]
        self.send_up(step)
        if step < self.downs:
            self.down_copy.wait_recv()
            owner = self.ring.chip(step - self.downs)
            self.twin[owner] = self.twin[owner] + self.down[step - 1]
            self.send_down(step)

    def collect(self):
        self.up_copy.wait_recv()
        self.down_copy.wait_recv()
        mine = self.ring.chip(0)
        total = (
            self.twin[mine].astype(f32)
            + self.up[self.ups - 1].astype(f32)
            + self.down[self.downs - 1].astype(f32)
        )
        self.own[...] = total.astype(bf16)
        index = 1 + self.ups + self.downs
        self.last = self.start(self.own, self.other, index, self.ring.across)

    def finish(self):
        self.last.wait_recv()
        self.sums[...] = self.own[...].astype(f32) + self.other[...].astype(f32)
        for copy in self.waiting:
            copy.wait_send()


class SmallSum:
    def __init__(self, ring, values, parts, mine, other, sums, sems):
        self.ring, self.values, self.parts = ring, values, parts
        self.mine, self.other, self.sums = mine, other, sums
        self.sems = sems
        self.rows = parts.shape[1]
        self.waiting = []

    def block(self, index):
        return pl.ds(pl.multiple_of(index * self.rows, 8), self.rows)

    def begin(self):
        ring = self.ring
        self.arriving = []
        for step in range(1, ring.size):
            other = lax.rem(ring.seq + step, ring.size)
            copy = remote(
                self.values.at[self.block(other)], self.parts.at[step],
                self.sems.at[0, step], self.sems.at[1, step], {"seq": other},
            )
            copy.start()
            self.arriving.append(copy)
            self.waiting.append(copy)

    def middle(self):
        for copy in self.arriving:
            copy.wait_recv()
        total = self.values[self.block(self.ring.seq)]
        for step in range(1, self.ring.size):
            total = total + self.parts[step]
        self.mine[...] = total
        copy = remote(
            self.mine, self.other, self.sems.at[0, 0], self.sems.at[1, 0], self.ring.across
        )
        copy.start()
        self.waiting.append(copy)
        copy.wait_recv()
        block = self.block(self.ring.seq)
        self.sums[block] = self.mine[...] + self.other[...]
        self.arriving = []
        for step in range(1, self.ring.size):
            other = lax.rem(self.ring.seq + step, self.ring.size)
            copy = remote(
                self.sums.at[block], self.sums.at[block],
                self.sems.at[2, step], self.sems.at[3, step], {"seq": other},
            )
            copy.start()
            self.waiting.append(copy)
            back = lax.rem(self.ring.seq + (self.ring.size - step), self.ring.size)
            self.arriving.append(
                remote(
                    self.sums.at[self.block(back)], self.sums.at[self.block(back)],
                    self.sems.at[2, step], self.sems.at[3, step], {"seq": other},
                )
            )

    def finish(self):
        for copy in self.arriving:
            copy.wait_recv()
        for copy in self.waiting:
            copy.wait_send()


def reduction_scratch(size, rows, columns):
    chips = size // 2
    ups, downs = chips // 2, (chips - 1) // 2
    return [
        pltpu.VMEM((chips, rows, columns), bf16),
        pltpu.VMEM((ups, rows, columns), bf16),
        pltpu.VMEM((downs, rows, columns), bf16),
        pltpu.VMEM((rows, columns), bf16),
        pltpu.VMEM((rows, columns), bf16),
        pltpu.SemaphoreType.DMA((2, 2 + ups + downs)),
    ]


def small_scratch(size, rows, columns):
    return [
        pltpu.VMEM((size, rows // size, columns), f32),
        pltpu.VMEM((rows // size, columns), f32),
        pltpu.VMEM((rows // size, columns), f32),
        pltpu.SemaphoreType.DMA((4, size)),
    ]


def reduce_kernel(size, large, small, *refs):
    ins, refs = refs[: large + small], refs[large + small :]
    outs, refs = refs[: large + small], refs[large + small :]
    ring = Ring(size)
    greet_all(ring)
    works = []
    for i in range(large):
        twin, up, down, own, other, sems = refs[6 * i : 6 * i + 6]
        works.append(Reduction(ring, ins[i], twin, up, down, own, other, outs[i], sems))
    refs = refs[6 * large :]
    sums = []
    for i in range(small):
        parts, mine, other, sems = refs[4 * i : 4 * i + 4]
        sums.append(SmallSum(ring, ins[large + i], parts, mine, other, outs[large + i], sems))
    for work in sums:
        work.begin()
    for work in works:
        work.begin()
    for work in works:
        work.merge()
    for work in sums:
        work.middle()
    for step in range(1, ring.count // 2):
        for work in works:
            work.advance(step)
    for work in works:
        work.collect()
    for work in works:
        work.finish()
    for work in sums:
        work.finish()


def reduce_all(size, grads, smalls):
    chips = size // 2
    grads = [g.reshape(chips, 2, g.shape[0] // size, g.shape[1]) for g in grads]
    scratch, shapes = [], []
    for g in grads:
        scratch += reduction_scratch(size, g.shape[2], g.shape[3])
        shapes.append(jax.ShapeDtypeStruct((g.shape[2], g.shape[3]), f32))
    for s in smalls:
        scratch += small_scratch(size, s.shape[0], s.shape[1])
        shapes.append(jax.ShapeDtypeStruct(s.shape, f32))
    vmem = pl.BlockSpec(memory_space=pltpu.VMEM)
    return pl.pallas_call(
        functools.partial(reduce_kernel, size, len(grads), len(smalls)),
        out_shape=shapes,
        in_specs=[vmem] * (len(grads) + len(smalls)),
        out_specs=[vmem] * len(shapes),
        scratch_shapes=scratch,
        compiler_params=pltpu.CompilerParams(
            collective_id=1, has_side_effects=True, vmem_limit_bytes=60 * 1024 * 1024
        ),
        name="reduce_all",
    )(*grads, *smalls)


class Gather:
    def __init__(self, ring, mine, full, sems):
        self.ring, self.mine, self.full, self.sems = ring, mine, full, sems
        self.ups = ring.count // 2
        self.downs = (ring.count - 1) // 2
        self.waiting, self.arriving = [], []

    def send(self, src, place, index, device):
        copy = remote(
            src, self.full.at[self.ring.chip(place), self.ring.core],
            self.sems.at[0, index], self.sems.at[1, index], device,
        )
        copy.start()
        self.waiting.append(copy)
        return copy

    def share(self, src, place, index):
        index = self.ups + self.downs + index
        self.send(src, place, index, self.ring.sibling)
        block = self.full.at[self.ring.chip(place), 1 - self.ring.core]
        self.arriving.append(
            remote(block, block, self.sems.at[0, index], self.sems.at[1, index], self.ring.sibling)
        )

    def wait_block(self, place, index, device):
        block = self.full.at[self.ring.chip(place), self.ring.core]
        remote(block, block, self.sems.at[0, index], self.sems.at[1, index], device).wait_recv()
        return block

    def begin(self):
        ring = self.ring
        self.send(self.mine, 0, 0, ring.device(1))
        self.send(self.mine, 0, self.ups, ring.device(-1))
        self.share(self.mine, 0, 0)
        self.local = pltpu.make_async_copy(
            self.mine, self.full.at[ring.chip(0), ring.core], self.sems.at[2, 0]
        )
        self.local.start()

    def advance(self, step):
        ring = self.ring
        block = self.wait_block(-step, step - 1, ring.device(1))
        if step < self.ups:
            self.send(block, -step, step, ring.device(1))
        self.share(block, -step, step)
        if step <= self.downs:
            block = self.wait_block(step, self.ups + step - 1, ring.device(-1))
            if step < self.downs:
                self.send(block, step, self.ups + step, ring.device(-1))
            self.share(block, step, self.ups + step)

    def finish(self):
        self.local.wait()
        for copy in self.arriving:
            copy.wait_recv()
        for copy in self.waiting:
            copy.wait_send()


def gather_sems(size):
    chips = size // 2
    return pltpu.SemaphoreType.DMA((3, 2 * chips))


def norm_rows(values):
    center = jnp.mean(values, axis=1, keepdims=True)
    centred = values - center
    variance = jnp.mean(centred * centred, axis=1, keepdims=True)
    return centred * lax.rsqrt(variance + 1e-05)


def front_kernel(
    size,
    x_ref, proj_ref, down_ref, vec_ref, net_ref, final_ref, rate_ref, mask_ref,
    table_ref, back_ref, feature_ref,
    win_ref, wout_ref, wup_ref, wdown_ref,
    z_ref, zh_ref, s_ref, conv_ref, uhat_ref, kern_ref, res_ref,
    n_ref, nt_ref, n2_ref, n2t_ref, y_ref, yt_ref,
    up_own, down_own, in_own, out_own, halo, halo_n, filt, zbuf, ulow, urecv, spec,
    win_sem, wout_sem, wup_sem, wdown_sem, halo_sem, u_sem,
):
    micro, count, width = x_ref.shape
    groups = 2
    slot = groups * count
    tile = 256
    tiles = width // tile
    ring = Ring(size)
    group = ring.pos
    greet_all(ring)

    in_own[...] = proj_ref[:, : 3 * width].astype(bf16)
    gather_in = Gather(ring, in_own, win_ref, win_sem)
    gather_in.begin()
    edge = remote(
        x_ref.at[:, pl.ds(count - 16, 16)], halo, halo_sem.at[0], halo_sem.at[1], ring.across
    )
    edge.start()
    out_own[...] = proj_ref[:, 3 * width : 4 * width].astype(bf16)
    up_own[...] = proj_ref[:, 4 * width :].astype(bf16)
    down_own[...] = down_ref[...].astype(bf16)
    gather_out = Gather(ring, out_own, wout_ref, wout_sem)
    gather_up = Gather(ring, up_own, wup_ref, wup_sem)
    gather_down = Gather(ring, down_own, wdown_ref, wdown_sem)

    frequency = net_ref[EMB + 3 + 2 * HID : EMB + 4 + 2 * HID]

    def filter_rows(at):
        rows = pl.ds(pl.multiple_of(at * tile, tile), tile)
        layer = jnp.dot(
            feature_ref[rows], net_ref[...], precision=highest, preferred_element_type=f32
        )
        layer = jnp.sin(frequency * layer)
        for first in (EMB + 1, EMB + 2 + HID):
            layer = (
                jnp.dot(
                    layer, net_ref[first : first + HID], precision=highest,
                    preferred_element_type=f32,
                )
                + net_ref[first + HID : first + HID + 1]
            )
            layer = jnp.sin(frequency * layer)
        shaped = jnp.dot(layer, final_ref[...], precision=highest, preferred_element_type=f32)
        at_row = lax.broadcasted_iota(jnp.int32, (tile, width), 0) + at * tile
        scaled = at_row.astype(f32) * (1.0 / slot)
        window = jnp.exp(-scaled * rate_ref[...]) + 0.05
        filt[rows] = (shaped * window).astype(bf16)

    row_blocks = slot // tile
    hops = gather_in.ups
    per = max(1, row_blocks // hops)
    for hop in range(hops):
        first, last = hop * row_blocks // hops, (hop + 1) * row_blocks // hops

        @pl.loop(first, last)
        def _(at):
            filter_rows(at)

        if hop + 1 < hops:
            gather_in.advance(hop + 1)

    gain, shift = vec_ref[0:1], vec_ref[1:2]

    @pl.loop(0, micro)
    def _(m):
        for part in range(count // tile):
            xh = norm_rows(x_ref[m, part * tile : (part + 1) * tile].astype(f32))
            normed = (xh * gain + shift).astype(bf16)
            n_ref[m, part * tile : (part + 1) * tile] = normed
            nt_ref[m, :, part * tile : (part + 1) * tile] = normed.T

    gather_in.advance(hops)
    gather_out.begin()
    gather_up.begin()
    gather_down.begin()

    parity = 1.0 - 2.0 * (
        lax.broadcasted_iota(jnp.int32, (count, tile), 0) % 2
    ).astype(f32)

    @pl.loop(0, tiles)
    def _(j):
        cols = pl.ds(pl.multiple_of(j * tile, tile), tile)
        zero = dot(table_ref[...], filt[:count, cols])
        kern_ref[0, :, cols] = zero.astype(bf16)
        one = dot(table_ref[...], filt[count:, cols])
        kern_ref[1, :count, cols] = (one[:count] - parity * zero[count:]).astype(bf16)
        kern_ref[1, count:, cols] = (one[count:] + parity * zero[:count]).astype(bf16)

    edge.wait_recv()
    for m in range(micro):
        xh = norm_rows(halo[m].astype(f32))
        halo_n[m] = (xh * gain + shift).astype(bf16)
    gather_in.finish()
    gather_out.advance(1)
    inside = jnp.where(group > 0, 1.0, 0.0).astype(f32)

    def project(m, j):
        parts = []
        for p in range(3):
            lane = pl.ds(pl.multiple_of(j * tile, tile), tile)
            cols = pl.ds(pl.multiple_of(p * width + j * tile, tile), tile)
            weight = win_ref[:, :, :, cols].reshape(width, tile)
            bias = vec_ref[4 + p : 5 + p, lane]
            z = dot(n_ref[m], weight) + bias
            zh = (dot(halo_n[m], weight) + bias) * inside
            z_ref[m, :, cols] = z.astype(bf16)
            zh_ref[m, :, cols] = zh.astype(bf16)
            zbuf[:16] = zh
            zbuf[16:] = z
            short = (
                vec_ref[13 + p : 14 + p, lane] * z
                + vec_ref[16 + p : 17 + p, lane] * zbuf[15 : 15 + count]
                + vec_ref[19 + p : 20 + p, lane] * zbuf[14 : 14 + count]
                + vec_ref[22 + p : 23 + p, lane]
            ).astype(bf16)
            s_ref[m, :, cols] = short
            parts.append(short)
        lane = pl.ds(pl.multiple_of(j * tile, tile), tile)
        ulow[m, :, lane] = (parts[1].astype(f32) * parts[2].astype(f32)).astype(bf16)

    sent = []
    for m in range(micro):

        @pl.loop(0, tiles)
        def _(j):
            project(m, j)

        copy = remote(
            ulow.at[m], urecv.at[m], u_sem.at[0, m], u_sem.at[1, m], ring.across
        )
        copy.start()
        sent.append(copy)
        if m == 0:
            gather_up.advance(1)
            gather_out.advance(2)

    gather_down.advance(1)
    gather_out.advance(3)

    for m in range(micro):

        @pl.loop(0, tiles)
        def _(j):
            lane = pl.ds(pl.multiple_of(j * tile, tile), tile)
            uhat_ref[0, m, :, lane] = dot(table_ref[...], ulow[m, :, lane]).astype(bf16)

    gather_up.advance(2)
    gather_out.advance(4)
    gather_out.finish()

    def mix(m, j):
        lane = pl.ds(pl.multiple_of(j * tile, tile), tile)
        other = dot(table_ref[...], urecv[m, :, lane]) * inside
        uhat_ref[1, m, :, lane] = other.astype(bf16)
        k0r, k0i = kern_ref[0, :count, lane].astype(f32), kern_ref[0, count:, lane].astype(f32)
        k1r, k1i = kern_ref[1, :count, lane].astype(f32), kern_ref[1, count:, lane].astype(f32)
        ur = uhat_ref[0, m, :count, lane].astype(f32)
        ui = uhat_ref[0, m, count:, lane].astype(f32)
        vr, vi = other[:count], other[count:]
        spec[:count] = (k0r * ur - k0i * ui + k1r * vr - k1i * vi).astype(bf16)
        spec[count:] = (k0r * ui + k0i * ur + k1r * vi + k1i * vr).astype(bf16)
        gated = s_ref[m, :, pl.ds(pl.multiple_of(width + j * tile, tile), tile)].astype(
            f32
        ) * s_ref[m, :, pl.ds(pl.multiple_of(2 * width + j * tile, tile), tile)].astype(f32)
        conv = dot(back_ref[...], spec[...]) * (1.0 / count) + vec_ref[25:26, lane] * gated
        conv_ref[m, :, lane] = conv.astype(bf16)
        y = (mask_ref[m] * s_ref[m, :, lane].astype(f32) * conv).astype(bf16)
        y_ref[m, :, lane] = y

    for m in range(micro):
        sent[m].wait_recv()

        @pl.loop(0, tiles)
        def _(j):
            mix(m, j)

        for part in range(count // tile):
            rows = slice(part * tile, (part + 1) * tile)
            y = y_ref[m, rows]
            yt_ref[m, :, rows] = y.T
            residual = (
                x_ref[m, rows].astype(f32)
                + dot(y, wout_ref[...].reshape(width, width))
                + vec_ref[7:8]
            )
            res_ref[m, rows] = residual
            normed = (norm_rows(residual) * vec_ref[2:3] + vec_ref[3:4]).astype(bf16)
            n2_ref[m, rows] = normed
            n2t_ref[m, :, rows] = normed.T
        if m == 0:
            gather_down.advance(2)
            gather_up.advance(3)
    gather_down.advance(3)
    gather_up.advance(4)
    gather_down.advance(4)
    gather_up.finish()
    gather_down.finish()
    edge.wait_send()
    for copy in sent:
        copy.wait_send()


def front(size, x, proj, down, vectors, net, final, rates, mask, table, table_back, feature):
    chips = size // 2
    micro, count, width = x.shape
    wide = down.shape[0] * size
    rows, down_rows = proj.shape[0], down.shape[0]
    vmem = pl.BlockSpec(memory_space=pltpu.VMEM)
    anywhere = pl.BlockSpec(memory_space=pl.ANY)

    def shape(dims, kind=bf16):
        return jax.ShapeDtypeStruct(dims, kind)

    outs = pl.pallas_call(
        functools.partial(front_kernel, size),
        out_shape=[
            shape((chips, 2, rows, 3 * width)),
            shape((chips, 2, rows, width)),
            shape((chips, 2, rows, wide)),
            shape((chips, 2, down_rows, width)),
            shape((micro, count, 3 * width)),
            shape((micro, 16, 3 * width)),
            shape((micro, count, 3 * width)),
            shape((micro, count, width)),
            shape((2, micro, 2 * count, width)),
            shape((2, 2 * count, width)),
            shape((micro, count, width), f32),
            shape((micro, count, width)),
            shape((micro, width, count)),
            shape((micro, count, width)),
            shape((micro, width, count)),
            shape((micro, count, width)),
            shape((micro, width, count)),
        ],
        in_specs=[vmem] * 11,
        out_specs=[vmem, vmem, anywhere, anywhere] + [vmem] * 13,
        scratch_shapes=[
            pltpu.VMEM((rows, wide), bf16),
            pltpu.VMEM((down_rows, width), bf16),
            pltpu.VMEM((rows, 3 * width), bf16),
            pltpu.VMEM((rows, width), bf16),
            pltpu.VMEM((micro, 16, width), bf16),
            pltpu.VMEM((micro, 16, width), bf16),
            pltpu.VMEM((2 * count, width), bf16),
            pltpu.VMEM((16 + count, 256), f32),
            pltpu.VMEM((micro, count, width), bf16),
            pltpu.VMEM((micro, count, width), bf16),
            pltpu.VMEM((2 * count, 256), bf16),
            gather_sems(size),
            gather_sems(size),
            gather_sems(size),
            gather_sems(size),
            pltpu.SemaphoreType.DMA((2,)),
            pltpu.SemaphoreType.DMA((2, micro)),
        ],
        compiler_params=pltpu.CompilerParams(
            collective_id=0, has_side_effects=True, vmem_limit_bytes=62 * 1024 * 1024
        ),
        name="front",
    )(x, proj, down, vectors, net, final, rates, mask, table, table_back, feature)
    return outs


def fits(size, groups, proj_rows, down_rows):
    return groups == 2 and size % 4 == 0 and proj_rows % 16 == 0 and down_rows % 16 == 0


def on_device(
    block_input,
    out_grad,
    lengths,
    decay_rates,
    proj_weights,
    proj_moment,
    proj_average,
    down_weights,
    down_moment,
    down_average,
    vectors,
    vector_moment,
    vector_average,
    filter_net,
    net_moment,
    net_average,
    filter_out,
    final_moment,
    final_average,
):
    micro = block_input.shape[0]
    count = block_input.shape[2]
    width = block_input.shape[3]
    groups = lax.axis_size("pos")
    slot_length = count * groups
    tokens_all = micro * count
    group = lax.axis_index("pos")
    tap = vectors[13:22].reshape(3, 3 * width)
    short_bias = vectors[22:25].reshape(-1)
    in_bias = vectors[4:7].reshape(-1)
    up_bias = vectors[8:12].reshape(-1)
    skip = vectors[25]

    table = jnp.asarray(transform_table(count))
    table_low = table.astype(bf16)
    every = jnp.arange(slot_length, dtype=jnp.int32)
    here = group * count + jnp.arange(count, dtype=jnp.int32)
    mask = (here[None, :] < lengths[:, 0][:, None]).astype(f32)[:, :, None]
    tokens_low = block_input[:, 0]
    size = lax.axis_size("seq")
    tuned = fits(size, groups, proj_weights.shape[0], down_weights.shape[0])

    def make_filter(net_values, final_values):
        return filter_fn(net_values, final_values, decay_rates, every, slot_length)

    filters, filter_back = jax.vjp(make_filter, filter_net, filter_out)
    def transform(values):
        return jnp.stack([dot(table_low, values[m]) for m in range(micro)])

    def transform_back(spectrum):
        low = spectrum.astype(bf16)
        return jnp.stack([dot_tn(table_low, low[m]) for m in range(micro)]) * (1.0 / count)

    if tuned:
        (
            in_weight, out_weight, up_weight, down_weight, z_low, z_edge, short, conv, u_hat,
            kernels, residual, normed, _, normed_two, _, y, _,
        ) = front(
            size, tokens_low, proj_weights, down_weights, vectors, filter_net, filter_out,
            decay_rates[None], mask, table_low, table_low.T, feature_table(slot_length),
        )
        in_weight = in_weight.reshape(width, 3 * width)
        out_weight = out_weight.reshape(width, width)
        up_weight = up_weight.reshape(width, -1)
        down_weight = down_weight.reshape(-1, width)
        z_long = jnp.concatenate([z_edge[:, 14:], z_low], axis=1).astype(f32)
        x0 = short[:, :, :width].astype(f32)
        x1 = short[:, :, width : 2 * width].astype(f32)
        v = short[:, :, 2 * width :].astype(f32)
        u = x1 * v
        conv = conv.astype(f32)
        u_hat = u_hat.astype(f32)
        kernels = kernels.astype(f32)
        residual = residual.reshape(tokens_all, width)
        normed = normed.reshape(tokens_all, width)
        normed_two = normed_two.reshape(tokens_all, width)
        y = y.reshape(tokens_all, width)
        xh_one, scale_one = norm_parts(tokens_low.astype(f32).reshape(tokens_all, width))
        xh_two, scale_two = norm_parts(residual)
    else:
        low_rows = proj_weights.astype(bf16)
        in_weight = lax.all_gather(low_rows[:, : 3 * width], "seq", axis=0, tiled=True)
        out_weight = lax.all_gather(low_rows[:, 3 * width : 4 * width], "seq", axis=0, tiled=True)
        up_weight = lax.all_gather(low_rows[:, 4 * width :], "seq", axis=0, tiled=True)
        down_weight = lax.all_gather(down_weights.astype(bf16), "seq", axis=0, tiled=True)

        pieces = filters.reshape(groups, count, width)
        spectra = [
            jnp.dot(table, pieces[d], precision=lax.Precision.HIGH, preferred_element_type=f32)
            for d in range(groups)
        ]
        kernels = [spectra[0]] + [spectra[d] + turned(spectra[d - 1], 1.0) for d in range(1, groups)]

        before = passed_along(tokens_low[:, -2:], "pos", 1)
        tokens = tokens_low.astype(f32).reshape(tokens_all, width)
        xh_one, scale_one = norm_parts(tokens)
        normed = (xh_one * vectors[0] + vectors[1]).astype(bf16)
        xh_before, _ = norm_parts(before.astype(f32).reshape(micro * 2, width))
        normed_before = (xh_before * vectors[0] + vectors[1]).astype(bf16)
        z = (dot(normed, in_weight) + in_bias).reshape(micro, count, 3 * width)
        z_before = (dot(normed_before, in_weight) + in_bias).reshape(micro, 2, 3 * width)
        z_before = jnp.where(group > 0, z_before, 0.0)
        z_long = jnp.concatenate([z_before, z], axis=1)
        short = (
            tap[0] * z_long[:, 2:] + tap[1] * z_long[:, 1:-1] + tap[2] * z_long[:, :-2] + short_bias
        ).astype(bf16)
        x0 = short[:, :, :width].astype(f32)
        x1 = short[:, :, width : 2 * width].astype(f32)
        v = short[:, :, 2 * width :].astype(f32)

        u = x1 * v
        u_low = u.astype(bf16)
        u_hat = [transform(u_low)]
        for d in range(1, groups):
            u_hat.append(transform(passed_along(u_low, "pos", d)))
        total = product(kernels[0], u_hat[0])
        for d in range(1, groups):
            total = total + product(kernels[d], u_hat[d])
        conv = transform_back(total) + skip * u
        y = (mask * x0 * conv).astype(bf16).reshape(tokens_all, width)
        residual = tokens + dot(y, out_weight) + vectors[7]
        xh_two, scale_two = norm_parts(residual)
        normed_two = (xh_two * vectors[2] + vectors[3]).astype(bf16)

    cot_low = out_grad[:, 0].reshape(tokens_all, width)
    cot = cot_low.astype(f32)
    pre = dot(normed_two, up_weight) + up_bias
    hidden, gelu_back = jax.vjp(jax.nn.gelu, pre)
    hidden_low = hidden.astype(bf16)
    block_output = (residual + dot(hidden_low, down_weight) + vectors[12]).astype(bf16)
    pre_grad = gelu_back(dot_nt(cot_low, down_weight))[0].astype(bf16)
    down_step = dot_tn(hidden_low, cot_low)
    up_step = dot_tn(normed_two, pre_grad)
    normed_two_grad = dot_nt(pre_grad, up_weight)
    part, gain_two, shift_two = norm_back(normed_two_grad, xh_two, scale_two, vectors[2])
    residual_grad = cot + part
    branch_low = residual_grad.astype(bf16)
    out_step = dot_tn(y, branch_low)
    y_grad = dot_nt(branch_low, out_weight).astype(bf16).astype(f32).reshape(micro, count, width)

    gw = mask * y_grad
    gx0 = gw * conv
    gc = gw * x0
    gc_low = gc.astype(bf16)
    skip_grad = jnp.sum(gc * u, axis=(0, 1))
    gc_hat = [transform(gc_low)]
    for d in range(1, groups):
        gc_hat.append(transform(passed_along(gc_low, "pos", -d)))
    back = product_conj(kernels[0], gc_hat[0])
    for d in range(1, groups):
        back = back + product_conj(kernels[d], gc_hat[d])
    gu = transform_back(back) + skip * gc
    kernel_grads = [jnp.sum(product_conj(u_hat[d], gc_hat[0]), axis=0) for d in range(groups)]
    filter_grads = []
    for d in range(groups):
        got = kernel_grads[d]
        if d + 1 < groups:
            got = got + turned(kernel_grads[d + 1], -1.0)
        filter_grads.append(dot_tn(table_low, got.astype(bf16)) * (1.0 / count))
    net_local, final_local = filter_back(jnp.concatenate(filter_grads, axis=0))
    short_grad = jnp.concatenate([gx0, gu * v, gu * x1], axis=-1).astype(bf16)
    after = passed_along(short_grad[:, :2], "pos", -1)
    short_long = jnp.concatenate([short_grad, after], axis=1).astype(f32)
    z_grad = (
        tap[0] * short_long[:, :-2] + tap[1] * short_long[:, 1:-1] + tap[2] * short_long[:, 2:]
    ).astype(bf16)
    here_grad = short_long[:, :-2]
    tap_grads = [
        jnp.sum(here_grad * z_long[:, 2 - k : 2 - k + count], axis=(0, 1)) for k in range(3)
    ]
    short_bias_grad = jnp.sum(here_grad, axis=(0, 1))
    z_grad = z_grad.reshape(tokens_all, 3 * width)
    in_step = dot_tn(normed, z_grad)
    in_bias_grad = jnp.sum(z_grad.astype(f32), axis=0)
    normed_grad = dot_nt(z_grad, in_weight)
    part, gain_one, shift_one = norm_back(normed_grad, xh_one, scale_one, vectors[0])
    input_grad = (residual_grad + part).astype(bf16)

    vector_local = jnp.concatenate(
        [
            gain_one[None],
            shift_one[None],
            gain_two[None],
            shift_two[None],
            in_bias_grad.reshape(3, width),
            jnp.sum(branch_low.astype(f32), axis=0)[None],
            jnp.sum(pre_grad.astype(f32), axis=0).reshape(4, width),
            jnp.sum(cot, axis=0)[None],
            jnp.stack(tap_grads).reshape(9, width),
            short_bias_grad.reshape(3, width),
            skip_grad[None],
        ],
        axis=0,
    )
    if tuned:
        net_flat = jnp.pad(net_local, ((0, 256 - net_local.shape[0]), (0, 128 - HID)))
        rest = jnp.concatenate([vector_local, final_local], axis=0)
        rest_rows = rest.shape[0]
        rest = jnp.pad(rest, ((0, -rest_rows % (8 * size)), (0, 0)))
        down_sum, up_sum, out_sum, in_sum, rest, net_sum = reduce_all(
            size,
            [down_step.astype(bf16), up_step.astype(bf16), out_step.astype(bf16), in_step.astype(bf16)],
            [rest, net_flat],
        )
        proj_sum = jnp.concatenate([in_sum, out_sum, up_sum], axis=1)
        vector_sum = rest[: vectors.shape[0]]
        final_sum = rest[vectors.shape[0] : rest_rows]
        net_sum = net_sum[: net_local.shape[0], :HID]
    else:
        proj_local = jnp.concatenate([in_step, out_step, up_step], axis=1).astype(bf16)
        proj_shard = lax.psum_scatter(proj_local, "seq", scatter_dimension=0, tiled=True)
        down_shard = lax.psum_scatter(
            down_step.astype(bf16), "seq", scatter_dimension=0, tiled=True
        )
        proj_sum = lax.psum(proj_shard, "pos").astype(f32)
        down_sum = lax.psum(down_shard, "pos").astype(f32)
        vector_sum, net_sum, final_sum = lax.psum(
            (vector_local, net_local, final_local), ("seq", "pos")
        )
    return (
        block_output.reshape(micro, 1, count, width),
        input_grad.reshape(micro, 1, count, width),
        *nesterov(proj_weights, proj_moment, proj_average, proj_sum, 0.0001),
        *nesterov(down_weights, down_moment, down_average, down_sum, 0.0001),
        *nesterov(vectors, vector_moment, vector_average, vector_sum, 0.001),
        *nesterov(filter_net, net_moment, net_average, net_sum, 0.0001),
        *nesterov(filter_out, final_moment, final_average, final_sum, 2e-06),
    )


def solution(mesh):
    tokens = P(None, "seq", "pos", None)
    rows = P("seq", None)
    whole = P()
    return jax.shard_map(
        on_device,
        mesh=mesh,
        in_specs=(tokens, tokens, P(None, "seq"), whole) + (rows,) * 6 + (whole,) * 9,
        out_specs=(tokens, tokens) + (rows,) * 8 + (whole,) * 12,
        check_vma=False,
    )
```

```python
import functools
import math

import jax
import jax.numpy as jnp
import numpy as np
from jax import lax
from jax.experimental import pallas as pl
from jax.experimental.pallas import tpu as pltpu
from jax.sharding import PartitionSpec as P

HID = 64
EMB = 33

highest = lax.Precision.HIGHEST
f32 = jnp.float32
bf16 = jnp.bfloat16


def passed_along(block, axis, distance):
    devices = range(lax.axis_size(axis))
    route = [(i - distance, i) for i in devices if i - distance in devices]
    return lax.ppermute(block, axis, route)


def dot(a, b):
    return lax.dot_general(a, b, (((1,), (0,)), ((), ())), preferred_element_type=f32)


def dot_tn(a, b):
    return lax.dot_general(a, b, (((0,), (0,)), ((), ())), preferred_element_type=f32)


def dot_nt(a, b):
    return lax.dot_general(a, b, (((1,), (1,)), ((), ())), preferred_element_type=f32)


def features(positions, slot_length):
    band_count = (EMB - 1) // 2
    scaled = positions.astype(f32) / slot_length
    bands = 0.0001 + jnp.arange(band_count, dtype=f32) * (
        (band_count - 1 - 0.0001) / (band_count - 1)
    )
    angles = 2.0 * math.pi * scaled[:, None] * bands[None, :]
    return jnp.concatenate([scaled[:, None], jnp.cos(angles), -jnp.sin(angles)], axis=1)


def filter_fn(net_values, final_values, rates, positions, slot_length):
    embedded = features(positions, slot_length)
    frequency = net_values[EMB + 3 + 2 * HID]
    layer_one = jnp.sin(
        frequency * (jnp.dot(embedded, net_values[:EMB], precision=highest) + net_values[EMB])
    )
    layer_two = jnp.sin(
        frequency
        * (
            jnp.dot(layer_one, net_values[EMB + 1 : EMB + 1 + HID], precision=highest)
            + net_values[EMB + 1 + HID]
        )
    )
    layer_three = jnp.sin(
        frequency
        * (
            jnp.dot(layer_two, net_values[EMB + 2 + HID : EMB + 2 + 2 * HID], precision=highest)
            + net_values[EMB + 2 + 2 * HID]
        )
    )
    shaped = jnp.dot(layer_three, final_values, precision=highest)
    scaled = positions.astype(f32) / slot_length
    window = jnp.exp(-scaled[:, None] * rates[None, :]) + 0.05
    return shaped * window


def transform_table(length):
    product = np.outer(2 * np.arange(length) + 1, np.arange(length)) % (4 * length)
    angle = product.astype(np.float64) * (math.pi / (2 * length))
    return np.concatenate([np.cos(angle), -np.sin(angle)], axis=0).astype(np.float32)


def feature_table(slot_length):
    scaled = np.arange(slot_length, dtype=np.float32) / np.float32(slot_length)
    band_count = (EMB - 1) // 2
    bands = (
        np.float32(0.0001)
        + np.arange(band_count, dtype=np.float32) * np.float32((band_count - 1 - 0.0001) / (band_count - 1))
    )
    angles = (np.float32(2.0 * math.pi) * scaled[:, None]) * bands[None, :]
    table = np.zeros((slot_length, EMB + 4 + 2 * HID), np.float32)
    table[:, 0] = scaled
    table[:, 1 : 1 + band_count] = np.cos(angles)
    table[:, 1 + band_count : EMB] = -np.sin(angles)
    table[:, EMB] = 1.0
    return jnp.asarray(table)


def halves(spectrum):
    half = spectrum.shape[-2] // 2
    return spectrum[..., :half, :], spectrum[..., half:, :]


def turned(spectrum, sign):
    re, im = halves(spectrum)
    parity = (1.0 - 2.0 * (jnp.arange(re.shape[-2]) % 2).astype(f32))[:, None] * sign
    return jnp.concatenate([-parity * im, parity * re], axis=-2)


def product(kernel, signal):
    kr, ki = halves(kernel)
    sr, si = halves(signal)
    return jnp.concatenate([kr * sr - ki * si, kr * si + ki * sr], axis=-2)


def product_conj(kernel, signal):
    kr, ki = halves(kernel)
    sr, si = halves(signal)
    return jnp.concatenate([kr * sr + ki * si, kr * si - ki * sr], axis=-2)


def nesterov(weight, moment, average, gradient, rate):
    moment_next = 0.9 * moment + gradient
    weight_next = weight - rate * (gradient + 0.9 * moment_next)
    average_next = 0.9 * average + 0.1 * weight_next
    return (gradient, weight_next, moment_next, average_next)


def norm_parts(values):
    center = jnp.mean(values, axis=-1, keepdims=True)
    centred = values - center
    variance = jnp.mean(centred * centred, axis=-1, keepdims=True)
    scale = lax.rsqrt(variance + 1e-05)
    return centred * scale, scale


def norm_back(grad, xh, scale, gain):
    q = grad * gain
    return (
        (q - jnp.mean(q, -1, keepdims=True) - xh * jnp.mean(q * xh, -1, keepdims=True)) * scale,
        jnp.sum(grad * xh, axis=0),
        jnp.sum(grad, axis=0),
    )


MESH = pl.DeviceIdType.MESH


class Ring:
    def __init__(self, size):
        self.size = size
        self.count = size // 2
        self.seq = lax.axis_index("seq")
        self.pos = lax.axis_index("pos")
        self.core = lax.rem(self.seq, 2)
        chip = self.seq // 2
        odd = lax.rem(chip, 2)
        self.place = (1 - odd) * (chip // 2) + odd * (self.count - 1 - chip // 2)

    def chip(self, shift):
        place = lax.rem(self.place + (shift + self.count), self.count)
        low = jnp.where(place < self.count // 2, 1, 0)
        return low * (2 * place) + (1 - low) * (2 * (self.count - 1 - place) + 1)

    def device(self, shift):
        return {"seq": 2 * self.chip(shift) + self.core}

    @property
    def sibling(self):
        return {"seq": self.seq + 1 - 2 * self.core}

    @property
    def across(self):
        return {"pos": 1 - self.pos}


def greet_all(ring):
    barrier = pltpu.get_barrier_semaphore()
    for step in range(1, ring.size):
        other = lax.rem(ring.seq + step, ring.size)
        pl.semaphore_signal(barrier, inc=1, device_id={"seq": other}, device_id_type=MESH)
    pl.semaphore_signal(barrier, inc=1, device_id=ring.across, device_id_type=MESH)
    pl.semaphore_wait(barrier, ring.size)


def remote(src, dst, send, recv, device):
    return pltpu.make_async_remote_copy(
        src_ref=src, dst_ref=dst, send_sem=send, recv_sem=recv, device_id=device,
        device_id_type=MESH,
    )


class Reduction:
    def __init__(self, ring, grad, twin, up, down, own, other, sums, sems):
        self.ring = ring
        self.grad, self.twin, self.up, self.down = grad, twin, up, down
        self.own, self.other, self.sums = own, other, sums
        self.sems = sems
        self.ups = ring.count // 2
        self.downs = (ring.count - 1) // 2
        self.waiting = []

    def start(self, src, dst, index, device):
        copy = remote(src, dst, self.sems.at[0, index], self.sems.at[1, index], device)
        copy.start()
        self.waiting.append(copy)
        return copy

    def begin(self):
        core = self.ring.core
        self.first = self.start(self.grad.at[:, 1 - core], self.twin, 0, self.ring.sibling)

    def merge(self):
        self.first.wait_recv()
        core = self.ring.core

        @pl.loop(0, self.ring.count)
        def _(chip):
            self.twin[chip] = self.twin[chip] + self.grad[chip, core]

        self.send_up(0)
        self.send_down(0)

    def send_up(self, step):
        owner = self.ring.chip(self.ups - step)
        self.up_copy = self.start(
            self.twin.at[owner], self.up.at[step], 1 + step, self.ring.device(1)
        )

    def send_down(self, step):
        owner = self.ring.chip(step - self.downs)
        self.down_copy = self.start(
            self.twin.at[owner], self.down.at[step], 1 + self.ups + step, self.ring.device(-1)
        )

    def advance(self, step):
        self.up_copy.wait_recv()
        owner = self.ring.chip(self.ups - step)
        self.twin[owner] = self.twin[owner] + self.up[step - 1]
        self.send_up(step)
        if step < self.downs:
            self.down_copy.wait_recv()
            owner = self.ring.chip(step - self.downs)
            self.twin[owner] = self.twin[owner] + self.down[step - 1]
            self.send_down(step)

    def collect(self):
        self.up_copy.wait_recv()
        self.down_copy.wait_recv()
        mine = self.ring.chip(0)
        total = (
            self.twin[mine].astype(f32)
            + self.up[self.ups - 1].astype(f32)
            + self.down[self.downs - 1].astype(f32)
        )
        self.own[...] = total.astype(bf16)
        index = 1 + self.ups + self.downs
        self.last = self.start(self.own, self.other, index, self.ring.across)

    def finish(self):
        self.last.wait_recv()
        self.sums[...] = self.own[...].astype(f32) + self.other[...].astype(f32)
        for copy in self.waiting:
            copy.wait_send()


class SmallSum:
    def __init__(self, ring, values, parts, mine, other, sums, sems):
        self.ring, self.values, self.parts = ring, values, parts
        self.mine, self.other, self.sums = mine, other, sums
        self.sems = sems
        self.rows = parts.shape[1]
        self.waiting = []

    def block(self, index):
        return pl.ds(pl.multiple_of(index * self.rows, 8), self.rows)

    def begin(self):
        ring = self.ring
        self.arriving = []
        for step in range(1, ring.size):
            other = lax.rem(ring.seq + step, ring.size)
            copy = remote(
                self.values.at[self.block(other)], self.parts.at[step],
                self.sems.at[0, step], self.sems.at[1, step], {"seq": other},
            )
            copy.start()
            self.arriving.append(copy)
            self.waiting.append(copy)

    def middle(self):
        for copy in self.arriving:
            copy.wait_recv()
        total = self.values[self.block(self.ring.seq)]
        for step in range(1, self.ring.size):
            total = total + self.parts[step]
        self.mine[...] = total
        copy = remote(
            self.mine, self.other, self.sems.at[0, 0], self.sems.at[1, 0], self.ring.across
        )
        copy.start()
        self.waiting.append(copy)
        copy.wait_recv()
        block = self.block(self.ring.seq)
        self.sums[block] = self.mine[...] + self.other[...]
        self.arriving = []
        for step in range(1, self.ring.size):
            other = lax.rem(self.ring.seq + step, self.ring.size)
            copy = remote(
                self.sums.at[block], self.sums.at[block],
                self.sems.at[2, step], self.sems.at[3, step], {"seq": other},
            )
            copy.start()
            self.waiting.append(copy)
            back = lax.rem(self.ring.seq + (self.ring.size - step), self.ring.size)
            self.arriving.append(
                remote(
                    self.sums.at[self.block(back)], self.sums.at[self.block(back)],
                    self.sems.at[2, step], self.sems.at[3, step], {"seq": other},
                )
            )

    def finish(self):
        for copy in self.arriving:
            copy.wait_recv()
        for copy in self.waiting:
            copy.wait_send()


def reduction_scratch(size, rows, columns):
    chips = size // 2
    ups, downs = chips // 2, (chips - 1) // 2
    return [
        pltpu.VMEM((chips, rows, columns), bf16),
        pltpu.VMEM((ups, rows, columns), bf16),
        pltpu.VMEM((downs, rows, columns), bf16),
        pltpu.VMEM((rows, columns), bf16),
        pltpu.VMEM((rows, columns), bf16),
        pltpu.SemaphoreType.DMA((2, 2 + ups + downs)),
    ]


def small_scratch(size, rows, columns):
    return [
        pltpu.VMEM((size, rows // size, columns), f32),
        pltpu.VMEM((rows // size, columns), f32),
        pltpu.VMEM((rows // size, columns), f32),
        pltpu.SemaphoreType.DMA((4, size)),
    ]


def reduce_kernel(size, large, small, *refs):
    ins, refs = refs[: large + small], refs[large + small :]
    outs, refs = refs[: large + small], refs[large + small :]
    ring = Ring(size)
    greet_all(ring)
    works = []
    for i in range(large):
        twin, up, down, own, other, sems = refs[6 * i : 6 * i + 6]
        works.append(Reduction(ring, ins[i], twin, up, down, own, other, outs[i], sems))
    refs = refs[6 * large :]
    sums = []
    for i in range(small):
        parts, mine, other, sems = refs[4 * i : 4 * i + 4]
        sums.append(SmallSum(ring, ins[large + i], parts, mine, other, outs[large + i], sems))
    for work in sums:
        work.begin()
    for work in works:
        work.begin()
    for work in works:
        work.merge()
    for work in sums:
        work.middle()
    for step in range(1, ring.count // 2):
        for work in works:
            work.advance(step)
    for work in works:
        work.collect()
    for work in works:
        work.finish()
    for work in sums:
        work.finish()


def reduce_all(size, grads, smalls):
    chips = size // 2
    grads = [g.reshape(chips, 2, g.shape[0] // size, g.shape[1]) for g in grads]
    scratch, shapes = [], []
    for g in grads:
        scratch += reduction_scratch(size, g.shape[2], g.shape[3])
        shapes.append(jax.ShapeDtypeStruct((g.shape[2], g.shape[3]), f32))
    for s in smalls:
        scratch += small_scratch(size, s.shape[0], s.shape[1])
        shapes.append(jax.ShapeDtypeStruct(s.shape, f32))
    vmem = pl.BlockSpec(memory_space=pltpu.VMEM)
    return pl.pallas_call(
        functools.partial(reduce_kernel, size, len(grads), len(smalls)),
        out_shape=shapes,
        in_specs=[vmem] * (len(grads) + len(smalls)),
        out_specs=[vmem] * len(shapes),
        scratch_shapes=scratch,
        compiler_params=pltpu.CompilerParams(
            collective_id=1, has_side_effects=True, vmem_limit_bytes=60 * 1024 * 1024
        ),
        name="reduce_all",
    )(*grads, *smalls)


class Gather:
    def __init__(self, ring, mine, full, sems):
        self.ring, self.mine, self.full, self.sems = ring, mine, full, sems
        self.ups = ring.count // 2
        self.downs = (ring.count - 1) // 2
        self.waiting, self.arriving = [], []

    def send(self, src, place, index, device):
        copy = remote(
            src, self.full.at[self.ring.chip(place), self.ring.core],
            self.sems.at[0, index], self.sems.at[1, index], device,
        )
        copy.start()
        self.waiting.append(copy)
        return copy

    def share(self, src, place, index):
        index = self.ups + self.downs + index
        self.send(src, place, index, self.ring.sibling)
        block = self.full.at[self.ring.chip(place), 1 - self.ring.core]
        self.arriving.append(
            remote(block, block, self.sems.at[0, index], self.sems.at[1, index], self.ring.sibling)
        )

    def wait_block(self, place, index, device):
        block = self.full.at[self.ring.chip(place), self.ring.core]
        remote(block, block, self.sems.at[0, index], self.sems.at[1, index], device).wait_recv()
        return block

    def begin(self):
        ring = self.ring
        self.send(self.mine, 0, 0, ring.device(1))
        self.send(self.mine, 0, self.ups, ring.device(-1))
        self.share(self.mine, 0, 0)
        self.local = pltpu.make_async_copy(
            self.mine, self.full.at[ring.chip(0), ring.core], self.sems.at[2, 0]
        )
        self.local.start()

    def advance(self, step):
        ring = self.ring
        block = self.wait_block(-step, step - 1, ring.device(1))
        if step < self.ups:
            self.send(block, -step, step, ring.device(1))
        self.share(block, -step, step)
        if step <= self.downs:
            block = self.wait_block(step, self.ups + step - 1, ring.device(-1))
            if step < self.downs:
                self.send(block, step, self.ups + step, ring.device(-1))
            self.share(block, step, self.ups + step)

    def finish(self):
        self.local.wait()
        for copy in self.arriving:
            copy.wait_recv()
        for copy in self.waiting:
            copy.wait_send()


def gather_sems(size):
    chips = size // 2
    return pltpu.SemaphoreType.DMA((3, 2 * chips))


def norm_rows(values):
    center = jnp.mean(values, axis=1, keepdims=True)
    centred = values - center
    variance = jnp.mean(centred * centred, axis=1, keepdims=True)
    return centred * lax.rsqrt(variance + 1e-05)


def front_kernel(
    size,
    x_ref, proj_ref, down_ref, vec_ref, net_ref, final_ref, rate_ref, mask_ref,
    table_ref, back_ref, feature_ref,
    win_ref, wout_ref, wup_ref, wdown_ref,
    z_ref, zh_ref, s_ref, conv_ref, uhat_ref, kern_ref, res_ref,
    n_ref, nt_ref, n2_ref, n2t_ref, y_ref, yt_ref,
    up_own, down_own, in_own, out_own, halo, halo_n, filt, zbuf, ulow, urecv, spec,
    win_sem, wout_sem, wup_sem, wdown_sem, halo_sem, u_sem,
):
    micro, count, width = x_ref.shape
    groups = 2
    slot = groups * count
    tile = 256
    tiles = width // tile
    ring = Ring(size)
    group = ring.pos
    greet_all(ring)

    in_own[...] = proj_ref[:, : 3 * width].astype(bf16)
    gather_in = Gather(ring, in_own, win_ref, win_sem)
    gather_in.begin()
    edge = remote(
        x_ref.at[:, pl.ds(count - 16, 16)], halo, halo_sem.at[0], halo_sem.at[1], ring.across
    )
    edge.start()
    out_own[...] = proj_ref[:, 3 * width : 4 * width].astype(bf16)
    up_own[...] = proj_ref[:, 4 * width :].astype(bf16)
    down_own[...] = down_ref[...].astype(bf16)
    gather_out = Gather(ring, out_own, wout_ref, wout_sem)
    gather_up = Gather(ring, up_own, wup_ref, wup_sem)
    gather_down = Gather(ring, down_own, wdown_ref, wdown_sem)

    frequency = net_ref[EMB + 3 + 2 * HID : EMB + 4 + 2 * HID]

    def filter_rows(at):
        rows = pl.ds(pl.multiple_of(at * tile, tile), tile)
        layer = jnp.dot(
            feature_ref[rows], net_ref[...], precision=highest, preferred_element_type=f32
        )
        layer = jnp.sin(frequency * layer)
        for first in (EMB + 1, EMB + 2 + HID):
            layer = (
                jnp.dot(
                    layer, net_ref[first : first + HID], precision=highest,
                    preferred_element_type=f32,
                )
                + net_ref[first + HID : first + HID + 1]
            )
            layer = jnp.sin(frequency * layer)
        shaped = jnp.dot(layer, final_ref[...], precision=highest, preferred_element_type=f32)
        at_row = lax.broadcasted_iota(jnp.int32, (tile, width), 0) + at * tile
        scaled = at_row.astype(f32) * (1.0 / slot)
        window = jnp.exp(-scaled * rate_ref[...]) + 0.05
        filt[rows] = (shaped * window).astype(bf16)

    row_blocks = slot // tile
    hops = gather_in.ups
    per = max(1, row_blocks // hops)
    for hop in range(hops):
        first, last = hop * row_blocks // hops, (hop + 1) * row_blocks // hops

        @pl.loop(first, last)
        def _(at):
            filter_rows(at)

        if hop + 1 < hops:
            gather_in.advance(hop + 1)

    gain, shift = vec_ref[0:1], vec_ref[1:2]

    @pl.loop(0, micro)
    def _(m):
        for part in range(count // tile):
            xh = norm_rows(x_ref[m, part * tile : (part + 1) * tile].astype(f32))
            normed = (xh * gain + shift).astype(bf16)
            n_ref[m, part * tile : (part + 1) * tile] = normed
            nt_ref[m, :, part * tile : (part + 1) * tile] = normed.T

    gather_in.advance(hops)
    gather_out.begin()
    gather_up.begin()
    gather_down.begin()

    parity = 1.0 - 2.0 * (
        lax.broadcasted_iota(jnp.int32, (count, tile), 0) % 2
    ).astype(f32)

    @pl.loop(0, tiles)
    def _(j):
        cols = pl.ds(pl.multiple_of(j * tile, tile), tile)
        zero = dot(table_ref[...], filt[:count, cols])
        kern_ref[0, :, cols] = zero.astype(bf16)
        one = dot(table_ref[...], filt[count:, cols])
        kern_ref[1, :count, cols] = (one[:count] - parity * zero[count:]).astype(bf16)
        kern_ref[1, count:, cols] = (one[count:] + parity * zero[:count]).astype(bf16)

    edge.wait_recv()
    for m in range(micro):
        xh = norm_rows(halo[m].astype(f32))
        halo_n[m] = (xh * gain + shift).astype(bf16)
    gather_in.finish()
    gather_out.advance(1)
    inside = jnp.where(group > 0, 1.0, 0.0).astype(f32)

    def project(m, j):
        parts = []
        for p in range(3):
            lane = pl.ds(pl.multiple_of(j * tile, tile), tile)
            cols = pl.ds(pl.multiple_of(p * width + j * tile, tile), tile)
            weight = win_ref[:, :, :, cols].reshape(width, tile)
            bias = vec_ref[4 + p : 5 + p, lane]
            z = dot(n_ref[m], weight) + bias
            zh = (dot(halo_n[m], weight) + bias) * inside
            z_ref[m, :, cols] = z.astype(bf16)
            zh_ref[m, :, cols] = zh.astype(bf16)
            zbuf[:16] = zh
            zbuf[16:] = z
            short = (
                vec_ref[13 + p : 14 + p, lane] * z
                + vec_ref[16 + p : 17 + p, lane] * zbuf[15 : 15 + count]
                + vec_ref[19 + p : 20 + p, lane] * zbuf[14 : 14 + count]
                + vec_ref[22 + p : 23 + p, lane]
            ).astype(bf16)
            s_ref[m, :, cols] = short
            parts.append(short)
        lane = pl.ds(pl.multiple_of(j * tile, tile), tile)
        ulow[m, :, lane] = (parts[1].astype(f32) * parts[2].astype(f32)).astype(bf16)

    sent = []
    for m in range(micro):

        @pl.loop(0, tiles)
        def _(j):
            project(m, j)

        copy = remote(
            ulow.at[m], urecv.at[m], u_sem.at[0, m], u_sem.at[1, m], ring.across
        )
        copy.start()
        sent.append(copy)
        if m == 0:
            gather_up.advance(1)
            gather_out.advance(2)

    gather_down.advance(1)
    gather_out.advance(3)

    for m in range(micro):

        @pl.loop(0, tiles)
        def _(j):
            lane = pl.ds(pl.multiple_of(j * tile, tile), tile)
            uhat_ref[0, m, :, lane] = dot(table_ref[...], ulow[m, :, lane]).astype(bf16)

    gather_up.advance(2)
    gather_out.advance(4)
    gather_out.finish()

    def mix(m, j):
        lane = pl.ds(pl.multiple_of(j * tile, tile), tile)
        other = dot(table_ref[...], urecv[m, :, lane]) * inside
        uhat_ref[1, m, :, lane] = other.astype(bf16)
        k0r, k0i = kern_ref[0, :count, lane].astype(f32), kern_ref[0, count:, lane].astype(f32)
        k1r, k1i = kern_ref[1, :count, lane].astype(f32), kern_ref[1, count:, lane].astype(f32)
        ur = uhat_ref[0, m, :count, lane].astype(f32)
        ui = uhat_ref[0, m, count:, lane].astype(f32)
        vr, vi = other[:count], other[count:]
        spec[:count] = (k0r * ur - k0i * ui + k1r * vr - k1i * vi).astype(bf16)
        spec[count:] = (k0r * ui + k0i * ur + k1r * vi + k1i * vr).astype(bf16)
        gated = s_ref[m, :, pl.ds(pl.multiple_of(width + j * tile, tile), tile)].astype(
            f32
        ) * s_ref[m, :, pl.ds(pl.multiple_of(2 * width + j * tile, tile), tile)].astype(f32)
        conv = dot(back_ref[...], spec[...]) * (1.0 / count) + vec_ref[25:26, lane] * gated
        conv_ref[m, :, lane] = conv.astype(bf16)
        y = (mask_ref[m] * s_ref[m, :, lane].astype(f32) * conv).astype(bf16)
        y_ref[m, :, lane] = y

    for m in range(micro):
        sent[m].wait_recv()

        @pl.loop(0, tiles)
        def _(j):
            mix(m, j)

        for part in range(count // tile):
            rows = slice(part * tile, (part + 1) * tile)
            y = y_ref[m, rows]
            yt_ref[m, :, rows] = y.T
            residual = (
                x_ref[m, rows].astype(f32)
                + dot(y, wout_ref[...].reshape(width, width))
                + vec_ref[7:8]
            )
            res_ref[m, rows] = residual
            normed = (norm_rows(residual) * vec_ref[2:3] + vec_ref[3:4]).astype(bf16)
            n2_ref[m, rows] = normed
            n2t_ref[m, :, rows] = normed.T
        if m == 0:
            gather_down.advance(2)
            gather_up.advance(3)
    gather_down.advance(3)
    gather_up.advance(4)
    gather_down.advance(4)
    gather_up.finish()
    gather_down.finish()
    edge.wait_send()
    for copy in sent:
        copy.wait_send()


def front(size, x, proj, down, vectors, net, final, rates, mask, table, table_back, feature):
    chips = size // 2
    micro, count, width = x.shape
    wide = down.shape[0] * size
    rows, down_rows = proj.shape[0], down.shape[0]
    vmem = pl.BlockSpec(memory_space=pltpu.VMEM)
    anywhere = pl.BlockSpec(memory_space=pl.ANY)

    def shape(dims, kind=bf16):
        return jax.ShapeDtypeStruct(dims, kind)

    outs = pl.pallas_call(
        functools.partial(front_kernel, size),
        out_shape=[
            shape((chips, 2, rows, 3 * width)),
            shape((chips, 2, rows, width)),
            shape((chips, 2, rows, wide)),
            shape((chips, 2, down_rows, width)),
            shape((micro, count, 3 * width)),
            shape((micro, 16, 3 * width)),
            shape((micro, count, 3 * width)),
            shape((micro, count, width)),
            shape((2, micro, 2 * count, width)),
            shape((2, 2 * count, width)),
            shape((micro, count, width), f32),
            shape((micro, count, width)),
            shape((micro, width, count)),
            shape((micro, count, width)),
            shape((micro, width, count)),
            shape((micro, count, width)),
            shape((micro, width, count)),
        ],
        in_specs=[vmem] * 11,
        out_specs=[vmem, vmem, anywhere, anywhere] + [vmem] * 13,
        scratch_shapes=[
            pltpu.VMEM((rows, wide), bf16),
            pltpu.VMEM((down_rows, width), bf16),
            pltpu.VMEM((rows, 3 * width), bf16),
            pltpu.VMEM((rows, width), bf16),
            pltpu.VMEM((micro, 16, width), bf16),
            pltpu.VMEM((micro, 16, width), bf16),
            pltpu.VMEM((2 * count, width), bf16),
            pltpu.VMEM((16 + count, 256), f32),
            pltpu.VMEM((micro, count, width), bf16),
            pltpu.VMEM((micro, count, width), bf16),
            pltpu.VMEM((2 * count, 256), bf16),
            gather_sems(size),
            gather_sems(size),
            gather_sems(size),
            gather_sems(size),
            pltpu.SemaphoreType.DMA((2,)),
            pltpu.SemaphoreType.DMA((2, micro)),
        ],
        compiler_params=pltpu.CompilerParams(
            collective_id=0, has_side_effects=True, vmem_limit_bytes=62 * 1024 * 1024
        ),
        name="front",
    )(x, proj, down, vectors, net, final, rates, mask, table, table_back, feature)
    return outs


GELU_SCALE = math.sqrt(2.0 / math.pi)


def gelu_pair(a):
    square = a * a
    bend = jnp.tanh(GELU_SCALE * a * (1.0 + 0.044715 * square))
    half = 0.5 * (1.0 + bend)
    slope = half + (0.5 * GELU_SCALE) * a * (1.0 - bend * bend) * (1.0 + 0.134145 * square)
    return a * half, slope


def mlp_kernel(
    n2_ref, n2t_ref, gm_ref, res_ref, vec_ref, wup_ref, wdown_ref, bias_ref,
    out_ref, gb_ref, dup_ref, ddown_ref, small_ref,
    acc_out, acc_gn, hid_ref, ga_ref,
):
    step, last = pl.program_id(0), pl.num_programs(0) - 1
    micro, count, width = n2_ref.shape
    chunk = bias_ref.shape[1]
    tile = 256
    wup = wup_ref[...].reshape(width, chunk)
    wdown = wdown_ref[...].reshape(chunk, width)
    bias = bias_ref[...]

    @pl.when(step == 0)
    def _():
        acc_out[...] = jnp.zeros_like(acc_out)
        acc_gn[...] = jnp.zeros_like(acc_gn)
        small_ref[...] = jnp.zeros_like(small_ref)

    bias_sum = jnp.zeros((1, chunk), f32)
    for m in range(micro):
        for part in range(count // tile):
            rows = slice(part * tile, (part + 1) * tile)
            hidden, slope = gelu_pair(dot(n2_ref[m, rows], wup) + bias)
            hidden = hidden.astype(bf16)
            ga = (dot_nt(gm_ref[m, rows], wdown) * slope).astype(bf16)
            hid_ref[m, rows] = hidden
            ga_ref[m, rows] = ga
            bias_sum = bias_sum + jnp.sum(ga.astype(f32), axis=0, keepdims=True)
            acc_out[m, rows] += dot(hidden, wdown)
            acc_gn[m, rows] += dot_nt(ga, wup)
    small_ref[pl.ds(4 + step, 1)] = bias_sum
    down_total = dot_tn(hid_ref[0], gm_ref[0])
    up_total = dot(n2t_ref[0], ga_ref[0])
    for m in range(1, micro):
        down_total = down_total + dot_tn(hid_ref[m], gm_ref[m])
        up_total = up_total + dot(n2t_ref[m], ga_ref[m])
    ddown_ref[...] = down_total.astype(bf16)
    dup_ref[...] = up_total.astype(bf16)

    @pl.when(step == last)
    def _():
        for m in range(micro):
            for part in range(count // tile):
                rows = slice(part * tile, (part + 1) * tile)
                residual = res_ref[m, rows]
                out_ref[m, rows] = (residual + acc_out[m, rows] + vec_ref[12:13]).astype(bf16)
                gx, gain_part, grad = norm_rows_back(acc_gn[m, rows], residual, vec_ref[2:3])
                gm = gm_ref[m, rows].astype(f32)
                low = (gm + gx).astype(bf16)
                gb_ref[m, rows] = low
                small_ref[0:1] += gain_part
                small_ref[1:2] += grad
                small_ref[2:3] += jnp.sum(low.astype(f32), axis=0, keepdims=True)
                small_ref[3:4] += jnp.sum(gm, axis=0, keepdims=True)


def norm_rows_back(grad, values, gain):
    center = jnp.mean(values, axis=1, keepdims=True)
    centred = values - center
    variance = jnp.mean(centred * centred, axis=1, keepdims=True)
    scale = lax.rsqrt(variance + 1e-05)
    xh = centred * scale
    q = grad * gain
    gx = scale * (
        q - jnp.mean(q, axis=1, keepdims=True) - xh * jnp.mean(q * xh, axis=1, keepdims=True)
    )
    return gx, jnp.sum(grad * xh, axis=0, keepdims=True), jnp.sum(grad, axis=0, keepdims=True)


def mlp(n2, n2t, gm, res, vectors, wup, wdown):
    micro, count, width = n2.shape
    chips, cores, rows, wide = wup.shape
    steps = wide // width
    per = chips // steps

    def whole(array):
        return pl.BlockSpec(array.shape, lambda i: (0,) * array.ndim)

    def shape(dims, kind=bf16):
        return jax.ShapeDtypeStruct(dims, kind)

    tokens = pl.BlockSpec((micro, count, width), lambda i: (0, 0, 0))
    return pl.pallas_call(
        mlp_kernel,
        grid=(steps,),
        in_specs=[
            whole(n2), whole(n2t), whole(gm), whole(res), whole(vectors),
            pl.BlockSpec((chips, cores, rows, width), lambda i: (0, 0, 0, i)),
            pl.BlockSpec((per, cores, wdown.shape[2], width), lambda i: (i, 0, 0, 0)),
            pl.BlockSpec((1, width), lambda i: (0, i)),
        ],
        out_specs=[
            tokens, tokens,
            pl.BlockSpec((width, width), lambda i: (0, i)),
            pl.BlockSpec((width, width), lambda i: (i, 0)),
            pl.BlockSpec((4 + steps, width), lambda i: (0, 0)),
        ],
        out_shape=[
            shape((micro, count, width)),
            shape((micro, count, width)),
            shape((width, wide)),
            shape((wide, width)),
            shape((4 + steps, width), f32),
        ],
        scratch_shapes=[
            pltpu.VMEM((micro, count, width), f32),
            pltpu.VMEM((micro, count, width), f32),
            pltpu.VMEM((micro, count, width), bf16),
            pltpu.VMEM((micro, count, width), bf16),
        ],
        compiler_params=pltpu.CompilerParams(vmem_limit_bytes=60 * 1024 * 1024),
        name="mlp",
    )(n2, n2t, gm, res, vectors, wup, wdown, vectors[8 : 8 + steps].reshape(1, wide))


def fits(size, groups, proj_rows, down_rows):
    return groups == 2 and size % 4 == 0 and proj_rows % 16 == 0 and down_rows % 16 == 0


def on_device(
    block_input,
    out_grad,
    lengths,
    decay_rates,
    proj_weights,
    proj_moment,
    proj_average,
    down_weights,
    down_moment,
    down_average,
    vectors,
    vector_moment,
    vector_average,
    filter_net,
    net_moment,
    net_average,
    filter_out,
    final_moment,
    final_average,
):
    micro = block_input.shape[0]
    count = block_input.shape[2]
    width = block_input.shape[3]
    groups = lax.axis_size("pos")
    slot_length = count * groups
    tokens_all = micro * count
    group = lax.axis_index("pos")
    tap = vectors[13:22].reshape(3, 3 * width)
    short_bias = vectors[22:25].reshape(-1)
    in_bias = vectors[4:7].reshape(-1)
    up_bias = vectors[8:12].reshape(-1)
    skip = vectors[25]

    table = jnp.asarray(transform_table(count))
    table_low = table.astype(bf16)
    every = jnp.arange(slot_length, dtype=jnp.int32)
    here = group * count + jnp.arange(count, dtype=jnp.int32)
    mask = (here[None, :] < lengths[:, 0][:, None]).astype(f32)[:, :, None]
    tokens_low = block_input[:, 0]
    size = lax.axis_size("seq")
    tuned = fits(size, groups, proj_weights.shape[0], down_weights.shape[0])

    def make_filter(net_values, final_values):
        return filter_fn(net_values, final_values, decay_rates, every, slot_length)

    filters, filter_back = jax.vjp(make_filter, filter_net, filter_out)
    def transform(values):
        return jnp.stack([dot(table_low, values[m]) for m in range(micro)])

    def transform_back(spectrum):
        low = spectrum.astype(bf16)
        return jnp.stack([dot_tn(table_low, low[m]) for m in range(micro)]) * (1.0 / count)

    if tuned:
        (
            in_weight, out_weight, up_weight, down_weight, z_low, z_edge, short, conv, u_hat,
            kernels, residual, normed, _, normed_two, normed_two_t, y, _,
        ) = front(
            size, tokens_low, proj_weights, down_weights, vectors, filter_net, filter_out,
            decay_rates[None], mask, table_low, table_low.T, feature_table(slot_length),
        )
        in_weight = in_weight.reshape(width, 3 * width)
        out_weight = out_weight.reshape(width, width)
        z_long = jnp.concatenate([z_edge[:, 14:], z_low], axis=1).astype(f32)
        x0 = short[:, :, :width].astype(f32)
        x1 = short[:, :, width : 2 * width].astype(f32)
        v = short[:, :, 2 * width :].astype(f32)
        u = x1 * v
        conv = conv.astype(f32)
        u_hat = u_hat.astype(f32)
        kernels = kernels.astype(f32)
        normed = normed.reshape(tokens_all, width)
        y = y.reshape(tokens_all, width)
        xh_one, scale_one = norm_parts(tokens_low.astype(f32).reshape(tokens_all, width))
    else:
        low_rows = proj_weights.astype(bf16)
        in_weight = lax.all_gather(low_rows[:, : 3 * width], "seq", axis=0, tiled=True)
        out_weight = lax.all_gather(low_rows[:, 3 * width : 4 * width], "seq", axis=0, tiled=True)
        up_weight = lax.all_gather(low_rows[:, 4 * width :], "seq", axis=0, tiled=True)
        down_weight = lax.all_gather(down_weights.astype(bf16), "seq", axis=0, tiled=True)

        pieces = filters.reshape(groups, count, width)
        spectra = [
            jnp.dot(table, pieces[d], precision=lax.Precision.HIGH, preferred_element_type=f32)
            for d in range(groups)
        ]
        kernels = [spectra[0]] + [spectra[d] + turned(spectra[d - 1], 1.0) for d in range(1, groups)]

        before = passed_along(tokens_low[:, -2:], "pos", 1)
        tokens = tokens_low.astype(f32).reshape(tokens_all, width)
        xh_one, scale_one = norm_parts(tokens)
        normed = (xh_one * vectors[0] + vectors[1]).astype(bf16)
        xh_before, _ = norm_parts(before.astype(f32).reshape(micro * 2, width))
        normed_before = (xh_before * vectors[0] + vectors[1]).astype(bf16)
        z = (dot(normed, in_weight) + in_bias).reshape(micro, count, 3 * width)
        z_before = (dot(normed_before, in_weight) + in_bias).reshape(micro, 2, 3 * width)
        z_before = jnp.where(group > 0, z_before, 0.0)
        z_long = jnp.concatenate([z_before, z], axis=1)
        short = (
            tap[0] * z_long[:, 2:] + tap[1] * z_long[:, 1:-1] + tap[2] * z_long[:, :-2] + short_bias
        ).astype(bf16)
        x0 = short[:, :, :width].astype(f32)
        x1 = short[:, :, width : 2 * width].astype(f32)
        v = short[:, :, 2 * width :].astype(f32)

        u = x1 * v
        u_low = u.astype(bf16)
        u_hat = [transform(u_low)]
        for d in range(1, groups):
            u_hat.append(transform(passed_along(u_low, "pos", d)))
        total = product(kernels[0], u_hat[0])
        for d in range(1, groups):
            total = total + product(kernels[d], u_hat[d])
        conv = transform_back(total) + skip * u
        y = (mask * x0 * conv).astype(bf16).reshape(tokens_all, width)
        residual = tokens + dot(y, out_weight) + vectors[7]
        xh_two, scale_two = norm_parts(residual)
        normed_two = (xh_two * vectors[2] + vectors[3]).astype(bf16)

    if tuned:
        block_output, branch_low, up_step, down_step, small = mlp(
            normed_two, normed_two_t, out_grad[:, 0], residual, vectors, up_weight, down_weight
        )
        branch_low = branch_low.reshape(tokens_all, width)
        residual_grad = branch_low.astype(f32)
        gain_two, shift_two = small[0], small[1]
        branch_sum, cot_sum, up_bias_sum = small[2], small[3], small[4:]
    else:
        cot_low = out_grad[:, 0].reshape(tokens_all, width)
        cot = cot_low.astype(f32)
        pre = dot(normed_two, up_weight) + up_bias
        hidden, gelu_back = jax.vjp(jax.nn.gelu, pre)
        hidden_low = hidden.astype(bf16)
        block_output = (residual + dot(hidden_low, down_weight) + vectors[12]).astype(bf16)
        pre_grad = gelu_back(dot_nt(cot_low, down_weight))[0].astype(bf16)
        down_step = dot_tn(hidden_low, cot_low)
        up_step = dot_tn(normed_two, pre_grad)
        normed_two_grad = dot_nt(pre_grad, up_weight)
        part, gain_two, shift_two = norm_back(normed_two_grad, xh_two, scale_two, vectors[2])
        residual_grad = cot + part
        branch_low = residual_grad.astype(bf16)
        branch_sum = jnp.sum(branch_low.astype(f32), axis=0)
        cot_sum = jnp.sum(cot, axis=0)
        up_bias_sum = jnp.sum(pre_grad.astype(f32), axis=0).reshape(-1, width)
    out_step = dot_tn(y, branch_low)
    y_grad = dot_nt(branch_low, out_weight).astype(bf16).astype(f32).reshape(micro, count, width)

    gw = mask * y_grad
    gx0 = gw * conv
    gc = gw * x0
    gc_low = gc.astype(bf16)
    skip_grad = jnp.sum(gc * u, axis=(0, 1))
    gc_hat = [transform(gc_low)]
    for d in range(1, groups):
        gc_hat.append(transform(passed_along(gc_low, "pos", -d)))
    back = product_conj(kernels[0], gc_hat[0])
    for d in range(1, groups):
        back = back + product_conj(kernels[d], gc_hat[d])
    gu = transform_back(back) + skip * gc
    kernel_grads = [jnp.sum(product_conj(u_hat[d], gc_hat[0]), axis=0) for d in range(groups)]
    filter_grads = []
    for d in range(groups):
        got = kernel_grads[d]
        if d + 1 < groups:
            got = got + turned(kernel_grads[d + 1], -1.0)
        filter_grads.append(dot_tn(table_low, got.astype(bf16)) * (1.0 / count))
    net_local, final_local = filter_back(jnp.concatenate(filter_grads, axis=0))
    short_grad = jnp.concatenate([gx0, gu * v, gu * x1], axis=-1).astype(bf16)
    after = passed_along(short_grad[:, :2], "pos", -1)
    short_long = jnp.concatenate([short_grad, after], axis=1).astype(f32)
    z_grad = (
        tap[0] * short_long[:, :-2] + tap[1] * short_long[:, 1:-1] + tap[2] * short_long[:, 2:]
    ).astype(bf16)
    here_grad = short_long[:, :-2]
    tap_grads = [
        jnp.sum(here_grad * z_long[:, 2 - k : 2 - k + count], axis=(0, 1)) for k in range(3)
    ]
    short_bias_grad = jnp.sum(here_grad, axis=(0, 1))
    z_grad = z_grad.reshape(tokens_all, 3 * width)
    in_step = dot_tn(normed, z_grad)
    in_bias_grad = jnp.sum(z_grad.astype(f32), axis=0)
    normed_grad = dot_nt(z_grad, in_weight)
    part, gain_one, shift_one = norm_back(normed_grad, xh_one, scale_one, vectors[0])
    input_grad = (residual_grad + part).astype(bf16)

    vector_local = jnp.concatenate(
        [
            gain_one[None],
            shift_one[None],
            gain_two[None],
            shift_two[None],
            in_bias_grad.reshape(3, width),
            branch_sum[None],
            up_bias_sum,
            cot_sum[None],
            jnp.stack(tap_grads).reshape(9, width),
            short_bias_grad.reshape(3, width),
            skip_grad[None],
        ],
        axis=0,
    )
    if tuned:
        net_flat = jnp.pad(net_local, ((0, 256 - net_local.shape[0]), (0, 128 - HID)))
        rest = jnp.concatenate([vector_local, final_local], axis=0)
        rest_rows = rest.shape[0]
        rest = jnp.pad(rest, ((0, -rest_rows % (8 * size)), (0, 0)))
        down_sum, up_sum, out_sum, in_sum, rest, net_sum = reduce_all(
            size,
            [down_step.astype(bf16), up_step.astype(bf16), out_step.astype(bf16), in_step.astype(bf16)],
            [rest, net_flat],
        )
        proj_sum = jnp.concatenate([in_sum, out_sum, up_sum], axis=1)
        vector_sum = rest[: vectors.shape[0]]
        final_sum = rest[vectors.shape[0] : rest_rows]
        net_sum = net_sum[: net_local.shape[0], :HID]
    else:
        proj_local = jnp.concatenate([in_step, out_step, up_step], axis=1).astype(bf16)
        proj_shard = lax.psum_scatter(proj_local, "seq", scatter_dimension=0, tiled=True)
        down_shard = lax.psum_scatter(
            down_step.astype(bf16), "seq", scatter_dimension=0, tiled=True
        )
        proj_sum = lax.psum(proj_shard, "pos").astype(f32)
        down_sum = lax.psum(down_shard, "pos").astype(f32)
        vector_sum, net_sum, final_sum = lax.psum(
            (vector_local, net_local, final_local), ("seq", "pos")
        )
    return (
        block_output.reshape(micro, 1, count, width),
        input_grad.reshape(micro, 1, count, width),
        *nesterov(proj_weights, proj_moment, proj_average, proj_sum, 0.0001),
        *nesterov(down_weights, down_moment, down_average, down_sum, 0.0001),
        *nesterov(vectors, vector_moment, vector_average, vector_sum, 0.001),
        *nesterov(filter_net, net_moment, net_average, net_sum, 0.0001),
        *nesterov(filter_out, final_moment, final_average, final_sum, 2e-06),
    )


def solution(mesh):
    tokens = P(None, "seq", "pos", None)
    rows = P("seq", None)
    whole = P()
    return jax.shard_map(
        on_device,
        mesh=mesh,
        in_specs=(tokens, tokens, P(None, "seq"), whole) + (rows,) * 6 + (whole,) * 9,
        out_specs=(tokens, tokens) + (rows,) * 8 + (whole,) * 12,
        check_vma=False,
    )
```

```python
import functools
import math

import jax
import jax.numpy as jnp
import numpy as np
from jax import lax
from jax.experimental import pallas as pl
from jax.experimental.pallas import tpu as pltpu
from jax.sharding import PartitionSpec as P

HID = 64
EMB = 33

highest = lax.Precision.HIGHEST
f32 = jnp.float32
bf16 = jnp.bfloat16


def passed_along(block, axis, distance):
    devices = range(lax.axis_size(axis))
    route = [(i - distance, i) for i in devices if i - distance in devices]
    return lax.ppermute(block, axis, route)


def dot(a, b):
    return lax.dot_general(a, b, (((1,), (0,)), ((), ())), preferred_element_type=f32)


def dot_tn(a, b):
    return lax.dot_general(a, b, (((0,), (0,)), ((), ())), preferred_element_type=f32)


def dot_nt(a, b):
    return lax.dot_general(a, b, (((1,), (1,)), ((), ())), preferred_element_type=f32)


def features(positions, slot_length):
    band_count = (EMB - 1) // 2
    scaled = positions.astype(f32) / slot_length
    bands = 0.0001 + jnp.arange(band_count, dtype=f32) * (
        (band_count - 1 - 0.0001) / (band_count - 1)
    )
    angles = 2.0 * math.pi * scaled[:, None] * bands[None, :]
    return jnp.concatenate([scaled[:, None], jnp.cos(angles), -jnp.sin(angles)], axis=1)


def filter_fn(net_values, final_values, rates, positions, slot_length):
    embedded = features(positions, slot_length)
    frequency = net_values[EMB + 3 + 2 * HID]
    layer_one = jnp.sin(
        frequency * (jnp.dot(embedded, net_values[:EMB], precision=highest) + net_values[EMB])
    )
    layer_two = jnp.sin(
        frequency
        * (
            jnp.dot(layer_one, net_values[EMB + 1 : EMB + 1 + HID], precision=highest)
            + net_values[EMB + 1 + HID]
        )
    )
    layer_three = jnp.sin(
        frequency
        * (
            jnp.dot(layer_two, net_values[EMB + 2 + HID : EMB + 2 + 2 * HID], precision=highest)
            + net_values[EMB + 2 + 2 * HID]
        )
    )
    shaped = jnp.dot(layer_three, final_values, precision=highest)
    scaled = positions.astype(f32) / slot_length
    window = jnp.exp(-scaled[:, None] * rates[None, :]) + 0.05
    return shaped * window


def transform_table(length):
    product = np.outer(2 * np.arange(length) + 1, np.arange(length)) % (4 * length)
    angle = product.astype(np.float64) * (math.pi / (2 * length))
    return np.concatenate([np.cos(angle), -np.sin(angle)], axis=0).astype(np.float32)


def feature_table(slot_length):
    scaled = np.arange(slot_length, dtype=np.float32) / np.float32(slot_length)
    band_count = (EMB - 1) // 2
    bands = np.float32(0.0001) + np.arange(band_count, dtype=np.float32) * np.float32(
        (band_count - 1 - 0.0001) / (band_count - 1)
    )
    angles = (np.float32(2.0 * math.pi) * scaled[:, None]) * bands[None, :]
    table = np.zeros((slot_length, 4 * HID), np.float32)
    table[:, 0] = scaled
    table[:, 1 : 1 + band_count] = np.cos(angles)
    table[:, 1 + band_count : EMB] = -np.sin(angles)
    table[:, EMB] = 1.0
    return table


def halves(spectrum):
    half = spectrum.shape[-2] // 2
    return spectrum[..., :half, :], spectrum[..., half:, :]


def turned(spectrum, sign):
    re, im = halves(spectrum)
    parity = (1.0 - 2.0 * (jnp.arange(re.shape[-2]) % 2).astype(f32))[:, None] * sign
    return jnp.concatenate([-parity * im, parity * re], axis=-2)


def product(kernel, signal):
    kr, ki = halves(kernel)
    sr, si = halves(signal)
    return jnp.concatenate([kr * sr - ki * si, kr * si + ki * sr], axis=-2)


def product_conj(kernel, signal):
    kr, ki = halves(kernel)
    sr, si = halves(signal)
    return jnp.concatenate([kr * sr + ki * si, kr * si - ki * sr], axis=-2)


def nesterov(weight, moment, average, gradient, rate):
    moment_next = 0.9 * moment + gradient
    weight_next = weight - rate * (gradient + 0.9 * moment_next)
    average_next = 0.9 * average + 0.1 * weight_next
    return (gradient, weight_next, moment_next, average_next)


def norm_parts(values):
    center = jnp.mean(values, axis=-1, keepdims=True)
    centred = values - center
    variance = jnp.mean(centred * centred, axis=-1, keepdims=True)
    scale = lax.rsqrt(variance + 1e-05)
    return centred * scale, scale


def norm_back(grad, xh, scale, gain):
    q = grad * gain
    return (
        (q - jnp.mean(q, -1, keepdims=True) - xh * jnp.mean(q * xh, -1, keepdims=True)) * scale,
        jnp.sum(grad * xh, axis=0),
        jnp.sum(grad, axis=0),
    )


MESH = pl.DeviceIdType.MESH


class Ring:
    def __init__(self, size):
        self.size = size
        self.count = size // 2
        self.seq = lax.axis_index("seq")
        self.pos = lax.axis_index("pos")
        self.core = lax.rem(self.seq, 2)
        chip = self.seq // 2
        odd = lax.rem(chip, 2)
        self.place = (1 - odd) * (chip // 2) + odd * (self.count - 1 - chip // 2)

    def chip(self, shift):
        place = lax.rem(self.place + (shift + self.count), self.count)
        low = jnp.where(place < self.count // 2, 1, 0)
        return low * (2 * place) + (1 - low) * (2 * (self.count - 1 - place) + 1)

    def device(self, shift):
        return {"seq": 2 * self.chip(shift) + self.core}

    @property
    def sibling(self):
        return {"seq": self.seq + 1 - 2 * self.core}

    @property
    def across(self):
        return {"pos": 1 - self.pos}


def greet_all(ring):
    barrier = pltpu.get_barrier_semaphore()
    for step in range(1, ring.size):
        other = lax.rem(ring.seq + step, ring.size)
        pl.semaphore_signal(barrier, inc=1, device_id={"seq": other}, device_id_type=MESH)
    pl.semaphore_signal(barrier, inc=1, device_id=ring.across, device_id_type=MESH)
    pl.semaphore_wait(barrier, ring.size)


def remote(src, dst, send, recv, device):
    return pltpu.make_async_remote_copy(
        src_ref=src, dst_ref=dst, send_sem=send, recv_sem=recv, device_id=device,
        device_id_type=MESH,
    )


class Reduction:
    def __init__(self, ring, grad, twin, up, down, own, other, sems, stage=None, stage_sems=None):
        self.ring = ring
        self.grad, self.twin, self.up, self.down = grad, twin, up, down
        self.own, self.other = own, other
        self.sems = sems
        self.stage, self.stage_sems = stage, stage_sems
        self.ups = ring.count // 2
        self.downs = (ring.count - 1) // 2

    def copies(self):
        ring = self.ring
        made = [(self.grad.at[:, 1 - ring.core], self.twin, ring.sibling)]
        for step in range(self.ups):
            block = self.twin.at[ring.chip(self.ups - step)]
            made.append((block, self.up.at[step], ring.device(1)))
        for step in range(self.downs):
            block = self.twin.at[ring.chip(step - self.downs)]
            made.append((block, self.down.at[step], ring.device(-1)))
        made.append((self.own, self.other, ring.across))
        return made

    def copy(self, index):
        src, dst, device = self.copies()[index]
        return remote(src, dst, self.sems.at[0, index], self.sems.at[1, index], device)

    def begin(self):
        self.copy(0).start()

    def fetch(self, chip, slot):
        return pltpu.make_async_copy(
            self.grad.at[chip, self.ring.core], self.stage.at[slot], self.stage_sems.at[slot]
        )

    def merge(self):
        core = self.ring.core
        count = self.ring.count
        if self.stage is None:
            self.copy(0).wait_recv()

            @pl.loop(0, count)
            def _(chip):
                self.twin[chip] = self.twin[chip] + self.grad[chip, core]

        else:
            self.fetch(0, 0).start()
            self.copy(0).wait_recv()

            @pl.loop(0, count)
            def _(chip):
                slot = lax.rem(chip, 2)

                @pl.when(chip + 1 < count)
                def _():
                    self.fetch(chip + 1, 1 - slot).start()

                self.fetch(chip, slot).wait()
                self.twin[chip] = self.twin[chip] + self.stage[slot]

        self.copy(1).start()
        self.copy(1 + self.ups).start()

    def advance(self, step):
        self.copy(step).wait_recv()
        owner = self.ring.chip(self.ups - step)
        self.twin[owner] = self.twin[owner] + self.up[step - 1]
        self.copy(1 + step).start()
        if step < self.downs:
            self.copy(self.ups + step).wait_recv()
            owner = self.ring.chip(step - self.downs)
            self.twin[owner] = self.twin[owner] + self.down[step - 1]
            self.copy(1 + self.ups + step).start()

    def collect(self):
        self.copy(self.ups).wait_recv()
        self.copy(self.ups + self.downs).wait_recv()
        mine = self.ring.chip(0)
        total = (
            self.twin[mine].astype(f32)
            + self.up[self.ups - 1].astype(f32)
            + self.down[self.downs - 1].astype(f32)
        )
        self.own[...] = total.astype(bf16)
        self.copy(1 + self.ups + self.downs).start()

    def result(self):
        self.copy(1 + self.ups + self.downs).wait_recv()
        return self.own[...].astype(f32) + self.other[...].astype(f32)

    def finish(self):
        for index in range(2 + self.ups + self.downs):
            self.copy(index).wait_send()


class SmallSum:
    def __init__(self, ring, values, parts, mine, other, sums, sems):
        self.ring, self.values, self.parts = ring, values, parts
        self.mine, self.other, self.sums = mine, other, sums
        self.sems = sems
        self.rows = parts.shape[1]
        self.waiting = []

    def block(self, index):
        return pl.ds(pl.multiple_of(index * self.rows, 8), self.rows)

    def begin(self):
        ring = self.ring
        self.arriving = []
        for step in range(1, ring.size):
            other = lax.rem(ring.seq + step, ring.size)
            copy = remote(
                self.values.at[self.block(other)], self.parts.at[step],
                self.sems.at[0, step], self.sems.at[1, step], {"seq": other},
            )
            copy.start()
            self.arriving.append(copy)
            self.waiting.append(copy)

    def add_up(self):
        for copy in self.arriving:
            copy.wait_recv()
        total = self.values[self.block(self.ring.seq)]
        for step in range(1, self.ring.size):
            total = total + self.parts[step]
        self.mine[...] = total
        self.crossing = remote(
            self.mine, self.other, self.sems.at[0, 0], self.sems.at[1, 0], self.ring.across
        )
        self.crossing.start()
        self.waiting.append(self.crossing)

    def spread(self):
        self.crossing.wait_recv()
        block = self.block(self.ring.seq)
        self.sums[block] = self.mine[...] + self.other[...]
        self.arriving = []
        for step in range(1, self.ring.size):
            other = lax.rem(self.ring.seq + step, self.ring.size)
            copy = remote(
                self.sums.at[block], self.sums.at[block],
                self.sems.at[2, step], self.sems.at[3, step], {"seq": other},
            )
            copy.start()
            self.waiting.append(copy)
            back = lax.rem(self.ring.seq + (self.ring.size - step), self.ring.size)
            self.arriving.append(
                remote(
                    self.sums.at[self.block(back)], self.sums.at[self.block(back)],
                    self.sems.at[2, step], self.sems.at[3, step], {"seq": other},
                )
            )

    def finish(self):
        for copy in self.arriving:
            copy.wait_recv()
        for copy in self.waiting:
            copy.wait_send()


def reduction_scratch(size, rows, columns):
    chips = size // 2
    ups, downs = chips // 2, (chips - 1) // 2
    return [
        pltpu.VMEM((chips, rows, columns), bf16),
        pltpu.VMEM((ups, rows, columns), bf16),
        pltpu.VMEM((downs, rows, columns), bf16),
        pltpu.VMEM((rows, columns), bf16),
        pltpu.VMEM((rows, columns), bf16),
        pltpu.SemaphoreType.DMA((2, 2 + ups + downs)),
    ]


def small_scratch(size, rows, columns):
    return [
        pltpu.VMEM((size, rows // size, columns), f32),
        pltpu.VMEM((rows // size, columns), f32),
        pltpu.VMEM((rows // size, columns), f32),
        pltpu.SemaphoreType.DMA((4, size)),
    ]


class Gather:
    def __init__(self, ring, mine, full, sems):
        self.ring, self.mine, self.full, self.sems = ring, mine, full, sems
        self.ups = ring.count // 2
        self.downs = (ring.count - 1) // 2
        self.waiting, self.arriving = [], []

    def send(self, src, place, index, device):
        copy = remote(
            src, self.full.at[self.ring.chip(place), self.ring.core],
            self.sems.at[0, index], self.sems.at[1, index], device,
        )
        copy.start()
        self.waiting.append(copy)
        return copy

    def share(self, src, place, index):
        index = self.ups + self.downs + index
        self.send(src, place, index, self.ring.sibling)
        block = self.full.at[self.ring.chip(place), 1 - self.ring.core]
        self.arriving.append(
            remote(block, block, self.sems.at[0, index], self.sems.at[1, index], self.ring.sibling)
        )

    def wait_block(self, place, index, device):
        block = self.full.at[self.ring.chip(place), self.ring.core]
        remote(block, block, self.sems.at[0, index], self.sems.at[1, index], device).wait_recv()
        return block

    def begin(self):
        ring = self.ring
        self.send(self.mine, 0, 0, ring.device(1))
        self.send(self.mine, 0, self.ups, ring.device(-1))
        self.share(self.mine, 0, 0)
        self.local = pltpu.make_async_copy(
            self.mine, self.full.at[ring.chip(0), ring.core], self.sems.at[2, 0]
        )
        self.local.start()

    def advance(self, step):
        ring = self.ring
        block = self.wait_block(-step, step - 1, ring.device(1))
        if step < self.ups:
            self.send(block, -step, step, ring.device(1))
        self.share(block, -step, step)
        if step <= self.downs:
            block = self.wait_block(step, self.ups + step - 1, ring.device(-1))
            if step < self.downs:
                self.send(block, step, self.ups + step, ring.device(-1))
            self.share(block, step, self.ups + step)

    def finish(self):
        self.local.wait()
        for copy in self.arriving:
            copy.wait_recv()
        for copy in self.waiting:
            copy.wait_send()


def gather_sems(size):
    chips = size // 2
    return pltpu.SemaphoreType.DMA((3, 2 * chips))


def norm_rows(values):
    center = jnp.mean(values, axis=1, keepdims=True)
    centred = values - center
    variance = jnp.mean(centred * centred, axis=1, keepdims=True)
    return centred * lax.rsqrt(variance + 1e-05)


def front_kernel(
    size,
    x_ref, proj_ref, down_ref, vec_ref, net_ref, final_ref, rate_ref, mask_ref,
    table_ref, back_ref, feature_ref,
    win_ref, wout_ref, wup_ref, wdown_ref,
    z_ref, zh_ref, s_ref, x0_ref, conv_ref, uhat_ref, kern_ref, res_ref,
    n_ref, nt_ref, n2_ref, n2t_ref, y_ref, yt_ref, pre_ref,
    up_own, down_own, in_own, out_own, halo, halo_n, filt, zbuf, ulow, urecv, spec,
    win_sem, wout_sem, wup_sem, wdown_sem, halo_sem, u_sem,
):
    micro, count, width = x_ref.shape
    groups = 2
    slot = groups * count
    tile = 256
    tiles = width // tile
    ring = Ring(size)
    group = ring.pos
    greet_all(ring)

    in_own[...] = proj_ref[:, : 3 * width].astype(bf16)
    gather_in = Gather(ring, in_own, win_ref, win_sem)
    gather_in.begin()
    edge = remote(
        x_ref.at[:, pl.ds(count - 16, 16)], halo, halo_sem.at[0], halo_sem.at[1], ring.across
    )
    edge.start()
    out_own[...] = proj_ref[:, 3 * width : 4 * width].astype(bf16)
    up_own[...] = proj_ref[:, 4 * width :].astype(bf16)
    down_own[...] = down_ref[...].astype(bf16)
    gather_out = Gather(ring, out_own, wout_ref, wout_sem)
    gather_up = Gather(ring, up_own, wup_ref, wup_sem)
    gather_down = Gather(ring, down_own, wdown_ref, wdown_sem)

    frequency = net_ref[EMB + 3 + 2 * HID : EMB + 4 + 2 * HID]

    def filter_rows(at):
        rows = pl.ds(pl.multiple_of(at * tile, tile), tile)
        layer = jnp.dot(
            feature_ref[rows, : net_ref.shape[0]], net_ref[...], precision=highest, preferred_element_type=f32
        )
        pre_ref[rows, :HID] = layer
        layer = jnp.sin(frequency * layer)
        for i, first in ((1, EMB + 1), (2, EMB + 2 + HID)):
            layer = (
                jnp.dot(
                    layer, net_ref[first : first + HID], precision=highest,
                    preferred_element_type=f32,
                )
                + net_ref[first + HID : first + HID + 1]
            )
            pre_ref[rows, i * HID : (i + 1) * HID] = layer
            layer = jnp.sin(frequency * layer)
        shaped = jnp.dot(layer, final_ref[...], precision=highest, preferred_element_type=f32)
        at_row = lax.broadcasted_iota(jnp.int32, (tile, width), 0) + at * tile
        scaled = at_row.astype(f32) * (1.0 / slot)
        window = jnp.exp(-scaled * rate_ref[...]) + 0.05
        filt[rows] = (shaped * window).astype(bf16)

    row_blocks = slot // tile
    hops = gather_in.ups
    per = max(1, row_blocks // hops)
    for hop in range(hops):
        first, last = hop * row_blocks // hops, (hop + 1) * row_blocks // hops

        @pl.loop(first, last)
        def _(at):
            filter_rows(at)

        if hop + 1 < hops:
            gather_in.advance(hop + 1)

    gain, shift = vec_ref[0:1], vec_ref[1:2]

    @pl.loop(0, micro)
    def _(m):
        for part in range(count // tile):
            xh = norm_rows(x_ref[m, part * tile : (part + 1) * tile].astype(f32))
            normed = (xh * gain + shift).astype(bf16)
            n_ref[m, part * tile : (part + 1) * tile] = normed
            nt_ref[m, :, part * tile : (part + 1) * tile] = normed.T

    gather_in.advance(hops)
    gather_out.begin()
    gather_up.begin()
    gather_down.begin()

    parity = 1.0 - 2.0 * (
        lax.broadcasted_iota(jnp.int32, (count, tile), 0) % 2
    ).astype(f32)

    @pl.loop(0, tiles)
    def _(j):
        cols = pl.ds(pl.multiple_of(j * tile, tile), tile)
        zero = dot(table_ref[...], filt[:count, cols])
        kern_ref[0, :, cols] = zero.astype(bf16)
        one = dot(table_ref[...], filt[count:, cols])
        kern_ref[1, :count, cols] = (one[:count] - parity * zero[count:]).astype(bf16)
        kern_ref[1, count:, cols] = (one[count:] + parity * zero[:count]).astype(bf16)

    edge.wait_recv()
    for m in range(micro):
        xh = norm_rows(halo[m].astype(f32))
        halo_n[m] = (xh * gain + shift).astype(bf16)
    gather_in.finish()
    gather_out.advance(1)
    inside = jnp.where(group > 0, 1.0, 0.0).astype(f32)

    def project(m, j):
        parts = []
        for p in range(3):
            lane = pl.ds(pl.multiple_of(j * tile, tile), tile)
            cols = pl.ds(pl.multiple_of(p * width + j * tile, tile), tile)
            weight = win_ref[:, :, :, cols].reshape(width, tile)
            bias = vec_ref[4 + p : 5 + p, lane]
            z = dot(n_ref[m], weight) + bias
            zh = (dot(halo_n[m], weight) + bias) * inside
            z_ref[m, :, cols] = z.astype(bf16)
            zh_ref[m, :, cols] = zh.astype(bf16)
            zbuf[:16] = zh
            zbuf[16:] = z
            short = (
                vec_ref[13 + p : 14 + p, lane] * z
                + vec_ref[16 + p : 17 + p, lane] * zbuf[15 : 15 + count]
                + vec_ref[19 + p : 20 + p, lane] * zbuf[14 : 14 + count]
                + vec_ref[22 + p : 23 + p, lane]
            ).astype(bf16)
            if p == 0:
                x0_ref[m, :, lane] = short
            s_ref[m, :, cols] = short
            parts.append(short)
        lane = pl.ds(pl.multiple_of(j * tile, tile), tile)
        ulow[m, :, lane] = (parts[1].astype(f32) * parts[2].astype(f32)).astype(bf16)

    sent = []
    for m in range(micro):

        @pl.loop(0, tiles)
        def _(j):
            project(m, j)

        copy = remote(
            ulow.at[m], urecv.at[m], u_sem.at[0, m], u_sem.at[1, m], ring.across
        )
        copy.start()
        sent.append(copy)
        if m == 0:
            gather_up.advance(1)
            gather_out.advance(2)

    gather_down.advance(1)
    gather_out.advance(3)

    for m in range(micro):

        @pl.loop(0, tiles)
        def _(j):
            lane = pl.ds(pl.multiple_of(j * tile, tile), tile)
            uhat_ref[0, m, :, lane] = dot(table_ref[...], ulow[m, :, lane]).astype(bf16)

    gather_up.advance(2)
    gather_out.advance(4)
    gather_out.finish()

    def mix(m, j):
        lane = pl.ds(pl.multiple_of(j * tile, tile), tile)
        other = dot(table_ref[...], urecv[m, :, lane]) * inside
        uhat_ref[1, m, :, lane] = other.astype(bf16)
        k0r, k0i = kern_ref[0, :count, lane].astype(f32), kern_ref[0, count:, lane].astype(f32)
        k1r, k1i = kern_ref[1, :count, lane].astype(f32), kern_ref[1, count:, lane].astype(f32)
        ur = uhat_ref[0, m, :count, lane].astype(f32)
        ui = uhat_ref[0, m, count:, lane].astype(f32)
        vr, vi = other[:count], other[count:]
        spec[:count] = (k0r * ur - k0i * ui + k1r * vr - k1i * vi).astype(bf16)
        spec[count:] = (k0r * ui + k0i * ur + k1r * vi + k1i * vr).astype(bf16)
        gated = s_ref[m, :, pl.ds(pl.multiple_of(width + j * tile, tile), tile)].astype(
            f32
        ) * s_ref[m, :, pl.ds(pl.multiple_of(2 * width + j * tile, tile), tile)].astype(f32)
        conv = dot(back_ref[...], spec[...]) * (1.0 / count) + vec_ref[25:26, lane] * gated
        conv_ref[m, :, lane] = conv.astype(bf16)
        y = (mask_ref[m] * s_ref[m, :, lane].astype(f32) * conv).astype(bf16)
        y_ref[m, :, lane] = y

    for m in range(micro):
        sent[m].wait_recv()

        @pl.loop(0, tiles)
        def _(j):
            mix(m, j)

        for part in range(count // tile):
            rows = slice(part * tile, (part + 1) * tile)
            y = y_ref[m, rows]
            yt_ref[m, :, rows] = y.T
            residual = (
                x_ref[m, rows].astype(f32)
                + dot(y, wout_ref[...].reshape(width, width))
                + vec_ref[7:8]
            )
            res_ref[m, rows] = residual
            normed = (norm_rows(residual) * vec_ref[2:3] + vec_ref[3:4]).astype(bf16)
            n2_ref[m, rows] = normed
            n2t_ref[m, :, rows] = normed.T
        if m == 0:
            gather_down.advance(2)
            gather_up.advance(3)
    gather_down.advance(3)
    gather_up.advance(4)
    gather_down.advance(4)
    gather_up.finish()
    gather_down.finish()
    edge.wait_send()
    for copy in sent:
        copy.wait_send()


def front(size, x, proj, down, vectors, net, final, rates, mask, table, table_back, feature):
    chips = size // 2
    micro, count, width = x.shape
    wide = down.shape[0] * size
    rows, down_rows = proj.shape[0], down.shape[0]
    vmem = pl.BlockSpec(memory_space=pltpu.VMEM)
    anywhere = pl.BlockSpec(memory_space=pl.ANY)

    def shape(dims, kind=bf16):
        return jax.ShapeDtypeStruct(dims, kind)

    outs = pl.pallas_call(
        functools.partial(front_kernel, size),
        out_shape=[
            shape((chips, 2, rows, 3 * width)),
            shape((chips, 2, rows, width)),
            shape((chips, 2, rows, wide)),
            shape((chips, 2, down_rows, width)),
            shape((micro, count, 3 * width)),
            shape((micro, 16, 3 * width)),
            shape((micro, count, 3 * width)),
            shape((micro, count, width)),
            shape((micro, count, width)),
            shape((2, micro, 2 * count, width)),
            shape((2, 2 * count, width)),
            shape((micro, count, width), f32),
            shape((micro, count, width)),
            shape((micro, width, count)),
            shape((micro, count, width)),
            shape((micro, width, count)),
            shape((micro, count, width)),
            shape((micro, width, count)),
            shape((2 * count, 4 * HID), f32),
        ],
        in_specs=[vmem] * 11,
        out_specs=[vmem, vmem, anywhere, anywhere] + [vmem] * 15,
        scratch_shapes=[
            pltpu.VMEM((rows, wide), bf16),
            pltpu.VMEM((down_rows, width), bf16),
            pltpu.VMEM((rows, 3 * width), bf16),
            pltpu.VMEM((rows, width), bf16),
            pltpu.VMEM((micro, 16, width), bf16),
            pltpu.VMEM((micro, 16, width), bf16),
            pltpu.VMEM((2 * count, width), bf16),
            pltpu.VMEM((16 + count, 256), f32),
            pltpu.VMEM((micro, count, width), bf16),
            pltpu.VMEM((micro, count, width), bf16),
            pltpu.VMEM((2 * count, 256), bf16),
            gather_sems(size),
            gather_sems(size),
            gather_sems(size),
            gather_sems(size),
            pltpu.SemaphoreType.DMA((2,)),
            pltpu.SemaphoreType.DMA((2, micro)),
        ],
        compiler_params=pltpu.CompilerParams(
            collective_id=0, has_side_effects=True, vmem_limit_bytes=62 * 1024 * 1024
        ),
        name="front",
    )(x, proj, down, vectors, net, final, rates, mask, table, table_back, feature)
    return outs


GELU_SCALE = math.sqrt(2.0 / math.pi)


def gelu_pair(a):
    square = a * a
    bend = jnp.tanh(GELU_SCALE * a * (1.0 + 0.044715 * square))
    half = 0.5 * (1.0 + bend)
    slope = half + (0.5 * GELU_SCALE) * a * (1.0 - bend * bend) * (1.0 + 0.134145 * square)
    return a * half, slope


def mlp_kernel(
    n2_ref, n2t_ref, gm_ref, res_ref, vec_ref, wup_ref, wdown_ref, bias_ref,
    out_ref, gb_ref, dup_ref, ddown_ref, small_ref,
    acc_out, acc_gn, hid_ref, ga_ref,
):
    step, last = pl.program_id(0), pl.num_programs(0) - 1
    micro, count, width = n2_ref.shape
    chunk = bias_ref.shape[1]
    tile = 256
    wup = wup_ref[...].reshape(width, chunk)
    wdown = wdown_ref[...].reshape(chunk, width)
    bias = bias_ref[...]

    @pl.when(step == 0)
    def _():
        acc_out[...] = jnp.zeros_like(acc_out)
        acc_gn[...] = jnp.zeros_like(acc_gn)
        small_ref[...] = jnp.zeros_like(small_ref)

    bias_sum = jnp.zeros((1, chunk), f32)
    for m in range(micro):
        for part in range(count // tile):
            rows = slice(part * tile, (part + 1) * tile)
            hidden, slope = gelu_pair(dot(n2_ref[m, rows], wup) + bias)
            hidden = hidden.astype(bf16)
            ga = (dot_nt(gm_ref[m, rows], wdown) * slope).astype(bf16)
            hid_ref[m, rows] = hidden
            ga_ref[m, rows] = ga
            bias_sum = bias_sum + jnp.sum(ga.astype(f32), axis=0, keepdims=True)
            acc_out[m, rows] += dot(hidden, wdown)
            acc_gn[m, rows] += dot_nt(ga, wup)
    small_ref[pl.ds(4 + step, 1)] = bias_sum
    down_total = dot_tn(hid_ref[0], gm_ref[0])
    up_total = dot(n2t_ref[0], ga_ref[0])
    for m in range(1, micro):
        down_total = down_total + dot_tn(hid_ref[m], gm_ref[m])
        up_total = up_total + dot(n2t_ref[m], ga_ref[m])
    ddown_ref[...] = down_total.astype(bf16)
    dup_ref[...] = up_total.astype(bf16)

    @pl.when(step == last)
    def _():
        for m in range(micro):
            for part in range(count // tile):
                rows = slice(part * tile, (part + 1) * tile)
                residual = res_ref[m, rows]
                out_ref[m, rows] = (residual + acc_out[m, rows] + vec_ref[12:13]).astype(bf16)
                gx, gain_part, grad = norm_rows_back(acc_gn[m, rows], residual, vec_ref[2:3])
                gm = gm_ref[m, rows].astype(f32)
                low = (gm + gx).astype(bf16)
                gb_ref[m, rows] = low
                small_ref[0:1] += gain_part
                small_ref[1:2] += grad
                small_ref[2:3] += jnp.sum(low.astype(f32), axis=0, keepdims=True)
                small_ref[3:4] += jnp.sum(gm, axis=0, keepdims=True)


def norm_rows_back(grad, values, gain):
    center = jnp.mean(values, axis=1, keepdims=True)
    centred = values - center
    variance = jnp.mean(centred * centred, axis=1, keepdims=True)
    scale = lax.rsqrt(variance + 1e-05)
    xh = centred * scale
    q = grad * gain
    gx = scale * (
        q - jnp.mean(q, axis=1, keepdims=True) - xh * jnp.mean(q * xh, axis=1, keepdims=True)
    )
    return gx, jnp.sum(grad * xh, axis=0, keepdims=True), jnp.sum(grad, axis=0, keepdims=True)


def mlp(n2, n2t, gm, res, vectors, wup, wdown):
    micro, count, width = n2.shape
    chips, cores, rows, wide = wup.shape
    steps = wide // width
    per = chips // steps

    def whole(array):
        return pl.BlockSpec(array.shape, lambda i: (0,) * array.ndim)

    def shape(dims, kind=bf16):
        return jax.ShapeDtypeStruct(dims, kind)

    tokens = pl.BlockSpec((micro, count, width), lambda i: (0, 0, 0))
    return pl.pallas_call(
        mlp_kernel,
        grid=(steps,),
        in_specs=[
            whole(n2), whole(n2t), whole(gm), whole(res), whole(vectors),
            pl.BlockSpec((chips, cores, rows, width), lambda i: (0, 0, 0, i)),
            pl.BlockSpec((per, cores, wdown.shape[2], width), lambda i: (i, 0, 0, 0)),
            pl.BlockSpec((1, width), lambda i: (0, i)),
        ],
        out_specs=[
            tokens, tokens,
            pl.BlockSpec((width, width), lambda i: (0, i)),
            pl.BlockSpec((width, width), lambda i: (i, 0)),
            pl.BlockSpec((4 + steps, width), lambda i: (0, 0)),
        ],
        out_shape=[
            shape((micro, count, width)),
            shape((micro, count, width)),
            shape((width, wide)),
            shape((wide, width)),
            shape((4 + steps, width), f32),
        ],
        scratch_shapes=[
            pltpu.VMEM((micro, count, width), f32),
            pltpu.VMEM((micro, count, width), f32),
            pltpu.VMEM((micro, count, width), bf16),
            pltpu.VMEM((micro, count, width), bf16),
        ],
        compiler_params=pltpu.CompilerParams(vmem_limit_bytes=60 * 1024 * 1024),
        name="mlp",
    )(n2, n2t, gm, res, vectors, wup, wdown, vectors[8 : 8 + steps].reshape(1, wide))


BACK_STREAMS = ("up", "down", "out", "in")


def back_kernel(size, names, *refs):
    ref = dict(zip(names, refs))
    x_ref, gb_ref, win_ref, wout_ref = ref["x"], ref["gb"], ref["win"], ref["wout"]
    vec_ref, mask_ref = ref["vec"], ref["mask"]
    table_ref, back_ref, zh_ref = ref["table"], ref["back"], ref["zh"]
    micro, count, width = x_ref.shape
    slot = 2 * count
    tile = 256
    tiles = width // tile
    ring = Ring(size)
    gw, gc, gcr, gz = ref["gw"], ref["gc"], ref["gcr"], ref["gz"]
    vsum, nsum = ref["vsum"], ref["nsum"]
    inside = jnp.where(ring.pos < 1, 1.0, 0.0).astype(f32)

    x0_ref, turned_ref = ref["gate"], ref["across"]

    def bring(name, dst, index):
        copy = pltpu.make_async_copy(ref[name], dst, ref["bring_sems"].at[index])
        copy.start()
        return copy

    gate_copy = bring("x0", x0_ref, 0)
    turned_copy = bring("yt", turned_ref, 1)
    greet_all(ring)
    red = {}
    for name in BACK_STREAMS:
        parts = [ref[name + "_" + k] for k in ("twin", "ups", "downs", "own", "other", "sems")]
        staged = name in ("up", "down")
        red[name] = Reduction(
            ring, ref["d" + name], *parts,
            stage=ref[name + "_stage"] if staged else None,
            stage_sems=ref[name + "_stage_sems"] if staged else None,
        )
    red["down"].begin()
    red["up"].begin()
    vsum[...] = jnp.zeros_like(vsum)
    nsum[...] = jnp.zeros_like(nsum)
    small = ref["small"]
    vsum[2:4] = small[0:2]
    vsum[7:8] = small[2:3]
    vsum[12:13] = small[3:4]
    vsum[8:12] = small[4:8]

    crossing = []
    gate_copy.wait()
    for m in range(micro):
        for part in range(count // tile):
            rows = slice(part * tile, (part + 1) * tile)
            gy = dot_nt(gb_ref[m, rows], wout_ref[...].reshape(width, width))
            gated = mask_ref[m, rows] * gy.astype(bf16).astype(f32)
            gw[m, rows] = gated.astype(bf16)
            gc[m, rows] = (gated * x0_ref[m, rows].astype(f32)).astype(bf16)
        copy = remote(
            gc.at[m], gcr.at[m], ref["gc_sem"].at[0, m], ref["gc_sem"].at[1, m], ring.across
        )
        copy.start()
        crossing.append(copy)

    def out_grad(j):
        cols = pl.ds(pl.multiple_of(j * tile, tile), tile)
        total = dot(turned_ref[0], gb_ref[0, :, cols])
        for m in range(1, micro):
            total = total + dot(turned_ref[m], gb_ref[m, :, cols])
        dout = ref["dout"]
        dout[:, :, :, cols] = total.astype(bf16).reshape(dout.shape[:3] + (tile,))

    turned_copy.wait()

    @pl.loop(0, tiles)
    def _(j):
        out_grad(j)

    turned_copy = bring("nt", turned_ref, 1)
    red["out"].begin()
    red["down"].merge()
    red["up"].merge()

    parity = 1.0 - 2.0 * (
        lax.broadcasted_iota(jnp.int32, (count, tile), 0) % 2
    ).astype(f32)
    gated_s, zs, uh, kn = ref["s_buf"], ref["z_buf"], ref["u_buf"], ref["k_buf"]
    gk = ref["gk"]
    gbuf, zbuf, spec = ref["gbuf"], ref["zbuf"], ref["spec"]
    first_rows, last_rows, next_rows = ref["first_rows"], ref["last_rows"], ref["next_rows"]
    total_steps = tiles * micro

    def loads(at, slot_at):
        j, m = at // micro, lax.rem(at, micro)
        lane = pl.multiple_of(j * tile, tile)
        made = []
        for p in range(2):
            cols = pl.ds(pl.multiple_of((p + 1) * width + lane, tile), tile)
            made.append((ref["s"].at[m, :, cols], gated_s.at[slot_at, p]))
        for p in range(3):
            cols = pl.ds(pl.multiple_of(p * width + lane, tile), tile)
            made.append((ref["z"].at[m, :, cols], zs.at[slot_at, p]))
        for d in range(2):
            made.append((ref["uhat"].at[d, m, :, pl.ds(lane, tile)], uh.at[slot_at, d]))
        made.append((ref["conv"].at[m, :, pl.ds(lane, tile)], ref["c_buf"].at[slot_at]))
        return [
            pltpu.make_async_copy(src, dst, ref["load_sems"].at[slot_at, i])
            for i, (src, dst) in enumerate(made)
        ]

    def load_kernel(at):
        lane = pl.ds(pl.multiple_of((at // micro) * tile, tile), tile)
        return pltpu.make_async_copy(
            ref["kern"].at[:, :, lane], kn, ref["bring_sems"].at[2]
        )

    for copy in loads(0, 0):
        copy.start()
    for copy in crossing:
        copy.wait_recv()
    red["out"].merge()
    red["down"].advance(1)
    red["up"].advance(1)
    gbuf[count:] = jnp.zeros_like(gbuf[count:])

    def unmix(at):
        j, m = at // micro, lax.rem(at, micro)
        slot_at = lax.rem(at, 2)
        lane = pl.ds(pl.multiple_of(j * tile, tile), tile)

        @pl.when(m == 0)
        def _():
            load_kernel(at).start()

        for copy in loads(at, slot_at):
            copy.wait()

        @pl.when(at + 1 < total_steps)
        def _():
            for copy in loads(at + 1, 1 - slot_at):
                copy.start()

        hat = dot(table_ref[...], gc[m, :, lane])
        far = dot(table_ref[...], gcr[m, :, lane]) * inside
        gr, gi = hat[:count], hat[count:]
        hr, hi = far[:count], far[count:]

        @pl.when(m == 0)
        def _():
            load_kernel(at).wait()

        k0r, k0i = kn[0, :count].astype(f32), kn[0, count:].astype(f32)
        k1r, k1i = kn[1, :count].astype(f32), kn[1, count:].astype(f32)
        spec[:count] = (k0r * gr + k0i * gi + k1r * hr + k1i * hi).astype(bf16)
        spec[count:] = (k0r * gi - k0i * gr + k1r * hi - k1i * hr).astype(bf16)
        keep = jnp.where(m > 0, 1.0, 0.0).astype(f32)
        for d in range(2):
            ur, ui = uh[slot_at, d, :count].astype(f32), uh[slot_at, d, count:].astype(f32)
            gk[d, :count] = gk[d, :count] * keep + (ur * gr + ui * gi)
            gk[d, count:] = gk[d, count:] * keep + (ur * gi - ui * gr)
        x1 = gated_s[slot_at, 0].astype(f32)
        v = gated_s[slot_at, 1].astype(f32)
        gate = gw[m, :, lane].astype(f32)
        gc_full = gate * x0_ref[m, :, lane].astype(f32)
        gu = dot(back_ref[...], spec[...]) * (1.0 / count) + vec_ref[25:26, lane] * gc_full
        vsum[25:26, lane] += jnp.sum(gc_full * x1 * v, axis=0, keepdims=True)
        for p in range(3):
            if p == 0:
                grad = gate * ref["c_buf"][slot_at].astype(f32)
            else:
                grad = gu * (v if p == 1 else x1)
            low = grad.astype(bf16)
            grad = low.astype(f32)
            cols = pl.ds(pl.multiple_of(p * width + j * tile, tile), tile)
            first_rows[m, :, cols] = low[:16]
            last_rows[m, :, cols] = low[count - 16 :]
            gbuf[:count] = grad
            gz[m, :, cols] = (
                vec_ref[13 + p : 14 + p, lane] * grad
                + vec_ref[16 + p : 17 + p, lane] * gbuf[1 : 1 + count]
                + vec_ref[19 + p : 20 + p, lane] * gbuf[2 : 2 + count]
            ).astype(bf16)
            zbuf[:16] = zh_ref[m, :, cols].astype(f32)
            zbuf[16:] = zs[slot_at, p].astype(f32)
            for k in range(3):
                row = 13 + 3 * k + p
                vsum[row : row + 1, lane] += jnp.sum(
                    grad * zbuf[16 - k : 16 - k + count], axis=0, keepdims=True
                )
            vsum[22 + p : 23 + p, lane] += jnp.sum(grad, axis=0, keepdims=True)

        @pl.when(m == micro - 1)
        def _():
            g1r, g1i = gk[1, :count], gk[1, count:]
            spec[:count] = (gk[0, :count] + parity * g1i).astype(bf16)
            spec[count:] = (gk[0, count:] - parity * g1r).astype(bf16)
            x0_ref[0, :, lane] = (dot(back_ref[...], spec[...]) * (1.0 / count)).astype(bf16)
            spec[:count] = g1r.astype(bf16)
            spec[count:] = g1i.astype(bf16)
            x0_ref[1, :, lane] = (dot(back_ref[...], spec[...]) * (1.0 / count)).astype(bf16)

    @pl.loop(0, total_steps)
    def _(at):
        unmix(at)

        @pl.when(at == total_steps // 3)
        def _():
            red["down"].advance(2)
            red["up"].advance(2)
            red["out"].advance(1)

    edge = remote(
        first_rows, next_rows, ref["edge_sem"].at[0], ref["edge_sem"].at[1], ring.across
    )
    edge.start()
    x_copy = bring("x", gw, 0)
    pre_copy = bring("pre", gk.at[0], 2)
    feature_copy = bring("feature", gk.at[1], 3)
    red["down"].advance(3)
    red["up"].advance(3)
    red["out"].advance(2)
    edge.wait_recv()
    for m in range(micro):
        for p in range(3):
            cols = slice(p * width, (p + 1) * width)
            own = last_rows[m, :, cols].astype(f32)
            ebuf = ref["ebuf"]
            ebuf[:16] = own
            ebuf[16:] = next_rows[m, :, cols].astype(f32) * inside
            gz[m, count - 16 :, cols] = (
                vec_ref[13 + p : 14 + p] * own
                + vec_ref[16 + p : 17 + p] * ebuf[1:17]
                + vec_ref[19 + p : 20 + p] * ebuf[2:18]
            ).astype(bf16)

    turned_copy.wait()
    for p in range(3):

        @pl.loop(0, tiles)
        def _(j):
            cols = pl.ds(pl.multiple_of(p * width + j * tile, tile), tile)
            lane = pl.ds(pl.multiple_of(j * tile, tile), tile)
            total = dot(turned_ref[0], gz[0, :, cols])
            bias = jnp.sum(gz[0, :, cols].astype(f32), axis=0, keepdims=True)
            for m in range(1, micro):
                total = total + dot(turned_ref[m], gz[m, :, cols])
                bias = bias + jnp.sum(gz[m, :, cols].astype(f32), axis=0, keepdims=True)
            din = ref["din"]
            din[:, :, :, cols] = total.astype(bf16).reshape(din.shape[:3] + (tile,))
            vsum[4 + p : 5 + p, lane] = bias

    red["in"].begin()
    red["out"].advance(3)
    red["down"].collect()
    red["up"].collect()
    x_copy.wait()
    for copy in crossing:
        copy.wait_send()
    for m in range(micro):
        for part in range(count // tile):
            rows = slice(part * tile, (part + 1) * tile)
            grad = dot_nt(gz[m, rows], win_ref[...].reshape(width, 3 * width))
            gx, gain_part, shift_part = norm_rows_back(
                grad, gw[m, rows].astype(f32), vec_ref[0:1]
            )
            gc[m, rows] = (gb_ref[m, rows].astype(f32) + gx).astype(bf16)
            vsum[0:1] += gain_part
            vsum[1:2] += shift_part
        if m == 0:
            red["in"].merge()
            red["out"].collect()

    grad_copy = pltpu.make_async_copy(gc, ref["input_grad"], ref["bring_sems"].at[0])
    grad_copy.start()

    net_ref = ref["net"]
    pre_copy.wait()
    feature_copy.wait()
    frequency = net_ref[EMB + 3 + 2 * HID : EMB + 4 + 2 * HID]
    final_low = ref["final"][...].astype(bf16)

    def filter_back(at):
        rows = pl.ds(pl.multiple_of(at * tile, tile), tile)
        at_row = lax.broadcasted_iota(jnp.int32, (tile, width), 0) + at * tile
        scaled = at_row.astype(f32) * (1.0 / slot)
        window = jnp.exp(-scaled * ref["rate"][...]) + 0.05
        half, inner = at // (count // tile), lax.rem(at, count // tile)
        held = x0_ref[half, pl.ds(pl.multiple_of(inner * tile, tile), tile)]
        shaped = (held.astype(f32) * window).astype(bf16)
        layers = [gk[0, rows, i * HID : (i + 1) * HID] for i in range(3)]
        acts = [jnp.sin(frequency * layer) for layer in layers]
        slopes = [jnp.cos(frequency * layer) for layer in layers]
        vsum[FINAL_ROW : FINAL_ROW + HID] += dot_tn(acts[2].astype(bf16), shaped)
        grad = dot_nt(shaped, final_low)
        freq_sum = jnp.zeros_like(frequency)
        for i in (2, 1, 0):
            turn = grad * slopes[i]
            freq_sum = freq_sum + jnp.sum(turn * layers[i], axis=0, keepdims=True)
            grad = turn * frequency
            if i == 0:
                nsum[: EMB + 1, :HID] += lax.dot_general(
                    gk[1, rows, : EMB + 1], grad, (((0,), (0,)), ((), ())),
                    precision=highest, preferred_element_type=f32,
                )
            else:
                first = EMB + 1 if i == 1 else EMB + 2 + HID
                nsum[first : first + HID, :HID] += lax.dot_general(
                    acts[i - 1], grad, (((0,), (0,)), ((), ())),
                    precision=highest, preferred_element_type=f32,
                )
                nsum[first + HID : first + HID + 1, :HID] += jnp.sum(grad, axis=0, keepdims=True)
                grad = lax.dot_general(
                    grad, net_ref[first : first + HID], (((1,), (1,)), ((), ())),
                    precision=highest, preferred_element_type=f32,
                )
        row = EMB + 3 + 2 * HID
        nsum[row : row + 1, :HID] += freq_sum

    blocks = slot // tile

    @pl.loop(0, blocks // 2)
    def _(at):
        filter_back(at)

    red["in"].advance(1)

    @pl.loop(blocks // 2, blocks)
    def _(at):
        filter_back(at)

    smalls = []
    for name, values in (("v", vsum), ("n", nsum)):
        parts = [ref[name + "_" + k] for k in ("parts", "mine", "other")]
        smalls.append(SmallSum(ring, values, *parts, ref[name + "_out"], ref[name + "_sems"]))
    for work in smalls:
        work.begin()
    red["in"].advance(2)
    for work in smalls:
        work.add_up()
    psum = ref["proj_sum"]
    wide = psum.shape[1] - 4 * width
    ref["down_sum"][...] = red["down"].result()
    psum[:, 4 * width : 4 * width + wide] = red["up"].result()
    psum[:, 3 * width : 4 * width] = red["out"].result()
    for work in smalls:
        work.spread()
    red["in"].advance(3)
    red["in"].collect()
    for work in smalls:
        work.finish()
    psum[:, : 3 * width] = red["in"].result()
    for work in red.values():
        work.finish()
    grad_copy.wait()
    edge.wait_send()


FINAL_ROW = 32


def back(size, arrays, dup, ddown):
    chips = size // 2
    micro, count, width = arrays["x"].shape
    rows, wide = dup.shape[2], dup.shape[3]
    down_rows = ddown.shape[2]
    vmem = pl.BlockSpec(memory_space=pltpu.VMEM)
    anywhere = pl.BlockSpec(memory_space=pl.ANY)
    arrays = dict(arrays, dup=dup, ddown=ddown)
    far = (
        "s", "z", "uhat", "kern", "dup", "ddown", "x", "x0", "yt", "nt", "conv", "pre", "feature"
    )
    specs = [anywhere if name in far else vmem for name in arrays]
    small_rows = 8 * size
    outs = {
        "input_grad": jax.ShapeDtypeStruct((micro, count, width), bf16),
        "proj_sum": jax.ShapeDtypeStruct((rows, 4 * width + wide), f32),
        "down_sum": jax.ShapeDtypeStruct((down_rows, width), f32),
        "v_out": jax.ShapeDtypeStruct((small_rows, width), f32),
        "n_out": jax.ShapeDtypeStruct((2 * small_rows, 128), f32),
    }
    dma = pltpu.SemaphoreType.DMA
    scratch = {
        "din": pltpu.VMEM((chips, 2, rows, 3 * width), bf16),
        "dout": pltpu.VMEM((chips, 2, rows, width), bf16),
        "gw": pltpu.VMEM((micro, count, width), bf16),
        "gc": pltpu.VMEM((micro, count, width), bf16),
        "gcr": pltpu.VMEM((micro, count, width), bf16),
        "gz": pltpu.VMEM((micro, count, 3 * width), bf16),
        "vsum": pltpu.VMEM((small_rows, width), f32),
        "nsum": pltpu.VMEM((2 * small_rows, 128), f32),
        "gate": pltpu.VMEM((micro, count, width), bf16),
        "across": pltpu.VMEM((micro, width, count), bf16),
        "c_buf": pltpu.VMEM((2, count, 256), bf16),
        "bring_sems": dma((4,)),
        "gk": pltpu.VMEM((2, 2 * count, 256), f32),
        "gbuf": pltpu.VMEM((count + 16, 256), f32),
        "zbuf": pltpu.VMEM((count + 16, 256), f32),
        "ebuf": pltpu.VMEM((32, width), f32),
        "spec": pltpu.VMEM((2 * count, 256), bf16),
        "first_rows": pltpu.VMEM((micro, 16, 3 * width), bf16),
        "last_rows": pltpu.VMEM((micro, 16, 3 * width), bf16),
        "next_rows": pltpu.VMEM((micro, 16, 3 * width), bf16),
        "s_buf": pltpu.VMEM((2, 2, count, 256), bf16),
        "z_buf": pltpu.VMEM((2, 3, count, 256), bf16),
        "u_buf": pltpu.VMEM((2, 2, 2 * count, 256), bf16),
        "k_buf": pltpu.VMEM((2, 2 * count, 256), bf16),
        "load_sems": dma((2, 8)),
        "gc_sem": dma((2, micro)),
        "edge_sem": dma((2,)),
        "up_stage": pltpu.VMEM((2, rows, wide), bf16),
        "down_stage": pltpu.VMEM((2, down_rows, width), bf16),
        "up_stage_sems": dma((2,)),
        "down_stage_sems": dma((2,)),
    }
    parts = ("twin", "ups", "downs", "own", "other", "sems")
    for name, dims in (
        ("up", (rows, wide)), ("down", (down_rows, width)), ("out", (rows, width)),
        ("in", (rows, 3 * width)),
    ):
        for part, made in zip(parts, reduction_scratch(size, *dims)):
            scratch[name + "_" + part] = made
    for name in ("v", "n"):
        dims = outs[name + "_out"].shape
        for part, made in zip(("parts", "mine", "other", "sems"), small_scratch(size, *dims)):
            scratch[name + "_" + part] = made
    names = tuple(arrays) + tuple(outs) + tuple(scratch)
    return pl.pallas_call(
        functools.partial(back_kernel, size, names),
        out_shape=list(outs.values()),
        in_specs=specs,
        out_specs=[anywhere] + [vmem] * (len(outs) - 1),
        scratch_shapes=list(scratch.values()),
        compiler_params=pltpu.CompilerParams(
            collective_id=1, has_side_effects=True, vmem_limit_bytes=63 * 1024 * 1024
        ),
        name="back",
    )(*arrays.values())


def fits(size, groups, tokens, proj_weights, down_weights):
    micro, _, count, width = tokens.shape
    wide = down_weights.shape[0] * size
    return (
        groups == 2
        and size % 4 == 0
        and size <= 16
        and proj_weights.shape[0] % 16 == 0
        and down_weights.shape[0] % 16 == 0
        and count % 256 == 0
        and width % 256 == 0
        and micro >= groups
        and micro * count <= 1024
        and wide % width == 0
        and size // 2 % (wide // width) == 0
        and proj_weights.shape[1] == 4 * width + wide
    )


def on_device_tuned(
    block_input,
    out_grad,
    lengths,
    decay_rates,
    proj_weights,
    proj_moment,
    proj_average,
    down_weights,
    down_moment,
    down_average,
    vectors,
    vector_moment,
    vector_average,
    filter_net,
    net_moment,
    net_average,
    filter_out,
    final_moment,
    final_average,
):
    micro = block_input.shape[0]
    count = block_input.shape[2]
    width = block_input.shape[3]
    size = lax.axis_size("seq")
    slot_length = count * lax.axis_size("pos")
    here = lax.axis_index("pos") * count + jnp.arange(count, dtype=jnp.int32)
    mask = (here[None, :] < lengths[:, 0][:, None]).astype(f32)[:, :, None]
    tokens = block_input[:, 0]
    plain_table = transform_table(count)
    table = jnp.asarray(plain_table, dtype=bf16)
    table_back = jnp.asarray(plain_table.T, dtype=bf16)
    feature = jnp.asarray(feature_table(slot_length))
    rates = decay_rates[None]
    (
        in_weight, out_weight, up_weight, down_weight, z, z_edge, short, x_zero, conv, u_hat,
        kernels, residual, _, normed_t, normed_two, normed_two_t, _, y_t, pre,
    ) = front(
        size, tokens, proj_weights, down_weights, vectors, filter_net, filter_out, rates, mask,
        table, table_back, feature,
    )
    block_output, branch_grad, up_step, down_step, small = mlp(
        normed_two, normed_two_t, out_grad[:, 0], residual, vectors, up_weight, down_weight
    )
    chips = size // 2
    input_grad, proj_sum, down_sum, rest, net_sum = back(
        size,
        {
            "x": tokens, "gb": branch_grad, "win": in_weight, "wout": out_weight,
            "x0": x_zero, "conv": conv, "vec": vectors, "mask": mask, "table": table,
            "back": table_back, "zh": z_edge, "nt": normed_t, "yt": y_t, "small": small,
            "net": filter_net, "final": filter_out, "rate": rates, "feature": feature,
            "pre": pre, "s": short, "z": z, "uhat": u_hat, "kern": kernels,
        },
        up_step.reshape(chips, 2, -1, up_step.shape[1]),
        down_step.reshape(chips, 2, -1, width),
    )
    vector_sum = rest[: vectors.shape[0]]
    final_sum = rest[FINAL_ROW : FINAL_ROW + HID]
    net_sum = net_sum[: filter_net.shape[0], :HID]
    return (
        block_output[:, None],
        input_grad[:, None],
        *nesterov(proj_weights, proj_moment, proj_average, proj_sum, 0.0001),
        *nesterov(down_weights, down_moment, down_average, down_sum, 0.0001),
        *nesterov(vectors, vector_moment, vector_average, vector_sum, 0.001),
        *nesterov(filter_net, net_moment, net_average, net_sum, 0.0001),
        *nesterov(filter_out, final_moment, final_average, final_sum, 2e-06),
    )


def on_device_plain(
    block_input,
    out_grad,
    lengths,
    decay_rates,
    proj_weights,
    proj_moment,
    proj_average,
    down_weights,
    down_moment,
    down_average,
    vectors,
    vector_moment,
    vector_average,
    filter_net,
    net_moment,
    net_average,
    filter_out,
    final_moment,
    final_average,
):
    micro = block_input.shape[0]
    count = block_input.shape[2]
    width = block_input.shape[3]
    groups = lax.axis_size("pos")
    slot_length = count * groups
    tokens_all = micro * count
    group = lax.axis_index("pos")
    tap = vectors[13:22].reshape(3, 3 * width)
    short_bias = vectors[22:25].reshape(-1)
    in_bias = vectors[4:7].reshape(-1)
    up_bias = vectors[8:12].reshape(-1)
    skip = vectors[25]

    low_rows = proj_weights.astype(bf16)
    in_weight = lax.all_gather(low_rows[:, : 3 * width], "seq", axis=0, tiled=True)
    out_weight = lax.all_gather(low_rows[:, 3 * width : 4 * width], "seq", axis=0, tiled=True)
    up_weight = lax.all_gather(low_rows[:, 4 * width :], "seq", axis=0, tiled=True)
    down_weight = lax.all_gather(down_weights.astype(bf16), "seq", axis=0, tiled=True)

    table = jnp.asarray(transform_table(count))
    table_low = table.astype(bf16)
    every = jnp.arange(slot_length, dtype=jnp.int32)

    def make_filter(net_values, final_values):
        return filter_fn(net_values, final_values, decay_rates, every, slot_length)

    filters, filter_back = jax.vjp(make_filter, filter_net, filter_out)
    pieces = filters.reshape(groups, count, width)
    spectra = [
        jnp.dot(table, pieces[d], precision=lax.Precision.HIGH, preferred_element_type=f32)
        for d in range(groups)
    ]
    kernels = [spectra[0]] + [spectra[d] + turned(spectra[d - 1], 1.0) for d in range(1, groups)]

    def transform(values):
        return jnp.stack([dot(table_low, values[m]) for m in range(micro)])

    def transform_back(spectrum):
        low = spectrum.astype(bf16)
        return jnp.stack([dot_tn(table_low, low[m]) for m in range(micro)]) * (1.0 / count)

    tokens_low = block_input[:, 0]
    before = passed_along(tokens_low[:, -2:], "pos", 1)
    tokens = tokens_low.astype(f32).reshape(tokens_all, width)
    xh_one, scale_one = norm_parts(tokens)
    normed = (xh_one * vectors[0] + vectors[1]).astype(bf16)
    xh_before, _ = norm_parts(before.astype(f32).reshape(micro * 2, width))
    normed_before = (xh_before * vectors[0] + vectors[1]).astype(bf16)
    z = (dot(normed, in_weight) + in_bias).reshape(micro, count, 3 * width)
    z_before = (dot(normed_before, in_weight) + in_bias).reshape(micro, 2, 3 * width)
    z_before = jnp.where(group > 0, z_before, 0.0)
    z_long = jnp.concatenate([z_before, z], axis=1)
    short = (
        tap[0] * z_long[:, 2:] + tap[1] * z_long[:, 1:-1] + tap[2] * z_long[:, :-2] + short_bias
    ).astype(bf16)
    x0 = short[:, :, :width].astype(f32)
    x1 = short[:, :, width : 2 * width].astype(f32)
    v = short[:, :, 2 * width :].astype(f32)

    u = x1 * v
    u_low = u.astype(bf16)
    u_hat = [transform(u_low)]
    for d in range(1, groups):
        u_hat.append(transform(passed_along(u_low, "pos", d)))
    total = product(kernels[0], u_hat[0])
    for d in range(1, groups):
        total = total + product(kernels[d], u_hat[d])
    conv = transform_back(total) + skip * u
    here = group * count + jnp.arange(count, dtype=jnp.int32)
    mask = (here[None, :] < lengths[:, 0][:, None]).astype(f32)[:, :, None]
    y = (mask * x0 * conv).astype(bf16).reshape(tokens_all, width)
    residual = tokens + dot(y, out_weight) + vectors[7]
    xh_two, scale_two = norm_parts(residual)
    normed_two = (xh_two * vectors[2] + vectors[3]).astype(bf16)

    cot_low = out_grad[:, 0].reshape(tokens_all, width)
    cot = cot_low.astype(f32)
    pre = dot(normed_two, up_weight) + up_bias
    hidden, gelu_back = jax.vjp(jax.nn.gelu, pre)
    hidden_low = hidden.astype(bf16)
    block_output = (residual + dot(hidden_low, down_weight) + vectors[12]).astype(bf16)
    pre_grad = gelu_back(dot_nt(cot_low, down_weight))[0].astype(bf16)
    down_step = dot_tn(hidden_low, cot_low)
    up_step = dot_tn(normed_two, pre_grad)
    normed_two_grad = dot_nt(pre_grad, up_weight)
    part, gain_two, shift_two = norm_back(normed_two_grad, xh_two, scale_two, vectors[2])
    residual_grad = cot + part
    branch_low = residual_grad.astype(bf16)
    out_step = dot_tn(y, branch_low)
    y_grad = dot_nt(branch_low, out_weight).astype(bf16).astype(f32).reshape(micro, count, width)

    gw = mask * y_grad
    gx0 = gw * conv
    gc = gw * x0
    gc_low = gc.astype(bf16)
    skip_grad = jnp.sum(gc * u, axis=(0, 1))
    gc_hat = [transform(gc_low)]
    for d in range(1, groups):
        gc_hat.append(transform(passed_along(gc_low, "pos", -d)))
    back = product_conj(kernels[0], gc_hat[0])
    for d in range(1, groups):
        back = back + product_conj(kernels[d], gc_hat[d])
    gu = transform_back(back) + skip * gc
    kernel_grads = [jnp.sum(product_conj(u_hat[d], gc_hat[0]), axis=0) for d in range(groups)]
    filter_grads = []
    for d in range(groups):
        got = kernel_grads[d]
        if d + 1 < groups:
            got = got + turned(kernel_grads[d + 1], -1.0)
        filter_grads.append(dot_tn(table_low, got.astype(bf16)) * (1.0 / count))
    net_local, final_local = filter_back(jnp.concatenate(filter_grads, axis=0))
    short_grad = jnp.concatenate([gx0, gu * v, gu * x1], axis=-1).astype(bf16)
    after = passed_along(short_grad[:, :2], "pos", -1)
    short_long = jnp.concatenate([short_grad, after], axis=1).astype(f32)
    z_grad = (
        tap[0] * short_long[:, :-2] + tap[1] * short_long[:, 1:-1] + tap[2] * short_long[:, 2:]
    ).astype(bf16)
    here_grad = short_long[:, :-2]
    tap_grads = [
        jnp.sum(here_grad * z_long[:, 2 - k : 2 - k + count], axis=(0, 1)) for k in range(3)
    ]
    short_bias_grad = jnp.sum(here_grad, axis=(0, 1))
    z_grad = z_grad.reshape(tokens_all, 3 * width)
    in_step = dot_tn(normed, z_grad)
    in_bias_grad = jnp.sum(z_grad.astype(f32), axis=0)
    normed_grad = dot_nt(z_grad, in_weight)
    part, gain_one, shift_one = norm_back(normed_grad, xh_one, scale_one, vectors[0])
    input_grad = (residual_grad + part).astype(bf16)

    vector_local = jnp.concatenate(
        [
            gain_one[None],
            shift_one[None],
            gain_two[None],
            shift_two[None],
            in_bias_grad.reshape(3, width),
            jnp.sum(branch_low.astype(f32), axis=0)[None],
            jnp.sum(pre_grad.astype(f32), axis=0).reshape(4, width),
            jnp.sum(cot, axis=0)[None],
            jnp.stack(tap_grads).reshape(9, width),
            short_bias_grad.reshape(3, width),
            skip_grad[None],
        ],
        axis=0,
    )
    proj_local = jnp.concatenate([in_step, out_step, up_step], axis=1).astype(bf16)
    proj_shard = lax.psum_scatter(proj_local, "seq", scatter_dimension=0, tiled=True)
    down_shard = lax.psum_scatter(down_step.astype(bf16), "seq", scatter_dimension=0, tiled=True)
    proj_sum = lax.psum(proj_shard, "pos").astype(f32)
    down_sum = lax.psum(down_shard, "pos").astype(f32)
    vector_sum, net_sum, final_sum = lax.psum(
        (vector_local, net_local, final_local), ("seq", "pos")
    )
    return (
        block_output.reshape(micro, 1, count, width),
        input_grad.reshape(micro, 1, count, width),
        *nesterov(proj_weights, proj_moment, proj_average, proj_sum, 0.0001),
        *nesterov(down_weights, down_moment, down_average, down_sum, 0.0001),
        *nesterov(vectors, vector_moment, vector_average, vector_sum, 0.001),
        *nesterov(filter_net, net_moment, net_average, net_sum, 0.0001),
        *nesterov(filter_out, final_moment, final_average, final_sum, 2e-06),
    )


def on_device(*arrays):
    tuned = fits(
        lax.axis_size("seq"), lax.axis_size("pos"), arrays[0], arrays[4], arrays[7]
    )
    return (on_device_tuned if tuned else on_device_plain)(*arrays)


def solution(mesh):
    tokens = P(None, "seq", "pos", None)
    rows = P("seq", None)
    whole = P()
    return jax.shard_map(
        on_device,
        mesh=mesh,
        in_specs=(tokens, tokens, P(None, "seq"), whole) + (rows,) * 6 + (whole,) * 9,
        out_specs=(tokens, tokens) + (rows,) * 8 + (whole,) * 12,
        check_vma=False,
    )
```

```python
import functools
import math
import types

import jax
import jax.numpy as jnp
import numpy as np
from jax import lax
from jax.experimental import pallas as pl
from jax.experimental.pallas import tpu as pltpu
from jax.sharding import PartitionSpec as P

HID = 64
EMB = 33

highest = lax.Precision.HIGHEST
f32 = jnp.float32
bf16 = jnp.bfloat16


def passed_along(block, axis, distance):
    devices = range(lax.axis_size(axis))
    route = [(i - distance, i) for i in devices if i - distance in devices]
    return lax.ppermute(block, axis, route)


def dot(a, b):
    return lax.dot_general(a, b, (((1,), (0,)), ((), ())), preferred_element_type=f32)


def dot_tn(a, b):
    return lax.dot_general(a, b, (((0,), (0,)), ((), ())), preferred_element_type=f32)


def dot_nt(a, b):
    return lax.dot_general(a, b, (((1,), (1,)), ((), ())), preferred_element_type=f32)


def features(positions, slot_length):
    band_count = (EMB - 1) // 2
    scaled = positions.astype(f32) / slot_length
    bands = 0.0001 + jnp.arange(band_count, dtype=f32) * (
        (band_count - 1 - 0.0001) / (band_count - 1)
    )
    angles = 2.0 * math.pi * scaled[:, None] * bands[None, :]
    return jnp.concatenate([scaled[:, None], jnp.cos(angles), -jnp.sin(angles)], axis=1)


def filter_fn(net_values, final_values, rates, positions, slot_length):
    embedded = features(positions, slot_length)
    frequency = net_values[EMB + 3 + 2 * HID]
    layer_one = jnp.sin(
        frequency * (jnp.dot(embedded, net_values[:EMB], precision=highest) + net_values[EMB])
    )
    layer_two = jnp.sin(
        frequency
        * (
            jnp.dot(layer_one, net_values[EMB + 1 : EMB + 1 + HID], precision=highest)
            + net_values[EMB + 1 + HID]
        )
    )
    layer_three = jnp.sin(
        frequency
        * (
            jnp.dot(layer_two, net_values[EMB + 2 + HID : EMB + 2 + 2 * HID], precision=highest)
            + net_values[EMB + 2 + 2 * HID]
        )
    )
    shaped = jnp.dot(layer_three, final_values, precision=highest)
    scaled = positions.astype(f32) / slot_length
    window = jnp.exp(-scaled[:, None] * rates[None, :]) + 0.05
    return shaped * window


def transform_table(length):
    product = np.outer(2 * np.arange(length) + 1, np.arange(length)) % (4 * length)
    angle = product.astype(np.float64) * (math.pi / (2 * length))
    return np.concatenate([np.cos(angle), -np.sin(angle)], axis=0).astype(np.float32)


def feature_table(slot_length):
    scaled = np.arange(slot_length, dtype=np.float32) / np.float32(slot_length)
    band_count = (EMB - 1) // 2
    bands = np.float32(0.0001) + np.arange(band_count, dtype=np.float32) * np.float32(
        (band_count - 1 - 0.0001) / (band_count - 1)
    )
    angles = (np.float32(2.0 * math.pi) * scaled[:, None]) * bands[None, :]
    table = np.zeros((slot_length, 4 * HID), np.float32)
    table[:, 0] = scaled
    table[:, 1 : 1 + band_count] = np.cos(angles)
    table[:, 1 + band_count : EMB] = -np.sin(angles)
    table[:, EMB] = 1.0
    return table


def halves(spectrum):
    half = spectrum.shape[-2] // 2
    return spectrum[..., :half, :], spectrum[..., half:, :]


def turned(spectrum, sign):
    re, im = halves(spectrum)
    parity = (1.0 - 2.0 * (jnp.arange(re.shape[-2]) % 2).astype(f32))[:, None] * sign
    return jnp.concatenate([-parity * im, parity * re], axis=-2)


def product(kernel, signal):
    kr, ki = halves(kernel)
    sr, si = halves(signal)
    return jnp.concatenate([kr * sr - ki * si, kr * si + ki * sr], axis=-2)


def product_conj(kernel, signal):
    kr, ki = halves(kernel)
    sr, si = halves(signal)
    return jnp.concatenate([kr * sr + ki * si, kr * si - ki * sr], axis=-2)


def nesterov(weight, moment, average, gradient, rate):
    moment_next = 0.9 * moment + gradient
    weight_next = weight - rate * (gradient + 0.9 * moment_next)
    average_next = 0.9 * average + 0.1 * weight_next
    return (gradient, weight_next, moment_next, average_next)


def norm_parts(values):
    center = jnp.mean(values, axis=-1, keepdims=True)
    centred = values - center
    variance = jnp.mean(centred * centred, axis=-1, keepdims=True)
    scale = lax.rsqrt(variance + 1e-05)
    return centred * scale, scale


def norm_back(grad, xh, scale, gain):
    q = grad * gain
    return (
        (q - jnp.mean(q, -1, keepdims=True) - xh * jnp.mean(q * xh, -1, keepdims=True)) * scale,
        jnp.sum(grad * xh, axis=0),
        jnp.sum(grad, axis=0),
    )


MESH = pl.DeviceIdType.MESH


class Ring:
    def __init__(self, size):
        self.size = size
        self.count = size // 2
        self.seq = lax.axis_index("seq")
        self.pos = lax.axis_index("pos")
        self.core = lax.rem(self.seq, 2)
        chip = self.seq // 2
        odd = lax.rem(chip, 2)
        self.place = (1 - odd) * (chip // 2) + odd * (self.count - 1 - chip // 2)

    def chip(self, shift):
        place = lax.rem(self.place + (shift + self.count), self.count)
        low = jnp.where(place < self.count // 2, 1, 0)
        return low * (2 * place) + (1 - low) * (2 * (self.count - 1 - place) + 1)

    def device(self, shift):
        return {"seq": 2 * self.chip(shift) + self.core}

    @property
    def sibling(self):
        return {"seq": self.seq + 1 - 2 * self.core}

    @property
    def across(self):
        return {"pos": 1 - self.pos}


def greet_all(ring):
    barrier = pltpu.get_barrier_semaphore()
    for step in range(1, ring.size):
        other = lax.rem(ring.seq + step, ring.size)
        pl.semaphore_signal(barrier, inc=1, device_id={"seq": other}, device_id_type=MESH)
    pl.semaphore_signal(barrier, inc=1, device_id=ring.across, device_id_type=MESH)
    pl.semaphore_wait(barrier, ring.size)


def remote(src, dst, send, recv, device):
    return pltpu.make_async_remote_copy(
        src_ref=src, dst_ref=dst, send_sem=send, recv_sem=recv, device_id=device,
        device_id_type=MESH,
    )


class Reduction:
    def __init__(self, ring, grad, twin, up, down, own, other, sems, stage=None, stage_sems=None):
        self.ring = ring
        self.grad, self.twin, self.up, self.down = grad, twin, up, down
        self.own, self.other = own, other
        self.sems = sems
        self.stage, self.stage_sems = stage, stage_sems
        self.ups = ring.count // 2
        self.downs = (ring.count - 1) // 2

    def copies(self):
        ring = self.ring
        made = [(self.grad.at[:, 1 - ring.core], self.twin, ring.sibling)]
        for step in range(self.ups):
            block = self.twin.at[ring.chip(self.ups - step)]
            made.append((block, self.up.at[step], ring.device(1)))
        for step in range(self.downs):
            block = self.twin.at[ring.chip(step - self.downs)]
            made.append((block, self.down.at[step], ring.device(-1)))
        made.append((self.own, self.other, ring.across))
        return made

    def copy(self, index):
        src, dst, device = self.copies()[index]
        return remote(src, dst, self.sems.at[0, index], self.sems.at[1, index], device)

    def begin(self):
        self.copy(0).start()

    def fetch(self, chip, slot):
        return pltpu.make_async_copy(
            self.grad.at[chip, self.ring.core], self.stage.at[slot], self.stage_sems.at[slot]
        )

    def merge(self):
        core = self.ring.core
        count = self.ring.count
        if self.stage is None:
            self.copy(0).wait_recv()

            @pl.loop(0, count)
            def _(chip):
                self.twin[chip] = self.twin[chip] + self.grad[chip, core]

        else:
            self.fetch(0, 0).start()
            self.copy(0).wait_recv()

            @pl.loop(0, count)
            def _(chip):
                slot = lax.rem(chip, 2)

                @pl.when(chip + 1 < count)
                def _():
                    self.fetch(chip + 1, 1 - slot).start()

                self.fetch(chip, slot).wait()
                self.twin[chip] = self.twin[chip] + self.stage[slot]

        self.copy(1).start()
        self.copy(1 + self.ups).start()

    def advance(self, step):
        self.copy(step).wait_recv()
        owner = self.ring.chip(self.ups - step)
        self.twin[owner] = self.twin[owner] + self.up[step - 1]
        self.copy(1 + step).start()
        if step < self.downs:
            self.copy(self.ups + step).wait_recv()
            owner = self.ring.chip(step - self.downs)
            self.twin[owner] = self.twin[owner] + self.down[step - 1]
            self.copy(1 + self.ups + step).start()

    def collect(self):
        self.copy(self.ups).wait_recv()
        self.copy(self.ups + self.downs).wait_recv()
        mine = self.ring.chip(0)
        total = (
            self.twin[mine].astype(f32)
            + self.up[self.ups - 1].astype(f32)
            + self.down[self.downs - 1].astype(f32)
        )
        self.own[...] = total.astype(bf16)
        self.copy(1 + self.ups + self.downs).start()

    def result(self):
        self.copy(1 + self.ups + self.downs).wait_recv()
        return self.own[...].astype(f32) + self.other[...].astype(f32)

    def finish(self):
        for index in range(2 + self.ups + self.downs):
            self.copy(index).wait_send()


class SmallSum:
    def __init__(self, ring, values, parts, mine, other, sums, sems):
        self.ring, self.values, self.parts = ring, values, parts
        self.mine, self.other, self.sums = mine, other, sums
        self.sems = sems
        self.rows = parts.shape[1]
        self.waiting = []

    def block(self, index):
        return pl.ds(pl.multiple_of(index * self.rows, 8), self.rows)

    def begin(self):
        ring = self.ring
        self.arriving = []
        for step in range(1, ring.size):
            other = lax.rem(ring.seq + step, ring.size)
            copy = remote(
                self.values.at[self.block(other)], self.parts.at[step],
                self.sems.at[0, step], self.sems.at[1, step], {"seq": other},
            )
            copy.start()
            self.arriving.append(copy)
            self.waiting.append(copy)

    def add_up(self):
        for copy in self.arriving:
            copy.wait_recv()
        total = self.values[self.block(self.ring.seq)]
        for step in range(1, self.ring.size):
            total = total + self.parts[step]
        self.mine[...] = total
        self.crossing = remote(
            self.mine, self.other, self.sems.at[0, 0], self.sems.at[1, 0], self.ring.across
        )
        self.crossing.start()
        self.waiting.append(self.crossing)

    def spread(self):
        self.crossing.wait_recv()
        block = self.block(self.ring.seq)
        self.sums[block] = self.mine[...] + self.other[...]
        self.arriving = []
        for step in range(1, self.ring.size):
            other = lax.rem(self.ring.seq + step, self.ring.size)
            copy = remote(
                self.sums.at[block], self.sums.at[block],
                self.sems.at[2, step], self.sems.at[3, step], {"seq": other},
            )
            copy.start()
            self.waiting.append(copy)
            back = lax.rem(self.ring.seq + (self.ring.size - step), self.ring.size)
            self.arriving.append(
                remote(
                    self.sums.at[self.block(back)], self.sums.at[self.block(back)],
                    self.sems.at[2, step], self.sems.at[3, step], {"seq": other},
                )
            )

    def finish(self):
        for copy in self.arriving:
            copy.wait_recv()
        for copy in self.waiting:
            copy.wait_send()


def reduction_scratch(size, rows, columns):
    chips = size // 2
    ups, downs = chips // 2, (chips - 1) // 2
    return [
        pltpu.VMEM((chips, rows, columns), bf16),
        pltpu.VMEM((ups, rows, columns), bf16),
        pltpu.VMEM((downs, rows, columns), bf16),
        pltpu.VMEM((rows, columns), bf16),
        pltpu.VMEM((rows, columns), bf16),
        pltpu.SemaphoreType.DMA((2, 2 + ups + downs)),
    ]


def small_scratch(size, rows, columns):
    return [
        pltpu.VMEM((size, rows // size, columns), f32),
        pltpu.VMEM((rows // size, columns), f32),
        pltpu.VMEM((rows // size, columns), f32),
        pltpu.SemaphoreType.DMA((4, size)),
    ]


class Gather:
    def __init__(self, ring, mine, full, sems):
        self.ring, self.mine, self.full, self.sems = ring, mine, full, sems
        self.ups = ring.count // 2
        self.downs = (ring.count - 1) // 2
        self.waiting, self.arriving = [], []

    def send(self, src, place, index, device):
        copy = remote(
            src, self.full.at[self.ring.chip(place), self.ring.core],
            self.sems.at[0, index], self.sems.at[1, index], device,
        )
        copy.start()
        self.waiting.append(copy)
        return copy

    def share(self, src, place, index):
        index = self.ups + self.downs + index
        self.send(src, place, index, self.ring.sibling)
        block = self.full.at[self.ring.chip(place), 1 - self.ring.core]
        self.arriving.append(
            remote(block, block, self.sems.at[0, index], self.sems.at[1, index], self.ring.sibling)
        )

    def wait_block(self, place, index, device):
        block = self.full.at[self.ring.chip(place), self.ring.core]
        remote(block, block, self.sems.at[0, index], self.sems.at[1, index], device).wait_recv()
        return block

    def begin(self):
        ring = self.ring
        self.send(self.mine, 0, 0, ring.device(1))
        self.send(self.mine, 0, self.ups, ring.device(-1))
        self.share(self.mine, 0, 0)
        self.local = pltpu.make_async_copy(
            self.mine, self.full.at[ring.chip(0), ring.core], self.sems.at[2, 0]
        )
        self.local.start()

    def advance(self, step):
        ring = self.ring
        block = self.wait_block(-step, step - 1, ring.device(1))
        if step < self.ups:
            self.send(block, -step, step, ring.device(1))
        self.share(block, -step, step)
        if step <= self.downs:
            block = self.wait_block(step, self.ups + step - 1, ring.device(-1))
            if step < self.downs:
                self.send(block, step, self.ups + step, ring.device(-1))
            self.share(block, step, self.ups + step)

    def arrive(self):
        self.local.wait()
        for copy in self.arriving:
            copy.wait_recv()

    def finish(self):
        for copy in self.waiting:
            copy.wait_send()


def gather_sems(size):
    chips = size // 2
    return pltpu.SemaphoreType.DMA((3, 2 * chips))


def norm_rows(values):
    center = jnp.mean(values, axis=1, keepdims=True)
    centred = values - center
    variance = jnp.mean(centred * centred, axis=1, keepdims=True)
    return centred * lax.rsqrt(variance + 1e-05)


TILE = 256


class Copies:
    def __init__(self, sems):
        self.sems, self.used, self.open = sems, 0, []

    def start(self, src, dst):
        copy = pltpu.make_async_copy(src, dst, self.sems.at[self.used])
        self.used += 1
        copy.start()
        return copy

    def out(self, src, dst):
        self.open.append(self.start(src, dst))

    def finish(self):
        for copy in self.open:
            copy.wait()


def valid_rows(length, first, rows, columns):
    at = lax.broadcasted_iota(jnp.int32, (rows, columns), 0) + first
    return jnp.where(at < length, 1.0, 0.0).astype(f32)


def front_kernel(size, names, *refs):
    ref = types.SimpleNamespace(**dict(zip(names, refs)))
    x, vec, net = ref.x_in, ref.vec, ref.net
    micro, count, width = x.shape
    slot = 2 * count
    tiles = width // TILE
    ring = Ring(size)
    copies = Copies(ref.copy_sems)
    proj_copy = copies.start(ref.proj, ref.proj_in)
    x_copy = copies.start(ref.x, x)
    down_copy = copies.start(ref.down, ref.down_in)
    feature_copy = copies.start(ref.feature, ref.feature_in)
    table_copy = copies.start(ref.table, ref.table_in)
    back_copy = copies.start(ref.back, ref.back_in)
    table, table_back = ref.table_in, ref.back_in
    inside = jnp.where(ring.pos > 0, 1.0, 0.0).astype(f32)

    proj_copy.wait()
    own = ref.in_own
    for j in range(tiles):
        for p in range(3):
            first = p * width + j * TILE
            own[j, :, p * TILE : (p + 1) * TILE] = ref.proj_in[:, first : first + TILE].astype(bf16)
    greet_all(ring)
    gather = [Gather(ring, own.at[j], ref.win_in.at[j], ref.win_sem.at[j]) for j in range(tiles)]
    gather_out = Gather(ring, ref.out_own, ref.wout_in, ref.wout_sem)
    gather_up = Gather(ring, ref.up_own, ref.wup, ref.wup_sem)
    gather_down = Gather(ring, ref.down_own, ref.wdown, ref.wdown_sem)
    gather[0].begin()
    gather[1].begin()
    x_copy.wait()
    edge = remote(
        x.at[:, pl.ds(count - 16, 16)], ref.halo, ref.halo_sem.at[0],
        ref.halo_sem.at[1], ring.across,
    )
    edge.start()

    gain, shift = vec[0:1], vec[1:2]
    normed_ref, turned_ref = ref.n_in, ref.nt_in

    def first_norm(m):
        for part in range(count // TILE):
            rows = slice(part * TILE, (part + 1) * TILE)
            normed = (norm_rows(x[m, rows].astype(f32)) * gain + shift).astype(bf16)
            normed_ref[m, rows] = normed
            turned_ref[m, :, rows] = normed.T

    first_norm(0)
    gather[0].advance(1)
    gather[1].advance(1)
    gather[2].begin()
    for m in range(1, micro):
        first_norm(m)
    copies.out(turned_ref, ref.nt)
    ref.out_own[...] = ref.proj_in[:, 3 * width : 4 * width].astype(bf16)
    gather[0].advance(2)
    gather[1].advance(2)
    edge.wait_recv()
    for m in range(micro):
        ref.halo_n[m] = (norm_rows(ref.halo[m].astype(f32)) * gain + shift).astype(bf16)
    feature_copy.wait()

    frequency = net[EMB + 3 + 2 * HID : EMB + 4 + 2 * HID]

    def filter_rows(at):
        rows = slice(at * TILE, (at + 1) * TILE)
        layer = jnp.dot(
            ref.feature_in[rows, : net.shape[0]], net[...], precision=highest,
            preferred_element_type=f32,
        )
        ref.pre_in[rows, :HID] = layer
        layer = jnp.sin(frequency * layer)
        for i, first in ((1, EMB + 1), (2, EMB + 2 + HID)):
            layer = (
                jnp.dot(
                    layer, net[first : first + HID], precision=highest,
                    preferred_element_type=f32,
                )
                + net[first + HID : first + HID + 1]
            )
            ref.pre_in[rows, i * HID : (i + 1) * HID] = layer
            layer = jnp.sin(frequency * layer)
        shaped = dot(layer.astype(bf16), ref.final[...].astype(bf16))
        at_row = lax.broadcasted_iota(jnp.int32, (TILE, width), 0) + at * TILE
        scaled = at_row.astype(f32) * (1.0 / slot)
        window = jnp.exp(-scaled * ref.rate[...]) + 0.05
        ref.filt[rows] = (shaped * window).astype(bf16)

    row_blocks = slot // TILE
    filter_rows(0)
    gather[0].advance(3)
    gather[1].advance(3)
    gather[2].advance(1)
    down_copy.wait()
    ref.up_own[...] = ref.proj_in[:, 4 * width :].astype(bf16)
    ref.down_own[...] = ref.down_in[...].astype(bf16)
    gather[0].advance(4)
    gather[2].advance(2)
    gather_out.begin()
    gather[1].advance(4)
    gather[0].arrive()

    z_in, s_in, ulow, urecv = ref.z_in, ref.s_in, ref.ulow, ref.urecv
    zbuf, spec = ref.zbuf, ref.spec
    crossing = []

    def project(j):
        weight = ref.win_in[j].reshape(width, 3 * TILE)
        bias = jnp.concatenate(
            [vec[4 + p : 5 + p, j * TILE : (j + 1) * TILE] for p in range(3)], axis=1
        )
        lane = slice(j * TILE, (j + 1) * TILE)

        @pl.loop(0, micro)
        def _(m):
            z = dot(normed_ref[m], weight) + bias
            zh = (dot(ref.halo_n[m], weight) + bias) * inside
            z_in[j, m] = z.astype(bf16)
            ref.zh_in[j, m] = zh.astype(bf16)
            zbuf[:16] = zh
            zbuf[16:] = z
            for p in range(3):
                cols = slice(p * TILE, (p + 1) * TILE)
                s_in[j, m, :, cols] = (
                    vec[13 + p : 14 + p, lane] * zbuf[16:, cols]
                    + vec[16 + p : 17 + p, lane] * zbuf[15 : 15 + count, cols]
                    + vec[19 + p : 20 + p, lane] * zbuf[14 : 14 + count, cols]
                    + vec[22 + p : 23 + p, lane]
                ).astype(bf16)
            ulow[j, m] = (
                s_in[j, m, :, TILE : 2 * TILE].astype(f32) * s_in[j, m, :, 2 * TILE :].astype(f32)
            ).astype(bf16)

        copy = remote(
            ulow.at[j], urecv.at[j], ref.u_sem.at[0, j], ref.u_sem.at[1, j], ring.across
        )
        copy.start()
        crossing.append(copy)
        copies.out(z_in.at[j], ref.z.at[j])
        copies.out(s_in.at[j], ref.s.at[j])

    project(0)
    gather[2].advance(3)
    gather_up.begin()
    gather[1].arrive()
    project(1)
    gather[2].advance(4)
    gather_down.begin()
    gather_out.advance(1)
    gather[2].arrive()
    project(2)
    copies.out(ref.zh_in, ref.zh)
    copies.out(ref.win_in, ref.win)
    gather_out.advance(2)
    for at in range(1, row_blocks):
        filter_rows(at)
        if at == 2:
            gather_up.advance(1)
            gather_out.advance(3)
    copies.out(ref.pre_in, ref.pre)
    gather_down.advance(1)
    gather_out.advance(4)
    gather_out.arrive()
    copies.out(ref.wout_in, ref.wout)
    table_copy.wait()
    back_copy.wait()

    parity = 1.0 - 2.0 * (
        lax.broadcasted_iota(jnp.int32, (count, TILE), 0) % 2
    ).astype(f32)
    kern, uhat = ref.kern_in, ref.uhat_in

    @pl.loop(0, tiles)
    def _(j):
        cols = pl.ds(pl.multiple_of(j * TILE, TILE), TILE)
        zero = dot(table[...], ref.filt[:count, cols])
        kern[j, 0] = zero.astype(bf16)
        one = dot(table[...], ref.filt[count:, cols])
        kern[j, 1, :count] = (one[:count] - parity * zero[count:]).astype(bf16)
        kern[j, 1, count:] = (one[count:] + parity * zero[:count]).astype(bf16)
        for m in range(micro):
            uhat[j, m, 0] = dot(table[...], ulow[j, m]).astype(bf16)

    copies.out(kern, ref.kern)
    gather_up.advance(2)

    def mix(j):
        crossing[j].wait_recv()
        lane = slice(j * TILE, (j + 1) * TILE)

        @pl.loop(0, micro)
        def _(m):
            other = dot(table[...], urecv[j, m]) * inside
            uhat[j, m, 1] = other.astype(bf16)
            k0r, k0i = kern[j, 0, :count].astype(f32), kern[j, 0, count:].astype(f32)
            k1r, k1i = kern[j, 1, :count].astype(f32), kern[j, 1, count:].astype(f32)
            ur, ui = uhat[j, m, 0, :count].astype(f32), uhat[j, m, 0, count:].astype(f32)
            vr, vi = other[:count], other[count:]
            spec[:count] = (k0r * ur - k0i * ui + k1r * vr - k1i * vi).astype(bf16)
            spec[count:] = (k0r * ui + k0i * ur + k1r * vi + k1i * vr).astype(bf16)
            gated = s_in[j, m, :, TILE : 2 * TILE].astype(f32) * s_in[j, m, :, 2 * TILE :].astype(f32)
            conv = dot(table_back[...], spec[...]) * (1.0 / count) + vec[25:26, lane] * gated
            ref.conv_in[j, m] = conv.astype(bf16)
            mask = valid_rows(ref.lens[m, 0], ring.pos * count, count, TILE)
            ref.y_in[m, :, lane] = (
                mask * s_in[j, m, :, :TILE].astype(f32) * conv
            ).astype(bf16)

        copies.out(ref.conv_in.at[j], ref.conv.at[j])
        copies.out(uhat.at[j], ref.uhat.at[j])

    for j in range(tiles):
        mix(j)
        if j == 0:
            gather_down.advance(2)
        if j == 1:
            gather_up.advance(3)

    for m in range(micro):
        for part in range(count // TILE):
            rows = slice(part * TILE, (part + 1) * TILE)
            y = ref.y_in[m, rows]
            ref.yt_in[m, :, rows] = y.T
            residual = (
                x[m, rows].astype(f32)
                + dot(y, ref.wout_in[...].reshape(width, width))
                + vec[7:8]
            )
            ref.res_in[m, rows] = residual
            normed = (norm_rows(residual) * vec[2:3] + vec[3:4]).astype(bf16)
            ref.n2_in[m, rows] = normed
            ref.n2t_in[m, :, rows] = normed.T
        for src, dst in (
            (ref.yt_in, ref.yt), (ref.res_in, ref.res), (ref.n2_in, ref.n2), (ref.n2t_in, ref.n2t)
        ):
            copies.out(src.at[m], dst.at[m])
        if m == 0:
            gather_down.advance(3)
    gather_up.advance(4)
    gather_down.advance(4)
    for work in (gather_up, gather_down):
        work.arrive()
    for work in gather + [gather_out, gather_up, gather_down]:
        work.finish()
    edge.wait_send()
    for copy in crossing:
        copy.wait_send()
    copies.finish()


def front(size, arrays):
    chips = size // 2
    micro, count, width = arrays["x"].shape
    rows, down_rows = arrays["proj"].shape[0], arrays["down"].shape[0]
    wide = down_rows * size
    tiles = width // TILE
    vmem = pl.BlockSpec(memory_space=pltpu.VMEM)
    anywhere = pl.BlockSpec(memory_space=pl.ANY)
    smem = pl.BlockSpec(memory_space=pltpu.SMEM)
    near = ("vec", "net", "final", "rate")
    kinds = dict(
        win=((tiles, chips, 2, rows, 3 * TILE), bf16),
        wout=((chips, 2, rows, width), bf16),
        z=((tiles, micro, count, 3 * TILE), bf16),
        zh=((tiles, micro, 16, 3 * TILE), bf16),
        s=((tiles, micro, count, 3 * TILE), bf16),
        conv=((tiles, micro, count, TILE), bf16),
        uhat=((tiles, micro, 2, 2 * count, TILE), bf16),
        kern=((tiles, 2, 2 * count, TILE), bf16),
        res=((micro, count, width), f32),
        nt=((micro, width, count), bf16),
        n2=((micro, count, width), bf16),
        n2t=((micro, width, count), bf16),
        yt=((micro, width, count), bf16),
        pre=((2 * count, 4 * HID), f32),
    )
    outs = dict(
        kinds,
        wup=((chips, 2, rows, wide), bf16),
        wdown=((chips, 2, down_rows, width), bf16),
    )
    dma = pltpu.SemaphoreType.DMA
    scratch = {
        name + "_in": pltpu.VMEM(*kind) for name, kind in kinds.items()
    }
    for name, array in arrays.items():
        if name not in near and name != "lens":
            scratch[name + "_in"] = pltpu.VMEM(array.shape, array.dtype)
    scratch.update(
        dict(
            n_in=pltpu.VMEM((micro, count, width), bf16),
            y_in=pltpu.VMEM((micro, count, width), bf16),
            in_own=pltpu.VMEM((tiles, rows, 3 * TILE), bf16),
            out_own=pltpu.VMEM((rows, width), bf16),
            up_own=pltpu.VMEM((rows, wide), bf16),
            down_own=pltpu.VMEM((down_rows, width), bf16),
            halo=pltpu.VMEM((micro, 16, width), bf16),
            halo_n=pltpu.VMEM((micro, 16, width), bf16),
            filt=pltpu.VMEM((2 * count, width), bf16),
            zbuf=pltpu.VMEM((16 + count, 3 * TILE), f32),
            ulow=pltpu.VMEM((tiles, micro, count, TILE), bf16),
            urecv=pltpu.VMEM((tiles, micro, count, TILE), bf16),
            spec=pltpu.VMEM((2 * count, TILE), bf16),
            win_sem=dma((tiles, 3, 2 * chips)),
            wout_sem=gather_sems(size),
            wup_sem=gather_sems(size),
            wdown_sem=gather_sems(size),
            halo_sem=dma((2,)),
            u_sem=dma((2, tiles)),
            copy_sems=dma((40,)),
        )
    )
    names = tuple(arrays) + tuple(outs) + tuple(scratch)
    made = pl.pallas_call(
        functools.partial(front_kernel, size, names),
        out_shape=[jax.ShapeDtypeStruct(*kind) for kind in outs.values()],
        in_specs=[
            smem if name == "lens" else vmem if name in near else anywhere for name in arrays
        ],
        out_specs=[anywhere] * len(outs),
        scratch_shapes=list(scratch.values()),
        compiler_params=pltpu.CompilerParams(
            collective_id=0, has_side_effects=True, vmem_limit_bytes=63 * 1024 * 1024
        ),
        name="front",
    )(*arrays.values())
    return dict(zip(outs, made))


GELU_SCALE = math.sqrt(2.0 / math.pi)


def gelu_pair(a):
    square = a * a
    bend = jnp.tanh(GELU_SCALE * a * (1.0 + 0.044715 * square))
    half = 0.5 * (1.0 + bend)
    slope = half + (0.5 * GELU_SCALE) * a * (1.0 - bend * bend) * (1.0 + 0.134145 * square)
    return a * half, slope


def mlp_kernel(
    n2_ref, n2t_ref, gm_ref, res_ref, vec_ref, wup_ref, wdown_ref, bias_ref,
    out_ref, gb_ref, dup_ref, ddown_ref, small_ref,
    acc_out, acc_gn, hid_ref, ga_ref,
):
    step, last = pl.program_id(0), pl.num_programs(0) - 1
    micro, count, width = n2_ref.shape
    chunk = bias_ref.shape[1]
    tile = 256
    wup = wup_ref[...].reshape(width, chunk)
    wdown = wdown_ref[...].reshape(chunk, width)
    bias = bias_ref[...]

    @pl.when(step == 0)
    def _():
        acc_out[...] = jnp.zeros_like(acc_out)
        acc_gn[...] = jnp.zeros_like(acc_gn)
        small_ref[...] = jnp.zeros_like(small_ref)

    bias_sum = jnp.zeros((1, chunk), f32)
    for m in range(micro):
        for part in range(count // tile):
            rows = slice(part * tile, (part + 1) * tile)
            hidden, slope = gelu_pair(dot(n2_ref[m, rows], wup) + bias)
            hidden = hidden.astype(bf16)
            ga = (dot_nt(gm_ref[m, rows], wdown) * slope).astype(bf16)
            hid_ref[m, rows] = hidden
            ga_ref[m, rows] = ga
            bias_sum = bias_sum + jnp.sum(ga.astype(f32), axis=0, keepdims=True)
            acc_out[m, rows] += dot(hidden, wdown)
            acc_gn[m, rows] += dot_nt(ga, wup)
    small_ref[pl.ds(4 + step, 1)] = bias_sum
    down_total = dot_tn(hid_ref[0], gm_ref[0])
    up_total = dot(n2t_ref[0], ga_ref[0])
    for m in range(1, micro):
        down_total = down_total + dot_tn(hid_ref[m], gm_ref[m])
        up_total = up_total + dot(n2t_ref[m], ga_ref[m])
    ddown_ref[...] = down_total.astype(bf16)
    dup_ref[...] = up_total.astype(bf16)

    @pl.when(step == last)
    def _():
        for m in range(micro):
            for part in range(count // tile):
                rows = slice(part * tile, (part + 1) * tile)
                residual = res_ref[m, rows]
                out_ref[m, rows] = (residual + acc_out[m, rows] + vec_ref[12:13]).astype(bf16)
                gx, gain_part, grad = norm_rows_back(acc_gn[m, rows], residual, vec_ref[2:3])
                gm = gm_ref[m, rows].astype(f32)
                low = (gm + gx).astype(bf16)
                gb_ref[m, rows] = low
                small_ref[0:1] += gain_part
                small_ref[1:2] += grad
                small_ref[2:3] += jnp.sum(low.astype(f32), axis=0, keepdims=True)
                small_ref[3:4] += jnp.sum(gm, axis=0, keepdims=True)


def norm_rows_back(grad, values, gain):
    center = jnp.mean(values, axis=1, keepdims=True)
    centred = values - center
    variance = jnp.mean(centred * centred, axis=1, keepdims=True)
    scale = lax.rsqrt(variance + 1e-05)
    xh = centred * scale
    q = grad * gain
    gx = scale * (
        q - jnp.mean(q, axis=1, keepdims=True) - xh * jnp.mean(q * xh, axis=1, keepdims=True)
    )
    return gx, jnp.sum(grad * xh, axis=0, keepdims=True), jnp.sum(grad, axis=0, keepdims=True)


def mlp(n2, n2t, gm, res, vectors, wup, wdown):
    micro, count, width = n2.shape
    chips, cores, rows, wide = wup.shape
    steps = wide // width
    per = chips // steps

    def whole(array):
        return pl.BlockSpec(array.shape, lambda i: (0,) * array.ndim)

    def shape(dims, kind=bf16):
        return jax.ShapeDtypeStruct(dims, kind)

    tokens = pl.BlockSpec((micro, count, width), lambda i: (0, 0, 0))
    return pl.pallas_call(
        mlp_kernel,
        grid=(steps,),
        in_specs=[
            whole(n2), whole(n2t), whole(gm), whole(res), whole(vectors),
            pl.BlockSpec((chips, cores, rows, width), lambda i: (0, 0, 0, i)),
            pl.BlockSpec((per, cores, wdown.shape[2], width), lambda i: (i, 0, 0, 0)),
            pl.BlockSpec((1, width), lambda i: (0, i)),
        ],
        out_specs=[
            tokens, tokens,
            pl.BlockSpec((width, width), lambda i: (0, i)),
            pl.BlockSpec((width, width), lambda i: (i, 0)),
            pl.BlockSpec((4 + steps, width), lambda i: (0, 0)),
        ],
        out_shape=[
            shape((micro, count, width)),
            shape((micro, count, width)),
            shape((width, wide)),
            shape((wide, width)),
            shape((4 + steps, width), f32),
        ],
        scratch_shapes=[
            pltpu.VMEM((micro, count, width), f32),
            pltpu.VMEM((micro, count, width), f32),
            pltpu.VMEM((micro, count, width), bf16),
            pltpu.VMEM((micro, count, width), bf16),
        ],
        compiler_params=pltpu.CompilerParams(vmem_limit_bytes=60 * 1024 * 1024),
        name="mlp",
    )(n2, n2t, gm, res, vectors, wup, wdown, vectors[8 : 8 + steps].reshape(1, wide))


FINAL_ROW = 32


def back_kernel(size, names, *refs):
    ref = types.SimpleNamespace(**dict(zip(names, refs)))
    gb, vec, table, table_back = ref.gb, ref.vec, ref.table, ref.back
    micro, count, width = gb.shape
    slot = 2 * count
    tiles = width // TILE
    ring = Ring(size)
    gw, gc, gcr, gz = ref.gw, ref.gc, ref.gcr, ref.gz
    vsum, nsum = ref.vsum, ref.nsum
    gate, turned = ref.gate, ref.turned
    inside = jnp.where(ring.pos < 1, 1.0, 0.0).astype(f32)
    copies = Copies(ref.copy_sems)
    gate_copies = [
        copies.start(ref.s.at[j, :, :, pl.ds(0, TILE)], gate.at[j]) for j in range(tiles)
    ]
    turned_copy = copies.start(ref.yt, turned)

    greet_all(ring)
    red = {}

    def parts_of(name):
        return [getattr(ref, name + str(k)) for k in range(6)]

    down = Reduction(ring, ref.ddown, *parts_of("down"), ref.down_stage, ref.down_stage_sems)
    up = Reduction(ring, ref.dup, *parts_of("up"), ref.up_stage, ref.up_stage_sems)
    out = Reduction(ring, ref.dout, *parts_of("out"))
    inner = [
        Reduction(ring, ref.din.at[j], *[part.at[j] for part in parts_of("in")])
        for j in range(tiles)
    ]
    down.begin()
    up.begin()
    vsum[...] = jnp.zeros_like(vsum)
    nsum[...] = jnp.zeros_like(nsum)
    small = ref.small
    vsum[2:4] = small[0:2]
    vsum[7:8] = small[2:3]
    vsum[12:13] = small[3:4]
    vsum[8:12] = small[4:8]

    crossing = []
    for j in range(tiles):
        gate_copies[j].wait()
        weight = ref.wout[...].reshape(width, width)[j * TILE : (j + 1) * TILE]

        @pl.loop(0, micro)
        def _(m):
            mask = valid_rows(ref.lens[m, 0], ring.pos * count, count, TILE)
            grad = mask * dot_nt(gb[m], weight).astype(bf16).astype(f32)
            gw[j, m] = grad.astype(bf16)
            gc[j, m] = (grad * gate[j, m].astype(f32)).astype(bf16)

        copy = remote(
            gc.at[j], gcr.at[j], ref.gc_sem.at[0, j], ref.gc_sem.at[1, j], ring.across
        )
        copy.start()
        crossing.append(copy)
    turned_copy.wait()

    @pl.loop(0, tiles)
    def _(j):
        cols = pl.ds(pl.multiple_of(j * TILE, TILE), TILE)
        total = dot(turned[0], gb[0, :, cols])
        for m in range(1, micro):
            total = total + dot(turned[m], gb[m, :, cols])
        dout = ref.dout
        dout[:, :, :, cols] = total.astype(bf16).reshape(dout.shape[:3] + (TILE,))

    turned_copy = copies.start(ref.nt, turned)
    out.begin()
    down.merge()
    up.merge()

    parity = 1.0 - 2.0 * (
        lax.broadcasted_iota(jnp.int32, (count, TILE), 0) % 2
    ).astype(f32)
    gk = ref.gk
    gbuf, zbuf, spec = ref.gbuf, ref.zbuf, ref.spec
    first_rows, last_rows, next_rows = ref.first_rows, ref.last_rows, ref.next_rows

    def loads(j, m, at):
        made = [
            (ref.s.at[j, m, :, pl.ds(TILE, 2 * TILE)], ref.s_buf.at[at]),
            (ref.z.at[j, m], ref.z_buf.at[at]),
            (ref.uhat.at[j, m], ref.u_buf.at[at]),
            (ref.conv.at[j, m], ref.c_buf.at[at]),
        ]
        return [
            pltpu.make_async_copy(src, dst, ref.load_sems.at[at, i])
            for i, (src, dst) in enumerate(made)
        ]

    def load_kernel(j):
        return pltpu.make_async_copy(ref.kern.at[j], ref.k_buf, ref.kernel_sem.at[0])

    def start_loads(j, m, at):
        for copy in loads(j, m, at):
            copy.start()

    start_loads(0, 0, 0)
    load_kernel(0).start()
    gbuf[count:] = jnp.zeros_like(gbuf[count:])

    def unmix(j):
        crossing[j].wait_recv()
        load_kernel(j).wait()
        lane = slice(j * TILE, (j + 1) * TILE)
        kn = ref.k_buf

        @pl.loop(0, micro)
        def _(m):
            at = lax.rem(j * micro + m, 2)
            for copy in loads(j, m, at):
                copy.wait()

            @pl.when(m + 1 < micro)
            def _():
                start_loads(j, m + 1, 1 - at)

            if j + 1 < tiles:

                @pl.when(m + 1 == micro)
                def _():
                    start_loads(j + 1, 0, 1 - at)

            hat = dot(table[...], gc[j, m])
            far = dot(table[...], gcr[j, m]) * inside
            gr, gi = hat[:count], hat[count:]
            hr, hi = far[:count], far[count:]
            k0r, k0i = kn[0, :count].astype(f32), kn[0, count:].astype(f32)
            k1r, k1i = kn[1, :count].astype(f32), kn[1, count:].astype(f32)
            spec[:count] = (k0r * gr + k0i * gi + k1r * hr + k1i * hi).astype(bf16)
            spec[count:] = (k0r * gi - k0i * gr + k1r * hi - k1i * hr).astype(bf16)
            keep = jnp.where(m > 0, 1.0, 0.0).astype(f32)
            uh = ref.u_buf
            for d in range(2):
                ur, ui = uh[at, d, :count].astype(f32), uh[at, d, count:].astype(f32)
                gk[d, :count] = gk[d, :count] * keep + (ur * gr + ui * gi)
                gk[d, count:] = gk[d, count:] * keep + (ur * gi - ui * gr)
            x1 = ref.s_buf[at, :, :TILE].astype(f32)
            v = ref.s_buf[at, :, TILE:].astype(f32)
            grad_w = gw[j, m].astype(f32)
            gc_full = grad_w * gate[j, m].astype(f32)
            gu = dot(table_back[...], spec[...]) * (1.0 / count) + vec[25:26, lane] * gc_full
            vsum[25:26, lane] += jnp.sum(gc_full * x1 * v, axis=0, keepdims=True)
            for p in range(3):
                if p == 0:
                    grad = grad_w * ref.c_buf[at].astype(f32)
                else:
                    grad = gu * (v if p == 1 else x1)
                low = grad.astype(bf16)
                grad = low.astype(f32)
                cols = slice(p * TILE, (p + 1) * TILE)
                first_rows[j, m, :, cols] = low[:16]
                last_rows[j, m, :, cols] = low[count - 16 :]
                gbuf[:count] = grad
                gz[j, m, :, cols] = (
                    vec[13 + p : 14 + p, lane] * grad
                    + vec[16 + p : 17 + p, lane] * gbuf[1 : 1 + count]
                    + vec[19 + p : 20 + p, lane] * gbuf[2 : 2 + count]
                ).astype(bf16)
                zbuf[:16] = ref.zh[j, m, :, cols].astype(f32)
                zbuf[16:] = ref.z_buf[at, :, cols].astype(f32)
                for k in range(3):
                    row = 13 + 3 * k + p
                    vsum[row : row + 1, lane] += jnp.sum(
                        grad * zbuf[16 - k : 16 - k + count], axis=0, keepdims=True
                    )
                vsum[22 + p : 23 + p, lane] += jnp.sum(grad, axis=0, keepdims=True)

        if j + 1 < tiles:
            load_kernel(j + 1).start()
        edge = remote(
            first_rows.at[j], next_rows.at[j], ref.edge_sem.at[0, j],
            ref.edge_sem.at[1, j], ring.across,
        )
        edge.start()
        g1r, g1i = gk[1, :count], gk[1, count:]
        spec[:count] = (gk[0, :count] + parity * g1i).astype(bf16)
        spec[count:] = (gk[0, count:] - parity * g1r).astype(bf16)
        gate[j, 0] = (dot(table_back[...], spec[...]) * (1.0 / count)).astype(bf16)
        spec[:count] = g1r.astype(bf16)
        spec[count:] = g1i.astype(bf16)
        gate[j, 1] = (dot(table_back[...], spec[...]) * (1.0 / count)).astype(bf16)
        return edge

    def project_back(j, edge):
        edge.wait_recv()
        lane = slice(j * TILE, (j + 1) * TILE)
        ebuf = ref.ebuf
        for m in range(micro):
            for p in range(3):
                cols = slice(p * TILE, (p + 1) * TILE)
                own = last_rows[j, m, :, cols].astype(f32)
                ebuf[:16] = own
                ebuf[16:] = next_rows[j, m, :, cols].astype(f32) * inside
                gz[j, m, count - 16 :, cols] = (
                    vec[13 + p : 14 + p, lane] * own
                    + vec[16 + p : 17 + p, lane] * ebuf[1:17]
                    + vec[19 + p : 20 + p, lane] * ebuf[2:18]
                ).astype(bf16)
        for p in range(3):
            cols = slice(p * TILE, (p + 1) * TILE)
            total = dot(turned[0], gz[j, 0, :, cols])
            bias = jnp.sum(gz[j, 0, :, cols].astype(f32), axis=0, keepdims=True)
            for m in range(1, micro):
                total = total + dot(turned[m], gz[j, m, :, cols])
                bias = bias + jnp.sum(gz[j, m, :, cols].astype(f32), axis=0, keepdims=True)
            din = ref.din
            din[j, :, :, :, cols] = total.astype(bf16).reshape(din.shape[1:4] + (TILE,))
            vsum[4 + p : 5 + p, lane] = bias
        inner[j].begin()

    edges = [unmix(0)]
    down.advance(1)
    up.advance(1)
    out.merge()
    edges.append(unmix(1))
    turned_copy.wait()
    project_back(0, edges[0])
    down.advance(2)
    up.advance(2)
    out.advance(1)
    inner[0].merge()
    edges.append(unmix(2))
    project_back(1, edges[1])
    x_copies = [
        copies.start(ref.x.at[:, :, pl.ds(j * TILE, TILE)], gcr.at[j]) for j in range(tiles)
    ]
    pre_copy = copies.start(ref.pre, gk.at[0])
    feature_copy = copies.start(ref.feature, gk.at[1])
    down.advance(3)
    up.advance(3)
    inner[1].merge()
    project_back(2, edges[2])
    out.advance(2)
    inner[0].advance(1)
    inner[1].advance(1)
    for copy in x_copies:
        copy.wait()
    for copy in crossing:
        copy.wait_send()

    for m in range(micro):
        for part in range(count // TILE):
            rows = slice(part * TILE, (part + 1) * TILE)
            grad = dot_nt(gz[0, m, rows], ref.win[0].reshape(width, 3 * TILE))
            for j in range(1, tiles):
                grad = grad + dot_nt(gz[j, m, rows], ref.win[j].reshape(width, 3 * TILE))
            tokens = jnp.concatenate([gcr[j, m, rows] for j in range(tiles)], axis=1)
            gx, gain_part, shift_part = norm_rows_back(grad, tokens.astype(f32), vec[0:1])
            total = (gb[m, rows].astype(f32) + gx).astype(bf16)
            for j in range(tiles):
                gc[j, m, rows] = total[:, j * TILE : (j + 1) * TILE]
            vsum[0:1] += gain_part
            vsum[1:2] += shift_part
        if m == 0:
            inner[2].merge()
            down.collect()
            up.collect()
            out.advance(3)
            inner[0].advance(2)
            inner[1].advance(2)
    for j in range(tiles):
        copies.out(gc.at[j], ref.input_grad.at[:, :, pl.ds(j * TILE, TILE)])
    inner[2].advance(1)
    inner[0].advance(3)
    inner[1].advance(3)
    out.collect()

    net = ref.net
    pre_copy.wait()
    feature_copy.wait()
    frequency = net[EMB + 3 + 2 * HID : EMB + 4 + 2 * HID]

    def filter_back(at):
        rows = pl.ds(pl.multiple_of(at * TILE, TILE), TILE)
        half, part = at // (count // TILE), lax.rem(at, count // TILE)
        held = pl.ds(pl.multiple_of(part * TILE, TILE), TILE)
        at_row = lax.broadcasted_iota(jnp.int32, (TILE, TILE), 0) + at * TILE
        scaled = at_row.astype(f32) * (1.0 / slot)
        layers = [gk[0, rows, i * HID : (i + 1) * HID] for i in range(3)]
        acts = [jnp.sin(frequency * layer) for layer in layers]
        slopes = [jnp.cos(frequency * layer) for layer in layers]
        last = acts[2].astype(bf16)
        grad = jnp.zeros((TILE, HID), f32)
        for j in range(tiles):
            lane = slice(j * TILE, (j + 1) * TILE)
            window = jnp.exp(-scaled * ref.rate[:, lane]) + 0.05
            shaped = (gate[j, half, held].astype(f32) * window).astype(bf16)
            vsum[FINAL_ROW : FINAL_ROW + HID, lane] += dot_tn(last, shaped)
            grad = grad + dot_nt(shaped, ref.final[:, lane].astype(bf16))
        freq_sum = jnp.zeros_like(frequency)
        for i in (2, 1, 0):
            turn = grad * slopes[i]
            freq_sum = freq_sum + jnp.sum(turn * layers[i], axis=0, keepdims=True)
            grad = turn * frequency
            if i == 0:
                nsum[: EMB + 1, :HID] += lax.dot_general(
                    gk[1, rows, : EMB + 1], grad, (((0,), (0,)), ((), ())),
                    precision=highest, preferred_element_type=f32,
                )
            else:
                first = EMB + 1 if i == 1 else EMB + 2 + HID
                nsum[first : first + HID, :HID] += lax.dot_general(
                    acts[i - 1], grad, (((0,), (0,)), ((), ())),
                    precision=highest, preferred_element_type=f32,
                )
                nsum[first + HID : first + HID + 1, :HID] += jnp.sum(grad, axis=0, keepdims=True)
                grad = lax.dot_general(
                    grad, net[first : first + HID], (((1,), (1,)), ((), ())),
                    precision=highest, preferred_element_type=f32,
                )
        row = EMB + 3 + 2 * HID
        nsum[row : row + 1, :HID] += freq_sum

    blocks = slot // TILE

    @pl.loop(0, blocks // 2)
    def _(at):
        filter_back(at)

    inner[2].advance(2)
    inner[0].collect()
    inner[1].collect()

    @pl.loop(blocks // 2, blocks)
    def _(at):
        filter_back(at)

    smalls = []
    for values, sums, name in ((vsum, ref.v_out, "v"), (nsum, ref.n_out, "n")):
        parts = [getattr(ref, name + str(k)) for k in range(4)]
        smalls.append(SmallSum(ring, values, *parts[:3], sums, parts[3]))
    for work in smalls:
        work.begin()
    inner[2].advance(3)
    psum = ref.proj_sum
    wide = psum.shape[1] - 4 * width
    ref.down_sum[...] = down.result()
    for work in smalls:
        work.add_up()
    psum[:, 4 * width : 4 * width + wide] = up.result()
    psum[:, 3 * width : 4 * width] = out.result()
    inner[2].collect()
    for work in smalls:
        work.spread()
    for j in range(tiles):
        total = inner[j].result()
        for p in range(3):
            first = p * width + j * TILE
            psum[:, first : first + TILE] = total[:, p * TILE : (p + 1) * TILE]
    for work in smalls:
        work.finish()
    for work in [down, up, out] + inner:
        work.finish()
    for edge in edges:
        edge.wait_send()
    copies.finish()


def back(size, arrays):
    chips = size // 2
    micro, count, width = arrays["gb"].shape
    rows, wide = arrays["dup"].shape[2:]
    down_rows = arrays["ddown"].shape[2]
    tiles = width // TILE
    vmem = pl.BlockSpec(memory_space=pltpu.VMEM)
    anywhere = pl.BlockSpec(memory_space=pl.ANY)
    smem = pl.BlockSpec(memory_space=pltpu.SMEM)
    near = ("gb", "vec", "net", "final", "rate", "table", "back", "win", "wout", "zh", "small")
    small_rows = 8 * size
    outs = dict(
        input_grad=((micro, count, width), bf16),
        proj_sum=((rows, 4 * width + wide), f32),
        down_sum=((down_rows, width), f32),
        v_out=((small_rows, width), f32),
        n_out=((2 * small_rows, 128), f32),
    )
    dma = pltpu.SemaphoreType.DMA
    tile_tokens = (tiles, micro, count, TILE)
    edge_rows = (tiles, micro, 16, 3 * TILE)
    scratch = dict(
        din=pltpu.VMEM((tiles, chips, 2, rows, 3 * TILE), bf16),
        dout=pltpu.VMEM((chips, 2, rows, width), bf16),
        gw=pltpu.VMEM(tile_tokens, bf16),
        gc=pltpu.VMEM(tile_tokens, bf16),
        gcr=pltpu.VMEM(tile_tokens, bf16),
        gate=pltpu.VMEM(tile_tokens, bf16),
        gz=pltpu.VMEM((tiles, micro, count, 3 * TILE), bf16),
        turned=pltpu.VMEM((micro, width, count), bf16),
        vsum=pltpu.VMEM((small_rows, width), f32),
        nsum=pltpu.VMEM((2 * small_rows, 128), f32),
        gk=pltpu.VMEM((2, 2 * count, TILE), f32),
        gbuf=pltpu.VMEM((count + 16, TILE), f32),
        zbuf=pltpu.VMEM((count + 16, TILE), f32),
        ebuf=pltpu.VMEM((32, TILE), f32),
        spec=pltpu.VMEM((2 * count, TILE), bf16),
        first_rows=pltpu.VMEM(edge_rows, bf16),
        last_rows=pltpu.VMEM(edge_rows, bf16),
        next_rows=pltpu.VMEM(edge_rows, bf16),
        s_buf=pltpu.VMEM((2, count, 2 * TILE), bf16),
        z_buf=pltpu.VMEM((2, count, 3 * TILE), bf16),
        u_buf=pltpu.VMEM((2, 2, 2 * count, TILE), bf16),
        c_buf=pltpu.VMEM((2, count, TILE), bf16),
        k_buf=pltpu.VMEM((2, 2 * count, TILE), bf16),
        load_sems=dma((2, 4)),
        kernel_sem=dma((1,)),
        gc_sem=dma((2, tiles)),
        edge_sem=dma((2, tiles)),
        copy_sems=dma((16,)),
        up_stage=pltpu.VMEM((2, rows, wide), bf16),
        down_stage=pltpu.VMEM((2, down_rows, width), bf16),
        up_stage_sems=dma((2,)),
        down_stage_sems=dma((2,)),
    )
    ups, downs = chips // 2, (chips - 1) // 2
    for name, lead, dims in (
        ("up", (), (rows, wide)), ("down", (), (down_rows, width)), ("out", (), (rows, width)),
        ("in", (tiles,), (rows, 3 * TILE)),
    ):
        made = [pltpu.VMEM(lead + (count,) + dims, bf16) for count in (chips, ups, downs)]
        made += [pltpu.VMEM(lead + dims, bf16)] * 2 + [dma(lead + (2, 2 + ups + downs))]
        for k, part in enumerate(made):
            scratch[name + str(k)] = part
    for name in ("v", "n"):
        for k, part in enumerate(small_scratch(size, *outs[name + "_out"][0])):
            scratch[name + str(k)] = part
    names = tuple(arrays) + tuple(outs) + tuple(scratch)
    return pl.pallas_call(
        functools.partial(back_kernel, size, names),
        out_shape=[jax.ShapeDtypeStruct(*kind) for kind in outs.values()],
        in_specs=[
            smem if name == "lens" else vmem if name in near else anywhere for name in arrays
        ],
        out_specs=[anywhere] + [vmem] * (len(outs) - 1),
        scratch_shapes=list(scratch.values()),
        compiler_params=pltpu.CompilerParams(
            collective_id=1, has_side_effects=True, vmem_limit_bytes=63 * 1024 * 1024
        ),
        name="back",
    )(*arrays.values())


def fits(size, groups, tokens, proj_weights, down_weights):
    micro, _, count, width = tokens.shape
    wide = down_weights.shape[0] * size
    return (
        groups == 2
        and size % 4 == 0
        and size == 16
        and proj_weights.shape[0] % 16 == 0
        and down_weights.shape[0] % 16 == 0
        and count % TILE == 0
        and width == 3 * TILE
        and micro >= groups
        and micro * count <= 1024
        and wide == 4 * width
        and proj_weights.shape[1] == 4 * width + wide
    )


def on_device_tuned(
    block_input,
    out_grad,
    lengths,
    decay_rates,
    proj_weights,
    proj_moment,
    proj_average,
    down_weights,
    down_moment,
    down_average,
    vectors,
    vector_moment,
    vector_average,
    filter_net,
    net_moment,
    net_average,
    filter_out,
    final_moment,
    final_average,
):
    micro, _, count, width = block_input.shape
    size = lax.axis_size("seq")
    tokens = block_input.reshape(micro, count, width)
    plain_table = transform_table(count)
    table = jnp.asarray(plain_table, dtype=bf16)
    table_back = jnp.asarray(plain_table.T, dtype=bf16)
    feature = jnp.asarray(feature_table(count * lax.axis_size("pos")))
    shared = dict(
        x=tokens, lens=lengths, vec=vectors, net=filter_net, final=filter_out,
        rate=decay_rates[None], table=table, back=table_back, feature=feature,
    )
    made = types.SimpleNamespace(**front(size, dict(shared, proj=proj_weights, down=down_weights)))
    block_output, branch_grad, up_step, down_step, small = mlp(
        made.n2, made.n2t, out_grad.reshape(micro, count, width), made.res, vectors,
        made.wup, made.wdown,
    )
    chips = size // 2
    input_grad, proj_sum, down_sum, rest, net_sum = back(
        size,
        dict(
            shared, win=made.win, wout=made.wout, z=made.z, zh=made.zh, s=made.s, conv=made.conv,
            uhat=made.uhat, kern=made.kern, nt=made.nt, yt=made.yt, pre=made.pre,
            gb=branch_grad, small=small,
            dup=up_step.reshape(chips, 2, -1, up_step.shape[1]),
            ddown=down_step.reshape(chips, 2, -1, width),
        ),
    )
    vector_sum = rest[: vectors.shape[0]]
    final_sum = rest[FINAL_ROW : FINAL_ROW + HID]
    net_sum = net_sum[: filter_net.shape[0], :HID]
    return (
        block_output.reshape(block_input.shape),
        input_grad.reshape(block_input.shape),
        *nesterov(proj_weights, proj_moment, proj_average, proj_sum, 0.0001),
        *nesterov(down_weights, down_moment, down_average, down_sum, 0.0001),
        *nesterov(vectors, vector_moment, vector_average, vector_sum, 0.001),
        *nesterov(filter_net, net_moment, net_average, net_sum, 0.0001),
        *nesterov(filter_out, final_moment, final_average, final_sum, 2e-06),
    )


def on_device_plain(
    block_input,
    out_grad,
    lengths,
    decay_rates,
    proj_weights,
    proj_moment,
    proj_average,
    down_weights,
    down_moment,
    down_average,
    vectors,
    vector_moment,
    vector_average,
    filter_net,
    net_moment,
    net_average,
    filter_out,
    final_moment,
    final_average,
):
    micro = block_input.shape[0]
    count = block_input.shape[2]
    width = block_input.shape[3]
    groups = lax.axis_size("pos")
    slot_length = count * groups
    tokens_all = micro * count
    group = lax.axis_index("pos")
    tap = vectors[13:22].reshape(3, 3 * width)
    short_bias = vectors[22:25].reshape(-1)
    in_bias = vectors[4:7].reshape(-1)
    up_bias = vectors[8:12].reshape(-1)
    skip = vectors[25]

    low_rows = proj_weights.astype(bf16)
    in_weight = lax.all_gather(low_rows[:, : 3 * width], "seq", axis=0, tiled=True)
    out_weight = lax.all_gather(low_rows[:, 3 * width : 4 * width], "seq", axis=0, tiled=True)
    up_weight = lax.all_gather(low_rows[:, 4 * width :], "seq", axis=0, tiled=True)
    down_weight = lax.all_gather(down_weights.astype(bf16), "seq", axis=0, tiled=True)

    table = jnp.asarray(transform_table(count))
    table_low = table.astype(bf16)
    every = jnp.arange(slot_length, dtype=jnp.int32)

    def make_filter(net_values, final_values):
        return filter_fn(net_values, final_values, decay_rates, every, slot_length)

    filters, filter_back = jax.vjp(make_filter, filter_net, filter_out)
    pieces = filters.reshape(groups, count, width)
    spectra = [
        jnp.dot(table, pieces[d], precision=lax.Precision.HIGH, preferred_element_type=f32)
        for d in range(groups)
    ]
    kernels = [spectra[0]] + [spectra[d] + turned(spectra[d - 1], 1.0) for d in range(1, groups)]

    def transform(values):
        return jnp.stack([dot(table_low, values[m]) for m in range(micro)])

    def transform_back(spectrum):
        low = spectrum.astype(bf16)
        return jnp.stack([dot_tn(table_low, low[m]) for m in range(micro)]) * (1.0 / count)

    tokens_low = block_input[:, 0]
    before = passed_along(tokens_low[:, -2:], "pos", 1)
    tokens = tokens_low.astype(f32).reshape(tokens_all, width)
    xh_one, scale_one = norm_parts(tokens)
    normed = (xh_one * vectors[0] + vectors[1]).astype(bf16)
    xh_before, _ = norm_parts(before.astype(f32).reshape(micro * 2, width))
    normed_before = (xh_before * vectors[0] + vectors[1]).astype(bf16)
    z = (dot(normed, in_weight) + in_bias).reshape(micro, count, 3 * width)
    z_before = (dot(normed_before, in_weight) + in_bias).reshape(micro, 2, 3 * width)
    z_before = jnp.where(group > 0, z_before, 0.0)
    z_long = jnp.concatenate([z_before, z], axis=1)
    short = (
        tap[0] * z_long[:, 2:] + tap[1] * z_long[:, 1:-1] + tap[2] * z_long[:, :-2] + short_bias
    ).astype(bf16)
    x0 = short[:, :, :width].astype(f32)
    x1 = short[:, :, width : 2 * width].astype(f32)
    v = short[:, :, 2 * width :].astype(f32)

    u = x1 * v
    u_low = u.astype(bf16)
    u_hat = [transform(u_low)]
    for d in range(1, groups):
        u_hat.append(transform(passed_along(u_low, "pos", d)))
    total = product(kernels[0], u_hat[0])
    for d in range(1, groups):
        total = total + product(kernels[d], u_hat[d])
    conv = transform_back(total) + skip * u
    here = group * count + jnp.arange(count, dtype=jnp.int32)
    mask = (here[None, :] < lengths[:, 0][:, None]).astype(f32)[:, :, None]
    y = (mask * x0 * conv).astype(bf16).reshape(tokens_all, width)
    residual = tokens + dot(y, out_weight) + vectors[7]
    xh_two, scale_two = norm_parts(residual)
    normed_two = (xh_two * vectors[2] + vectors[3]).astype(bf16)

    cot_low = out_grad[:, 0].reshape(tokens_all, width)
    cot = cot_low.astype(f32)
    pre = dot(normed_two, up_weight) + up_bias
    hidden, gelu_back = jax.vjp(jax.nn.gelu, pre)
    hidden_low = hidden.astype(bf16)
    block_output = (residual + dot(hidden_low, down_weight) + vectors[12]).astype(bf16)
    pre_grad = gelu_back(dot_nt(cot_low, down_weight))[0].astype(bf16)
    down_step = dot_tn(hidden_low, cot_low)
    up_step = dot_tn(normed_two, pre_grad)
    normed_two_grad = dot_nt(pre_grad, up_weight)
    part, gain_two, shift_two = norm_back(normed_two_grad, xh_two, scale_two, vectors[2])
    residual_grad = cot + part
    branch_low = residual_grad.astype(bf16)
    out_step = dot_tn(y, branch_low)
    y_grad = dot_nt(branch_low, out_weight).astype(bf16).astype(f32).reshape(micro, count, width)

    gw = mask * y_grad
    gx0 = gw * conv
    gc = gw * x0
    gc_low = gc.astype(bf16)
    skip_grad = jnp.sum(gc * u, axis=(0, 1))
    gc_hat = [transform(gc_low)]
    for d in range(1, groups):
        gc_hat.append(transform(passed_along(gc_low, "pos", -d)))
    back = product_conj(kernels[0], gc_hat[0])
    for d in range(1, groups):
        back = back + product_conj(kernels[d], gc_hat[d])
    gu = transform_back(back) + skip * gc
    kernel_grads = [jnp.sum(product_conj(u_hat[d], gc_hat[0]), axis=0) for d in range(groups)]
    filter_grads = []
    for d in range(groups):
        got = kernel_grads[d]
        if d + 1 < groups:
            got = got + turned(kernel_grads[d + 1], -1.0)
        filter_grads.append(dot_tn(table_low, got.astype(bf16)) * (1.0 / count))
    net_local, final_local = filter_back(jnp.concatenate(filter_grads, axis=0))
    short_grad = jnp.concatenate([gx0, gu * v, gu * x1], axis=-1).astype(bf16)
    after = passed_along(short_grad[:, :2], "pos", -1)
    short_long = jnp.concatenate([short_grad, after], axis=1).astype(f32)
    z_grad = (
        tap[0] * short_long[:, :-2] + tap[1] * short_long[:, 1:-1] + tap[2] * short_long[:, 2:]
    ).astype(bf16)
    here_grad = short_long[:, :-2]
    tap_grads = [
        jnp.sum(here_grad * z_long[:, 2 - k : 2 - k + count], axis=(0, 1)) for k in range(3)
    ]
    short_bias_grad = jnp.sum(here_grad, axis=(0, 1))
    z_grad = z_grad.reshape(tokens_all, 3 * width)
    in_step = dot_tn(normed, z_grad)
    in_bias_grad = jnp.sum(z_grad.astype(f32), axis=0)
    normed_grad = dot_nt(z_grad, in_weight)
    part, gain_one, shift_one = norm_back(normed_grad, xh_one, scale_one, vectors[0])
    input_grad = (residual_grad + part).astype(bf16)

    vector_local = jnp.concatenate(
        [
            gain_one[None],
            shift_one[None],
            gain_two[None],
            shift_two[None],
            in_bias_grad.reshape(3, width),
            jnp.sum(branch_low.astype(f32), axis=0)[None],
            jnp.sum(pre_grad.astype(f32), axis=0).reshape(4, width),
            jnp.sum(cot, axis=0)[None],
            jnp.stack(tap_grads).reshape(9, width),
            short_bias_grad.reshape(3, width),
            skip_grad[None],
        ],
        axis=0,
    )
    proj_local = jnp.concatenate([in_step, out_step, up_step], axis=1).astype(bf16)
    proj_shard = lax.psum_scatter(proj_local, "seq", scatter_dimension=0, tiled=True)
    down_shard = lax.psum_scatter(down_step.astype(bf16), "seq", scatter_dimension=0, tiled=True)
    proj_sum = lax.psum(proj_shard, "pos").astype(f32)
    down_sum = lax.psum(down_shard, "pos").astype(f32)
    vector_sum, net_sum, final_sum = lax.psum(
        (vector_local, net_local, final_local), ("seq", "pos")
    )
    return (
        block_output.reshape(micro, 1, count, width),
        input_grad.reshape(micro, 1, count, width),
        *nesterov(proj_weights, proj_moment, proj_average, proj_sum, 0.0001),
        *nesterov(down_weights, down_moment, down_average, down_sum, 0.0001),
        *nesterov(vectors, vector_moment, vector_average, vector_sum, 0.001),
        *nesterov(filter_net, net_moment, net_average, net_sum, 0.0001),
        *nesterov(filter_out, final_moment, final_average, final_sum, 2e-06),
    )


def on_device(*arrays):
    tuned = fits(
        lax.axis_size("seq"), lax.axis_size("pos"), arrays[0], arrays[4], arrays[7]
    )
    return (on_device_tuned if tuned else on_device_plain)(*arrays)


def solution(mesh):
    tokens = P(None, "seq", "pos", None)
    rows = P("seq", None)
    whole = P()
    return jax.shard_map(
        on_device,
        mesh=mesh,
        in_specs=(tokens, tokens, P(None, "seq"), whole) + (rows,) * 6 + (whole,) * 9,
        out_specs=(tokens, tokens) + (rows,) * 8 + (whole,) * 12,
        check_vma=False,
    )
```

```python
import functools
import math
import types

import jax
import jax.numpy as jnp
import numpy as np
from jax import lax
from jax.experimental import pallas as pl
from jax.experimental.pallas import tpu as pltpu
from jax.sharding import PartitionSpec as P

HID = 64
EMB = 33

highest = lax.Precision.HIGHEST
f32 = jnp.float32
bf16 = jnp.bfloat16


def passed_along(block, axis, distance):
    devices = range(lax.axis_size(axis))
    route = [(i - distance, i) for i in devices if i - distance in devices]
    return lax.ppermute(block, axis, route)


def dot(a, b):
    return lax.dot_general(a, b, (((1,), (0,)), ((), ())), preferred_element_type=f32)


def dot_tn(a, b):
    return lax.dot_general(a, b, (((0,), (0,)), ((), ())), preferred_element_type=f32)


def dot_nt(a, b):
    return lax.dot_general(a, b, (((1,), (1,)), ((), ())), preferred_element_type=f32)


def features(positions, slot_length):
    band_count = (EMB - 1) // 2
    scaled = positions.astype(f32) / slot_length
    bands = 0.0001 + jnp.arange(band_count, dtype=f32) * (
        (band_count - 1 - 0.0001) / (band_count - 1)
    )
    angles = 2.0 * math.pi * scaled[:, None] * bands[None, :]
    return jnp.concatenate([scaled[:, None], jnp.cos(angles), -jnp.sin(angles)], axis=1)


def filter_fn(net_values, final_values, rates, positions, slot_length):
    embedded = features(positions, slot_length)
    frequency = net_values[EMB + 3 + 2 * HID]
    layer_one = jnp.sin(
        frequency * (jnp.dot(embedded, net_values[:EMB], precision=highest) + net_values[EMB])
    )
    layer_two = jnp.sin(
        frequency
        * (
            jnp.dot(layer_one, net_values[EMB + 1 : EMB + 1 + HID], precision=highest)
            + net_values[EMB + 1 + HID]
        )
    )
    layer_three = jnp.sin(
        frequency
        * (
            jnp.dot(layer_two, net_values[EMB + 2 + HID : EMB + 2 + 2 * HID], precision=highest)
            + net_values[EMB + 2 + 2 * HID]
        )
    )
    shaped = jnp.dot(layer_three, final_values, precision=highest)
    scaled = positions.astype(f32) / slot_length
    window = jnp.exp(-scaled[:, None] * rates[None, :]) + 0.05
    return shaped * window


def transform_table(length):
    product = np.outer(2 * np.arange(length) + 1, np.arange(length)) % (4 * length)
    angle = product.astype(np.float64) * (math.pi / (2 * length))
    return np.concatenate([np.cos(angle), -np.sin(angle)], axis=0).astype(np.float32)


def feature_table(slot_length):
    scaled = np.arange(slot_length, dtype=np.float32) / np.float32(slot_length)
    band_count = (EMB - 1) // 2
    bands = np.float32(0.0001) + np.arange(band_count, dtype=np.float32) * np.float32(
        (band_count - 1 - 0.0001) / (band_count - 1)
    )
    angles = (np.float32(2.0 * math.pi) * scaled[:, None]) * bands[None, :]
    table = np.zeros((slot_length, 4 * HID), np.float32)
    table[:, 0] = scaled
    table[:, 1 : 1 + band_count] = np.cos(angles)
    table[:, 1 + band_count : EMB] = -np.sin(angles)
    table[:, EMB] = 1.0
    return table


def halves(spectrum):
    half = spectrum.shape[-2] // 2
    return spectrum[..., :half, :], spectrum[..., half:, :]


def turned(spectrum, sign):
    re, im = halves(spectrum)
    parity = (1.0 - 2.0 * (jnp.arange(re.shape[-2]) % 2).astype(f32))[:, None] * sign
    return jnp.concatenate([-parity * im, parity * re], axis=-2)


def product(kernel, signal):
    kr, ki = halves(kernel)
    sr, si = halves(signal)
    return jnp.concatenate([kr * sr - ki * si, kr * si + ki * sr], axis=-2)


def product_conj(kernel, signal):
    kr, ki = halves(kernel)
    sr, si = halves(signal)
    return jnp.concatenate([kr * sr + ki * si, kr * si - ki * sr], axis=-2)


def nesterov(weight, moment, average, gradient, rate):
    moment_next = 0.9 * moment + gradient
    weight_next = weight - rate * (gradient + 0.9 * moment_next)
    average_next = 0.9 * average + 0.1 * weight_next
    return (gradient, weight_next, moment_next, average_next)


def norm_parts(values):
    center = jnp.mean(values, axis=-1, keepdims=True)
    centred = values - center
    variance = jnp.mean(centred * centred, axis=-1, keepdims=True)
    scale = lax.rsqrt(variance + 1e-05)
    return centred * scale, scale


def norm_back(grad, xh, scale, gain):
    q = grad * gain
    return (
        (q - jnp.mean(q, -1, keepdims=True) - xh * jnp.mean(q * xh, -1, keepdims=True)) * scale,
        jnp.sum(grad * xh, axis=0),
        jnp.sum(grad, axis=0),
    )


MESH = pl.DeviceIdType.MESH


class Ring:
    def __init__(self, size):
        self.size = size
        self.count = size // 2
        self.seq = lax.axis_index("seq")
        self.pos = lax.axis_index("pos")
        self.core = lax.rem(self.seq, 2)
        chip = self.seq // 2
        odd = lax.rem(chip, 2)
        self.place = (1 - odd) * (chip // 2) + odd * (self.count - 1 - chip // 2)

    def chip(self, shift):
        place = lax.rem(self.place + (shift + self.count), self.count)
        low = jnp.where(place < self.count // 2, 1, 0)
        return low * (2 * place) + (1 - low) * (2 * (self.count - 1 - place) + 1)

    def device(self, shift):
        return {"seq": 2 * self.chip(shift) + self.core}

    @property
    def sibling(self):
        return {"seq": self.seq + 1 - 2 * self.core}

    @property
    def across(self):
        return {"pos": 1 - self.pos}


def greet_all(ring):
    barrier = pltpu.get_barrier_semaphore()
    for step in range(1, ring.size):
        other = lax.rem(ring.seq + step, ring.size)
        pl.semaphore_signal(barrier, inc=1, device_id={"seq": other}, device_id_type=MESH)
    pl.semaphore_signal(barrier, inc=1, device_id=ring.across, device_id_type=MESH)
    pl.semaphore_wait(barrier, ring.size)


def remote(src, dst, send, recv, device):
    return pltpu.make_async_remote_copy(
        src_ref=src, dst_ref=dst, send_sem=send, recv_sem=recv, device_id=device,
        device_id_type=MESH,
    )


class Reduction:
    def __init__(self, ring, grad, twin, up, down, own, other, sems, stage=None, stage_sems=None):
        self.ring = ring
        self.grad, self.twin, self.up, self.down = grad, twin, up, down
        self.own, self.other = own, other
        self.sems = sems
        self.stage, self.stage_sems = stage, stage_sems
        self.ups = ring.count // 2
        self.downs = (ring.count - 1) // 2

    def copies(self):
        ring = self.ring
        made = [(self.grad.at[:, 1 - ring.core], self.twin, ring.sibling)]
        for step in range(self.ups):
            block = self.twin.at[ring.chip(self.ups - step)]
            made.append((block, self.up.at[step], ring.device(1)))
        for step in range(self.downs):
            block = self.twin.at[ring.chip(step - self.downs)]
            made.append((block, self.down.at[step], ring.device(-1)))
        made.append((self.own, self.other, ring.across))
        return made

    def copy(self, index):
        src, dst, device = self.copies()[index]
        return remote(src, dst, self.sems.at[0, index], self.sems.at[1, index], device)

    def begin(self):
        self.copy(0).start()

    def fetch(self, chip, slot):
        return pltpu.make_async_copy(
            self.grad.at[chip, self.ring.core], self.stage.at[slot], self.stage_sems.at[slot]
        )

    def merge(self):
        core = self.ring.core
        count = self.ring.count
        if self.stage is None:
            self.copy(0).wait_recv()

            @pl.loop(0, count)
            def _(chip):
                self.twin[chip] = self.twin[chip] + self.grad[chip, core]

        else:
            self.fetch(0, 0).start()
            self.copy(0).wait_recv()

            @pl.loop(0, count)
            def _(chip):
                slot = lax.rem(chip, 2)

                @pl.when(chip + 1 < count)
                def _():
                    self.fetch(chip + 1, 1 - slot).start()

                self.fetch(chip, slot).wait()
                self.twin[chip] = self.twin[chip] + self.stage[slot]

        self.copy(1).start()
        self.copy(1 + self.ups).start()

    def advance(self, step):
        self.copy(step).wait_recv()
        owner = self.ring.chip(self.ups - step)
        self.twin[owner] = self.twin[owner] + self.up[step - 1]
        self.copy(1 + step).start()
        if step < self.downs:
            self.copy(self.ups + step).wait_recv()
            owner = self.ring.chip(step - self.downs)
            self.twin[owner] = self.twin[owner] + self.down[step - 1]
            self.copy(1 + self.ups + step).start()

    def collect(self):
        self.copy(self.ups).wait_recv()
        self.copy(self.ups + self.downs).wait_recv()
        mine = self.ring.chip(0)
        total = (
            self.twin[mine].astype(f32)
            + self.up[self.ups - 1].astype(f32)
            + self.down[self.downs - 1].astype(f32)
        )
        self.own[...] = total.astype(bf16)
        self.copy(1 + self.ups + self.downs).start()

    def result(self):
        self.copy(1 + self.ups + self.downs).wait_recv()
        return self.own[...].astype(f32) + self.other[...].astype(f32)

    def finish(self):
        for index in range(2 + self.ups + self.downs):
            self.copy(index).wait_send()


class SmallSum:
    def __init__(self, ring, values, parts, mine, other, sums, sems):
        self.ring, self.values, self.parts = ring, values, parts
        self.mine, self.other, self.sums = mine, other, sums
        self.sems = sems
        self.rows = parts.shape[1]
        self.waiting = []

    def block(self, index):
        return pl.ds(pl.multiple_of(index * self.rows, 8), self.rows)

    def begin(self):
        ring = self.ring
        self.arriving = []
        for step in range(1, ring.size):
            other = lax.rem(ring.seq + step, ring.size)
            copy = remote(
                self.values.at[self.block(other)], self.parts.at[step],
                self.sems.at[0, step], self.sems.at[1, step], {"seq": other},
            )
            copy.start()
            self.arriving.append(copy)
            self.waiting.append(copy)

    def add_up(self):
        for copy in self.arriving:
            copy.wait_recv()
        total = self.values[self.block(self.ring.seq)]
        for step in range(1, self.ring.size):
            total = total + self.parts[step]
        self.mine[...] = total
        self.crossing = remote(
            self.mine, self.other, self.sems.at[0, 0], self.sems.at[1, 0], self.ring.across
        )
        self.crossing.start()
        self.waiting.append(self.crossing)

    def spread(self):
        self.crossing.wait_recv()
        block = self.block(self.ring.seq)
        self.sums[block] = self.mine[...] + self.other[...]
        self.arriving = []
        for step in range(1, self.ring.size):
            other = lax.rem(self.ring.seq + step, self.ring.size)
            copy = remote(
                self.sums.at[block], self.sums.at[block],
                self.sems.at[2, step], self.sems.at[3, step], {"seq": other},
            )
            copy.start()
            self.waiting.append(copy)
            back = lax.rem(self.ring.seq + (self.ring.size - step), self.ring.size)
            self.arriving.append(
                remote(
                    self.sums.at[self.block(back)], self.sums.at[self.block(back)],
                    self.sems.at[2, step], self.sems.at[3, step], {"seq": other},
                )
            )

    def finish(self):
        for copy in self.arriving:
            copy.wait_recv()
        for copy in self.waiting:
            copy.wait_send()


def reduction_scratch(size, rows, columns):
    chips = size // 2
    ups, downs = chips // 2, (chips - 1) // 2
    return [
        pltpu.VMEM((chips, rows, columns), bf16),
        pltpu.VMEM((ups, rows, columns), bf16),
        pltpu.VMEM((downs, rows, columns), bf16),
        pltpu.VMEM((rows, columns), bf16),
        pltpu.VMEM((rows, columns), bf16),
        pltpu.SemaphoreType.DMA((2, 2 + ups + downs)),
    ]


def small_scratch(size, rows, columns):
    return [
        pltpu.VMEM((size, rows // size, columns), f32),
        pltpu.VMEM((rows // size, columns), f32),
        pltpu.VMEM((rows // size, columns), f32),
        pltpu.SemaphoreType.DMA((4, size)),
    ]


class Gather:
    def __init__(self, ring, mine, full, sems):
        self.ring, self.mine, self.full, self.sems = ring, mine, full, sems
        self.ups = ring.count // 2
        self.downs = (ring.count - 1) // 2
        self.waiting, self.arriving = [], []

    def send(self, src, place, index, device):
        copy = remote(
            src, self.full.at[self.ring.chip(place), self.ring.core],
            self.sems.at[0, index], self.sems.at[1, index], device,
        )
        copy.start()
        self.waiting.append(copy)
        return copy

    def share(self, src, place, index):
        index = self.ups + self.downs + index
        self.send(src, place, index, self.ring.sibling)
        block = self.full.at[self.ring.chip(place), 1 - self.ring.core]
        self.arriving.append(
            remote(block, block, self.sems.at[0, index], self.sems.at[1, index], self.ring.sibling)
        )

    def wait_block(self, place, index, device):
        block = self.full.at[self.ring.chip(place), self.ring.core]
        remote(block, block, self.sems.at[0, index], self.sems.at[1, index], device).wait_recv()
        return block

    def begin(self):
        ring = self.ring
        self.send(self.mine, 0, 0, ring.device(1))
        self.send(self.mine, 0, self.ups, ring.device(-1))
        self.share(self.mine, 0, 0)
        self.local = pltpu.make_async_copy(
            self.mine, self.full.at[ring.chip(0), ring.core], self.sems.at[2, 0]
        )
        self.local.start()

    def advance(self, step):
        ring = self.ring
        block = self.wait_block(-step, step - 1, ring.device(1))
        if step < self.ups:
            self.send(block, -step, step, ring.device(1))
        self.share(block, -step, step)
        if step <= self.downs:
            block = self.wait_block(step, self.ups + step - 1, ring.device(-1))
            if step < self.downs:
                self.send(block, step, self.ups + step, ring.device(-1))
            self.share(block, step, self.ups + step)

    def arrive(self):
        self.local.wait()
        for copy in self.arriving:
            copy.wait_recv()

    def finish(self):
        for copy in self.waiting:
            copy.wait_send()


def gather_sems(size):
    chips = size // 2
    return pltpu.SemaphoreType.DMA((3, 2 * chips))


PI_PARTS = (3.140625, 9.676535897932384e-4)


def sin_cos(x):
    turns = jnp.floor(x * (1.0 / math.pi) + 0.5)
    rest = (x - turns * PI_PARTS[0]) - turns * PI_PARTS[1]
    half = turns * 0.5
    sign = 1.0 - 4.0 * (half - jnp.floor(half))
    square = rest * rest
    odd = 1.0 / 6227020800.0
    for factor in (-1.0 / 39916800.0, 1.0 / 362880.0, -1.0 / 5040.0, 1.0 / 120.0, -1.0 / 6.0):
        odd = odd * square + factor
    even = 1.0 / 479001600.0
    for factor in (-1.0 / 3628800.0, 1.0 / 40320.0, -1.0 / 720.0, 1.0 / 24.0, -0.5):
        even = even * square + factor
    signed = sign * rest
    return signed + signed * square * odd, sign + sign * square * even


def norm_rows(values):
    center = jnp.mean(values, axis=1, keepdims=True)
    centred = values - center
    variance = jnp.mean(centred * centred, axis=1, keepdims=True)
    return centred * lax.rsqrt(variance + 1e-05)


TILE = 256


class Copies:
    def __init__(self, sems):
        self.sems, self.used, self.open = sems, 0, []

    def start(self, src, dst):
        copy = pltpu.make_async_copy(src, dst, self.sems.at[self.used])
        self.used += 1
        copy.start()
        return copy

    def out(self, src, dst):
        self.open.append(self.start(src, dst))

    def finish(self):
        for copy in self.open:
            copy.wait()


def valid_rows(length, first, rows, columns):
    at = lax.broadcasted_iota(jnp.int32, (rows, columns), 0) + first
    return jnp.where(at < length, 1.0, 0.0).astype(f32)


def front_kernel(size, names, *refs):
    ref = types.SimpleNamespace(**dict(zip(names, refs)))
    x, vec, net = ref.x_in, ref.vec, ref.net_in
    micro, count, width = x.shape
    slot = 2 * count
    tiles = width // TILE
    ring = Ring(size)
    copies = Copies(ref.copy_sems)
    proj_copy = copies.start(ref.proj, ref.proj_in)
    x_copy = copies.start(ref.x, x)
    down_copy = copies.start(ref.down, ref.down_in)
    feature_copy = copies.start(ref.feature, ref.feature_in)
    table_copy = copies.start(ref.table, ref.table_in)
    back_copy = copies.start(ref.back, ref.back_in)
    table, table_back = ref.table_in, ref.back_in
    inside = jnp.where(ring.pos > 0, 1.0, 0.0).astype(f32)

    proj_copy.wait()
    own = ref.in_own
    for j in range(tiles):
        for p in range(3):
            first = p * width + j * TILE
            own[j, :, p * TILE : (p + 1) * TILE] = ref.proj_in[:, first : first + TILE].astype(bf16)
    greet_all(ring)
    gather = [Gather(ring, own.at[j], ref.win_in.at[j], ref.win_sem.at[j]) for j in range(tiles)]
    gather_out = Gather(ring, ref.out_own, ref.wout_in, ref.wout_sem)
    gather_up = Gather(ring, ref.up_own, ref.wup, ref.wup_sem)
    gather_down = Gather(ring, ref.down_own, ref.wdown, ref.wdown_sem)
    gather[0].begin()
    gather[1].begin()
    x_copy.wait()
    edge = remote(
        x.at[:, pl.ds(count - 16, 16)], ref.halo, ref.halo_sem.at[0],
        ref.halo_sem.at[1], ring.across,
    )
    edge.start()

    gain, shift = vec[0:1], vec[1:2]
    normed_ref, turned_ref = ref.n_in, ref.nt_in

    def first_norm(m):
        for part in range(count // TILE):
            rows = slice(part * TILE, (part + 1) * TILE)
            normed = (norm_rows(x[m, rows].astype(f32)) * gain + shift).astype(bf16)
            normed_ref[m, rows] = normed
            turned_ref[m, :, rows] = normed.T

    first_norm(0)
    gather[0].advance(1)
    gather[1].advance(1)
    gather[2].begin()
    for m in range(1, micro):
        first_norm(m)
    copies.out(turned_ref, ref.nt)
    ref.out_own[...] = ref.proj_in[:, 3 * width : 4 * width].astype(bf16)
    gather[0].advance(2)
    gather[1].advance(2)
    edge.wait_recv()
    for m in range(micro):
        ref.halo_n[m] = (norm_rows(ref.halo[m].astype(f32)) * gain + shift).astype(bf16)
    feature_copy.wait()

    net[...] = ref.net[...].T
    frequency = net[EMB + 3 + 2 * HID : EMB + 4 + 2 * HID]
    rates = ref.rate[...].reshape(1, width)

    def filter_rows(at):
        rows = slice(at * TILE, (at + 1) * TILE)
        layer = jnp.dot(
            ref.feature_in[rows, : net.shape[0]], net[...], precision=highest,
            preferred_element_type=f32,
        )
        ref.pre_in[rows, :HID] = layer
        layer = sin_cos(frequency * layer)[0]
        for i, first in ((1, EMB + 1), (2, EMB + 2 + HID)):
            layer = (
                jnp.dot(
                    layer, net[first : first + HID], precision=highest,
                    preferred_element_type=f32,
                )
                + net[first + HID : first + HID + 1]
            )
            ref.pre_in[rows, i * HID : (i + 1) * HID] = layer
            layer = sin_cos(frequency * layer)[0]
        shaped = dot(layer.astype(bf16), ref.final[...].astype(bf16))
        at_row = lax.broadcasted_iota(jnp.int32, (TILE, width), 0) + at * TILE
        scaled = at_row.astype(f32) * (1.0 / slot)
        window = jnp.exp(-scaled * rates) + 0.05
        ref.filt[rows] = (shaped * window).astype(bf16)

    row_blocks = slot // TILE
    filter_rows(0)
    gather[0].advance(3)
    gather[1].advance(3)
    gather[2].advance(1)
    down_copy.wait()
    ref.up_own[...] = ref.proj_in[:, 4 * width :].astype(bf16)
    ref.down_own[...] = ref.down_in[...].astype(bf16)
    gather[0].advance(4)
    gather[2].advance(2)
    gather_out.begin()
    gather[1].advance(4)
    gather[0].arrive()

    z_in, s_in, ulow, urecv = ref.z_in, ref.s_in, ref.ulow, ref.urecv
    zbuf, spec = ref.zbuf, ref.spec
    crossing = []

    def project(j):
        weight = ref.win_in[j].reshape(width, 3 * TILE)
        bias = jnp.concatenate(
            [vec[4 + p : 5 + p, j * TILE : (j + 1) * TILE] for p in range(3)], axis=1
        )
        lane = slice(j * TILE, (j + 1) * TILE)

        @pl.loop(0, micro)
        def _(m):
            z = dot(normed_ref[m], weight) + bias
            zh = (dot(ref.halo_n[m], weight) + bias) * inside
            z_in[j, m] = z.astype(bf16)
            ref.zh_in[j, m] = zh.astype(bf16)
            zbuf[:16] = zh
            zbuf[16:] = z
            for p in range(3):
                cols = slice(p * TILE, (p + 1) * TILE)
                s_in[j, m, :, cols] = (
                    vec[13 + p : 14 + p, lane] * zbuf[16:, cols]
                    + vec[16 + p : 17 + p, lane] * zbuf[15 : 15 + count, cols]
                    + vec[19 + p : 20 + p, lane] * zbuf[14 : 14 + count, cols]
                    + vec[22 + p : 23 + p, lane]
                ).astype(bf16)
            ulow[j, m] = (
                s_in[j, m, :, TILE : 2 * TILE].astype(f32) * s_in[j, m, :, 2 * TILE :].astype(f32)
            ).astype(bf16)

        copy = remote(
            ulow.at[j], urecv.at[j], ref.u_sem.at[0, j], ref.u_sem.at[1, j], ring.across
        )
        copy.start()
        crossing.append(copy)
        copies.out(z_in.at[j], ref.z.at[j])
        copies.out(s_in.at[j], ref.s.at[j])

    project(0)
    gather[2].advance(3)
    gather_up.begin()
    gather[1].arrive()
    project(1)
    gather[2].advance(4)
    gather_down.begin()
    gather_out.advance(1)
    gather[2].arrive()
    project(2)
    copies.out(ref.zh_in, ref.zh)
    copies.out(ref.win_in, ref.win)
    gather_out.advance(2)
    for at in range(1, row_blocks):
        filter_rows(at)
        if at == 2:
            gather_up.advance(1)
            gather_out.advance(3)
    copies.out(ref.pre_in, ref.pre)
    gather_down.advance(1)
    gather_out.advance(4)
    gather_out.arrive()
    copies.out(ref.wout_in, ref.wout)
    table_copy.wait()
    back_copy.wait()

    parity = 1.0 - 2.0 * (
        lax.broadcasted_iota(jnp.int32, (count, TILE), 0) % 2
    ).astype(f32)
    kern, uhat = ref.kern_in, ref.uhat_in

    @pl.loop(0, tiles)
    def _(j):
        cols = pl.ds(pl.multiple_of(j * TILE, TILE), TILE)
        zero = dot(table[...], ref.filt[:count, cols])
        kern[j, 0] = zero.astype(bf16)
        one = dot(table[...], ref.filt[count:, cols])
        kern[j, 1, :count] = (one[:count] - parity * zero[count:]).astype(bf16)
        kern[j, 1, count:] = (one[count:] + parity * zero[:count]).astype(bf16)
        for m in range(micro):
            uhat[j, m, 0] = dot(table[...], ulow[j, m]).astype(bf16)

    copies.out(kern, ref.kern)
    gather_up.advance(2)

    def mix(j):
        crossing[j].wait_recv()
        lane = slice(j * TILE, (j + 1) * TILE)

        @pl.loop(0, micro)
        def _(m):
            other = dot(table[...], urecv[j, m]) * inside
            uhat[j, m, 1] = other.astype(bf16)
            k0r, k0i = kern[j, 0, :count].astype(f32), kern[j, 0, count:].astype(f32)
            k1r, k1i = kern[j, 1, :count].astype(f32), kern[j, 1, count:].astype(f32)
            ur, ui = uhat[j, m, 0, :count].astype(f32), uhat[j, m, 0, count:].astype(f32)
            vr, vi = other[:count], other[count:]
            spec[:count] = (k0r * ur - k0i * ui + k1r * vr - k1i * vi).astype(bf16)
            spec[count:] = (k0r * ui + k0i * ur + k1r * vi + k1i * vr).astype(bf16)
            gated = s_in[j, m, :, TILE : 2 * TILE].astype(f32) * s_in[j, m, :, 2 * TILE :].astype(f32)
            conv = dot(table_back[...], spec[...]) * (1.0 / count) + vec[25:26, lane] * gated
            ref.conv_in[j, m] = conv.astype(bf16)
            mask = valid_rows(ref.lens[0, m], ring.pos * count, count, TILE)
            ref.y_in[m, :, lane] = (
                mask * s_in[j, m, :, :TILE].astype(f32) * conv
            ).astype(bf16)

        copies.out(ref.conv_in.at[j], ref.conv.at[j])
        copies.out(uhat.at[j], ref.uhat.at[j])

    for j in range(tiles):
        mix(j)
        if j == 0:
            gather_down.advance(2)
        if j == 1:
            gather_up.advance(3)

    for m in range(micro):
        branch = dot(ref.y_in[m], ref.wout_in[...].reshape(width, width))
        for part in range(count // TILE):
            rows = slice(part * TILE, (part + 1) * TILE)
            ref.yt_in[m, :, rows] = ref.y_in[m, rows].T
            residual = x[m, rows].astype(f32) + branch[rows] + vec[7:8]
            ref.res_in[m, rows] = residual
            normed = (norm_rows(residual) * vec[2:3] + vec[3:4]).astype(bf16)
            ref.n2_in[m, rows] = normed
            ref.n2t_in[m, :, rows] = normed.T
        for src, dst in (
            (ref.yt_in, ref.yt), (ref.res_in, ref.res), (ref.n2_in, ref.n2), (ref.n2t_in, ref.n2t)
        ):
            copies.out(src.at[m], dst.at[m])
        if m == 0:
            gather_down.advance(3)
    gather_up.advance(4)
    gather_down.advance(4)
    for work in (gather_up, gather_down):
        work.arrive()
    for work in gather + [gather_out, gather_up, gather_down]:
        work.finish()
    edge.wait_send()
    for copy in crossing:
        copy.wait_send()
    copies.finish()


def front(size, arrays):
    chips = size // 2
    micro, count, width = arrays["x"].shape
    rows, down_rows = arrays["proj"].shape[0], arrays["down"].shape[0]
    wide = down_rows * size
    tiles = width // TILE
    vmem = pl.BlockSpec(memory_space=pltpu.VMEM)
    anywhere = pl.BlockSpec(memory_space=pl.ANY)
    smem = pl.BlockSpec(memory_space=pltpu.SMEM)
    near = ("vec", "net", "final", "rate")
    kinds = dict(
        win=((tiles, chips, 2, rows, 3 * TILE), bf16),
        wout=((chips, 2, rows, width), bf16),
        z=((tiles, micro, count, 3 * TILE), bf16),
        zh=((tiles, micro, 16, 3 * TILE), bf16),
        s=((tiles, micro, count, 3 * TILE), bf16),
        conv=((tiles, micro, count, TILE), bf16),
        uhat=((tiles, micro, 2, 2 * count, TILE), bf16),
        kern=((tiles, 2, 2 * count, TILE), bf16),
        res=((micro, count, width), f32),
        nt=((micro, width, count), bf16),
        n2=((micro, count, width), bf16),
        n2t=((micro, width, count), bf16),
        yt=((micro, width, count), bf16),
        pre=((2 * count, 4 * HID), f32),
    )
    outs = dict(
        kinds,
        wup=((chips, 2, rows, wide), bf16),
        wdown=((chips, 2, down_rows, width), bf16),
    )
    dma = pltpu.SemaphoreType.DMA
    scratch = {
        name + "_in": pltpu.VMEM(*kind) for name, kind in kinds.items()
    }
    for name, array in arrays.items():
        if name not in near and name != "lens":
            scratch[name + "_in"] = pltpu.VMEM(array.shape, array.dtype)
    scratch.update(
        dict(
            n_in=pltpu.VMEM((micro, count, width), bf16),
            net_in=pltpu.VMEM((EMB + 4 + 2 * HID, HID), f32),
            y_in=pltpu.VMEM((micro, count, width), bf16),
            in_own=pltpu.VMEM((tiles, rows, 3 * TILE), bf16),
            out_own=pltpu.VMEM((rows, width), bf16),
            up_own=pltpu.VMEM((rows, wide), bf16),
            down_own=pltpu.VMEM((down_rows, width), bf16),
            halo=pltpu.VMEM((micro, 16, width), bf16),
            halo_n=pltpu.VMEM((micro, 16, width), bf16),
            filt=pltpu.VMEM((2 * count, width), bf16),
            zbuf=pltpu.VMEM((16 + count, 3 * TILE), f32),
            ulow=pltpu.VMEM((tiles, micro, count, TILE), bf16),
            urecv=pltpu.VMEM((tiles, micro, count, TILE), bf16),
            spec=pltpu.VMEM((2 * count, TILE), bf16),
            win_sem=dma((tiles, 3, 2 * chips)),
            wout_sem=gather_sems(size),
            wup_sem=gather_sems(size),
            wdown_sem=gather_sems(size),
            halo_sem=dma((2,)),
            u_sem=dma((2, tiles)),
            copy_sems=dma((40,)),
        )
    )
    names = tuple(arrays) + tuple(outs) + tuple(scratch)
    made = pl.pallas_call(
        functools.partial(front_kernel, size, names),
        out_shape=[jax.ShapeDtypeStruct(*kind) for kind in outs.values()],
        in_specs=[
            smem if name == "lens" else vmem if name in near else anywhere for name in arrays
        ],
        out_specs=[anywhere] * len(outs),
        scratch_shapes=list(scratch.values()),
        compiler_params=pltpu.CompilerParams(
            collective_id=0, has_side_effects=True, vmem_limit_bytes=63 * 1024 * 1024
        ),
        name="front",
    )(*arrays.values())
    return dict(zip(outs, made))


GELU_SCALE = math.sqrt(2.0 / math.pi)


def gelu_pair(a):
    square = a * a
    half = 0.5 + 0.5 * jnp.tanh(a * (GELU_SCALE + (GELU_SCALE * 0.044715) * square))
    hidden = a * half
    bend = 2.0 * GELU_SCALE + (2.0 * GELU_SCALE * 0.134145) * square
    return hidden, half + (hidden - hidden * half) * bend


def mlp_kernel(
    n2_ref, n2t_ref, gm_ref, res_ref, vec_ref, wup_ref, wdown_ref,
    out_ref, gb_ref, dup_ref, ddown_ref, small_ref,
    acc_out, acc_gn, hid_ref, ga_ref,
):
    step, last = pl.program_id(0), pl.num_programs(0) - 1
    micro, count, width = n2_ref.shape
    chunk = width
    tile = 256
    wup = wup_ref[...].reshape(width, chunk)
    wdown = wdown_ref[...].reshape(chunk, width)
    bias = vec_ref[pl.ds(8 + step, 1)]

    @pl.when(step == 0)
    def _():
        acc_out[...] = jnp.zeros_like(acc_out)
        acc_gn[...] = jnp.zeros_like(acc_gn)
        small_ref[...] = jnp.zeros_like(small_ref)

    bias_sum = jnp.zeros((1, chunk), f32)
    ahead = dot(n2_ref[0], wup), dot_nt(gm_ref[0], wdown)
    for m in range(micro):
        pre, grad = ahead
        if m + 1 < micro:
            ahead = dot(n2_ref[m + 1], wup), dot_nt(gm_ref[m + 1], wdown)
        hidden, slope = gelu_pair(pre + bias)
        hidden = hidden.astype(bf16)
        ga = (grad * slope).astype(bf16)
        hid_ref[m] = hidden
        ga_ref[m] = ga
        bias_sum = bias_sum + jnp.sum(ga.astype(f32), axis=0, keepdims=True)
        acc_out[m] += dot(hidden, wdown)
        acc_gn[m] += dot_nt(ga, wup)
    small_ref[pl.ds(4 + step, 1)] = bias_sum
    down_total = dot_tn(hid_ref[0], gm_ref[0])
    up_total = dot(n2t_ref[0], ga_ref[0])
    for m in range(1, micro):
        down_total = down_total + dot_tn(hid_ref[m], gm_ref[m])
        up_total = up_total + dot(n2t_ref[m], ga_ref[m])
    ddown_ref[...] = down_total.astype(bf16)
    dup_ref[...] = up_total.astype(bf16)

    @pl.when(step == last)
    def _():
        for m in range(micro):
            for part in range(count // tile):
                rows = slice(part * tile, (part + 1) * tile)
                residual = res_ref[m, rows]
                out_ref[m, rows] = (residual + acc_out[m, rows] + vec_ref[12:13]).astype(bf16)
                gx, gain_part, grad = norm_rows_back(acc_gn[m, rows], residual, vec_ref[2:3])
                gm = gm_ref[m, rows].astype(f32)
                low = (gm + gx).astype(bf16)
                gb_ref[m, rows] = low
                small_ref[0:1] += gain_part
                small_ref[1:2] += grad
                small_ref[2:3] += jnp.sum(low.astype(f32), axis=0, keepdims=True)
                small_ref[3:4] += jnp.sum(gm, axis=0, keepdims=True)


def norm_rows_back(grad, values, gain):
    center = jnp.mean(values, axis=1, keepdims=True)
    centred = values - center
    variance = jnp.mean(centred * centred, axis=1, keepdims=True)
    scale = lax.rsqrt(variance + 1e-05)
    xh = centred * scale
    q = grad * gain
    gx = scale * (
        q - jnp.mean(q, axis=1, keepdims=True) - xh * jnp.mean(q * xh, axis=1, keepdims=True)
    )
    return gx, jnp.sum(grad * xh, axis=0, keepdims=True), jnp.sum(grad, axis=0, keepdims=True)


def mlp(n2, n2t, gm, res, vectors, wup, wdown):
    micro, count, width = n2.shape
    chips, cores, rows, wide = wup.shape
    steps = wide // width
    per = chips // steps

    def whole(array):
        return pl.BlockSpec(array.shape, lambda i: (0,) * array.ndim)

    def shape(dims, kind=bf16):
        return jax.ShapeDtypeStruct(dims, kind)

    tokens = pl.BlockSpec((micro, count, width), lambda i: (0, 0, 0))
    return pl.pallas_call(
        mlp_kernel,
        grid=(steps,),
        in_specs=[
            whole(n2), whole(n2t), whole(gm), whole(res), whole(vectors),
            pl.BlockSpec((chips, cores, rows, width), lambda i: (0, 0, 0, i)),
            pl.BlockSpec((per, cores, wdown.shape[2], width), lambda i: (i, 0, 0, 0)),
        ],
        out_specs=[
            tokens, tokens,
            pl.BlockSpec((width, width), lambda i: (0, i)),
            pl.BlockSpec((width, width), lambda i: (i, 0)),
            pl.BlockSpec((4 + steps, width), lambda i: (0, 0)),
        ],
        out_shape=[
            shape((micro, count, width)),
            shape((micro, count, width)),
            shape((width, wide)),
            shape((wide, width)),
            shape((4 + steps, width), f32),
        ],
        scratch_shapes=[
            pltpu.VMEM((micro, count, width), f32),
            pltpu.VMEM((micro, count, width), f32),
            pltpu.VMEM((micro, count, width), bf16),
            pltpu.VMEM((micro, count, width), bf16),
        ],
        compiler_params=pltpu.CompilerParams(vmem_limit_bytes=60 * 1024 * 1024),
        name="mlp",
    )(n2, n2t, gm, res, vectors, wup, wdown)


def update_kernel(rates, firsts, *refs):
    count = len(rates)
    ins, outs = refs[: 4 * count], refs[4 * count :]
    for i, (rate, first) in enumerate(zip(rates, firsts)):
        grad_ref, weight_ref, moment_ref, average_ref = ins[4 * i : 4 * i + 4]
        rows, columns = weight_ref.shape
        stepped = nesterov(
            weight_ref[...], moment_ref[...], average_ref[...],
            grad_ref[first : first + rows, :columns], rate,
        )
        for out, value in zip(outs[4 * i : 4 * i + 4], stepped):
            out[...] = value


def update(sets):
    steps = 4
    arrays, in_specs, out_specs, shapes = [], [], [], []

    def spec(shape, cut):
        if cut is None:
            return pl.BlockSpec(shape, lambda i: (0, 0))
        if cut:
            return pl.BlockSpec((shape[0], shape[1] // steps), lambda i: (0, i))
        return pl.BlockSpec((shape[0] // steps, shape[1]), lambda i: (i, 0))

    for grad, weight, moment, average, rate, first, cut in sets:
        arrays += [grad, weight, moment, average]
        in_specs += [spec(grad.shape, cut)] + [spec(weight.shape, cut)] * 3
        out_specs += [spec(weight.shape, cut)] * 4
        shapes += [jax.ShapeDtypeStruct(weight.shape, f32)] * 4
    made = pl.pallas_call(
        functools.partial(update_kernel, [s[4] for s in sets], [s[5] for s in sets]),
        grid=(steps,),
        in_specs=in_specs,
        out_specs=out_specs,
        out_shape=shapes,
        compiler_params=pltpu.CompilerParams(vmem_limit_bytes=40 * 1024 * 1024),
        name="update",
    )(*arrays)
    return [made[4 * i : 4 * i + 4] for i in range(len(sets))]


FINAL_ROW = 32


def back_kernel(size, names, *refs):
    ref = types.SimpleNamespace(**dict(zip(names, refs)))
    gb, vec, table, table_back = ref.gb, ref.vec, ref.table, ref.back
    micro, count, width = gb.shape
    slot = 2 * count
    tiles = width // TILE
    ring = Ring(size)
    gw, gc, gcr, gz = ref.gw, ref.gc, ref.gcr, ref.gz
    vsum, nsum = ref.vsum, ref.nsum
    gate, turned = ref.gate, ref.turned
    inside = jnp.where(ring.pos < 1, 1.0, 0.0).astype(f32)
    copies = Copies(ref.copy_sems)
    gate_copies = [
        copies.start(ref.s.at[j, :, :, pl.ds(0, TILE)], gate.at[j]) for j in range(tiles)
    ]
    turned_copy = copies.start(ref.yt, turned)

    greet_all(ring)
    red = {}

    def parts_of(name):
        return [getattr(ref, name + str(k)) for k in range(6)]

    down = Reduction(ring, ref.ddown, *parts_of("down"), ref.down_stage, ref.down_stage_sems)
    up = Reduction(ring, ref.dup, *parts_of("up"), ref.up_stage, ref.up_stage_sems)
    out = Reduction(ring, ref.dout, *parts_of("out"))
    inner = [
        Reduction(ring, ref.din.at[j], *[part.at[j] for part in parts_of("in")])
        for j in range(tiles)
    ]
    down.begin()
    up.begin()
    vsum[...] = jnp.zeros_like(vsum)
    nsum[...] = jnp.zeros_like(nsum)
    small = ref.small
    vsum[2:4] = small[0:2]
    vsum[7:8] = small[2:3]
    vsum[12:13] = small[3:4]
    vsum[8:12] = small[4:8]

    crossing = []
    for j in range(tiles):
        gate_copies[j].wait()
        weight = ref.wout[...].reshape(width, width)[j * TILE : (j + 1) * TILE]

        @pl.loop(0, micro)
        def _(m):
            mask = valid_rows(ref.lens[0, m], ring.pos * count, count, TILE)
            grad = mask * dot_nt(gb[m], weight).astype(bf16).astype(f32)
            gw[j, m] = grad.astype(bf16)
            gc[j, m] = (grad * gate[j, m].astype(f32)).astype(bf16)

        copy = remote(
            gc.at[j], gcr.at[j], ref.gc_sem.at[0, j], ref.gc_sem.at[1, j], ring.across
        )
        copy.start()
        crossing.append(copy)
    turned_copy.wait()

    @pl.loop(0, tiles)
    def _(j):
        cols = pl.ds(pl.multiple_of(j * TILE, TILE), TILE)
        total = dot(turned[0], gb[0, :, cols])
        for m in range(1, micro):
            total = total + dot(turned[m], gb[m, :, cols])
        dout = ref.dout
        dout[:, :, :, cols] = total.astype(bf16).reshape(dout.shape[:3] + (TILE,))

    turned_copy = copies.start(ref.nt, turned)
    out.begin()
    down.merge()
    up.merge()

    parity = 1.0 - 2.0 * (
        lax.broadcasted_iota(jnp.int32, (count, TILE), 0) % 2
    ).astype(f32)
    gk = ref.gk
    gbuf, zbuf, spec = ref.gbuf, ref.zbuf, ref.spec
    first_rows, last_rows, next_rows = ref.first_rows, ref.last_rows, ref.next_rows

    def loads(j, m, at):
        made = [
            (ref.s.at[j, m, :, pl.ds(TILE, 2 * TILE)], ref.s_buf.at[at]),
            (ref.z.at[j, m], ref.z_buf.at[at]),
            (ref.uhat.at[j, m], ref.u_buf.at[at]),
            (ref.conv.at[j, m], ref.c_buf.at[at]),
        ]
        return [
            pltpu.make_async_copy(src, dst, ref.load_sems.at[at, i])
            for i, (src, dst) in enumerate(made)
        ]

    def load_kernel(j):
        return pltpu.make_async_copy(ref.kern.at[j], ref.k_buf, ref.kernel_sem.at[0])

    def start_loads(j, m, at):
        for copy in loads(j, m, at):
            copy.start()

    start_loads(0, 0, 0)
    load_kernel(0).start()
    gbuf[count:] = jnp.zeros_like(gbuf[count:])

    def unmix(j):
        crossing[j].wait_recv()
        load_kernel(j).wait()
        lane = slice(j * TILE, (j + 1) * TILE)
        kn = ref.k_buf

        @pl.loop(0, micro)
        def _(m):
            at = lax.rem(j * micro + m, 2)
            for copy in loads(j, m, at):
                copy.wait()

            @pl.when(m + 1 < micro)
            def _():
                start_loads(j, m + 1, 1 - at)

            if j + 1 < tiles:

                @pl.when(m + 1 == micro)
                def _():
                    start_loads(j + 1, 0, 1 - at)

            hat = dot(table[...], gc[j, m])
            far = dot(table[...], gcr[j, m]) * inside
            gr, gi = hat[:count], hat[count:]
            hr, hi = far[:count], far[count:]
            k0r, k0i = kn[0, :count].astype(f32), kn[0, count:].astype(f32)
            k1r, k1i = kn[1, :count].astype(f32), kn[1, count:].astype(f32)
            spec[:count] = (k0r * gr + k0i * gi + k1r * hr + k1i * hi).astype(bf16)
            spec[count:] = (k0r * gi - k0i * gr + k1r * hi - k1i * hr).astype(bf16)
            keep = jnp.where(m > 0, 1.0, 0.0).astype(f32)
            uh = ref.u_buf
            for d in range(2):
                ur, ui = uh[at, d, :count].astype(f32), uh[at, d, count:].astype(f32)
                gk[d, :count] = gk[d, :count] * keep + (ur * gr + ui * gi)
                gk[d, count:] = gk[d, count:] * keep + (ur * gi - ui * gr)
            x1 = ref.s_buf[at, :, :TILE].astype(f32)
            v = ref.s_buf[at, :, TILE:].astype(f32)
            grad_w = gw[j, m].astype(f32)
            gc_full = grad_w * gate[j, m].astype(f32)
            gu = dot(table_back[...], spec[...]) * (1.0 / count) + vec[25:26, lane] * gc_full
            vsum[25:26, lane] += jnp.sum(gc_full * x1 * v, axis=0, keepdims=True)
            for p in range(3):
                if p == 0:
                    grad = grad_w * ref.c_buf[at].astype(f32)
                else:
                    grad = gu * (v if p == 1 else x1)
                low = grad.astype(bf16)
                grad = low.astype(f32)
                cols = slice(p * TILE, (p + 1) * TILE)
                first_rows[j, m, :, cols] = low[:16]
                last_rows[j, m, :, cols] = low[count - 16 :]
                gbuf[:count] = grad
                gz[j, m, :, cols] = (
                    vec[13 + p : 14 + p, lane] * grad
                    + vec[16 + p : 17 + p, lane] * gbuf[1 : 1 + count]
                    + vec[19 + p : 20 + p, lane] * gbuf[2 : 2 + count]
                ).astype(bf16)
                zbuf[:16] = ref.zh[j, m, :, cols].astype(f32)
                zbuf[16:] = ref.z_buf[at, :, cols].astype(f32)
                for k in range(3):
                    row = 13 + 3 * k + p
                    vsum[row : row + 1, lane] += jnp.sum(
                        grad * zbuf[16 - k : 16 - k + count], axis=0, keepdims=True
                    )
                vsum[22 + p : 23 + p, lane] += jnp.sum(grad, axis=0, keepdims=True)

        if j + 1 < tiles:
            load_kernel(j + 1).start()
        edge = remote(
            first_rows.at[j], next_rows.at[j], ref.edge_sem.at[0, j],
            ref.edge_sem.at[1, j], ring.across,
        )
        edge.start()
        g1r, g1i = gk[1, :count], gk[1, count:]
        spec[:count] = (gk[0, :count] + parity * g1i).astype(bf16)
        spec[count:] = (gk[0, count:] - parity * g1r).astype(bf16)
        gate[j, 0] = (dot(table_back[...], spec[...]) * (1.0 / count)).astype(bf16)
        spec[:count] = g1r.astype(bf16)
        spec[count:] = g1i.astype(bf16)
        gate[j, 1] = (dot(table_back[...], spec[...]) * (1.0 / count)).astype(bf16)
        return edge

    def project_back(j, edge):
        edge.wait_recv()
        lane = slice(j * TILE, (j + 1) * TILE)
        ebuf = ref.ebuf
        for m in range(micro):
            for p in range(3):
                cols = slice(p * TILE, (p + 1) * TILE)
                own = last_rows[j, m, :, cols].astype(f32)
                ebuf[:16] = own
                ebuf[16:] = next_rows[j, m, :, cols].astype(f32) * inside
                gz[j, m, count - 16 :, cols] = (
                    vec[13 + p : 14 + p, lane] * own
                    + vec[16 + p : 17 + p, lane] * ebuf[1:17]
                    + vec[19 + p : 20 + p, lane] * ebuf[2:18]
                ).astype(bf16)
        for p in range(3):
            cols = slice(p * TILE, (p + 1) * TILE)
            total = dot(turned[0], gz[j, 0, :, cols])
            bias = jnp.sum(gz[j, 0, :, cols].astype(f32), axis=0, keepdims=True)
            for m in range(1, micro):
                total = total + dot(turned[m], gz[j, m, :, cols])
                bias = bias + jnp.sum(gz[j, m, :, cols].astype(f32), axis=0, keepdims=True)
            din = ref.din
            din[j, :, :, :, cols] = total.astype(bf16).reshape(din.shape[1:4] + (TILE,))
            vsum[4 + p : 5 + p, lane] = bias
        inner[j].begin()

    edges = [unmix(0)]
    down.advance(1)
    up.advance(1)
    out.merge()
    edges.append(unmix(1))
    turned_copy.wait()
    project_back(0, edges[0])
    down.advance(2)
    up.advance(2)
    out.advance(1)
    inner[0].merge()
    edges.append(unmix(2))
    project_back(1, edges[1])
    x_copies = [
        copies.start(ref.x.at[:, :, pl.ds(j * TILE, TILE)], gcr.at[j]) for j in range(tiles)
    ]
    pre_copy = copies.start(ref.pre, gk.at[0])
    feature_copy = copies.start(ref.feature, gk.at[1])
    down.advance(3)
    up.advance(3)
    inner[1].merge()
    project_back(2, edges[2])
    out.advance(2)
    inner[0].advance(1)
    inner[1].advance(1)
    for copy in x_copies:
        copy.wait()
    for copy in crossing:
        copy.wait_send()

    for m in range(micro):
        normed_grad = dot_nt(gz[0, m], ref.win[0].reshape(width, 3 * TILE))
        for j in range(1, tiles):
            normed_grad = normed_grad + dot_nt(gz[j, m], ref.win[j].reshape(width, 3 * TILE))
        for part in range(count // TILE):
            rows = slice(part * TILE, (part + 1) * TILE)
            grad = normed_grad[rows]
            tokens = jnp.concatenate([gcr[j, m, rows] for j in range(tiles)], axis=1)
            gx, gain_part, shift_part = norm_rows_back(grad, tokens.astype(f32), vec[0:1])
            total = (gb[m, rows].astype(f32) + gx).astype(bf16)
            for j in range(tiles):
                gc[j, m, rows] = total[:, j * TILE : (j + 1) * TILE]
            vsum[0:1] += gain_part
            vsum[1:2] += shift_part
        if m == 0:
            inner[2].merge()
            down.collect()
            up.collect()
            out.advance(3)
            inner[0].advance(2)
            inner[1].advance(2)
    for j in range(tiles):
        copies.out(gc.at[j], ref.input_grad.at[:, :, pl.ds(j * TILE, TILE)])
    inner[2].advance(1)
    inner[0].advance(3)
    inner[1].advance(3)
    out.collect()

    net = ref.net_in
    net[...] = ref.net[...].T
    rates = ref.rate[...].reshape(1, width)
    final_low = ref.final[...].astype(bf16)
    pre_copy.wait()
    feature_copy.wait()
    frequency = net[EMB + 3 + 2 * HID : EMB + 4 + 2 * HID]

    def filter_back(at):
        rows = pl.ds(pl.multiple_of(at * TILE, TILE), TILE)
        half, part = at // (count // TILE), lax.rem(at, count // TILE)
        held = pl.ds(pl.multiple_of(part * TILE, TILE), TILE)
        at_row = lax.broadcasted_iota(jnp.int32, (TILE, TILE), 0) + at * TILE
        scaled = at_row.astype(f32) * (1.0 / slot)
        layers = [gk[0, rows, i * HID : (i + 1) * HID] for i in range(3)]
        many = jnp.concatenate([frequency] * 4, axis=1)
        act, slope = sin_cos(many * gk[0, rows])
        acts = [act[:, i * HID : (i + 1) * HID] for i in range(3)]
        slopes = [slope[:, i * HID : (i + 1) * HID] for i in range(3)]
        last = acts[2].astype(bf16)
        grad = jnp.zeros((TILE, HID), f32)
        for j in range(tiles):
            lane = slice(j * TILE, (j + 1) * TILE)
            window = jnp.exp(-scaled * rates[:, lane]) + 0.05
            shaped = (gate[j, half, held].astype(f32) * window).astype(bf16)
            vsum[FINAL_ROW : FINAL_ROW + HID, lane] += dot_tn(last, shaped)
            grad = grad + dot_nt(shaped, final_low[:, lane])
        freq_sum = jnp.zeros_like(frequency)
        for i in (2, 1, 0):
            turn = grad * slopes[i]
            freq_sum = freq_sum + jnp.sum(turn * layers[i], axis=0, keepdims=True)
            grad = turn * frequency
            if i == 0:
                nsum[: EMB + 1, :HID] += lax.dot_general(
                    gk[1, rows, : EMB + 1], grad, (((0,), (0,)), ((), ())),
                    precision=highest, preferred_element_type=f32,
                )
            else:
                first = EMB + 1 if i == 1 else EMB + 2 + HID
                nsum[first : first + HID, :HID] += lax.dot_general(
                    acts[i - 1], grad, (((0,), (0,)), ((), ())),
                    precision=highest, preferred_element_type=f32,
                )
                nsum[first + HID : first + HID + 1, :HID] += jnp.sum(grad, axis=0, keepdims=True)
                grad = lax.dot_general(
                    grad, net[first : first + HID], (((1,), (1,)), ((), ())),
                    precision=highest, preferred_element_type=f32,
                )
        row = EMB + 3 + 2 * HID
        nsum[row : row + 1, :HID] += freq_sum

    blocks = slot // TILE

    @pl.loop(0, blocks // 2)
    def _(at):
        filter_back(at)

    inner[2].advance(2)
    inner[0].collect()
    inner[1].collect()

    @pl.loop(blocks // 2, blocks)
    def _(at):
        filter_back(at)

    smalls = []
    for values, sums, name in ((vsum, ref.v_out, "v"), (nsum, ref.n_out, "n")):
        parts = [getattr(ref, name + str(k)) for k in range(4)]
        smalls.append(SmallSum(ring, values, *parts[:3], sums, parts[3]))
    for work in smalls:
        work.begin()
    inner[2].advance(3)
    psum = ref.proj_sum
    wide = psum.shape[1] - 4 * width
    ref.down_sum[...] = down.result()
    for work in smalls:
        work.add_up()
    psum[:, 4 * width : 4 * width + wide] = up.result()
    psum[:, 3 * width : 4 * width] = out.result()
    inner[2].collect()
    for work in smalls:
        work.spread()
    for j in range(tiles):
        total = inner[j].result()
        for p in range(3):
            first = p * width + j * TILE
            psum[:, first : first + TILE] = total[:, p * TILE : (p + 1) * TILE]
    for work in smalls:
        work.finish()
    ref.net_sum[...] = ref.n_out[:, :HID].T
    for work in [down, up, out] + inner:
        work.finish()
    for edge in edges:
        edge.wait_send()
    copies.finish()


def back(size, arrays):
    chips = size // 2
    micro, count, width = arrays["gb"].shape
    rows, wide = arrays["dup"].shape[2:]
    down_rows = arrays["ddown"].shape[2]
    tiles = width // TILE
    vmem = pl.BlockSpec(memory_space=pltpu.VMEM)
    anywhere = pl.BlockSpec(memory_space=pl.ANY)
    smem = pl.BlockSpec(memory_space=pltpu.SMEM)
    near = ("gb", "vec", "net", "final", "rate", "table", "back", "win", "wout", "zh", "small")
    small_rows = 8 * size
    outs = dict(
        input_grad=((micro, count, width), bf16),
        proj_sum=((rows, 4 * width + wide), f32),
        down_sum=((down_rows, width), f32),
        v_out=((small_rows, width), f32),
        n_out=((2 * small_rows, 128), f32),
        net_sum=((HID, 2 * small_rows), f32),
    )
    dma = pltpu.SemaphoreType.DMA
    tile_tokens = (tiles, micro, count, TILE)
    edge_rows = (tiles, micro, 16, 3 * TILE)
    scratch = dict(
        din=pltpu.VMEM((tiles, chips, 2, rows, 3 * TILE), bf16),
        dout=pltpu.VMEM((chips, 2, rows, width), bf16),
        gw=pltpu.VMEM(tile_tokens, bf16),
        gc=pltpu.VMEM(tile_tokens, bf16),
        gcr=pltpu.VMEM(tile_tokens, bf16),
        gate=pltpu.VMEM(tile_tokens, bf16),
        gz=pltpu.VMEM((tiles, micro, count, 3 * TILE), bf16),
        turned=pltpu.VMEM((micro, width, count), bf16),
        vsum=pltpu.VMEM((small_rows, width), f32),
        nsum=pltpu.VMEM((2 * small_rows, 128), f32),
        net_in=pltpu.VMEM((EMB + 4 + 2 * HID, HID), f32),
        gk=pltpu.VMEM((2, 2 * count, TILE), f32),
        gbuf=pltpu.VMEM((count + 16, TILE), f32),
        zbuf=pltpu.VMEM((count + 16, TILE), f32),
        ebuf=pltpu.VMEM((32, TILE), f32),
        spec=pltpu.VMEM((2 * count, TILE), bf16),
        first_rows=pltpu.VMEM(edge_rows, bf16),
        last_rows=pltpu.VMEM(edge_rows, bf16),
        next_rows=pltpu.VMEM(edge_rows, bf16),
        s_buf=pltpu.VMEM((2, count, 2 * TILE), bf16),
        z_buf=pltpu.VMEM((2, count, 3 * TILE), bf16),
        u_buf=pltpu.VMEM((2, 2, 2 * count, TILE), bf16),
        c_buf=pltpu.VMEM((2, count, TILE), bf16),
        k_buf=pltpu.VMEM((2, 2 * count, TILE), bf16),
        load_sems=dma((2, 4)),
        kernel_sem=dma((1,)),
        gc_sem=dma((2, tiles)),
        edge_sem=dma((2, tiles)),
        copy_sems=dma((16,)),
        up_stage=pltpu.VMEM((2, rows, wide), bf16),
        down_stage=pltpu.VMEM((2, down_rows, width), bf16),
        up_stage_sems=dma((2,)),
        down_stage_sems=dma((2,)),
    )
    ups, downs = chips // 2, (chips - 1) // 2
    for name, lead, dims in (
        ("up", (), (rows, wide)), ("down", (), (down_rows, width)), ("out", (), (rows, width)),
        ("in", (tiles,), (rows, 3 * TILE)),
    ):
        made = [pltpu.VMEM(lead + (count,) + dims, bf16) for count in (chips, ups, downs)]
        made += [pltpu.VMEM(lead + dims, bf16)] * 2 + [dma(lead + (2, 2 + ups + downs))]
        for k, part in enumerate(made):
            scratch[name + str(k)] = part
    for name in ("v", "n"):
        for k, part in enumerate(small_scratch(size, *outs[name + "_out"][0])):
            scratch[name + str(k)] = part
    names = tuple(arrays) + tuple(outs) + tuple(scratch)
    return pl.pallas_call(
        functools.partial(back_kernel, size, names),
        out_shape=[jax.ShapeDtypeStruct(*kind) for kind in outs.values()],
        in_specs=[
            smem if name == "lens" else vmem if name in near else anywhere for name in arrays
        ],
        out_specs=[anywhere] + [vmem] * (len(outs) - 1),
        scratch_shapes=list(scratch.values()),
        compiler_params=pltpu.CompilerParams(
            collective_id=1, has_side_effects=True, vmem_limit_bytes=63 * 1024 * 1024
        ),
        name="back",
    )(*arrays.values())


def fits(size, groups, tokens, proj_weights, down_weights):
    micro, _, count, width = tokens.shape
    wide = down_weights.shape[0] * size
    return (
        groups == 2
        and size % 4 == 0
        and size == 16
        and proj_weights.shape[0] % 16 == 0
        and down_weights.shape[0] % 16 == 0
        and count % TILE == 0
        and width == 3 * TILE
        and micro >= groups
        and micro * count <= 1024
        and wide == 4 * width
        and proj_weights.shape[1] == 4 * width + wide
    )


def on_device_tuned(
    block_input,
    out_grad,
    lengths,
    decay_rates,
    proj_weights,
    proj_moment,
    proj_average,
    down_weights,
    down_moment,
    down_average,
    vectors,
    vector_moment,
    vector_average,
    filter_net,
    net_moment,
    net_average,
    filter_out,
    final_moment,
    final_average,
):
    micro, _, count, width = block_input.shape
    size = lax.axis_size("seq")
    tokens = block_input.reshape(micro, count, width)
    plain_table = transform_table(count)
    table = jnp.asarray(plain_table, dtype=bf16)
    table_back = jnp.asarray(plain_table.T, dtype=bf16)
    feature = jnp.asarray(feature_table(count * lax.axis_size("pos")))
    shared = dict(
        x=tokens, lens=lengths.T, vec=vectors, net=filter_net.T, final=filter_out,
        rate=decay_rates, table=table, back=table_back, feature=feature,
    )
    made = types.SimpleNamespace(**front(size, dict(shared, proj=proj_weights, down=down_weights)))
    block_output, branch_grad, up_step, down_step, small = mlp(
        made.n2, made.n2t, out_grad.reshape(micro, count, width), made.res, vectors,
        made.wup, made.wdown,
    )
    chips = size // 2
    input_grad, proj_sum, down_sum, rest, _, net_sum = back(
        size,
        dict(
            shared, win=made.win, wout=made.wout, z=made.z, zh=made.zh, s=made.s, conv=made.conv,
            uhat=made.uhat, kern=made.kern, nt=made.nt, yt=made.yt, pre=made.pre,
            gb=branch_grad, small=small,
            dup=up_step.reshape(chips, 2, -1, up_step.shape[1]),
            ddown=down_step.reshape(chips, 2, -1, width),
        ),
    )
    steps = update(
        [
            (proj_sum, proj_weights, proj_moment, proj_average, 0.0001, 0, 1),
            (down_sum, down_weights, down_moment, down_average, 0.0001, 0, 0),
            (rest, vectors, vector_moment, vector_average, 0.001, 0, None),
            (net_sum, filter_net.T, net_moment.T, net_average.T, 0.0001, 0, None),
            (rest, filter_out, final_moment, final_average, 2e-06, FINAL_ROW, None),
        ]
    )
    steps[3] = [array.T for array in steps[3]]
    return (
        block_output.reshape(block_input.shape),
        input_grad.reshape(block_input.shape),
        *steps[0], *steps[1], *steps[2], *steps[3], *steps[4],
    )


def on_device_plain(
    block_input,
    out_grad,
    lengths,
    decay_rates,
    proj_weights,
    proj_moment,
    proj_average,
    down_weights,
    down_moment,
    down_average,
    vectors,
    vector_moment,
    vector_average,
    filter_net,
    net_moment,
    net_average,
    filter_out,
    final_moment,
    final_average,
):
    micro = block_input.shape[0]
    count = block_input.shape[2]
    width = block_input.shape[3]
    groups = lax.axis_size("pos")
    slot_length = count * groups
    tokens_all = micro * count
    group = lax.axis_index("pos")
    tap = vectors[13:22].reshape(3, 3 * width)
    short_bias = vectors[22:25].reshape(-1)
    in_bias = vectors[4:7].reshape(-1)
    up_bias = vectors[8:12].reshape(-1)
    skip = vectors[25]

    low_rows = proj_weights.astype(bf16)
    in_weight = lax.all_gather(low_rows[:, : 3 * width], "seq", axis=0, tiled=True)
    out_weight = lax.all_gather(low_rows[:, 3 * width : 4 * width], "seq", axis=0, tiled=True)
    up_weight = lax.all_gather(low_rows[:, 4 * width :], "seq", axis=0, tiled=True)
    down_weight = lax.all_gather(down_weights.astype(bf16), "seq", axis=0, tiled=True)

    table = jnp.asarray(transform_table(count))
    table_low = table.astype(bf16)
    every = jnp.arange(slot_length, dtype=jnp.int32)

    def make_filter(net_values, final_values):
        return filter_fn(net_values, final_values, decay_rates, every, slot_length)

    filters, filter_back = jax.vjp(make_filter, filter_net, filter_out)
    pieces = filters.reshape(groups, count, width)
    spectra = [
        jnp.dot(table, pieces[d], precision=lax.Precision.HIGH, preferred_element_type=f32)
        for d in range(groups)
    ]
    kernels = [spectra[0]] + [spectra[d] + turned(spectra[d - 1], 1.0) for d in range(1, groups)]

    def transform(values):
        return jnp.stack([dot(table_low, values[m]) for m in range(micro)])

    def transform_back(spectrum):
        low = spectrum.astype(bf16)
        return jnp.stack([dot_tn(table_low, low[m]) for m in range(micro)]) * (1.0 / count)

    tokens_low = block_input[:, 0]
    before = passed_along(tokens_low[:, -2:], "pos", 1)
    tokens = tokens_low.astype(f32).reshape(tokens_all, width)
    xh_one, scale_one = norm_parts(tokens)
    normed = (xh_one * vectors[0] + vectors[1]).astype(bf16)
    xh_before, _ = norm_parts(before.astype(f32).reshape(micro * 2, width))
    normed_before = (xh_before * vectors[0] + vectors[1]).astype(bf16)
    z = (dot(normed, in_weight) + in_bias).reshape(micro, count, 3 * width)
    z_before = (dot(normed_before, in_weight) + in_bias).reshape(micro, 2, 3 * width)
    z_before = jnp.where(group > 0, z_before, 0.0)
    z_long = jnp.concatenate([z_before, z], axis=1)
    short = (
        tap[0] * z_long[:, 2:] + tap[1] * z_long[:, 1:-1] + tap[2] * z_long[:, :-2] + short_bias
    ).astype(bf16)
    x0 = short[:, :, :width].astype(f32)
    x1 = short[:, :, width : 2 * width].astype(f32)
    v = short[:, :, 2 * width :].astype(f32)

    u = x1 * v
    u_low = u.astype(bf16)
    u_hat = [transform(u_low)]
    for d in range(1, groups):
        u_hat.append(transform(passed_along(u_low, "pos", d)))
    total = product(kernels[0], u_hat[0])
    for d in range(1, groups):
        total = total + product(kernels[d], u_hat[d])
    conv = transform_back(total) + skip * u
    here = group * count + jnp.arange(count, dtype=jnp.int32)
    mask = (here[None, :] < lengths[:, 0][:, None]).astype(f32)[:, :, None]
    y = (mask * x0 * conv).astype(bf16).reshape(tokens_all, width)
    residual = tokens + dot(y, out_weight) + vectors[7]
    xh_two, scale_two = norm_parts(residual)
    normed_two = (xh_two * vectors[2] + vectors[3]).astype(bf16)

    cot_low = out_grad[:, 0].reshape(tokens_all, width)
    cot = cot_low.astype(f32)
    pre = dot(normed_two, up_weight) + up_bias
    hidden, gelu_back = jax.vjp(jax.nn.gelu, pre)
    hidden_low = hidden.astype(bf16)
    block_output = (residual + dot(hidden_low, down_weight) + vectors[12]).astype(bf16)
    pre_grad = gelu_back(dot_nt(cot_low, down_weight))[0].astype(bf16)
    down_step = dot_tn(hidden_low, cot_low)
    up_step = dot_tn(normed_two, pre_grad)
    normed_two_grad = dot_nt(pre_grad, up_weight)
    part, gain_two, shift_two = norm_back(normed_two_grad, xh_two, scale_two, vectors[2])
    residual_grad = cot + part
    branch_low = residual_grad.astype(bf16)
    out_step = dot_tn(y, branch_low)
    y_grad = dot_nt(branch_low, out_weight).astype(bf16).astype(f32).reshape(micro, count, width)

    gw = mask * y_grad
    gx0 = gw * conv
    gc = gw * x0
    gc_low = gc.astype(bf16)
    skip_grad = jnp.sum(gc * u, axis=(0, 1))
    gc_hat = [transform(gc_low)]
    for d in range(1, groups):
        gc_hat.append(transform(passed_along(gc_low, "pos", -d)))
    back = product_conj(kernels[0], gc_hat[0])
    for d in range(1, groups):
        back = back + product_conj(kernels[d], gc_hat[d])
    gu = transform_back(back) + skip * gc
    kernel_grads = [jnp.sum(product_conj(u_hat[d], gc_hat[0]), axis=0) for d in range(groups)]
    filter_grads = []
    for d in range(groups):
        got = kernel_grads[d]
        if d + 1 < groups:
            got = got + turned(kernel_grads[d + 1], -1.0)
        filter_grads.append(dot_tn(table_low, got.astype(bf16)) * (1.0 / count))
    net_local, final_local = filter_back(jnp.concatenate(filter_grads, axis=0))
    short_grad = jnp.concatenate([gx0, gu * v, gu * x1], axis=-1).astype(bf16)
    after = passed_along(short_grad[:, :2], "pos", -1)
    short_long = jnp.concatenate([short_grad, after], axis=1).astype(f32)
    z_grad = (
        tap[0] * short_long[:, :-2] + tap[1] * short_long[:, 1:-1] + tap[2] * short_long[:, 2:]
    ).astype(bf16)
    here_grad = short_long[:, :-2]
    tap_grads = [
        jnp.sum(here_grad * z_long[:, 2 - k : 2 - k + count], axis=(0, 1)) for k in range(3)
    ]
    short_bias_grad = jnp.sum(here_grad, axis=(0, 1))
    z_grad = z_grad.reshape(tokens_all, 3 * width)
    in_step = dot_tn(normed, z_grad)
    in_bias_grad = jnp.sum(z_grad.astype(f32), axis=0)
    normed_grad = dot_nt(z_grad, in_weight)
    part, gain_one, shift_one = norm_back(normed_grad, xh_one, scale_one, vectors[0])
    input_grad = (residual_grad + part).astype(bf16)

    vector_local = jnp.concatenate(
        [
            gain_one[None],
            shift_one[None],
            gain_two[None],
            shift_two[None],
            in_bias_grad.reshape(3, width),
            jnp.sum(branch_low.astype(f32), axis=0)[None],
            jnp.sum(pre_grad.astype(f32), axis=0).reshape(4, width),
            jnp.sum(cot, axis=0)[None],
            jnp.stack(tap_grads).reshape(9, width),
            short_bias_grad.reshape(3, width),
            skip_grad[None],
        ],
        axis=0,
    )
    proj_local = jnp.concatenate([in_step, out_step, up_step], axis=1).astype(bf16)
    proj_shard = lax.psum_scatter(proj_local, "seq", scatter_dimension=0, tiled=True)
    down_shard = lax.psum_scatter(down_step.astype(bf16), "seq", scatter_dimension=0, tiled=True)
    proj_sum = lax.psum(proj_shard, "pos").astype(f32)
    down_sum = lax.psum(down_shard, "pos").astype(f32)
    vector_sum, net_sum, final_sum = lax.psum(
        (vector_local, net_local, final_local), ("seq", "pos")
    )
    return (
        block_output.reshape(micro, 1, count, width),
        input_grad.reshape(micro, 1, count, width),
        *nesterov(proj_weights, proj_moment, proj_average, proj_sum, 0.0001),
        *nesterov(down_weights, down_moment, down_average, down_sum, 0.0001),
        *nesterov(vectors, vector_moment, vector_average, vector_sum, 0.001),
        *nesterov(filter_net, net_moment, net_average, net_sum, 0.0001),
        *nesterov(filter_out, final_moment, final_average, final_sum, 2e-06),
    )


def on_device(*arrays):
    tuned = fits(
        lax.axis_size("seq"), lax.axis_size("pos"), arrays[0], arrays[4], arrays[7]
    )
    return (on_device_tuned if tuned else on_device_plain)(*arrays)


def solution(mesh):
    tokens = P(None, "seq", "pos", None)
    rows = P("seq", None)
    whole = P()
    return jax.shard_map(
        on_device,
        mesh=mesh,
        in_specs=(tokens, tokens, P(None, "seq"), whole) + (rows,) * 6 + (whole,) * 9,
        out_specs=(tokens, tokens) + (rows,) * 8 + (whole,) * 12,
        check_vma=False,
    )
```

```python
import functools
import math
import types

import jax
import jax.numpy as jnp
import numpy as np
from jax import lax
from jax.experimental import pallas as pl
from jax.experimental.pallas import tpu as pltpu
from jax.sharding import PartitionSpec as P

HID = 64
EMB = 33

highest = lax.Precision.HIGHEST
f32 = jnp.float32
bf16 = jnp.bfloat16


def passed_along(block, axis, distance):
    devices = range(lax.axis_size(axis))
    route = [(i - distance, i) for i in devices if i - distance in devices]
    return lax.ppermute(block, axis, route)


def dot(a, b):
    return lax.dot_general(a, b, (((1,), (0,)), ((), ())), preferred_element_type=f32)


def dot_tn(a, b):
    return lax.dot_general(a, b, (((0,), (0,)), ((), ())), preferred_element_type=f32)


def dot_nt(a, b):
    return lax.dot_general(a, b, (((1,), (1,)), ((), ())), preferred_element_type=f32)


def features(positions, slot_length):
    band_count = (EMB - 1) // 2
    scaled = positions.astype(f32) / slot_length
    bands = 0.0001 + jnp.arange(band_count, dtype=f32) * (
        (band_count - 1 - 0.0001) / (band_count - 1)
    )
    angles = 2.0 * math.pi * scaled[:, None] * bands[None, :]
    return jnp.concatenate([scaled[:, None], jnp.cos(angles), -jnp.sin(angles)], axis=1)


def filter_fn(net_values, final_values, rates, positions, slot_length):
    embedded = features(positions, slot_length)
    frequency = net_values[EMB + 3 + 2 * HID]
    layer_one = jnp.sin(
        frequency * (jnp.dot(embedded, net_values[:EMB], precision=highest) + net_values[EMB])
    )
    layer_two = jnp.sin(
        frequency
        * (
            jnp.dot(layer_one, net_values[EMB + 1 : EMB + 1 + HID], precision=highest)
            + net_values[EMB + 1 + HID]
        )
    )
    layer_three = jnp.sin(
        frequency
        * (
            jnp.dot(layer_two, net_values[EMB + 2 + HID : EMB + 2 + 2 * HID], precision=highest)
            + net_values[EMB + 2 + 2 * HID]
        )
    )
    shaped = jnp.dot(layer_three, final_values, precision=highest)
    scaled = positions.astype(f32) / slot_length
    window = jnp.exp(-scaled[:, None] * rates[None, :]) + 0.05
    return shaped * window


def transform_table(length):
    product = np.outer(2 * np.arange(length) + 1, np.arange(length)) % (4 * length)
    angle = product.astype(np.float64) * (math.pi / (2 * length))
    return np.concatenate([np.cos(angle), -np.sin(angle)], axis=0).astype(np.float32)


def feature_table(slot_length):
    scaled = np.arange(slot_length, dtype=np.float32) / np.float32(slot_length)
    band_count = (EMB - 1) // 2
    bands = np.float32(0.0001) + np.arange(band_count, dtype=np.float32) * np.float32(
        (band_count - 1 - 0.0001) / (band_count - 1)
    )
    angles = (np.float32(2.0 * math.pi) * scaled[:, None]) * bands[None, :]
    table = np.zeros((slot_length, 4 * HID), np.float32)
    table[:, 0] = scaled
    table[:, 1 : 1 + band_count] = np.cos(angles)
    table[:, 1 + band_count : EMB] = -np.sin(angles)
    table[:, EMB] = 1.0
    return table


def halves(spectrum):
    half = spectrum.shape[-2] // 2
    return spectrum[..., :half, :], spectrum[..., half:, :]


def turned(spectrum, sign):
    re, im = halves(spectrum)
    parity = (1.0 - 2.0 * (jnp.arange(re.shape[-2]) % 2).astype(f32))[:, None] * sign
    return jnp.concatenate([-parity * im, parity * re], axis=-2)


def product(kernel, signal):
    kr, ki = halves(kernel)
    sr, si = halves(signal)
    return jnp.concatenate([kr * sr - ki * si, kr * si + ki * sr], axis=-2)


def product_conj(kernel, signal):
    kr, ki = halves(kernel)
    sr, si = halves(signal)
    return jnp.concatenate([kr * sr + ki * si, kr * si - ki * sr], axis=-2)


def nesterov(weight, moment, average, gradient, rate):
    moment_next = 0.9 * moment + gradient
    weight_next = weight - rate * (gradient + 0.9 * moment_next)
    average_next = 0.9 * average + 0.1 * weight_next
    return (gradient, weight_next, moment_next, average_next)


def norm_parts(values):
    center = jnp.mean(values, axis=-1, keepdims=True)
    centred = values - center
    variance = jnp.mean(centred * centred, axis=-1, keepdims=True)
    scale = lax.rsqrt(variance + 1e-05)
    return centred * scale, scale


def norm_back(grad, xh, scale, gain):
    q = grad * gain
    return (
        (q - jnp.mean(q, -1, keepdims=True) - xh * jnp.mean(q * xh, -1, keepdims=True)) * scale,
        jnp.sum(grad * xh, axis=0),
        jnp.sum(grad, axis=0),
    )


MESH = pl.DeviceIdType.MESH


class Ring:
    def __init__(self, size):
        self.size = size
        self.count = size // 2
        self.seq = lax.axis_index("seq")
        self.pos = lax.axis_index("pos")
        self.core = lax.rem(self.seq, 2)
        chip = self.seq // 2
        odd = lax.rem(chip, 2)
        self.place = (1 - odd) * (chip // 2) + odd * (self.count - 1 - chip // 2)

    def chip(self, shift):
        place = lax.rem(self.place + (shift + self.count), self.count)
        low = jnp.where(place < self.count // 2, 1, 0)
        return low * (2 * place) + (1 - low) * (2 * (self.count - 1 - place) + 1)

    def device(self, shift):
        return {"seq": 2 * self.chip(shift) + self.core}

    @property
    def sibling(self):
        return {"seq": self.seq + 1 - 2 * self.core}

    @property
    def across(self):
        return {"pos": 1 - self.pos}


def greet_all(ring):
    barrier = pltpu.get_barrier_semaphore()
    for step in range(1, ring.size):
        other = lax.rem(ring.seq + step, ring.size)
        pl.semaphore_signal(barrier, inc=1, device_id={"seq": other}, device_id_type=MESH)
    pl.semaphore_signal(barrier, inc=1, device_id=ring.across, device_id_type=MESH)
    pl.semaphore_wait(barrier, ring.size)


def remote(src, dst, send, recv, device):
    return pltpu.make_async_remote_copy(
        src_ref=src, dst_ref=dst, send_sem=send, recv_sem=recv, device_id=device,
        device_id_type=MESH,
    )


class Reduction:
    def __init__(self, ring, grad, twin, up, down, own, other, sems, stage=None, stage_sems=None):
        self.ring = ring
        self.grad, self.twin, self.up, self.down = grad, twin, up, down
        self.own, self.other = own, other
        self.sems = sems
        self.stage, self.stage_sems = stage, stage_sems
        self.ups = ring.count // 2
        self.downs = (ring.count - 1) // 2

    def copies(self):
        ring = self.ring
        made = [(self.grad.at[:, 1 - ring.core], self.twin, ring.sibling)]
        for step in range(self.ups):
            block = self.twin.at[ring.chip(self.ups - step)]
            made.append((block, self.up.at[step], ring.device(1)))
        for step in range(self.downs):
            block = self.twin.at[ring.chip(step - self.downs)]
            made.append((block, self.down.at[step], ring.device(-1)))
        made.append((self.own, self.other, ring.across))
        return made

    def copy(self, index):
        src, dst, device = self.copies()[index]
        return remote(src, dst, self.sems.at[0, index], self.sems.at[1, index], device)

    def begin(self):
        self.copy(0).start()

    def fetch(self, chip, slot):
        return pltpu.make_async_copy(
            self.grad.at[chip, self.ring.core], self.stage.at[slot], self.stage_sems.at[slot]
        )

    def merge(self):
        core = self.ring.core
        count = self.ring.count
        if self.stage is None:
            self.copy(0).wait_recv()

            @pl.loop(0, count)
            def _(chip):
                self.twin[chip] = self.twin[chip] + self.grad[chip, core]

        else:
            self.fetch(0, 0).start()
            self.copy(0).wait_recv()

            @pl.loop(0, count)
            def _(chip):
                slot = lax.rem(chip, 2)

                @pl.when(chip + 1 < count)
                def _():
                    self.fetch(chip + 1, 1 - slot).start()

                self.fetch(chip, slot).wait()
                self.twin[chip] = self.twin[chip] + self.stage[slot]

        self.copy(1).start()
        self.copy(1 + self.ups).start()

    def advance(self, step):
        self.copy(step).wait_recv()
        owner = self.ring.chip(self.ups - step)
        self.twin[owner] = self.twin[owner] + self.up[step - 1]
        self.copy(1 + step).start()
        if step < self.downs:
            self.copy(self.ups + step).wait_recv()
            owner = self.ring.chip(step - self.downs)
            self.twin[owner] = self.twin[owner] + self.down[step - 1]
            self.copy(1 + self.ups + step).start()

    def collect(self):
        self.copy(self.ups).wait_recv()
        self.copy(self.ups + self.downs).wait_recv()
        mine = self.ring.chip(0)
        total = (
            self.twin[mine].astype(f32)
            + self.up[self.ups - 1].astype(f32)
            + self.down[self.downs - 1].astype(f32)
        )
        self.own[...] = total.astype(bf16)
        self.copy(1 + self.ups + self.downs).start()

    def result(self):
        self.copy(1 + self.ups + self.downs).wait_recv()
        return self.own[...].astype(f32) + self.other[...].astype(f32)

    def finish(self):
        for index in range(2 + self.ups + self.downs):
            self.copy(index).wait_send()


class SmallSum:
    def __init__(self, ring, values, parts, mine, other, sums, sems):
        self.ring, self.values, self.parts = ring, values, parts
        self.mine, self.other, self.sums = mine, other, sums
        self.sems = sems
        self.rows = parts.shape[1]
        self.waiting = []

    def block(self, index):
        return pl.ds(pl.multiple_of(index * self.rows, 8), self.rows)

    def begin(self):
        ring = self.ring
        self.arriving = []
        for step in range(1, ring.size):
            other = lax.rem(ring.seq + step, ring.size)
            copy = remote(
                self.values.at[self.block(other)], self.parts.at[step],
                self.sems.at[0, step], self.sems.at[1, step], {"seq": other},
            )
            copy.start()
            self.arriving.append(copy)
            self.waiting.append(copy)

    def add_up(self):
        for copy in self.arriving:
            copy.wait_recv()
        total = self.values[self.block(self.ring.seq)]
        for step in range(1, self.ring.size):
            total = total + self.parts[step]
        self.mine[...] = total
        self.crossing = remote(
            self.mine, self.other, self.sems.at[0, 0], self.sems.at[1, 0], self.ring.across
        )
        self.crossing.start()
        self.waiting.append(self.crossing)

    def spread(self):
        self.crossing.wait_recv()
        block = self.block(self.ring.seq)
        self.sums[block] = self.mine[...] + self.other[...]
        self.arriving = []
        for step in range(1, self.ring.size):
            other = lax.rem(self.ring.seq + step, self.ring.size)
            copy = remote(
                self.sums.at[block], self.sums.at[block],
                self.sems.at[2, step], self.sems.at[3, step], {"seq": other},
            )
            copy.start()
            self.waiting.append(copy)
            back = lax.rem(self.ring.seq + (self.ring.size - step), self.ring.size)
            self.arriving.append(
                remote(
                    self.sums.at[self.block(back)], self.sums.at[self.block(back)],
                    self.sems.at[2, step], self.sems.at[3, step], {"seq": other},
                )
            )

    def finish(self):
        for copy in self.arriving:
            copy.wait_recv()
        for copy in self.waiting:
            copy.wait_send()


def reduction_scratch(size, rows, columns):
    chips = size // 2
    ups, downs = chips // 2, (chips - 1) // 2
    return [
        pltpu.VMEM((chips, rows, columns), bf16),
        pltpu.VMEM((ups, rows, columns), bf16),
        pltpu.VMEM((downs, rows, columns), bf16),
        pltpu.VMEM((rows, columns), bf16),
        pltpu.VMEM((rows, columns), bf16),
        pltpu.SemaphoreType.DMA((2, 2 + ups + downs)),
    ]


def small_scratch(size, rows, columns):
    return [
        pltpu.VMEM((size, rows // size, columns), f32),
        pltpu.VMEM((rows // size, columns), f32),
        pltpu.VMEM((rows // size, columns), f32),
        pltpu.SemaphoreType.DMA((4, size)),
    ]


class Gather:
    def __init__(self, ring, mine, full, sems):
        self.ring, self.mine, self.full, self.sems = ring, mine, full, sems
        self.ups = ring.count // 2
        self.downs = (ring.count - 1) // 2
        self.waiting, self.arriving = [], []

    def send(self, src, place, index, device):
        copy = remote(
            src, self.full.at[self.ring.chip(place), self.ring.core],
            self.sems.at[0, index], self.sems.at[1, index], device,
        )
        copy.start()
        self.waiting.append(copy)
        return copy

    def share(self, src, place, index):
        index = self.ups + self.downs + index
        self.send(src, place, index, self.ring.sibling)
        block = self.full.at[self.ring.chip(place), 1 - self.ring.core]
        self.arriving.append(
            remote(block, block, self.sems.at[0, index], self.sems.at[1, index], self.ring.sibling)
        )

    def wait_block(self, place, index, device):
        block = self.full.at[self.ring.chip(place), self.ring.core]
        remote(block, block, self.sems.at[0, index], self.sems.at[1, index], device).wait_recv()
        return block

    def begin(self):
        ring = self.ring
        self.send(self.mine, 0, 0, ring.device(1))
        self.send(self.mine, 0, self.ups, ring.device(-1))
        self.share(self.mine, 0, 0)
        self.local = pltpu.make_async_copy(
            self.mine, self.full.at[ring.chip(0), ring.core], self.sems.at[2, 0]
        )
        self.local.start()

    def advance(self, step):
        ring = self.ring
        block = self.wait_block(-step, step - 1, ring.device(1))
        if step < self.ups:
            self.send(block, -step, step, ring.device(1))
        self.share(block, -step, step)
        if step <= self.downs:
            block = self.wait_block(step, self.ups + step - 1, ring.device(-1))
            if step < self.downs:
                self.send(block, step, self.ups + step, ring.device(-1))
            self.share(block, step, self.ups + step)

    def arrive(self):
        self.local.wait()
        for copy in self.arriving:
            copy.wait_recv()

    def finish(self):
        for copy in self.waiting:
            copy.wait_send()


def gather_sems(size):
    chips = size // 2
    return pltpu.SemaphoreType.DMA((3, 2 * chips))


PI_PARTS = (3.140625, 9.676535897932384e-4)


def sin_cos(x):
    turns = jnp.floor(x * (1.0 / math.pi) + 0.5)
    rest = (x - turns * PI_PARTS[0]) - turns * PI_PARTS[1]
    half = turns * 0.5
    sign = 1.0 - 4.0 * (half - jnp.floor(half))
    square = rest * rest
    odd = 1.0 / 6227020800.0
    for factor in (-1.0 / 39916800.0, 1.0 / 362880.0, -1.0 / 5040.0, 1.0 / 120.0, -1.0 / 6.0):
        odd = odd * square + factor
    even = 1.0 / 479001600.0
    for factor in (-1.0 / 3628800.0, 1.0 / 40320.0, -1.0 / 720.0, 1.0 / 24.0, -0.5):
        even = even * square + factor
    signed = sign * rest
    return signed + signed * square * odd, sign + sign * square * even


def norm_rows(values):
    center = jnp.mean(values, axis=1, keepdims=True)
    centred = values - center
    variance = jnp.mean(centred * centred, axis=1, keepdims=True)
    return centred * lax.rsqrt(variance + 1e-05)


TILE = 256


class Copies:
    def __init__(self, sems):
        self.sems, self.used, self.open = sems, 0, []

    def start(self, src, dst):
        copy = pltpu.make_async_copy(src, dst, self.sems.at[self.used])
        self.used += 1
        copy.start()
        return copy

    def out(self, src, dst):
        self.open.append(self.start(src, dst))

    def finish(self):
        for copy in self.open:
            copy.wait()


def valid_rows(length, first, rows, columns):
    at = lax.broadcasted_iota(jnp.int32, (rows, columns), 0) + first
    return jnp.where(at < length, 1.0, 0.0).astype(f32)


def blocks(rows, step):
    return [slice(at, at + step) for at in range(0, rows, step)]


def folded(values):
    return jnp.sum(values.reshape(-1, 8, values.shape[1]), axis=0)


def front_kernel(size, names, *refs):
    ref = types.SimpleNamespace(**dict(zip(names, refs)))
    x, vec, net = ref.x_in, ref.vec, ref.net_in
    micro, count, width = x.shape
    slot = 2 * count
    tiles = width // TILE
    ring = Ring(size)
    copies = Copies(ref.copy_sems)
    proj_copy = copies.start(ref.proj, ref.proj_in)
    x_copy = copies.start(ref.x, x)
    down_copy = copies.start(ref.down, ref.down_in)
    feature_copy = copies.start(ref.feature, ref.feature_in)
    table_copy = copies.start(ref.table, ref.table_in)
    back_copy = copies.start(ref.back, ref.back_in)
    table, table_back = ref.table_in, ref.back_in
    inside = jnp.where(ring.pos > 0, 1.0, 0.0).astype(f32)

    proj_copy.wait()
    own = ref.in_own
    for j in range(tiles):
        for p in range(3):
            first = p * width + j * TILE
            own[j, :, p * TILE : (p + 1) * TILE] = ref.proj_in[:, first : first + TILE].astype(bf16)
    greet_all(ring)
    gather = [Gather(ring, own.at[j], ref.win_in.at[j], ref.win_sem.at[j]) for j in range(tiles)]
    gather_out = Gather(ring, ref.out_own, ref.wout_in, ref.wout_sem)
    gather_up = Gather(ring, ref.up_own, ref.wup, ref.wup_sem)
    gather_down = Gather(ring, ref.down_own, ref.wdown, ref.wdown_sem)
    gather[0].begin()
    gather[1].begin()
    x_copy.wait()
    edge = remote(
        x.at[:, pl.ds(count - 16, 16)], ref.halo, ref.halo_sem.at[0],
        ref.halo_sem.at[1], ring.across,
    )
    edge.start()

    gain, shift = vec[0:1], vec[1:2]
    normed_ref, turned_ref = ref.n_in, ref.nt_in

    def first_norm(m):
        for rows in blocks(count, 16):
            normed_ref[m, rows] = (norm_rows(x[m, rows].astype(f32)) * gain + shift).astype(bf16)
        for rows in blocks(count, TILE):
            turned_ref[m, :, rows] = normed_ref[m, rows].T

    first_norm(0)
    gather[0].advance(1)
    gather[1].advance(1)
    gather[2].begin()
    for m in range(1, micro):
        first_norm(m)
    copies.out(turned_ref, ref.nt)
    ref.out_own[...] = ref.proj_in[:, 3 * width : 4 * width].astype(bf16)
    gather[0].advance(2)
    gather[1].advance(2)
    edge.wait_recv()
    for m in range(micro):
        ref.halo_n[m] = (norm_rows(ref.halo[m].astype(f32)) * gain + shift).astype(bf16)
    feature_copy.wait()

    net[...] = ref.net[...].T
    frequency = net[EMB + 3 + 2 * HID : EMB + 4 + 2 * HID]
    rates = ref.rate[...].reshape(1, width)

    def sines(layer):
        parts = [sin_cos(frequency * layer[part])[0] for part in blocks(TILE, 64)]
        return jnp.concatenate(parts, axis=0)

    def filter_rows(at):
        rows = slice(at * TILE, (at + 1) * TILE)
        layer = jnp.dot(
            ref.feature_in[rows, : net.shape[0]], net[...], precision=highest,
            preferred_element_type=f32,
        )
        ref.pre_in[rows, :HID] = layer
        layer = sines(layer)
        for i, first in ((1, EMB + 1), (2, EMB + 2 + HID)):
            layer = (
                jnp.dot(
                    layer, net[first : first + HID], precision=highest,
                    preferred_element_type=f32,
                )
                + net[first + HID : first + HID + 1]
            )
            ref.pre_in[rows, i * HID : (i + 1) * HID] = layer
            layer = sines(layer)
        shaped = dot(layer.astype(bf16), ref.final[...].astype(bf16))
        for part in blocks(TILE, 16):
            at_row = lax.broadcasted_iota(jnp.int32, (16, width), 0) + (at * TILE + part.start)
            window = jnp.exp(at_row.astype(f32) * (rates * (-1.0 / slot))) + 0.05
            first = at * TILE + part.start
            ref.filt[first : first + 16] = (shaped[part] * window).astype(bf16)

    row_blocks = slot // TILE
    filter_rows(0)
    gather[0].advance(3)
    gather[1].advance(3)
    gather[2].advance(1)
    down_copy.wait()
    ref.up_own[...] = ref.proj_in[:, 4 * width :].astype(bf16)
    ref.down_own[...] = ref.down_in[...].astype(bf16)
    gather[0].advance(4)
    gather[2].advance(2)
    gather_out.begin()
    gather[1].advance(4)
    gather[0].arrive()

    z_in, s_in, ulow, urecv = ref.z_in, ref.s_in, ref.ulow, ref.urecv
    zbuf, spec = ref.zbuf, ref.spec
    crossing = []

    def project(j):
        weight = ref.win_in[j].reshape(width, 3 * TILE)
        bias = jnp.concatenate(
            [vec[4 + p : 5 + p, j * TILE : (j + 1) * TILE] for p in range(3)], axis=1
        )
        lane = slice(j * TILE, (j + 1) * TILE)
        taps = [[vec[13 + 3 * k + p : 14 + 3 * k + p, lane] for p in range(3)] for k in range(3)]
        constant = [
            (taps[0][p] + taps[1][p] + taps[2][p]) * vec[4 + p : 5 + p, lane]
            + vec[22 + p : 23 + p, lane]
            for p in range(3)
        ]

        @pl.loop(0, micro)
        def _(m):
            zbuf[16:] = dot(normed_ref[m], weight)
            zbuf[:16] = dot(ref.halo_n[m], weight) * inside + bias * (inside - 1.0)
            ref.zh_in[j, m] = (zbuf[:16] + bias).astype(bf16)
            for rows in blocks(count, 32):
                parts = []
                for p in range(3):
                    cols = slice(p * TILE, (p + 1) * TILE)
                    first = rows.start
                    z = zbuf[first + 16 : first + 48, cols]
                    z_in[j, m, rows, cols] = (z + bias[:, cols]).astype(bf16)
                    short = (
                        taps[0][p] * z
                        + taps[1][p] * zbuf[first + 15 : first + 47, cols]
                        + taps[2][p] * zbuf[first + 14 : first + 46, cols]
                        + constant[p]
                    ).astype(bf16)
                    s_in[j, m, rows, cols] = short
                    parts.append(short.astype(f32))
                ulow[j, m, rows] = (parts[1] * parts[2]).astype(bf16)

        copy = remote(
            ulow.at[j], urecv.at[j], ref.u_sem.at[0, j], ref.u_sem.at[1, j], ring.across
        )
        copy.start()
        crossing.append(copy)
        copies.out(z_in.at[j], ref.z.at[j])
        copies.out(s_in.at[j], ref.s.at[j])

    project(0)
    gather[2].advance(3)
    gather_up.begin()
    gather[1].arrive()
    project(1)
    gather[2].advance(4)
    gather_down.begin()
    gather_out.advance(1)
    gather[2].arrive()
    project(2)
    copies.out(ref.zh_in, ref.zh)
    copies.out(ref.win_in, ref.win)
    gather_out.advance(2)
    for at in range(1, row_blocks):
        filter_rows(at)
        if at == 2:
            gather_up.advance(1)
            gather_out.advance(3)
    copies.out(ref.pre_in, ref.pre)
    gather_down.advance(1)
    gather_out.advance(4)
    gather_out.arrive()
    copies.out(ref.wout_in, ref.wout)
    table_copy.wait()
    back_copy.wait()

    parity = 1.0 - 2.0 * (lax.broadcasted_iota(jnp.int32, (16, TILE), 0) % 2).astype(f32)
    kern, uhat = ref.kern_in, ref.uhat_in
    one, two = ref.one, ref.two

    @pl.loop(0, tiles)
    def _(j):
        cols = pl.ds(pl.multiple_of(j * TILE, TILE), TILE)
        one[...] = dot(table[...], ref.filt[:count, cols])
        two[...] = dot(table[...], ref.filt[count:, cols])
        for re in blocks(count, 16):
            im = slice(re.start + count, re.stop + count)
            kern[j, 0, re] = one[re].astype(bf16)
            kern[j, 0, im] = one[im].astype(bf16)
            kern[j, 1, re] = (two[re] - parity * one[im]).astype(bf16)
            kern[j, 1, im] = (two[im] + parity * one[re]).astype(bf16)
        for m in range(micro):
            uhat[j, m, 0] = dot(table[...], ulow[j, m]).astype(bf16)

    copies.out(kern, ref.kern)
    gather_up.advance(2)

    def mix(j):
        crossing[j].wait_recv()
        lane = slice(j * TILE, (j + 1) * TILE)

        @pl.loop(0, micro)
        def _(m):
            one[...] = dot(table[...], urecv[j, m])
            for re in blocks(count, 16):
                im = slice(re.start + count, re.stop + count)
                k0r, k0i = kern[j, 0, re].astype(f32), kern[j, 0, im].astype(f32)
                k1r, k1i = kern[j, 1, re].astype(f32), kern[j, 1, im].astype(f32)
                ur, ui = uhat[j, m, 0, re].astype(f32), uhat[j, m, 0, im].astype(f32)
                vr, vi = one[re] * inside, one[im] * inside
                uhat[j, m, 1, re] = vr.astype(bf16)
                uhat[j, m, 1, im] = vi.astype(bf16)
                spec[re] = (k0r * ur - k0i * ui + k1r * vr - k1i * vi).astype(bf16)
                spec[im] = (k0r * ui + k0i * ur + k1r * vi + k1i * vr).astype(bf16)
            two[:count] = dot(table_back[...], spec[...])
            length = ref.lens[0, m] - ring.pos * count
            for rows in blocks(count, 32):
                gated = s_in[j, m, rows, TILE : 2 * TILE].astype(f32) * s_in[
                    j, m, rows, 2 * TILE :
                ].astype(f32)
                conv = two[rows] * (1.0 / count) + vec[25:26, lane] * gated
                ref.conv_in[j, m, rows] = conv.astype(bf16)
                mask = valid_rows(length, rows.start, 32, TILE)
                ref.y_in[m, rows, lane] = (
                    mask * s_in[j, m, rows, :TILE].astype(f32) * conv
                ).astype(bf16)

        copies.out(ref.conv_in.at[j], ref.conv.at[j])
        copies.out(uhat.at[j], ref.uhat.at[j])

    for j in range(tiles):
        mix(j)
        if j == 0:
            gather_down.advance(2)
        if j == 1:
            gather_up.advance(3)

    for m in range(micro):
        ref.res_in[m] = dot(ref.y_in[m], ref.wout_in[...].reshape(width, width))
        for rows in blocks(count, TILE):
            ref.yt_in[m, :, rows] = ref.y_in[m, rows].T
        for rows in blocks(count, 16):
            residual = x[m, rows].astype(f32) + ref.res_in[m, rows] + vec[7:8]
            ref.res_in[m, rows] = residual
            ref.n2_in[m, rows] = (norm_rows(residual) * vec[2:3] + vec[3:4]).astype(bf16)
        for rows in blocks(count, TILE):
            ref.n2t_in[m, :, rows] = ref.n2_in[m, rows].T
        for src, dst in (
            (ref.yt_in, ref.yt), (ref.res_in, ref.res), (ref.n2_in, ref.n2), (ref.n2t_in, ref.n2t)
        ):
            copies.out(src.at[m], dst.at[m])
        if m == 0:
            gather_down.advance(3)
    gather_up.advance(4)
    gather_down.advance(4)
    for work in (gather_up, gather_down):
        work.arrive()
    for work in gather + [gather_out, gather_up, gather_down]:
        work.finish()
    edge.wait_send()
    for copy in crossing:
        copy.wait_send()
    copies.finish()


def front(size, arrays):
    chips = size // 2
    micro, count, width = arrays["x"].shape
    rows, down_rows = arrays["proj"].shape[0], arrays["down"].shape[0]
    wide = down_rows * size
    tiles = width // TILE
    vmem = pl.BlockSpec(memory_space=pltpu.VMEM)
    anywhere = pl.BlockSpec(memory_space=pl.ANY)
    smem = pl.BlockSpec(memory_space=pltpu.SMEM)
    near = ("vec", "net", "final", "rate")
    kinds = dict(
        win=((tiles, chips, 2, rows, 3 * TILE), bf16),
        wout=((chips, 2, rows, width), bf16),
        z=((tiles, micro, count, 3 * TILE), bf16),
        zh=((tiles, micro, 16, 3 * TILE), bf16),
        s=((tiles, micro, count, 3 * TILE), bf16),
        conv=((tiles, micro, count, TILE), bf16),
        uhat=((tiles, micro, 2, 2 * count, TILE), bf16),
        kern=((tiles, 2, 2 * count, TILE), bf16),
        res=((micro, count, width), f32),
        nt=((micro, width, count), bf16),
        n2=((micro, count, width), bf16),
        n2t=((micro, width, count), bf16),
        yt=((micro, width, count), bf16),
        pre=((2 * count, 4 * HID), f32),
    )
    outs = dict(
        kinds,
        wup=((chips, 2, rows, wide), bf16),
        wdown=((chips, 2, down_rows, width), bf16),
    )
    dma = pltpu.SemaphoreType.DMA
    scratch = {
        name + "_in": pltpu.VMEM(*kind) for name, kind in kinds.items()
    }
    for name, array in arrays.items():
        if name not in near and name != "lens":
            scratch[name + "_in"] = pltpu.VMEM(array.shape, array.dtype)
    scratch.update(
        dict(
            n_in=pltpu.VMEM((micro, count, width), bf16),
            one=pltpu.VMEM((2 * count, TILE), f32),
            two=pltpu.VMEM((2 * count, TILE), f32),
            net_in=pltpu.VMEM((EMB + 4 + 2 * HID, HID), f32),
            y_in=pltpu.VMEM((micro, count, width), bf16),
            in_own=pltpu.VMEM((tiles, rows, 3 * TILE), bf16),
            out_own=pltpu.VMEM((rows, width), bf16),
            up_own=pltpu.VMEM((rows, wide), bf16),
            down_own=pltpu.VMEM((down_rows, width), bf16),
            halo=pltpu.VMEM((micro, 16, width), bf16),
            halo_n=pltpu.VMEM((micro, 16, width), bf16),
            filt=pltpu.VMEM((2 * count, width), bf16),
            zbuf=pltpu.VMEM((16 + count, 3 * TILE), f32),
            ulow=pltpu.VMEM((tiles, micro, count, TILE), bf16),
            urecv=pltpu.VMEM((tiles, micro, count, TILE), bf16),
            spec=pltpu.VMEM((2 * count, TILE), bf16),
            win_sem=dma((tiles, 3, 2 * chips)),
            wout_sem=gather_sems(size),
            wup_sem=gather_sems(size),
            wdown_sem=gather_sems(size),
            halo_sem=dma((2,)),
            u_sem=dma((2, tiles)),
            copy_sems=dma((40,)),
        )
    )
    names = tuple(arrays) + tuple(outs) + tuple(scratch)
    made = pl.pallas_call(
        functools.partial(front_kernel, size, names),
        out_shape=[jax.ShapeDtypeStruct(*kind) for kind in outs.values()],
        in_specs=[
            smem if name == "lens" else vmem if name in near else anywhere for name in arrays
        ],
        out_specs=[anywhere] * len(outs),
        scratch_shapes=list(scratch.values()),
        compiler_params=pltpu.CompilerParams(
            collective_id=0, has_side_effects=True, vmem_limit_bytes=63 * 1024 * 1024
        ),
        name="front",
    )(*arrays.values())
    return dict(zip(outs, made))


GELU_SCALE = math.sqrt(2.0 / math.pi)


def gelu_pair(a):
    square = a * a
    half = 0.5 + 0.5 * jnp.tanh(a * (GELU_SCALE + (GELU_SCALE * 0.044715) * square))
    hidden = a * half
    bend = 2.0 * GELU_SCALE + (2.0 * GELU_SCALE * 0.134145) * square
    return hidden, half + (hidden - hidden * half) * bend


def mlp_kernel(
    n2_ref, n2t_ref, gm_ref, res_ref, vec_ref, wup_ref, wdown_ref,
    out_ref, gb_ref, dup_ref, ddown_ref, small_ref,
    acc_out, acc_gn, hid_ref, ga_ref, pre_ref, grad_ref,
):
    step, last = pl.program_id(0), pl.num_programs(0) - 1
    micro, count, width = n2_ref.shape
    chunk = width
    tile = 256
    wup = wup_ref[...].reshape(width, chunk)
    wdown = wdown_ref[...].reshape(chunk, width)
    bias = vec_ref[pl.ds(8 + step, 1)]

    @pl.when(step == 0)
    def _():
        acc_out[...] = jnp.zeros_like(acc_out)
        acc_gn[...] = jnp.zeros_like(acc_gn)
        small_ref[...] = jnp.zeros_like(small_ref)

    tile = 256
    bias_sum = jnp.zeros((8, chunk), f32)
    pre_ref[0] = dot(n2_ref[0], wup)
    grad_ref[0] = dot_nt(gm_ref[0], wdown)
    for m in range(micro):
        if m + 1 < micro:
            pre_ref[m + 1] = dot(n2_ref[m + 1], wup)
            grad_ref[m + 1] = dot_nt(gm_ref[m + 1], wdown)
        sums = []
        for first in range(0, chunk, tile):
            cols = slice(first, first + tile)
            part = jnp.zeros((8, tile), f32)
            for rows in blocks(count, 32):
                hidden, slope = gelu_pair(pre_ref[m, rows, cols] + bias[:, cols])
                hid_ref[m, rows, cols] = hidden.astype(bf16)
                ga = (grad_ref[m, rows, cols] * slope).astype(bf16)
                ga_ref[m, rows, cols] = ga
                part = part + folded(ga.astype(f32))
            sums.append(part)
        bias_sum = bias_sum + jnp.concatenate(sums, axis=1)
        acc_out[m] += dot(hid_ref[m], wdown)
        acc_gn[m] += dot_nt(ga_ref[m], wup)
    small_ref[pl.ds(4 + step, 1)] = jnp.sum(bias_sum, axis=0, keepdims=True)
    down_total = dot_tn(hid_ref[0], gm_ref[0])
    up_total = dot(n2t_ref[0], ga_ref[0])
    for m in range(1, micro):
        down_total = down_total + dot_tn(hid_ref[m], gm_ref[m])
        up_total = up_total + dot(n2t_ref[m], ga_ref[m])
    ddown_ref[...] = down_total.astype(bf16)
    dup_ref[...] = up_total.astype(bf16)

    @pl.when(step == last)
    def _():
        sums = [jnp.zeros((8, width), f32)] * 4
        for m in range(micro):
            for rows in blocks(count, 16):
                residual = res_ref[m, rows]
                out_ref[m, rows] = (residual + acc_out[m, rows] + vec_ref[12:13]).astype(bf16)
                gx, gain_part, grad = norm_rows_back(acc_gn[m, rows], residual, vec_ref[2:3])
                gm = gm_ref[m, rows].astype(f32)
                low = (gm + gx).astype(bf16)
                gb_ref[m, rows] = low
                parts = (gain_part, grad, low.astype(f32), gm)
                sums = [total + folded(part) for total, part in zip(sums, parts)]
        for k in range(4):
            small_ref[k : k + 1] = jnp.sum(sums[k], axis=0, keepdims=True)


def norm_rows_back(grad, values, gain):
    center = jnp.mean(values, axis=1, keepdims=True)
    centred = values - center
    variance = jnp.mean(centred * centred, axis=1, keepdims=True)
    scale = lax.rsqrt(variance + 1e-05)
    xh = centred * scale
    q = grad * gain
    gx = scale * (
        q - jnp.mean(q, axis=1, keepdims=True) - xh * jnp.mean(q * xh, axis=1, keepdims=True)
    )
    return gx, grad * xh, grad


def mlp(n2, n2t, gm, res, vectors, wup, wdown):
    micro, count, width = n2.shape
    chips, cores, rows, wide = wup.shape
    steps = wide // width
    per = chips // steps

    def whole(array):
        return pl.BlockSpec(array.shape, lambda i: (0,) * array.ndim)

    def shape(dims, kind=bf16):
        return jax.ShapeDtypeStruct(dims, kind)

    tokens = pl.BlockSpec((micro, count, width), lambda i: (0, 0, 0))
    return pl.pallas_call(
        mlp_kernel,
        grid=(steps,),
        in_specs=[
            whole(n2), whole(n2t), whole(gm), whole(res), whole(vectors),
            pl.BlockSpec((chips, cores, rows, width), lambda i: (0, 0, 0, i)),
            pl.BlockSpec((per, cores, wdown.shape[2], width), lambda i: (i, 0, 0, 0)),
        ],
        out_specs=[
            tokens, tokens,
            pl.BlockSpec((width, width), lambda i: (0, i)),
            pl.BlockSpec((width, width), lambda i: (i, 0)),
            pl.BlockSpec((4 + steps, width), lambda i: (0, 0)),
        ],
        out_shape=[
            shape((micro, count, width)),
            shape((micro, count, width)),
            shape((width, wide)),
            shape((wide, width)),
            shape((4 + steps, width), f32),
        ],
        scratch_shapes=[
            pltpu.VMEM((micro, count, width), f32),
            pltpu.VMEM((micro, count, width), f32),
            pltpu.VMEM((micro, count, width), bf16),
            pltpu.VMEM((micro, count, width), bf16),
            pltpu.VMEM((micro, count, width), f32),
            pltpu.VMEM((micro, count, width), f32),
        ],
        compiler_params=pltpu.CompilerParams(vmem_limit_bytes=63 * 1024 * 1024),
        name="mlp",
    )(n2, n2t, gm, res, vectors, wup, wdown)


def update_kernel(rates, firsts, *refs):
    count = len(rates)
    ins, outs = refs[: 4 * count], refs[4 * count :]
    for i, (rate, first) in enumerate(zip(rates, firsts)):
        grad_ref, weight_ref, moment_ref, average_ref = ins[4 * i : 4 * i + 4]
        rows, columns = weight_ref.shape
        stepped = nesterov(
            weight_ref[...], moment_ref[...], average_ref[...],
            grad_ref[first : first + rows, :columns], rate,
        )
        for out, value in zip(outs[4 * i : 4 * i + 4], stepped):
            out[...] = value


def update(sets):
    steps = 4
    arrays, in_specs, out_specs, shapes = [], [], [], []

    def spec(shape, cut):
        if cut is None:
            return pl.BlockSpec(shape, lambda i: (0, 0))
        if cut:
            return pl.BlockSpec((shape[0], shape[1] // steps), lambda i: (0, i))
        return pl.BlockSpec((shape[0] // steps, shape[1]), lambda i: (i, 0))

    for grad, weight, moment, average, rate, first, cut in sets:
        arrays += [grad, weight, moment, average]
        in_specs += [spec(grad.shape, cut)] + [spec(weight.shape, cut)] * 3
        out_specs += [spec(weight.shape, cut)] * 4
        shapes += [jax.ShapeDtypeStruct(weight.shape, f32)] * 4
    made = pl.pallas_call(
        functools.partial(update_kernel, [s[4] for s in sets], [s[5] for s in sets]),
        grid=(steps,),
        in_specs=in_specs,
        out_specs=out_specs,
        out_shape=shapes,
        compiler_params=pltpu.CompilerParams(vmem_limit_bytes=63 * 1024 * 1024),
        name="update",
    )(*arrays)
    return [made[4 * i : 4 * i + 4] for i in range(len(sets))]


FINAL_ROW = 32


def back_kernel(size, names, *refs):
    ref = types.SimpleNamespace(**dict(zip(names, refs)))
    gb, vec, table, table_back = ref.gb, ref.vec, ref.table, ref.back
    micro, count, width = gb.shape
    slot = 2 * count
    tiles = width // TILE
    ring = Ring(size)
    gw, gc, gcr, gz = ref.gw, ref.gc, ref.gcr, ref.gz
    vsum, nsum = ref.vsum, ref.nsum
    one, two = ref.one, ref.two
    gate, turned = ref.gate, ref.turned
    inside = jnp.where(ring.pos < 1, 1.0, 0.0).astype(f32)
    copies = Copies(ref.copy_sems)
    gate_copies = [
        copies.start(ref.s.at[j, :, :, pl.ds(0, TILE)], gate.at[j]) for j in range(tiles)
    ]
    wout = ref.din.at[0]
    wout_copy = copies.start(ref.wout, wout)
    turned_copy = copies.start(ref.yt, turned)

    greet_all(ring)
    red = {}

    def parts_of(name):
        return [getattr(ref, name + str(k)) for k in range(6)]

    down = Reduction(ring, ref.ddown, *parts_of("down"), ref.down_stage, ref.down_stage_sems)
    up = Reduction(ring, ref.dup, *parts_of("up"), ref.up_stage, ref.up_stage_sems)
    out = Reduction(ring, ref.dout, *parts_of("out"))
    inner = [
        Reduction(ring, ref.din.at[j], *[part.at[j] for part in parts_of("in")])
        for j in range(tiles)
    ]
    down.begin()
    up.begin()
    vsum[...] = jnp.zeros_like(vsum)
    nsum[...] = jnp.zeros_like(nsum)
    small = ref.small
    vsum[2:4] = small[0:2]
    vsum[7:8] = small[2:3]
    vsum[12:13] = small[3:4]
    vsum[8:12] = small[4:8]

    crossing = []
    wout_copy.wait()
    for j in range(tiles):
        gate_copies[j].wait()
        weight = wout[...].reshape(width, width)[j * TILE : (j + 1) * TILE]

        @pl.loop(0, micro)
        def _(m):
            one[:count] = dot_nt(gb[m], weight)
            length = ref.lens[0, m] - ring.pos * count
            for rows in blocks(count, 32):
                mask = valid_rows(length, rows.start, 32, TILE)
                grad = mask * one[rows].astype(bf16).astype(f32)
                gw[j, m, rows] = grad.astype(bf16)
                gc[j, m, rows] = (grad * gate[j, m, rows].astype(f32)).astype(bf16)

        copy = remote(
            gc.at[j], gcr.at[j], ref.gc_sem.at[0, j], ref.gc_sem.at[1, j], ring.across
        )
        copy.start()
        crossing.append(copy)
    turned_copy.wait()

    @pl.loop(0, tiles)
    def _(j):
        cols = pl.ds(pl.multiple_of(j * TILE, TILE), TILE)
        total = dot(turned[0], gb[0, :, cols])
        for m in range(1, micro):
            total = total + dot(turned[m], gb[m, :, cols])
        dout = ref.dout
        dout[:, :, :, cols] = total.astype(bf16).reshape(dout.shape[:3] + (TILE,))

    turned_copy = copies.start(ref.nt, turned)
    out.begin()
    down.merge()
    up.merge()

    parity = 1.0 - 2.0 * (lax.broadcasted_iota(jnp.int32, (16, TILE), 0) % 2).astype(f32)
    gk = ref.gk
    gbuf, zbuf, spec = ref.gbuf, ref.zbuf, ref.spec
    first_rows, last_rows, next_rows = ref.first_rows, ref.last_rows, ref.next_rows

    def loads(j, m, at):
        made = [
            (ref.s.at[j, m, :, pl.ds(TILE, 2 * TILE)], ref.s_buf.at[at]),
            (ref.z.at[j, m], ref.z_buf.at[at]),
            (ref.uhat.at[j, m], ref.u_buf.at[at]),
            (ref.conv.at[j, m], ref.c_buf.at[at]),
        ]
        return [
            pltpu.make_async_copy(src, dst, ref.load_sems.at[at, i])
            for i, (src, dst) in enumerate(made)
        ]

    def load_kernel(j):
        return pltpu.make_async_copy(ref.kern.at[j], ref.k_buf, ref.kernel_sem.at[0])

    def start_loads(j, m, at):
        for copy in loads(j, m, at):
            copy.start()

    start_loads(0, 0, 0)
    load_kernel(0).start()
    gbuf[:, count:] = jnp.zeros_like(gbuf[:, count:])

    def unmix(j):
        crossing[j].wait_recv()
        load_kernel(j).wait()
        lane = slice(j * TILE, (j + 1) * TILE)
        kn = ref.k_buf

        @pl.loop(0, micro)
        def _(m):
            at = lax.rem(j * micro + m, 2)
            for copy in loads(j, m, at):
                copy.wait()

            @pl.when(m + 1 < micro)
            def _():
                start_loads(j, m + 1, 1 - at)

            if j + 1 < tiles:

                @pl.when(m + 1 == micro)
                def _():
                    start_loads(j + 1, 0, 1 - at)

            one[...] = dot(table[...], gc[j, m])
            two[...] = dot(table[...], gcr[j, m])
            keep = jnp.where(m > 0, 1.0, 0.0).astype(f32)
            uh = ref.u_buf
            for re in blocks(count, 16):
                im = slice(re.start + count, re.stop + count)
                gr, gi = one[re], one[im]
                hr, hi = two[re] * inside, two[im] * inside
                k0r, k0i = kn[0, re].astype(f32), kn[0, im].astype(f32)
                k1r, k1i = kn[1, re].astype(f32), kn[1, im].astype(f32)
                spec[re] = (k0r * gr + k0i * gi + k1r * hr + k1i * hi).astype(bf16)
                spec[im] = (k0r * gi - k0i * gr + k1r * hi - k1i * hr).astype(bf16)
                for d in range(2):
                    ur, ui = uh[at, d, re].astype(f32), uh[at, d, im].astype(f32)
                    gk[d, re] = gk[d, re] * keep + (ur * gr + ui * gi)
                    gk[d, im] = gk[d, im] * keep + (ur * gi - ui * gr)
            two[:count] = dot(table_back[...], spec[...])
            skip_sum = jnp.zeros((8, TILE), f32)
            for rows in blocks(count, 32):
                x1 = ref.s_buf[at, rows, :TILE].astype(f32)
                v = ref.s_buf[at, rows, TILE:].astype(f32)
                grad_w = gw[j, m, rows].astype(f32)
                gc_full = grad_w * gate[j, m, rows].astype(f32)
                gu = two[rows] * (1.0 / count) + vec[25:26, lane] * gc_full
                skip_sum = skip_sum + folded(gc_full * (x1 * v))
                grads = (grad_w * ref.c_buf[at, rows].astype(f32), gu * v, gu * x1)
                for p in range(3):
                    low = grads[p].astype(bf16)
                    gbuf[p, rows] = low.astype(f32)
                    if rows.start == 0:
                        first_rows[j, m, :, p * TILE : (p + 1) * TILE] = low[:16]
                    if rows.stop == count:
                        last_rows[j, m, :, p * TILE : (p + 1) * TILE] = low[16:]
            vsum[25:26, lane] += jnp.sum(skip_sum, axis=0, keepdims=True)
            for p in range(3):
                cols = slice(p * TILE, (p + 1) * TILE)
                zbuf[:16] = ref.zh[j, m, :, cols].astype(f32)
                for rows in blocks(count, 32):
                    zbuf[rows.start + 16 : rows.stop + 16] = ref.z_buf[at, rows, cols].astype(f32)
                taps = [vec[13 + 3 * k + p : 14 + 3 * k + p, lane] for k in range(3)]
                sums = [jnp.zeros((8, TILE), f32) for _ in range(4)]
                for rows in blocks(count, 32):
                    first = rows.start
                    grad = gbuf[p, rows]
                    gz[j, m, rows, cols] = (
                        taps[0] * grad
                        + taps[1] * gbuf[p, first + 1 : first + 33]
                        + taps[2] * gbuf[p, first + 2 : first + 34]
                    ).astype(bf16)
                    for k in range(3):
                        sums[k] = sums[k] + folded(grad * zbuf[first + 16 - k : first + 48 - k])
                    sums[3] = sums[3] + folded(grad)
                for k in range(4):
                    row = 13 + 3 * k + p
                    vsum[row : row + 1, lane] += jnp.sum(sums[k], axis=0, keepdims=True)

        if j + 1 < tiles:
            load_kernel(j + 1).start()
        edge = remote(
            first_rows.at[j], next_rows.at[j], ref.edge_sem.at[0, j],
            ref.edge_sem.at[1, j], ring.across,
        )
        edge.start()
        for re in blocks(count, 16):
            im = slice(re.start + count, re.stop + count)
            spec[re] = (gk[0, re] + parity * gk[1, im]).astype(bf16)
            spec[im] = (gk[0, im] - parity * gk[1, re]).astype(bf16)
        two[:count] = dot(table_back[...], spec[...])
        for re in blocks(2 * count, 16):
            spec[re] = gk[1, re].astype(bf16)
        two[count:] = dot(table_back[...], spec[...])
        for rows in blocks(count, 16):
            gate[j, 0, rows] = (two[rows] * (1.0 / count)).astype(bf16)
            second = two[rows.start + count : rows.stop + count]
            gate[j, 1, rows] = (second * (1.0 / count)).astype(bf16)
        return edge

    def project_back(j, edge):
        edge.wait_recv()
        lane = slice(j * TILE, (j + 1) * TILE)
        ebuf = ref.ebuf
        for m in range(micro):
            for p in range(3):
                cols = slice(p * TILE, (p + 1) * TILE)
                own = last_rows[j, m, :, cols].astype(f32)
                ebuf[:16] = own
                ebuf[16:] = next_rows[j, m, :, cols].astype(f32) * inside
                gz[j, m, count - 16 :, cols] = (
                    vec[13 + p : 14 + p, lane] * own
                    + vec[16 + p : 17 + p, lane] * ebuf[1:17]
                    + vec[19 + p : 20 + p, lane] * ebuf[2:18]
                ).astype(bf16)
        for p in range(3):
            cols = slice(p * TILE, (p + 1) * TILE)
            total = dot(turned[0], gz[j, 0, :, cols])
            for m in range(1, micro):
                total = total + dot(turned[m], gz[j, m, :, cols])
            din = ref.din
            din[j, :, :, :, cols] = total.astype(bf16).reshape(din.shape[1:4] + (TILE,))
            bias = jnp.zeros((8, TILE), f32)
            for m in range(micro):
                for rows in blocks(count, 32):
                    bias = bias + folded(gz[j, m, rows, cols].astype(f32))
            vsum[4 + p : 5 + p, lane] = jnp.sum(bias, axis=0, keepdims=True)
        inner[j].begin()

    edges = [unmix(0)]
    down.advance(1)
    up.advance(1)
    out.merge()
    edges.append(unmix(1))
    turned_copy.wait()
    project_back(0, edges[0])
    down.advance(2)
    up.advance(2)
    out.advance(1)
    inner[0].merge()
    edges.append(unmix(2))
    project_back(1, edges[1])
    x_copies = [
        copies.start(ref.x.at[:, :, pl.ds(j * TILE, TILE)], gcr.at[j]) for j in range(tiles)
    ]
    pre_copy = copies.start(ref.pre, gk.at[0])
    feature_copy = copies.start(ref.feature, gk.at[1])
    down.advance(3)
    up.advance(3)
    inner[1].merge()
    project_back(2, edges[2])
    out.advance(2)
    inner[0].advance(1)
    inner[1].advance(1)
    for copy in x_copies:
        copy.wait()
    for copy in crossing:
        copy.wait_send()

    for m in range(micro):
        for t in range(tiles):
            total = 0.0
            for j in range(tiles):
                weight = ref.win[j].reshape(width, 3 * TILE)[t * TILE : (t + 1) * TILE]
                total = total + dot_nt(gz[j, m], weight)
            gbuf[t, :count] = total
        sums = [jnp.zeros((8, width), f32)] * 2
        for rows in blocks(count, 16):
            tokens = jnp.concatenate([gcr[j, m, rows] for j in range(tiles)], axis=1)
            grad = jnp.concatenate([gbuf[t, rows] for t in range(tiles)], axis=1)
            gx, gain_part, shift_part = norm_rows_back(grad, tokens.astype(f32), vec[0:1])
            sums = [sums[0] + folded(gain_part), sums[1] + folded(shift_part)]
            total = (gb[m, rows].astype(f32) + gx).astype(bf16)
            for j in range(tiles):
                gc[j, m, rows] = total[:, j * TILE : (j + 1) * TILE]
        vsum[0:1] += jnp.sum(sums[0], axis=0, keepdims=True)
        vsum[1:2] += jnp.sum(sums[1], axis=0, keepdims=True)
        if m == 0:
            inner[2].merge()
            down.collect()
            up.collect()
            out.advance(3)
            inner[0].advance(2)
            inner[1].advance(2)
    for j in range(tiles):
        copies.out(gc.at[j], ref.input_grad.at[:, :, pl.ds(j * TILE, TILE)])
    inner[2].advance(1)
    inner[0].advance(3)
    inner[1].advance(3)
    out.collect()

    net = ref.net_in
    net[...] = ref.net[...].T
    rates = ref.rate[...].reshape(1, width)
    final_low = ref.final[...].astype(bf16)
    pre_copy.wait()
    feature_copy.wait()
    frequency = net[EMB + 3 + 2 * HID : EMB + 4 + 2 * HID]

    def filter_back(at):
        rows = pl.ds(pl.multiple_of(at * TILE, TILE), TILE)
        half, part = at // (count // TILE), lax.rem(at, count // TILE)
        layers = [gk[0, rows, i * HID : (i + 1) * HID] for i in range(3)]
        many = jnp.concatenate([frequency] * 4, axis=1)
        pairs = []
        for block in blocks(TILE, 32):
            held_rows = pl.ds(pl.multiple_of(at * TILE + block.start, 32), 32)
            pairs.append(sin_cos(many * gk[0, held_rows]))
        act = jnp.concatenate([pair[0] for pair in pairs], axis=0)
        slope = jnp.concatenate([pair[1] for pair in pairs], axis=0)
        acts = [act[:, i * HID : (i + 1) * HID] for i in range(3)]
        slopes = [slope[:, i * HID : (i + 1) * HID] for i in range(3)]
        last = acts[2].astype(bf16)
        grad = jnp.zeros((TILE, HID), f32)
        for j in range(tiles):
            lane = slice(j * TILE, (j + 1) * TILE)
            pieces = []
            for block in blocks(TILE, 32):
                at_row = lax.broadcasted_iota(jnp.int32, (32, TILE), 0) + (
                    at * TILE + block.start
                )
                window = jnp.exp(at_row.astype(f32) * (rates[:, lane] * (-1.0 / slot))) + 0.05
                held = pl.ds(pl.multiple_of(part * TILE + block.start, 32), 32)
                pieces.append((gate[j, half, held].astype(f32) * window).astype(bf16))
            shaped = jnp.concatenate(pieces, axis=0)
            vsum[FINAL_ROW : FINAL_ROW + HID, lane] += dot_tn(last, shaped)
            grad = grad + dot_nt(shaped, final_low[:, lane])
        freq_sum = jnp.zeros_like(frequency)
        for i in (2, 1, 0):
            turn = grad * slopes[i]
            freq_sum = freq_sum + jnp.sum(turn * layers[i], axis=0, keepdims=True)
            grad = turn * frequency
            if i == 0:
                nsum[: EMB + 1, :HID] += lax.dot_general(
                    gk[1, rows, : EMB + 1], grad, (((0,), (0,)), ((), ())),
                    precision=highest, preferred_element_type=f32,
                )
            else:
                first = EMB + 1 if i == 1 else EMB + 2 + HID
                nsum[first : first + HID, :HID] += lax.dot_general(
                    acts[i - 1], grad, (((0,), (0,)), ((), ())),
                    precision=highest, preferred_element_type=f32,
                )
                nsum[first + HID : first + HID + 1, :HID] += jnp.sum(grad, axis=0, keepdims=True)
                grad = lax.dot_general(
                    grad, net[first : first + HID], (((1,), (1,)), ((), ())),
                    precision=highest, preferred_element_type=f32,
                )
        row = EMB + 3 + 2 * HID
        nsum[row : row + 1, :HID] += freq_sum

    row_blocks = slot // TILE

    @pl.loop(0, row_blocks // 2)
    def _(at):
        filter_back(at)

    inner[2].advance(2)
    inner[0].collect()
    inner[1].collect()

    @pl.loop(row_blocks // 2, row_blocks)
    def _(at):
        filter_back(at)

    smalls = []
    for values, sums, name in ((vsum, ref.v_out, "v"), (nsum, ref.n_out, "n")):
        parts = [getattr(ref, name + str(k)) for k in range(4)]
        smalls.append(SmallSum(ring, values, *parts[:3], sums, parts[3]))
    for work in smalls:
        work.begin()
    inner[2].advance(3)
    psum = ref.proj_sum
    wide = psum.shape[1] - 4 * width
    ref.down_sum[...] = down.result()
    for work in smalls:
        work.add_up()
    psum[:, 4 * width : 4 * width + wide] = up.result()
    psum[:, 3 * width : 4 * width] = out.result()
    inner[2].collect()
    for work in smalls:
        work.spread()
    for j in range(tiles):
        total = inner[j].result()
        for p in range(3):
            first = p * width + j * TILE
            psum[:, first : first + TILE] = total[:, p * TILE : (p + 1) * TILE]
    for work in smalls:
        work.finish()
    ref.net_sum[...] = ref.n_out[:, :HID].T
    for work in [down, up, out] + inner:
        work.finish()
    for edge in edges:
        edge.wait_send()
    copies.finish()


def back(size, arrays):
    chips = size // 2
    micro, count, width = arrays["gb"].shape
    rows, wide = arrays["dup"].shape[2:]
    down_rows = arrays["ddown"].shape[2]
    tiles = width // TILE
    vmem = pl.BlockSpec(memory_space=pltpu.VMEM)
    anywhere = pl.BlockSpec(memory_space=pl.ANY)
    smem = pl.BlockSpec(memory_space=pltpu.SMEM)
    near = ("gb", "vec", "net", "final", "rate", "table", "back", "win", "zh", "small")
    small_rows = 8 * size
    outs = dict(
        input_grad=((micro, count, width), bf16),
        proj_sum=((rows, 4 * width + wide), f32),
        down_sum=((down_rows, width), f32),
        v_out=((small_rows, width), f32),
        n_out=((2 * small_rows, 128), f32),
        net_sum=((HID, 2 * small_rows), f32),
    )
    dma = pltpu.SemaphoreType.DMA
    tile_tokens = (tiles, micro, count, TILE)
    edge_rows = (tiles, micro, 16, 3 * TILE)
    scratch = dict(
        din=pltpu.VMEM((tiles, chips, 2, rows, 3 * TILE), bf16),
        dout=pltpu.VMEM((chips, 2, rows, width), bf16),
        gw=pltpu.VMEM(tile_tokens, bf16),
        gc=pltpu.VMEM(tile_tokens, bf16),
        gcr=pltpu.VMEM(tile_tokens, bf16),
        gate=pltpu.VMEM(tile_tokens, bf16),
        gz=pltpu.VMEM((tiles, micro, count, 3 * TILE), bf16),
        turned=pltpu.VMEM((micro, width, count), bf16),
        vsum=pltpu.VMEM((small_rows, width), f32),
        nsum=pltpu.VMEM((2 * small_rows, 128), f32),
        net_in=pltpu.VMEM((EMB + 4 + 2 * HID, HID), f32),
        gk=pltpu.VMEM((2, 2 * count, TILE), f32),
        gbuf=pltpu.VMEM((3, count + 16, TILE), f32),
        one=pltpu.VMEM((2 * count, TILE), f32),
        two=pltpu.VMEM((2 * count, TILE), f32),
        zbuf=pltpu.VMEM((count + 16, TILE), f32),
        ebuf=pltpu.VMEM((32, TILE), f32),
        spec=pltpu.VMEM((2 * count, TILE), bf16),
        first_rows=pltpu.VMEM(edge_rows, bf16),
        last_rows=pltpu.VMEM(edge_rows, bf16),
        next_rows=pltpu.VMEM(edge_rows, bf16),
        s_buf=pltpu.VMEM((2, count, 2 * TILE), bf16),
        z_buf=pltpu.VMEM((2, count, 3 * TILE), bf16),
        u_buf=pltpu.VMEM((2, 2, 2 * count, TILE), bf16),
        c_buf=pltpu.VMEM((2, count, TILE), bf16),
        k_buf=pltpu.VMEM((2, 2 * count, TILE), bf16),
        load_sems=dma((2, 4)),
        kernel_sem=dma((1,)),
        gc_sem=dma((2, tiles)),
        edge_sem=dma((2, tiles)),
        copy_sems=dma((16,)),
        up_stage=pltpu.VMEM((2, rows, wide), bf16),
        down_stage=pltpu.VMEM((2, down_rows, width), bf16),
        up_stage_sems=dma((2,)),
        down_stage_sems=dma((2,)),
    )
    ups, downs = chips // 2, (chips - 1) // 2
    for name, lead, dims in (
        ("up", (), (rows, wide)), ("down", (), (down_rows, width)), ("out", (), (rows, width)),
        ("in", (tiles,), (rows, 3 * TILE)),
    ):
        made = [pltpu.VMEM(lead + (count,) + dims, bf16) for count in (chips, ups, downs)]
        made += [pltpu.VMEM(lead + dims, bf16)] * 2 + [dma(lead + (2, 2 + ups + downs))]
        for k, part in enumerate(made):
            scratch[name + str(k)] = part
    for name in ("v", "n"):
        for k, part in enumerate(small_scratch(size, *outs[name + "_out"][0])):
            scratch[name + str(k)] = part
    names = tuple(arrays) + tuple(outs) + tuple(scratch)
    return pl.pallas_call(
        functools.partial(back_kernel, size, names),
        out_shape=[jax.ShapeDtypeStruct(*kind) for kind in outs.values()],
        in_specs=[
            smem if name == "lens" else vmem if name in near else anywhere for name in arrays
        ],
        out_specs=[anywhere] + [vmem] * (len(outs) - 1),
        scratch_shapes=list(scratch.values()),
        compiler_params=pltpu.CompilerParams(
            collective_id=1, has_side_effects=True, vmem_limit_bytes=63 * 1024 * 1024
        ),
        name="back",
    )(*arrays.values())


def fits(size, groups, tokens, proj_weights, down_weights):
    micro, _, count, width = tokens.shape
    wide = down_weights.shape[0] * size
    return (
        groups == 2
        and size % 4 == 0
        and size == 16
        and proj_weights.shape[0] % 16 == 0
        and down_weights.shape[0] % 16 == 0
        and count % TILE == 0
        and width == 3 * TILE
        and micro >= groups
        and micro * count <= 1024
        and wide == 4 * width
        and proj_weights.shape[1] == 4 * width + wide
    )


def on_device_tuned(
    block_input,
    out_grad,
    lengths,
    decay_rates,
    proj_weights,
    proj_moment,
    proj_average,
    down_weights,
    down_moment,
    down_average,
    vectors,
    vector_moment,
    vector_average,
    filter_net,
    net_moment,
    net_average,
    filter_out,
    final_moment,
    final_average,
):
    micro, _, count, width = block_input.shape
    size = lax.axis_size("seq")
    tokens = block_input.reshape(micro, count, width)
    plain_table = transform_table(count)
    table = jnp.asarray(plain_table, dtype=bf16)
    table_back = jnp.asarray(plain_table.T, dtype=bf16)
    feature = jnp.asarray(feature_table(count * lax.axis_size("pos")))
    shared = dict(
        x=tokens, lens=lengths.T, vec=vectors, net=filter_net.T, final=filter_out,
        rate=decay_rates, table=table, back=table_back, feature=feature,
    )
    made = types.SimpleNamespace(**front(size, dict(shared, proj=proj_weights, down=down_weights)))
    block_output, branch_grad, up_step, down_step, small = mlp(
        made.n2, made.n2t, out_grad.reshape(micro, count, width), made.res, vectors,
        made.wup, made.wdown,
    )
    chips = size // 2
    input_grad, proj_sum, down_sum, rest, _, net_sum = back(
        size,
        dict(
            shared, win=made.win, wout=made.wout, z=made.z, zh=made.zh, s=made.s, conv=made.conv,
            uhat=made.uhat, kern=made.kern, nt=made.nt, yt=made.yt, pre=made.pre,
            gb=branch_grad, small=small,
            dup=up_step.reshape(chips, 2, -1, up_step.shape[1]),
            ddown=down_step.reshape(chips, 2, -1, width),
        ),
    )
    steps = update(
        [
            (proj_sum, proj_weights, proj_moment, proj_average, 0.0001, 0, 1),
            (down_sum, down_weights, down_moment, down_average, 0.0001, 0, 0),
            (rest, vectors, vector_moment, vector_average, 0.001, 0, None),
            (net_sum, filter_net.T, net_moment.T, net_average.T, 0.0001, 0, None),
            (rest, filter_out, final_moment, final_average, 2e-06, FINAL_ROW, None),
        ]
    )
    steps[3] = [array.T for array in steps[3]]
    return (
        block_output.reshape(block_input.shape),
        input_grad.reshape(block_input.shape),
        *steps[0], *steps[1], *steps[2], *steps[3], *steps[4],
    )


def on_device_plain(
    block_input,
    out_grad,
    lengths,
    decay_rates,
    proj_weights,
    proj_moment,
    proj_average,
    down_weights,
    down_moment,
    down_average,
    vectors,
    vector_moment,
    vector_average,
    filter_net,
    net_moment,
    net_average,
    filter_out,
    final_moment,
    final_average,
):
    micro = block_input.shape[0]
    count = block_input.shape[2]
    width = block_input.shape[3]
    groups = lax.axis_size("pos")
    slot_length = count * groups
    tokens_all = micro * count
    group = lax.axis_index("pos")
    tap = vectors[13:22].reshape(3, 3 * width)
    short_bias = vectors[22:25].reshape(-1)
    in_bias = vectors[4:7].reshape(-1)
    up_bias = vectors[8:12].reshape(-1)
    skip = vectors[25]

    low_rows = proj_weights.astype(bf16)
    in_weight = lax.all_gather(low_rows[:, : 3 * width], "seq", axis=0, tiled=True)
    out_weight = lax.all_gather(low_rows[:, 3 * width : 4 * width], "seq", axis=0, tiled=True)
    up_weight = lax.all_gather(low_rows[:, 4 * width :], "seq", axis=0, tiled=True)
    down_weight = lax.all_gather(down_weights.astype(bf16), "seq", axis=0, tiled=True)

    table = jnp.asarray(transform_table(count))
    table_low = table.astype(bf16)
    every = jnp.arange(slot_length, dtype=jnp.int32)

    def make_filter(net_values, final_values):
        return filter_fn(net_values, final_values, decay_rates, every, slot_length)

    filters, filter_back = jax.vjp(make_filter, filter_net, filter_out)
    pieces = filters.reshape(groups, count, width)
    spectra = [
        jnp.dot(table, pieces[d], precision=lax.Precision.HIGH, preferred_element_type=f32)
        for d in range(groups)
    ]
    kernels = [spectra[0]] + [spectra[d] + turned(spectra[d - 1], 1.0) for d in range(1, groups)]

    def transform(values):
        return jnp.stack([dot(table_low, values[m]) for m in range(micro)])

    def transform_back(spectrum):
        low = spectrum.astype(bf16)
        return jnp.stack([dot_tn(table_low, low[m]) for m in range(micro)]) * (1.0 / count)

    tokens_low = block_input[:, 0]
    before = passed_along(tokens_low[:, -2:], "pos", 1)
    tokens = tokens_low.astype(f32).reshape(tokens_all, width)
    xh_one, scale_one = norm_parts(tokens)
    normed = (xh_one * vectors[0] + vectors[1]).astype(bf16)
    xh_before, _ = norm_parts(before.astype(f32).reshape(micro * 2, width))
    normed_before = (xh_before * vectors[0] + vectors[1]).astype(bf16)
    z = (dot(normed, in_weight) + in_bias).reshape(micro, count, 3 * width)
    z_before = (dot(normed_before, in_weight) + in_bias).reshape(micro, 2, 3 * width)
    z_before = jnp.where(group > 0, z_before, 0.0)
    z_long = jnp.concatenate([z_before, z], axis=1)
    short = (
        tap[0] * z_long[:, 2:] + tap[1] * z_long[:, 1:-1] + tap[2] * z_long[:, :-2] + short_bias
    ).astype(bf16)
    x0 = short[:, :, :width].astype(f32)
    x1 = short[:, :, width : 2 * width].astype(f32)
    v = short[:, :, 2 * width :].astype(f32)

    u = x1 * v
    u_low = u.astype(bf16)
    u_hat = [transform(u_low)]
    for d in range(1, groups):
        u_hat.append(transform(passed_along(u_low, "pos", d)))
    total = product(kernels[0], u_hat[0])
    for d in range(1, groups):
        total = total + product(kernels[d], u_hat[d])
    conv = transform_back(total) + skip * u
    here = group * count + jnp.arange(count, dtype=jnp.int32)
    mask = (here[None, :] < lengths[:, 0][:, None]).astype(f32)[:, :, None]
    y = (mask * x0 * conv).astype(bf16).reshape(tokens_all, width)
    residual = tokens + dot(y, out_weight) + vectors[7]
    xh_two, scale_two = norm_parts(residual)
    normed_two = (xh_two * vectors[2] + vectors[3]).astype(bf16)

    cot_low = out_grad[:, 0].reshape(tokens_all, width)
    cot = cot_low.astype(f32)
    pre = dot(normed_two, up_weight) + up_bias
    hidden, gelu_back = jax.vjp(jax.nn.gelu, pre)
    hidden_low = hidden.astype(bf16)
    block_output = (residual + dot(hidden_low, down_weight) + vectors[12]).astype(bf16)
    pre_grad = gelu_back(dot_nt(cot_low, down_weight))[0].astype(bf16)
    down_step = dot_tn(hidden_low, cot_low)
    up_step = dot_tn(normed_two, pre_grad)
    normed_two_grad = dot_nt(pre_grad, up_weight)
    part, gain_two, shift_two = norm_back(normed_two_grad, xh_two, scale_two, vectors[2])
    residual_grad = cot + part
    branch_low = residual_grad.astype(bf16)
    out_step = dot_tn(y, branch_low)
    y_grad = dot_nt(branch_low, out_weight).astype(bf16).astype(f32).reshape(micro, count, width)

    gw = mask * y_grad
    gx0 = gw * conv
    gc = gw * x0
    gc_low = gc.astype(bf16)
    skip_grad = jnp.sum(gc * u, axis=(0, 1))
    gc_hat = [transform(gc_low)]
    for d in range(1, groups):
        gc_hat.append(transform(passed_along(gc_low, "pos", -d)))
    back = product_conj(kernels[0], gc_hat[0])
    for d in range(1, groups):
        back = back + product_conj(kernels[d], gc_hat[d])
    gu = transform_back(back) + skip * gc
    kernel_grads = [jnp.sum(product_conj(u_hat[d], gc_hat[0]), axis=0) for d in range(groups)]
    filter_grads = []
    for d in range(groups):
        got = kernel_grads[d]
        if d + 1 < groups:
            got = got + turned(kernel_grads[d + 1], -1.0)
        filter_grads.append(dot_tn(table_low, got.astype(bf16)) * (1.0 / count))
    net_local, final_local = filter_back(jnp.concatenate(filter_grads, axis=0))
    short_grad = jnp.concatenate([gx0, gu * v, gu * x1], axis=-1).astype(bf16)
    after = passed_along(short_grad[:, :2], "pos", -1)
    short_long = jnp.concatenate([short_grad, after], axis=1).astype(f32)
    z_grad = (
        tap[0] * short_long[:, :-2] + tap[1] * short_long[:, 1:-1] + tap[2] * short_long[:, 2:]
    ).astype(bf16)
    here_grad = short_long[:, :-2]
    tap_grads = [
        jnp.sum(here_grad * z_long[:, 2 - k : 2 - k + count], axis=(0, 1)) for k in range(3)
    ]
    short_bias_grad = jnp.sum(here_grad, axis=(0, 1))
    z_grad = z_grad.reshape(tokens_all, 3 * width)
    in_step = dot_tn(normed, z_grad)
    in_bias_grad = jnp.sum(z_grad.astype(f32), axis=0)
    normed_grad = dot_nt(z_grad, in_weight)
    part, gain_one, shift_one = norm_back(normed_grad, xh_one, scale_one, vectors[0])
    input_grad = (residual_grad + part).astype(bf16)

    vector_local = jnp.concatenate(
        [
            gain_one[None],
            shift_one[None],
            gain_two[None],
            shift_two[None],
            in_bias_grad.reshape(3, width),
            jnp.sum(branch_low.astype(f32), axis=0)[None],
            jnp.sum(pre_grad.astype(f32), axis=0).reshape(4, width),
            jnp.sum(cot, axis=0)[None],
            jnp.stack(tap_grads).reshape(9, width),
            short_bias_grad.reshape(3, width),
            skip_grad[None],
        ],
        axis=0,
    )
    proj_local = jnp.concatenate([in_step, out_step, up_step], axis=1).astype(bf16)
    proj_shard = lax.psum_scatter(proj_local, "seq", scatter_dimension=0, tiled=True)
    down_shard = lax.psum_scatter(down_step.astype(bf16), "seq", scatter_dimension=0, tiled=True)
    proj_sum = lax.psum(proj_shard, "pos").astype(f32)
    down_sum = lax.psum(down_shard, "pos").astype(f32)
    vector_sum, net_sum, final_sum = lax.psum(
        (vector_local, net_local, final_local), ("seq", "pos")
    )
    return (
        block_output.reshape(micro, 1, count, width),
        input_grad.reshape(micro, 1, count, width),
        *nesterov(proj_weights, proj_moment, proj_average, proj_sum, 0.0001),
        *nesterov(down_weights, down_moment, down_average, down_sum, 0.0001),
        *nesterov(vectors, vector_moment, vector_average, vector_sum, 0.001),
        *nesterov(filter_net, net_moment, net_average, net_sum, 0.0001),
        *nesterov(filter_out, final_moment, final_average, final_sum, 2e-06),
    )


def on_device(*arrays):
    tuned = fits(
        lax.axis_size("seq"), lax.axis_size("pos"), arrays[0], arrays[4], arrays[7]
    )
    return (on_device_tuned if tuned else on_device_plain)(*arrays)


def solution(mesh):
    tokens = P(None, "seq", "pos", None)
    rows = P("seq", None)
    whole = P()
    return jax.shard_map(
        on_device,
        mesh=mesh,
        in_specs=(tokens, tokens, P(None, "seq"), whole) + (rows,) * 6 + (whole,) * 9,
        out_specs=(tokens, tokens) + (rows,) * 8 + (whole,) * 12,
        check_vma=False,
    )
```

```python
import functools
import math
import types

import jax
import jax.numpy as jnp
import numpy as np
from jax import lax
from jax.experimental import pallas as pl
from jax.experimental.pallas import tpu as pltpu
from jax.sharding import PartitionSpec as P

HID = 64
EMB = 33

highest = lax.Precision.HIGHEST
f32 = jnp.float32
bf16 = jnp.bfloat16


def passed_along(block, axis, distance):
    devices = range(lax.axis_size(axis))
    route = [(i - distance, i) for i in devices if i - distance in devices]
    return lax.ppermute(block, axis, route)


def dot(a, b):
    return lax.dot_general(a, b, (((1,), (0,)), ((), ())), preferred_element_type=f32)


def dot_tn(a, b):
    return lax.dot_general(a, b, (((0,), (0,)), ((), ())), preferred_element_type=f32)


def dot_nt(a, b):
    return lax.dot_general(a, b, (((1,), (1,)), ((), ())), preferred_element_type=f32)


def features(positions, slot_length):
    band_count = (EMB - 1) // 2
    scaled = positions.astype(f32) / slot_length
    bands = 0.0001 + jnp.arange(band_count, dtype=f32) * (
        (band_count - 1 - 0.0001) / (band_count - 1)
    )
    angles = 2.0 * math.pi * scaled[:, None] * bands[None, :]
    return jnp.concatenate([scaled[:, None], jnp.cos(angles), -jnp.sin(angles)], axis=1)


def filter_fn(net_values, final_values, rates, positions, slot_length):
    embedded = features(positions, slot_length)
    frequency = net_values[EMB + 3 + 2 * HID]
    layer_one = jnp.sin(
        frequency * (jnp.dot(embedded, net_values[:EMB], precision=highest) + net_values[EMB])
    )
    layer_two = jnp.sin(
        frequency
        * (
            jnp.dot(layer_one, net_values[EMB + 1 : EMB + 1 + HID], precision=highest)
            + net_values[EMB + 1 + HID]
        )
    )
    layer_three = jnp.sin(
        frequency
        * (
            jnp.dot(layer_two, net_values[EMB + 2 + HID : EMB + 2 + 2 * HID], precision=highest)
            + net_values[EMB + 2 + 2 * HID]
        )
    )
    shaped = jnp.dot(layer_three, final_values, precision=highest)
    scaled = positions.astype(f32) / slot_length
    window = jnp.exp(-scaled[:, None] * rates[None, :]) + 0.05
    return shaped * window


def transform_table(length):
    product = np.outer(2 * np.arange(length) + 1, np.arange(length)) % (4 * length)
    angle = product.astype(np.float64) * (math.pi / (2 * length))
    return np.concatenate([np.cos(angle), -np.sin(angle)], axis=0).astype(np.float32)


def feature_table(slot_length):
    scaled = np.arange(slot_length, dtype=np.float32) / np.float32(slot_length)
    band_count = (EMB - 1) // 2
    bands = np.float32(0.0001) + np.arange(band_count, dtype=np.float32) * np.float32(
        (band_count - 1 - 0.0001) / (band_count - 1)
    )
    angles = (np.float32(2.0 * math.pi) * scaled[:, None]) * bands[None, :]
    table = np.zeros((slot_length, 4 * HID), np.float32)
    table[:, 0] = scaled
    table[:, 1 : 1 + band_count] = np.cos(angles)
    table[:, 1 + band_count : EMB] = -np.sin(angles)
    table[:, EMB] = 1.0
    return table


def halves(spectrum):
    half = spectrum.shape[-2] // 2
    return spectrum[..., :half, :], spectrum[..., half:, :]


def turned(spectrum, sign):
    re, im = halves(spectrum)
    parity = (1.0 - 2.0 * (jnp.arange(re.shape[-2]) % 2).astype(f32))[:, None] * sign
    return jnp.concatenate([-parity * im, parity * re], axis=-2)


def product(kernel, signal):
    kr, ki = halves(kernel)
    sr, si = halves(signal)
    return jnp.concatenate([kr * sr - ki * si, kr * si + ki * sr], axis=-2)


def product_conj(kernel, signal):
    kr, ki = halves(kernel)
    sr, si = halves(signal)
    return jnp.concatenate([kr * sr + ki * si, kr * si - ki * sr], axis=-2)


def nesterov(weight, moment, average, gradient, rate):
    moment_next = 0.9 * moment + gradient
    weight_next = weight - rate * (gradient + 0.9 * moment_next)
    average_next = 0.9 * average + 0.1 * weight_next
    return (gradient, weight_next, moment_next, average_next)


def norm_parts(values):
    center = jnp.mean(values, axis=-1, keepdims=True)
    centred = values - center
    variance = jnp.mean(centred * centred, axis=-1, keepdims=True)
    scale = lax.rsqrt(variance + 1e-05)
    return centred * scale, scale


def norm_back(grad, xh, scale, gain):
    q = grad * gain
    return (
        (q - jnp.mean(q, -1, keepdims=True) - xh * jnp.mean(q * xh, -1, keepdims=True)) * scale,
        jnp.sum(grad * xh, axis=0),
        jnp.sum(grad, axis=0),
    )


MESH = pl.DeviceIdType.MESH


class Ring:
    def __init__(self, size):
        self.size = size
        self.count = size // 2
        self.seq = lax.axis_index("seq")
        self.pos = lax.axis_index("pos")
        self.core = lax.rem(self.seq, 2)
        chip = self.seq // 2
        odd = lax.rem(chip, 2)
        self.place = (1 - odd) * (chip // 2) + odd * (self.count - 1 - chip // 2)

    def chip(self, shift):
        place = lax.rem(self.place + (shift + self.count), self.count)
        low = jnp.where(place < self.count // 2, 1, 0)
        return low * (2 * place) + (1 - low) * (2 * (self.count - 1 - place) + 1)

    def device(self, shift):
        return {"seq": 2 * self.chip(shift) + self.core}

    @property
    def sibling(self):
        return {"seq": self.seq + 1 - 2 * self.core}

    @property
    def across(self):
        return {"pos": 1 - self.pos}


def greet_all(ring):
    barrier = pltpu.get_barrier_semaphore()
    for step in range(1, ring.size):
        other = lax.rem(ring.seq + step, ring.size)
        pl.semaphore_signal(barrier, inc=1, device_id={"seq": other}, device_id_type=MESH)
    pl.semaphore_signal(barrier, inc=1, device_id=ring.across, device_id_type=MESH)
    pl.semaphore_wait(barrier, ring.size)


def remote(src, dst, send, recv, device):
    return pltpu.make_async_remote_copy(
        src_ref=src, dst_ref=dst, send_sem=send, recv_sem=recv, device_id=device,
        device_id_type=MESH,
    )


class Reduction:
    def __init__(
        self, ring, turn, grad, twin, up, down, own, other, sems, stage=None, stage_sems=None
    ):
        self.ring, self.turn = ring, turn
        self.grad, self.twin, self.up, self.down = grad, twin, up, down
        self.own, self.other = own, other
        self.sems = sems
        self.stage, self.stage_sems = stage, stage_sems
        self.ups = ring.count // 2
        self.downs = (ring.count - 1) // 2

    def chip(self, shift):
        return self.ring.chip(shift * self.turn)

    def copies(self):
        ring = self.ring
        made = [(self.grad.at[:, 1 - ring.core], self.twin, ring.sibling)]
        for step in range(self.ups):
            block = self.twin.at[self.chip(self.ups - step)]
            made.append((block, self.up.at[step], ring.device(self.turn)))
        for step in range(self.downs):
            block = self.twin.at[self.chip(step - self.downs)]
            made.append((block, self.down.at[step], ring.device(-self.turn)))
        made.append((self.own, self.other, ring.across))
        return made

    def copy(self, index):
        src, dst, device = self.copies()[index]
        return remote(src, dst, self.sems.at[0, index], self.sems.at[1, index], device)

    def begin(self):
        self.copy(0).start()

    def fetch(self, chip, slot):
        return pltpu.make_async_copy(
            self.grad.at[chip, self.ring.core], self.stage.at[slot], self.stage_sems.at[slot]
        )

    def merge(self):
        core = self.ring.core
        count = self.ring.count
        if self.stage is None:
            self.copy(0).wait_recv()

            @pl.loop(0, count)
            def _(chip):
                self.twin[chip] = self.twin[chip] + self.grad[chip, core]

        else:
            self.fetch(0, 0).start()
            self.copy(0).wait_recv()

            @pl.loop(0, count)
            def _(chip):
                slot = lax.rem(chip, 2)

                @pl.when(chip + 1 < count)
                def _():
                    self.fetch(chip + 1, 1 - slot).start()

                self.fetch(chip, slot).wait()
                self.twin[chip] = self.twin[chip] + self.stage[slot]

        self.copy(1).start()
        self.copy(1 + self.ups).start()

    def advance(self, step):
        self.copy(step).wait_recv()
        owner = self.chip(self.ups - step)
        self.twin[owner] = self.twin[owner] + self.up[step - 1]
        self.copy(1 + step).start()
        if step < self.downs:
            self.copy(self.ups + step).wait_recv()
            owner = self.chip(step - self.downs)
            self.twin[owner] = self.twin[owner] + self.down[step - 1]
            self.copy(1 + self.ups + step).start()

    def collect(self):
        self.copy(self.ups).wait_recv()
        self.copy(self.ups + self.downs).wait_recv()
        mine = self.chip(0)
        total = (
            self.twin[mine].astype(f32)
            + self.up[self.ups - 1].astype(f32)
            + self.down[self.downs - 1].astype(f32)
        )
        self.own[...] = total.astype(bf16)
        self.copy(1 + self.ups + self.downs).start()

    def result(self):
        self.copy(1 + self.ups + self.downs).wait_recv()
        return self.own[...].astype(f32) + self.other[...].astype(f32)

    def finish(self):
        for index in range(2 + self.ups + self.downs):
            self.copy(index).wait_send()


class SmallSum:
    def __init__(self, ring, values, parts, mine, other, sums, sems):
        self.ring, self.values, self.parts = ring, values, parts
        self.mine, self.other, self.sums = mine, other, sums
        self.sems = sems
        self.rows = parts.shape[1]
        self.waiting = []

    def block(self, index):
        return pl.ds(pl.multiple_of(index * self.rows, 8), self.rows)

    def begin(self):
        ring = self.ring
        self.arriving = []
        for step in range(1, ring.size):
            other = lax.rem(ring.seq + step, ring.size)
            copy = remote(
                self.values.at[self.block(other)], self.parts.at[step],
                self.sems.at[0, step], self.sems.at[1, step], {"seq": other},
            )
            copy.start()
            self.arriving.append(copy)
            self.waiting.append(copy)

    def add_up(self):
        for copy in self.arriving:
            copy.wait_recv()
        total = self.values[self.block(self.ring.seq)]
        for step in range(1, self.ring.size):
            total = total + self.parts[step]
        self.mine[...] = total
        self.crossing = remote(
            self.mine, self.other, self.sems.at[0, 0], self.sems.at[1, 0], self.ring.across
        )
        self.crossing.start()
        self.waiting.append(self.crossing)

    def spread(self):
        self.crossing.wait_recv()
        block = self.block(self.ring.seq)
        self.sums[block] = self.mine[...] + self.other[...]
        self.arriving = []
        for step in range(1, self.ring.size):
            other = lax.rem(self.ring.seq + step, self.ring.size)
            copy = remote(
                self.sums.at[block], self.sums.at[block],
                self.sems.at[2, step], self.sems.at[3, step], {"seq": other},
            )
            copy.start()
            self.waiting.append(copy)
            back = lax.rem(self.ring.seq + (self.ring.size - step), self.ring.size)
            self.arriving.append(
                remote(
                    self.sums.at[self.block(back)], self.sums.at[self.block(back)],
                    self.sems.at[2, step], self.sems.at[3, step], {"seq": other},
                )
            )

    def finish(self):
        for copy in self.arriving:
            copy.wait_recv()
        for copy in self.waiting:
            copy.wait_send()


def reduction_scratch(size, rows, columns):
    chips = size // 2
    ups, downs = chips // 2, (chips - 1) // 2
    return [
        pltpu.VMEM((chips, rows, columns), bf16),
        pltpu.VMEM((ups, rows, columns), bf16),
        pltpu.VMEM((downs, rows, columns), bf16),
        pltpu.VMEM((rows, columns), bf16),
        pltpu.VMEM((rows, columns), bf16),
        pltpu.SemaphoreType.DMA((2, 2 + ups + downs)),
    ]


def small_scratch(size, rows, columns):
    return [
        pltpu.VMEM((size, rows // size, columns), f32),
        pltpu.VMEM((rows // size, columns), f32),
        pltpu.VMEM((rows // size, columns), f32),
        pltpu.SemaphoreType.DMA((4, size)),
    ]


class Gather:
    def __init__(self, ring, turn, mine, full, sems):
        self.ring, self.turn = ring, turn
        self.mine, self.full, self.sems = mine, full, sems
        self.ups = ring.count // 2
        self.downs = (ring.count - 1) // 2
        self.waiting, self.arriving = [], []

    def send(self, src, place, index, device):
        copy = remote(
            src, self.full.at[self.ring.chip(place * self.turn), self.ring.core],
            self.sems.at[0, index], self.sems.at[1, index], device,
        )
        copy.start()
        self.waiting.append(copy)
        return copy

    def share(self, src, place, index):
        index = self.ups + self.downs + index
        self.send(src, place, index, self.ring.sibling)
        block = self.full.at[self.ring.chip(place * self.turn), 1 - self.ring.core]
        self.arriving.append(
            remote(block, block, self.sems.at[0, index], self.sems.at[1, index], self.ring.sibling)
        )

    def wait_block(self, place, index, device):
        block = self.full.at[self.ring.chip(place * self.turn), self.ring.core]
        remote(block, block, self.sems.at[0, index], self.sems.at[1, index], device).wait_recv()
        return block

    def begin(self):
        ring = self.ring
        self.send(self.mine, 0, 0, ring.device(self.turn))
        self.send(self.mine, 0, self.ups, ring.device(-self.turn))
        self.share(self.mine, 0, 0)
        self.local = pltpu.make_async_copy(
            self.mine, self.full.at[ring.chip(0), ring.core], self.sems.at[2, 0]
        )
        self.local.start()

    def advance(self, step):
        ring = self.ring
        block = self.wait_block(-step, step - 1, ring.device(self.turn))
        if step < self.ups:
            self.send(block, -step, step, ring.device(self.turn))
        self.share(block, -step, step)
        if step <= self.downs:
            block = self.wait_block(step, self.ups + step - 1, ring.device(-self.turn))
            if step < self.downs:
                self.send(block, step, self.ups + step, ring.device(-self.turn))
            self.share(block, step, self.ups + step)

    def arrive(self):
        self.local.wait()
        for copy in self.arriving:
            copy.wait_recv()

    def finish(self):
        for copy in self.waiting:
            copy.wait_send()


def gather_sems(size):
    chips = size // 2
    return pltpu.SemaphoreType.DMA((3, 2 * chips))


PI_PARTS = (3.140625, 9.676535897932384e-4)


def sin_cos(x):
    turns = jnp.floor(x * (1.0 / math.pi) + 0.5)
    rest = (x - turns * PI_PARTS[0]) - turns * PI_PARTS[1]
    half = turns * 0.5
    sign = 1.0 - 4.0 * (half - jnp.floor(half))
    square = rest * rest
    odd = 1.0 / 6227020800.0
    for factor in (-1.0 / 39916800.0, 1.0 / 362880.0, -1.0 / 5040.0, 1.0 / 120.0, -1.0 / 6.0):
        odd = odd * square + factor
    even = 1.0 / 479001600.0
    for factor in (-1.0 / 3628800.0, 1.0 / 40320.0, -1.0 / 720.0, 1.0 / 24.0, -0.5):
        even = even * square + factor
    signed = sign * rest
    return signed + signed * square * odd, sign + sign * square * even


def norm_rows(values):
    center = jnp.mean(values, axis=1, keepdims=True)
    centred = values - center
    variance = jnp.mean(centred * centred, axis=1, keepdims=True)
    return centred * lax.rsqrt(variance + 1e-05)


TILE = 256


class Copies:
    def __init__(self, sems):
        self.sems, self.used, self.open = sems, 0, []

    def start(self, src, dst):
        copy = pltpu.make_async_copy(src, dst, self.sems.at[self.used])
        self.used += 1
        copy.start()
        return copy

    def out(self, src, dst):
        copy = self.start(src, dst)
        self.open.append(copy)
        return copy

    def settle(self, copy):
        copy.wait()
        self.open = [other for other in self.open if other is not copy]

    def finish(self):
        for copy in self.open:
            copy.wait()


def valid_rows(length, first, rows, columns):
    at = lax.broadcasted_iota(jnp.int32, (rows, columns), 0) + first
    return jnp.where(at < length, 1.0, 0.0).astype(f32)


def blocks(rows, step):
    return [slice(at, at + step) for at in range(0, rows, step)]


def folded(values):
    return jnp.sum(values.reshape(-1, 8, values.shape[1]), axis=0)


def front_kernel(size, names, *refs):
    ref = types.SimpleNamespace(**dict(zip(names, refs)))
    x, vec, net = ref.x_in, ref.vec, ref.net_in
    micro, count, width = x.shape
    slot = 2 * count
    tiles = width // TILE
    ring = Ring(size)
    copies = Copies(ref.copy_sems)
    proj_copy = copies.start(ref.proj, ref.proj_in)
    x_copy = copies.start(ref.x, x)
    down_copy = copies.start(ref.down, ref.down_in)
    feature_copy = copies.start(ref.feature, ref.feature_in)
    table_copy = copies.start(ref.table, ref.table_in)
    back_copy = copies.start(ref.back, ref.back_in)
    table, table_back = ref.table_in, ref.back_in
    inside = jnp.where(ring.pos > 0, 1.0, 0.0).astype(f32)

    proj_copy.wait()
    own = ref.in_own
    for j in range(tiles):
        for p in range(3):
            first = p * width + j * TILE
            own[j, :, p * TILE : (p + 1) * TILE] = ref.proj_in[:, first : first + TILE].astype(bf16)
    greet_all(ring)
    gather = [Gather(ring, 1 - 2 * (j % 2), own.at[j], ref.win_in.at[j], ref.win_sem.at[j]) for j in range(tiles)]
    gather_out = Gather(ring, -1, ref.out_own, ref.wout_in, ref.wout_sem)
    gather_up = Gather(ring, 1, ref.up_own, ref.wup, ref.wup_sem)
    gather_down = Gather(ring, -1, ref.down_own, ref.wdown, ref.wdown_sem)
    gather[0].begin()
    gather[1].begin()
    x_copy.wait()
    edge = remote(
        x.at[:, pl.ds(count - 16, 16)], ref.halo, ref.halo_sem.at[0],
        ref.halo_sem.at[1], ring.across,
    )
    edge.start()

    gain, shift = vec[0:1], vec[1:2]
    normed_ref, turned_ref = ref.n_in, ref.nt_in

    def first_norm(m):
        for rows in blocks(count, 16):
            normed_ref[m, rows] = (norm_rows(x[m, rows].astype(f32)) * gain + shift).astype(bf16)
        for rows in blocks(count, TILE):
            turned_ref[m, :, rows] = normed_ref[m, rows].T

    first_norm(0)
    gather[0].advance(1)
    gather[1].advance(1)
    gather[2].begin()
    for m in range(1, micro):
        first_norm(m)
    copies.out(turned_ref, ref.nt)
    ref.out_own[...] = ref.proj_in[:, 3 * width : 4 * width].astype(bf16)
    gather[0].advance(2)
    gather[1].advance(2)
    edge.wait_recv()
    for m in range(micro):
        ref.halo_n[m] = (norm_rows(ref.halo[m].astype(f32)) * gain + shift).astype(bf16)
    feature_copy.wait()

    net[...] = ref.net[...].T
    frequency = net[EMB + 3 + 2 * HID : EMB + 4 + 2 * HID]
    rates = ref.rate[...].reshape(1, width)

    def sines(layer):
        parts = [sin_cos(frequency * layer[part])[0] for part in blocks(TILE, 64)]
        return jnp.concatenate(parts, axis=0)

    def filter_rows(at):
        rows = slice(at * TILE, (at + 1) * TILE)
        layer = jnp.dot(
            ref.feature_in[rows, : net.shape[0]], net[...], precision=highest,
            preferred_element_type=f32,
        )
        ref.pre_in[rows, :HID] = layer
        layer = sines(layer)
        for i, first in ((1, EMB + 1), (2, EMB + 2 + HID)):
            layer = (
                jnp.dot(
                    layer, net[first : first + HID], precision=highest,
                    preferred_element_type=f32,
                )
                + net[first + HID : first + HID + 1]
            )
            ref.pre_in[rows, i * HID : (i + 1) * HID] = layer
            layer = sines(layer)
        shaped = dot(layer.astype(bf16), ref.final[...].astype(bf16))
        for part in blocks(TILE, 16):
            at_row = lax.broadcasted_iota(jnp.int32, (16, width), 0) + (at * TILE + part.start)
            window = jnp.exp(at_row.astype(f32) * (rates * (-1.0 / slot))) + 0.05
            first = at * TILE + part.start
            ref.filt[first : first + 16] = (shaped[part] * window).astype(bf16)

    row_blocks = slot // TILE
    filter_rows(0)
    gather[0].advance(3)
    gather[1].advance(3)
    gather[2].advance(1)
    down_copy.wait()
    ref.up_own[...] = ref.proj_in[:, 4 * width :].astype(bf16)
    ref.down_own[...] = ref.down_in[...].astype(bf16)
    gather[0].advance(4)
    gather[2].advance(2)
    gather_out.begin()
    gather[1].advance(4)
    gather[0].arrive()

    z_in, s_in, ulow, urecv = ref.z_in, ref.s_in, ref.ulow, ref.urecv
    zbuf, spec = ref.zbuf, ref.spec
    crossing, held = [], []

    def project(j):
        weight = ref.win_in[j].reshape(width, 3 * TILE)
        bias = jnp.concatenate(
            [vec[4 + p : 5 + p, j * TILE : (j + 1) * TILE] for p in range(3)], axis=1
        )
        lane = slice(j * TILE, (j + 1) * TILE)
        taps = [[vec[13 + 3 * k + p : 14 + 3 * k + p, lane] for p in range(3)] for k in range(3)]
        constant = [
            (taps[0][p] + taps[1][p] + taps[2][p]) * vec[4 + p : 5 + p, lane]
            + vec[22 + p : 23 + p, lane]
            for p in range(3)
        ]

        @pl.loop(0, micro)
        def _(m):
            zbuf[16:] = dot(normed_ref[m], weight)
            zbuf[:16] = dot(ref.halo_n[m], weight) * inside + bias * (inside - 1.0)
            ref.zh_in[j, m] = (zbuf[:16] + bias).astype(bf16)
            for rows in blocks(count, 32):
                parts = []
                for p in range(3):
                    cols = slice(p * TILE, (p + 1) * TILE)
                    first = rows.start
                    z = zbuf[first + 16 : first + 48, cols]
                    z_in[j, m, rows, cols] = (z + bias[:, cols]).astype(bf16)
                    short = (
                        taps[0][p] * z
                        + taps[1][p] * zbuf[first + 15 : first + 47, cols]
                        + taps[2][p] * zbuf[first + 14 : first + 46, cols]
                        + constant[p]
                    ).astype(bf16)
                    s_in[j, m, rows, cols] = short
                    parts.append(short.astype(f32))
                ulow[j, m, rows] = (parts[1] * parts[2]).astype(bf16)

        copy = remote(
            ulow.at[j], urecv.at[j], ref.u_sem.at[0, j], ref.u_sem.at[1, j], ring.across
        )
        copy.start()
        crossing.append(copy)
        held.append(copies.out(z_in.at[j], ref.z.at[j]))
        held.append(copies.out(s_in.at[j], ref.s.at[j]))

    project(0)
    gather[2].advance(3)
    gather_up.begin()
    gather[1].arrive()
    project(1)
    gather[2].advance(4)
    gather_down.begin()
    gather_out.advance(1)
    gather[2].arrive()
    project(2)
    copies.out(ref.zh_in, ref.zh)
    held.append(copies.out(ref.win_in, ref.win))
    gather_out.advance(2)
    for at in range(1, row_blocks):
        filter_rows(at)
        if at == 2:
            gather_up.advance(1)
            gather_out.advance(3)
    copies.out(ref.pre_in, ref.pre)
    gather_down.advance(1)
    gather_out.advance(4)
    gather_out.arrive()
    copies.out(ref.wout_in, ref.wout)
    table_copy.wait()
    back_copy.wait()

    parity = 1.0 - 2.0 * (lax.broadcasted_iota(jnp.int32, (16, TILE), 0) % 2).astype(f32)
    kern, uhat = ref.kern_in, ref.uhat_in
    one, two = ref.one, ref.two

    @pl.loop(0, tiles)
    def _(j):
        cols = pl.ds(pl.multiple_of(j * TILE, TILE), TILE)
        one[...] = dot(table[...], ref.filt[:count, cols])
        two[...] = dot(table[...], ref.filt[count:, cols])
        for re in blocks(count, 16):
            im = slice(re.start + count, re.stop + count)
            kern[j, 0, re] = one[re].astype(bf16)
            kern[j, 0, im] = one[im].astype(bf16)
            kern[j, 1, re] = (two[re] - parity * one[im]).astype(bf16)
            kern[j, 1, im] = (two[im] + parity * one[re]).astype(bf16)
        for m in range(micro):
            uhat[j, m, 0] = dot(table[...], ulow[j, m]).astype(bf16)

    copies.out(kern, ref.kern)
    gather_up.advance(2)

    def mix(j):
        crossing[j].wait_recv()
        lane = slice(j * TILE, (j + 1) * TILE)

        @pl.loop(0, micro)
        def _(m):
            one[...] = dot(table[...], urecv[j, m])
            for re in blocks(count, 16):
                im = slice(re.start + count, re.stop + count)
                k0r, k0i = kern[j, 0, re].astype(f32), kern[j, 0, im].astype(f32)
                k1r, k1i = kern[j, 1, re].astype(f32), kern[j, 1, im].astype(f32)
                ur, ui = uhat[j, m, 0, re].astype(f32), uhat[j, m, 0, im].astype(f32)
                vr, vi = one[re] * inside, one[im] * inside
                uhat[j, m, 1, re] = vr.astype(bf16)
                uhat[j, m, 1, im] = vi.astype(bf16)
                spec[re] = (k0r * ur - k0i * ui + k1r * vr - k1i * vi).astype(bf16)
                spec[im] = (k0r * ui + k0i * ur + k1r * vi + k1i * vr).astype(bf16)
            two[:count] = dot(table_back[...], spec[...])
            length = ref.lens[0, m] - ring.pos * count
            for rows in blocks(count, 32):
                gated = s_in[j, m, rows, TILE : 2 * TILE].astype(f32) * s_in[
                    j, m, rows, 2 * TILE :
                ].astype(f32)
                conv = two[rows] * (1.0 / count) + vec[25:26, lane] * gated
                ref.conv_in[j, m, rows] = conv.astype(bf16)
                mask = valid_rows(length, rows.start, 32, TILE)
                ref.y_in[m, rows, lane] = (
                    mask * s_in[j, m, rows, :TILE].astype(f32) * conv
                ).astype(bf16)

        copies.out(ref.conv_in.at[j], ref.conv.at[j])
        copies.out(uhat.at[j], ref.uhat.at[j])

    for j in range(tiles):
        mix(j)
        if j == 0:
            gather_down.advance(2)
        if j == 1:
            gather_up.advance(3)

    for m in range(micro):
        ref.res_in[m] = dot(ref.y_in[m], ref.wout_in[...].reshape(width, width))
        for rows in blocks(count, TILE):
            ref.yt_in[m, :, rows] = ref.y_in[m, rows].T
        for rows in blocks(count, 16):
            residual = x[m, rows].astype(f32) + ref.res_in[m, rows] + vec[7:8]
            ref.res_in[m, rows] = residual
            ref.n2_in[m, rows] = (norm_rows(residual) * vec[2:3] + vec[3:4]).astype(bf16)
        for rows in blocks(count, TILE):
            ref.n2t_in[m, :, rows] = ref.n2_in[m, rows].T
        for src, dst in (
            (ref.yt_in, ref.yt), (ref.res_in, ref.res), (ref.n2_in, ref.n2), (ref.n2t_in, ref.n2t)
        ):
            copies.out(src.at[m], dst.at[m])
        if m == 0:
            gather_up.advance(4)
    gather_up.arrive()

    for copy in held:
        copies.settle(copy)
    for work in gather:
        work.finish()
    chunks = ref.hid.shape[0]

    def chunk_load(c):
        cols = pl.ds(c * width, width)
        return copies.start(ref.wup.at[:, :, :, cols], ref.win_in.at[c % 3])

    loading = [chunk_load(0)]
    leaving = []
    for c in range(chunks):
        if c + 1 < chunks:
            loading.append(chunk_load(c + 1))
        loading[c].wait()
        if c >= 2:
            for copy in leaving[c - 2]:
                copies.settle(copy)
        stage = z_in if c % 2 == 0 else s_in
        weight = ref.win_in[c % 3].reshape(width, width)
        bias = vec[8 + c : 9 + c]

        @pl.loop(0, micro)
        def _(m):
            zbuf[:count] = dot(ref.n2_in[m], weight)
            for first in range(0, width, TILE):
                cols = slice(first, first + TILE)
                for rows in blocks(count, 32):
                    hidden, slope = gelu_pair(zbuf[rows, cols] + bias[:, cols])
                    stage[0, m, rows, cols] = hidden.astype(bf16)
                    stage[1, m, rows, cols] = slope.astype(bf16)

        leaving.append(
            [copies.out(stage.at[0], ref.hid.at[c]), copies.out(stage.at[1], ref.slope.at[c])]
        )
        if c == 0:
            gather_down.advance(3)
        if c == 2:
            gather_down.advance(4)
    gather_down.arrive()
    for work in (gather_out, gather_up, gather_down):
        work.finish()
    edge.wait_send()
    for copy in crossing:
        copy.wait_send()
    copies.finish()


def front(size, arrays):
    chips = size // 2
    micro, count, width = arrays["x"].shape
    rows, down_rows = arrays["proj"].shape[0], arrays["down"].shape[0]
    wide = down_rows * size
    tiles = width // TILE
    vmem = pl.BlockSpec(memory_space=pltpu.VMEM)
    anywhere = pl.BlockSpec(memory_space=pl.ANY)
    smem = pl.BlockSpec(memory_space=pltpu.SMEM)
    near = ("vec", "net", "final", "rate")
    kinds = dict(
        win=((tiles, chips, 2, rows, 3 * TILE), bf16),
        wout=((chips, 2, rows, width), bf16),
        z=((tiles, micro, count, 3 * TILE), bf16),
        zh=((tiles, micro, 16, 3 * TILE), bf16),
        s=((tiles, micro, count, 3 * TILE), bf16),
        conv=((tiles, micro, count, TILE), bf16),
        uhat=((tiles, micro, 2, 2 * count, TILE), bf16),
        kern=((tiles, 2, 2 * count, TILE), bf16),
        res=((micro, count, width), f32),
        nt=((micro, width, count), bf16),
        n2=((micro, count, width), bf16),
        n2t=((micro, width, count), bf16),
        yt=((micro, width, count), bf16),
        pre=((2 * count, 4 * HID), f32),
    )
    outs = dict(
        kinds,
        wup=((chips, 2, rows, wide), bf16),
        wdown=((chips, 2, down_rows, width), bf16),
        hid=((wide // width, micro, count, width), bf16),
        slope=((wide // width, micro, count, width), bf16),
    )
    dma = pltpu.SemaphoreType.DMA
    scratch = {
        name + "_in": pltpu.VMEM(*kind) for name, kind in kinds.items()
    }
    for name, array in arrays.items():
        if name not in near and name != "lens":
            scratch[name + "_in"] = pltpu.VMEM(array.shape, array.dtype)
    scratch.update(
        dict(
            n_in=pltpu.VMEM((micro, count, width), bf16),
            one=pltpu.VMEM((2 * count, TILE), f32),
            two=pltpu.VMEM((2 * count, TILE), f32),
            net_in=pltpu.VMEM((EMB + 4 + 2 * HID, HID), f32),
            y_in=pltpu.VMEM((micro, count, width), bf16),
            in_own=pltpu.VMEM((tiles, rows, 3 * TILE), bf16),
            out_own=pltpu.VMEM((rows, width), bf16),
            up_own=pltpu.VMEM((rows, wide), bf16),
            down_own=pltpu.VMEM((down_rows, width), bf16),
            halo=pltpu.VMEM((micro, 16, width), bf16),
            halo_n=pltpu.VMEM((micro, 16, width), bf16),
            filt=pltpu.VMEM((2 * count, width), bf16),
            zbuf=pltpu.VMEM((16 + count, 3 * TILE), f32),
            ulow=pltpu.VMEM((tiles, micro, count, TILE), bf16),
            urecv=pltpu.VMEM((tiles, micro, count, TILE), bf16),
            spec=pltpu.VMEM((2 * count, TILE), bf16),
            win_sem=dma((tiles, 3, 2 * chips)),
            wout_sem=gather_sems(size),
            wup_sem=gather_sems(size),
            wdown_sem=gather_sems(size),
            halo_sem=dma((2,)),
            u_sem=dma((2, tiles)),
            copy_sems=dma((56,)),
        )
    )
    names = tuple(arrays) + tuple(outs) + tuple(scratch)
    made = pl.pallas_call(
        functools.partial(front_kernel, size, names),
        out_shape=[jax.ShapeDtypeStruct(*kind) for kind in outs.values()],
        in_specs=[
            smem if name == "lens" else vmem if name in near else anywhere for name in arrays
        ],
        out_specs=[anywhere] * len(outs),
        scratch_shapes=list(scratch.values()),
        compiler_params=pltpu.CompilerParams(
            collective_id=0, has_side_effects=True, vmem_limit_bytes=63 * 1024 * 1024
        ),
        name="front",
    )(*arrays.values())
    return dict(zip(outs, made))


GELU_SCALE = math.sqrt(2.0 / math.pi)


def gelu_pair(a):
    square = a * a
    half = 0.5 + 0.5 * jnp.tanh(a * (GELU_SCALE + (GELU_SCALE * 0.044715) * square))
    hidden = a * half
    bend = 2.0 * GELU_SCALE + (2.0 * GELU_SCALE * 0.134145) * square
    return hidden, half + (hidden - hidden * half) * bend


def mlp_kernel(
    hid_ref, slope_ref, n2t_ref, gm_ref, res_ref, vec_ref, wup_ref, wdown_ref,
    out_ref, gb_ref, dup_ref, ddown_ref, small_ref,
    acc_out, acc_gn, ga_ref, grad_ref,
):
    step, last = pl.program_id(0), pl.num_programs(0) - 1
    micro, count, width = gm_ref.shape
    chunk = width
    tile = 256
    wup = wup_ref[...].reshape(width, chunk)
    wdown = wdown_ref[...].reshape(chunk, width)

    @pl.when(step == 0)
    def _():
        acc_out[...] = jnp.zeros_like(acc_out)
        acc_gn[...] = jnp.zeros_like(acc_gn)
        small_ref[...] = jnp.zeros_like(small_ref)

    tile = 256
    bias_sum = jnp.zeros((8, chunk), f32)
    for m in range(micro):
        grad_ref[m] = dot_nt(gm_ref[m], wdown)
    for m in range(micro):
        acc_out[m] += dot(hid_ref[0, m], wdown)
        sums = []
        for first in range(0, chunk, tile):
            cols = slice(first, first + tile)
            part = jnp.zeros((8, tile), f32)
            for rows in blocks(count, 32):
                ga = (grad_ref[m, rows, cols] * slope_ref[0, m, rows, cols].astype(f32)).astype(bf16)
                ga_ref[m, rows, cols] = ga
                part = part + folded(ga.astype(f32))
            sums.append(part)
        bias_sum = bias_sum + jnp.concatenate(sums, axis=1)
        acc_gn[m] += dot_nt(ga_ref[m], wup)
    small_ref[pl.ds(4 + step, 1)] = jnp.sum(bias_sum, axis=0, keepdims=True)
    down_total = dot_tn(hid_ref[0, 0], gm_ref[0])
    up_total = dot(n2t_ref[0], ga_ref[0])
    for m in range(1, micro):
        down_total = down_total + dot_tn(hid_ref[0, m], gm_ref[m])
        up_total = up_total + dot(n2t_ref[m], ga_ref[m])
    ddown_ref[...] = down_total.astype(bf16)
    dup_ref[...] = up_total.astype(bf16)

    @pl.when(step == last)
    def _():
        sums = [jnp.zeros((8, width), f32)] * 4
        for m in range(micro):
            for rows in blocks(count, 16):
                residual = res_ref[m, rows]
                out_ref[m, rows] = (residual + acc_out[m, rows] + vec_ref[12:13]).astype(bf16)
                gx, gain_part, grad = norm_rows_back(acc_gn[m, rows], residual, vec_ref[2:3])
                gm = gm_ref[m, rows].astype(f32)
                low = (gm + gx).astype(bf16)
                gb_ref[m, rows] = low
                parts = (gain_part, grad, low.astype(f32), gm)
                sums = [total + folded(part) for total, part in zip(sums, parts)]
        for k in range(4):
            small_ref[k : k + 1] = jnp.sum(sums[k], axis=0, keepdims=True)


def norm_rows_back(grad, values, gain):
    center = jnp.mean(values, axis=1, keepdims=True)
    centred = values - center
    variance = jnp.mean(centred * centred, axis=1, keepdims=True)
    scale = lax.rsqrt(variance + 1e-05)
    xh = centred * scale
    q = grad * gain
    gx = scale * (
        q - jnp.mean(q, axis=1, keepdims=True) - xh * jnp.mean(q * xh, axis=1, keepdims=True)
    )
    return gx, grad * xh, grad


def mlp(hid, slope, n2t, gm, res, vectors, wup, wdown):
    micro, count, width = gm.shape
    chips, cores, rows, wide = wup.shape
    steps = wide // width
    per = chips // steps

    def whole(array):
        return pl.BlockSpec(array.shape, lambda i: (0,) * array.ndim)

    def shape(dims, kind=bf16):
        return jax.ShapeDtypeStruct(dims, kind)

    tokens = pl.BlockSpec((micro, count, width), lambda i: (0, 0, 0))
    return pl.pallas_call(
        mlp_kernel,
        grid=(steps,),
        in_specs=[
            pl.BlockSpec((1, micro, count, width), lambda i: (i, 0, 0, 0)),
            pl.BlockSpec((1, micro, count, width), lambda i: (i, 0, 0, 0)),
            whole(n2t), whole(gm), whole(res), whole(vectors),
            pl.BlockSpec((chips, cores, rows, width), lambda i: (0, 0, 0, i)),
            pl.BlockSpec((per, cores, wdown.shape[2], width), lambda i: (i, 0, 0, 0)),
        ],
        out_specs=[
            tokens, tokens,
            pl.BlockSpec((width, width), lambda i: (0, i)),
            pl.BlockSpec((width, width), lambda i: (i, 0)),
            pl.BlockSpec((4 + steps, width), lambda i: (0, 0)),
        ],
        out_shape=[
            shape((micro, count, width)),
            shape((micro, count, width)),
            shape((width, wide)),
            shape((wide, width)),
            shape((4 + steps, width), f32),
        ],
        scratch_shapes=[
            pltpu.VMEM((micro, count, width), f32),
            pltpu.VMEM((micro, count, width), f32),
            pltpu.VMEM((micro, count, width), bf16),
            pltpu.VMEM((micro, count, width), f32),
        ],
        compiler_params=pltpu.CompilerParams(vmem_limit_bytes=63 * 1024 * 1024),
        name="mlp",
    )(hid, slope, n2t, gm, res, vectors, wup, wdown)


def update_kernel(rates, firsts, *refs):
    count = len(rates)
    kept_in, kept_out, refs = refs[0], refs[4 * count + 1], refs[1 : 4 * count + 1] + refs[4 * count + 2 :]
    kept_out[...] = kept_in[...]
    ins, outs = refs[: 4 * count], refs[4 * count :]
    for i, (rate, first) in enumerate(zip(rates, firsts)):
        grad_ref, weight_ref, moment_ref, average_ref = ins[4 * i : 4 * i + 4]
        rows, columns = weight_ref.shape
        stepped = nesterov(
            weight_ref[...], moment_ref[...], average_ref[...],
            grad_ref[first : first + rows, :columns], rate,
        )
        for out, value in zip(outs[4 * i : 4 * i + 4], stepped):
            out[...] = value


def update(kept, sets):
    steps = 4
    held = pl.BlockSpec(
        (kept.shape[0], kept.shape[1] // steps, kept.shape[2]), lambda i: (0, i, 0)
    )
    arrays, in_specs, out_specs = [kept], [held], [held]
    shapes = [jax.ShapeDtypeStruct(kept.shape, kept.dtype)]

    def spec(shape, cut):
        if cut is None:
            return pl.BlockSpec(shape, lambda i: (0, 0))
        if cut:
            return pl.BlockSpec((shape[0], shape[1] // steps), lambda i: (0, i))
        return pl.BlockSpec((shape[0] // steps, shape[1]), lambda i: (i, 0))

    for grad, weight, moment, average, rate, first, cut in sets:
        arrays += [grad, weight, moment, average]
        in_specs += [spec(grad.shape, cut)] + [spec(weight.shape, cut)] * 3
        out_specs += [spec(weight.shape, cut)] * 4
        shapes += [jax.ShapeDtypeStruct(weight.shape, f32)] * 4
    made = pl.pallas_call(
        functools.partial(update_kernel, [s[4] for s in sets], [s[5] for s in sets]),
        grid=(steps,),
        in_specs=in_specs,
        out_specs=out_specs,
        out_shape=shapes,
        compiler_params=pltpu.CompilerParams(vmem_limit_bytes=63 * 1024 * 1024),
        name="update",
    )(*arrays)
    return made[0], [made[4 * i + 1 : 4 * i + 5] for i in range(len(sets))]


FINAL_ROW = 32


def back_kernel(size, names, *refs):
    ref = types.SimpleNamespace(**dict(zip(names, refs)))
    gb, vec, table, table_back = ref.gb, ref.vec, ref.table, ref.back
    micro, count, width = gb.shape
    slot = 2 * count
    tiles = width // TILE
    ring = Ring(size)
    gw, gc, gcr, gz = ref.gw, ref.gc, ref.gcr, ref.gz
    vsum, nsum = ref.vsum, ref.nsum
    one, two = ref.one, ref.two
    gate, turned = ref.gate, ref.turned
    inside = jnp.where(ring.pos < 1, 1.0, 0.0).astype(f32)
    first_half, second_half = ring.pos == 0, ring.pos == 1
    copies = Copies(ref.copy_sems)
    gate_copies = [
        copies.start(ref.s.at[j, :, :, pl.ds(0, TILE)], gate.at[j]) for j in range(tiles)
    ]
    wout = ref.din.at[0]
    wout_copy = copies.start(ref.wout, wout)
    turned_copy = copies.start(ref.yt, turned)

    greet_all(ring)
    red = {}

    def parts_of(name):
        return [getattr(ref, name + str(k)) for k in range(6)]

    down = Reduction(ring, -1, ref.ddown, *parts_of("down"), ref.down_stage, ref.down_stage_sems)
    up = Reduction(ring, 1, ref.dup, *parts_of("up"), ref.up_stage, ref.up_stage_sems)
    out = Reduction(ring, -1, ref.dout, *parts_of("out"))
    inner = [
        Reduction(ring, 1 - 2 * (j % 2), ref.din.at[j], *[part.at[j] for part in parts_of("in")])
        for j in range(tiles)
    ]
    down.begin()
    up.begin()
    vsum[...] = jnp.zeros_like(vsum)
    nsum[...] = jnp.zeros_like(nsum)
    small = ref.small
    vsum[2:4] = small[0:2]
    vsum[7:8] = small[2:3]
    vsum[12:13] = small[3:4]
    vsum[8:12] = small[4:8]

    crossing = []
    wout_copy.wait()
    for j in range(tiles):
        gate_copies[j].wait()
        weight = wout[...].reshape(width, width)[j * TILE : (j + 1) * TILE]

        @pl.loop(0, micro)
        def _(m):
            one[:count] = dot_nt(gb[m], weight)
            length = ref.lens[0, m] - ring.pos * count
            for rows in blocks(count, 32):
                mask = valid_rows(length, rows.start, 32, TILE)
                grad = mask * one[rows].astype(bf16).astype(f32)
                gw[j, m, rows] = grad.astype(bf16)
                gc[j, m, rows] = (grad * gate[j, m, rows].astype(f32)).astype(bf16)

        copy = remote(
            gc.at[j], gcr.at[j], ref.gc_sem.at[0, j], ref.gc_sem.at[1, j], ring.across
        )
        copy.start()
        crossing.append(copy)
    turned_copy.wait()

    @pl.loop(0, tiles)
    def _(j):
        cols = pl.ds(pl.multiple_of(j * TILE, TILE), TILE)
        total = dot(turned[0], gb[0, :, cols])
        for m in range(1, micro):
            total = total + dot(turned[m], gb[m, :, cols])
        dout = ref.dout
        dout[:, :, :, cols] = total.astype(bf16).reshape(dout.shape[:3] + (TILE,))

    turned_copy = copies.start(ref.nt, turned)
    out.begin()
    down.merge()
    up.merge()

    parity = 1.0 - 2.0 * (lax.broadcasted_iota(jnp.int32, (16, TILE), 0) % 2).astype(f32)
    gk = ref.gk
    gbuf, zbuf, spec = ref.gbuf, ref.zbuf, ref.spec
    first_rows, last_rows, next_rows = ref.first_rows, ref.last_rows, ref.next_rows

    def loads(j, m, at):
        made = [
            (ref.s.at[j, m, :, pl.ds(TILE, 2 * TILE)], ref.s_buf.at[at]),
            (ref.z.at[j, m], ref.z_buf.at[at]),
            (ref.uhat.at[j, m], ref.u_buf.at[at]),
            (ref.conv.at[j, m], ref.c_buf.at[at]),
        ]
        return [
            pltpu.make_async_copy(src, dst, ref.load_sems.at[at, i])
            for i, (src, dst) in enumerate(made)
        ]

    def load_kernel(j):
        return pltpu.make_async_copy(ref.kern.at[j], ref.k_buf, ref.kernel_sem.at[0])

    def start_loads(j, m, at):
        for copy in loads(j, m, at):
            copy.start()

    start_loads(0, 0, 0)
    load_kernel(0).start()
    gbuf[:, count:] = jnp.zeros_like(gbuf[:, count:])

    def unmix(j):
        crossing[j].wait_recv()
        load_kernel(j).wait()
        lane = slice(j * TILE, (j + 1) * TILE)
        kn = ref.k_buf

        @pl.loop(0, micro)
        def _(m):
            at = lax.rem(j * micro + m, 2)
            for copy in loads(j, m, at):
                copy.wait()

            @pl.when(m + 1 < micro)
            def _():
                start_loads(j, m + 1, 1 - at)

            if j + 1 < tiles:

                @pl.when(m + 1 == micro)
                def _():
                    start_loads(j + 1, 0, 1 - at)

            one[...] = dot(table[...], gc[j, m])
            keep = jnp.where(m > 0, 1.0, 0.0).astype(f32)
            uh = ref.u_buf

            def filter_grad(d, re, im, gr, gi):
                ur, ui = uh[at, d, re].astype(f32), uh[at, d, im].astype(f32)
                gk[d, re] = gk[d, re] * keep + (ur * gr + ui * gi)
                gk[d, im] = gk[d, im] * keep + (ur * gi - ui * gr)

            @pl.when(first_half)
            def _():
                two[...] = dot(table[...], gcr[j, m])
                for re in blocks(count, 16):
                    im = slice(re.start + count, re.stop + count)
                    gr, gi, hr, hi = one[re], one[im], two[re], two[im]
                    k0r, k0i = kn[0, re].astype(f32), kn[0, im].astype(f32)
                    k1r, k1i = kn[1, re].astype(f32), kn[1, im].astype(f32)
                    spec[re] = (k0r * gr + k0i * gi + k1r * hr + k1i * hi).astype(bf16)
                    spec[im] = (k0r * gi - k0i * gr + k1r * hi - k1i * hr).astype(bf16)
                    filter_grad(0, re, im, gr, gi)

            @pl.when(second_half)
            def _():
                for re in blocks(count, 16):
                    im = slice(re.start + count, re.stop + count)
                    gr, gi = one[re], one[im]
                    k0r, k0i = kn[0, re].astype(f32), kn[0, im].astype(f32)
                    spec[re] = (k0r * gr + k0i * gi).astype(bf16)
                    spec[im] = (k0r * gi - k0i * gr).astype(bf16)
                    filter_grad(0, re, im, gr, gi)
                    filter_grad(1, re, im, gr, gi)

            two[:count] = dot(table_back[...], spec[...])
            skip_sum = jnp.zeros((8, TILE), f32)
            for rows in blocks(count, 32):
                x1 = ref.s_buf[at, rows, :TILE].astype(f32)
                v = ref.s_buf[at, rows, TILE:].astype(f32)
                grad_w = gw[j, m, rows].astype(f32)
                gc_full = grad_w * gate[j, m, rows].astype(f32)
                gu = two[rows] * (1.0 / count) + vec[25:26, lane] * gc_full
                skip_sum = skip_sum + folded(gc_full * (x1 * v))
                grads = (grad_w * ref.c_buf[at, rows].astype(f32), gu * v, gu * x1)
                for p in range(3):
                    low = grads[p].astype(bf16)
                    gbuf[p, rows] = low.astype(f32)
                    if rows.start == 0:
                        first_rows[j, m, :, p * TILE : (p + 1) * TILE] = low[:16]
                    if rows.stop == count:
                        last_rows[j, m, :, p * TILE : (p + 1) * TILE] = low[16:]
            vsum[25:26, lane] += jnp.sum(skip_sum, axis=0, keepdims=True)
            for p in range(3):
                cols = slice(p * TILE, (p + 1) * TILE)
                zbuf[:16] = ref.zh[j, m, :, cols].astype(f32)
                for rows in blocks(count, 32):
                    zbuf[rows.start + 16 : rows.stop + 16] = ref.z_buf[at, rows, cols].astype(f32)
                taps = [vec[13 + 3 * k + p : 14 + 3 * k + p, lane] for k in range(3)]
                sums = [jnp.zeros((8, TILE), f32) for _ in range(4)]
                for rows in blocks(count, 32):
                    first = rows.start
                    grad = gbuf[p, rows]
                    gz[j, m, rows, cols] = (
                        taps[0] * grad
                        + taps[1] * gbuf[p, first + 1 : first + 33]
                        + taps[2] * gbuf[p, first + 2 : first + 34]
                    ).astype(bf16)
                    for k in range(3):
                        sums[k] = sums[k] + folded(grad * zbuf[first + 16 - k : first + 48 - k])
                    sums[3] = sums[3] + folded(grad)
                for k in range(4):
                    row = 13 + 3 * k + p
                    vsum[row : row + 1, lane] += jnp.sum(sums[k], axis=0, keepdims=True)

        if j + 1 < tiles:
            load_kernel(j + 1).start()
        edge = remote(
            first_rows.at[j], next_rows.at[j], ref.edge_sem.at[0, j],
            ref.edge_sem.at[1, j], ring.across,
        )
        edge.start()
        @pl.when(first_half)
        def _():
            for re in blocks(2 * count, 16):
                spec[re] = gk[0, re].astype(bf16)
            gate[j, 1] = jnp.zeros_like(gate[j, 1])

        @pl.when(second_half)
        def _():
            for re in blocks(2 * count, 16):
                spec[re] = gk[1, re].astype(bf16)
            two[count:] = dot(table_back[...], spec[...])
            for rows in blocks(count, 16):
                second = two[rows.start + count : rows.stop + count]
                gate[j, 1, rows] = (second * (1.0 / count)).astype(bf16)
            for re in blocks(count, 16):
                im = slice(re.start + count, re.stop + count)
                spec[re] = (gk[0, re] + parity * gk[1, im]).astype(bf16)
                spec[im] = (gk[0, im] - parity * gk[1, re]).astype(bf16)

        two[:count] = dot(table_back[...], spec[...])
        for rows in blocks(count, 16):
            gate[j, 0, rows] = (two[rows] * (1.0 / count)).astype(bf16)
        return edge

    def project_back(j, edge):
        edge.wait_recv()
        lane = slice(j * TILE, (j + 1) * TILE)
        ebuf = ref.ebuf
        for m in range(micro):
            for p in range(3):
                cols = slice(p * TILE, (p + 1) * TILE)
                own = last_rows[j, m, :, cols].astype(f32)
                ebuf[:16] = own
                ebuf[16:] = next_rows[j, m, :, cols].astype(f32) * inside
                gz[j, m, count - 16 :, cols] = (
                    vec[13 + p : 14 + p, lane] * own
                    + vec[16 + p : 17 + p, lane] * ebuf[1:17]
                    + vec[19 + p : 20 + p, lane] * ebuf[2:18]
                ).astype(bf16)
        for p in range(3):
            cols = slice(p * TILE, (p + 1) * TILE)
            total = dot(turned[0], gz[j, 0, :, cols])
            for m in range(1, micro):
                total = total + dot(turned[m], gz[j, m, :, cols])
            din = ref.din
            din[j, :, :, :, cols] = total.astype(bf16).reshape(din.shape[1:4] + (TILE,))
            bias = jnp.zeros((8, TILE), f32)
            for m in range(micro):
                for rows in blocks(count, 32):
                    bias = bias + folded(gz[j, m, rows, cols].astype(f32))
            vsum[4 + p : 5 + p, lane] = jnp.sum(bias, axis=0, keepdims=True)
        inner[j].begin()

    edges = [unmix(0)]
    down.advance(1)
    up.advance(1)
    out.merge()
    edges.append(unmix(1))
    turned_copy.wait()
    project_back(0, edges[0])
    down.advance(2)
    up.advance(2)
    out.advance(1)
    inner[0].merge()
    edges.append(unmix(2))
    project_back(1, edges[1])
    x_copies = [
        copies.start(ref.x.at[:, :, pl.ds(j * TILE, TILE)], gcr.at[j]) for j in range(tiles)
    ]
    pre_copy = copies.start(ref.pre, gk.at[0])
    feature_copy = copies.start(ref.feature, gk.at[1])
    down.advance(3)
    up.advance(3)
    inner[1].merge()
    project_back(2, edges[2])
    out.advance(2)
    inner[0].advance(1)
    inner[1].advance(1)
    for copy in x_copies:
        copy.wait()
    for copy in crossing:
        copy.wait_send()

    for m in range(micro):
        for t in range(tiles):
            total = 0.0
            for j in range(tiles):
                weight = ref.win[j].reshape(width, 3 * TILE)[t * TILE : (t + 1) * TILE]
                total = total + dot_nt(gz[j, m], weight)
            gbuf[t, :count] = total
        sums = [jnp.zeros((8, width), f32)] * 2
        for rows in blocks(count, 16):
            tokens = jnp.concatenate([gcr[j, m, rows] for j in range(tiles)], axis=1)
            grad = jnp.concatenate([gbuf[t, rows] for t in range(tiles)], axis=1)
            gx, gain_part, shift_part = norm_rows_back(grad, tokens.astype(f32), vec[0:1])
            sums = [sums[0] + folded(gain_part), sums[1] + folded(shift_part)]
            total = (gb[m, rows].astype(f32) + gx).astype(bf16)
            for j in range(tiles):
                gc[j, m, rows] = total[:, j * TILE : (j + 1) * TILE]
        vsum[0:1] += jnp.sum(sums[0], axis=0, keepdims=True)
        vsum[1:2] += jnp.sum(sums[1], axis=0, keepdims=True)
        if m == 0:
            inner[2].merge()
            down.collect()
            up.collect()
            out.advance(3)
            inner[0].advance(2)
            inner[1].advance(2)
    for j in range(tiles):
        copies.out(gc.at[j], ref.input_grad.at[:, :, pl.ds(j * TILE, TILE)])
    inner[2].advance(1)
    inner[0].advance(3)
    inner[1].advance(3)
    out.collect()

    net = ref.net_in
    net[...] = ref.net[...].T
    rates = ref.rate[...].reshape(1, width)
    final_low = ref.final[...].astype(bf16)
    pre_copy.wait()
    feature_copy.wait()
    frequency = net[EMB + 3 + 2 * HID : EMB + 4 + 2 * HID]

    def filter_back(at):
        rows = pl.ds(pl.multiple_of(at * TILE, TILE), TILE)
        half, part = at // (count // TILE), lax.rem(at, count // TILE)
        layers = [gk[0, rows, i * HID : (i + 1) * HID] for i in range(3)]
        many = jnp.concatenate([frequency] * 4, axis=1)
        pairs = []
        for block in blocks(TILE, 32):
            held_rows = pl.ds(pl.multiple_of(at * TILE + block.start, 32), 32)
            pairs.append(sin_cos(many * gk[0, held_rows]))
        act = jnp.concatenate([pair[0] for pair in pairs], axis=0)
        slope = jnp.concatenate([pair[1] for pair in pairs], axis=0)
        acts = [act[:, i * HID : (i + 1) * HID] for i in range(3)]
        slopes = [slope[:, i * HID : (i + 1) * HID] for i in range(3)]
        last = acts[2].astype(bf16)
        grad = jnp.zeros((TILE, HID), f32)
        for j in range(tiles):
            lane = slice(j * TILE, (j + 1) * TILE)
            pieces = []
            for block in blocks(TILE, 32):
                at_row = lax.broadcasted_iota(jnp.int32, (32, TILE), 0) + (
                    at * TILE + block.start
                )
                window = jnp.exp(at_row.astype(f32) * (rates[:, lane] * (-1.0 / slot))) + 0.05
                held = pl.ds(pl.multiple_of(part * TILE + block.start, 32), 32)
                pieces.append((gate[j, half, held].astype(f32) * window).astype(bf16))
            shaped = jnp.concatenate(pieces, axis=0)
            vsum[FINAL_ROW : FINAL_ROW + HID, lane] += dot_tn(last, shaped)
            grad = grad + dot_nt(shaped, final_low[:, lane])
        freq_sum = jnp.zeros_like(frequency)
        for i in (2, 1, 0):
            turn = grad * slopes[i]
            freq_sum = freq_sum + jnp.sum(turn * layers[i], axis=0, keepdims=True)
            grad = turn * frequency
            if i == 0:
                nsum[: EMB + 1, :HID] += lax.dot_general(
                    gk[1, rows, : EMB + 1], grad, (((0,), (0,)), ((), ())),
                    precision=highest, preferred_element_type=f32,
                )
            else:
                first = EMB + 1 if i == 1 else EMB + 2 + HID
                nsum[first : first + HID, :HID] += lax.dot_general(
                    acts[i - 1], grad, (((0,), (0,)), ((), ())),
                    precision=highest, preferred_element_type=f32,
                )
                nsum[first + HID : first + HID + 1, :HID] += jnp.sum(grad, axis=0, keepdims=True)
                grad = lax.dot_general(
                    grad, net[first : first + HID], (((1,), (1,)), ((), ())),
                    precision=highest, preferred_element_type=f32,
                )
        row = EMB + 3 + 2 * HID
        nsum[row : row + 1, :HID] += freq_sum

    row_blocks = slot // TILE

    @pl.loop(0, row_blocks // 2)
    def _(at):
        filter_back(at)

    inner[2].advance(2)
    inner[0].collect()
    inner[1].collect()

    @pl.loop(row_blocks // 2, row_blocks)
    def _(at):
        filter_back(at)

    smalls = []
    for values, sums, name in ((vsum, ref.v_out, "v"), (nsum, ref.n_out, "n")):
        parts = [getattr(ref, name + str(k)) for k in range(4)]
        smalls.append(SmallSum(ring, values, *parts[:3], sums, parts[3]))
    for work in smalls:
        work.begin()
    inner[2].advance(3)
    psum = ref.proj_sum
    wide = psum.shape[1] - 4 * width
    ref.down_sum[...] = down.result()
    for work in smalls:
        work.add_up()
    psum[:, 4 * width : 4 * width + wide] = up.result()
    psum[:, 3 * width : 4 * width] = out.result()
    inner[2].collect()
    for work in smalls:
        work.spread()
    for j in range(tiles):
        total = inner[j].result()
        for p in range(3):
            first = p * width + j * TILE
            psum[:, first : first + TILE] = total[:, p * TILE : (p + 1) * TILE]
    for work in smalls:
        work.finish()
    ref.net_sum[...] = ref.n_out[:, :HID].T
    for work in [down, up, out] + inner:
        work.finish()
    for edge in edges:
        edge.wait_send()
    copies.finish()


def back(size, arrays):
    chips = size // 2
    micro, count, width = arrays["gb"].shape
    rows, wide = arrays["dup"].shape[2:]
    down_rows = arrays["ddown"].shape[2]
    tiles = width // TILE
    vmem = pl.BlockSpec(memory_space=pltpu.VMEM)
    anywhere = pl.BlockSpec(memory_space=pl.ANY)
    smem = pl.BlockSpec(memory_space=pltpu.SMEM)
    near = ("gb", "vec", "net", "final", "rate", "table", "back", "win", "zh", "small")
    small_rows = 8 * size
    outs = dict(
        input_grad=((micro, count, width), bf16),
        proj_sum=((rows, 4 * width + wide), f32),
        down_sum=((down_rows, width), f32),
        v_out=((small_rows, width), f32),
        n_out=((2 * small_rows, 128), f32),
        net_sum=((HID, 2 * small_rows), f32),
    )
    dma = pltpu.SemaphoreType.DMA
    tile_tokens = (tiles, micro, count, TILE)
    edge_rows = (tiles, micro, 16, 3 * TILE)
    scratch = dict(
        din=pltpu.VMEM((tiles, chips, 2, rows, 3 * TILE), bf16),
        dout=pltpu.VMEM((chips, 2, rows, width), bf16),
        gw=pltpu.VMEM(tile_tokens, bf16),
        gc=pltpu.VMEM(tile_tokens, bf16),
        gcr=pltpu.VMEM(tile_tokens, bf16),
        gate=pltpu.VMEM(tile_tokens, bf16),
        gz=pltpu.VMEM((tiles, micro, count, 3 * TILE), bf16),
        turned=pltpu.VMEM((micro, width, count), bf16),
        vsum=pltpu.VMEM((small_rows, width), f32),
        nsum=pltpu.VMEM((2 * small_rows, 128), f32),
        net_in=pltpu.VMEM((EMB + 4 + 2 * HID, HID), f32),
        gk=pltpu.VMEM((2, 2 * count, TILE), f32),
        gbuf=pltpu.VMEM((3, count + 16, TILE), f32),
        one=pltpu.VMEM((2 * count, TILE), f32),
        two=pltpu.VMEM((2 * count, TILE), f32),
        zbuf=pltpu.VMEM((count + 16, TILE), f32),
        ebuf=pltpu.VMEM((32, TILE), f32),
        spec=pltpu.VMEM((2 * count, TILE), bf16),
        first_rows=pltpu.VMEM(edge_rows, bf16),
        last_rows=pltpu.VMEM(edge_rows, bf16),
        next_rows=pltpu.VMEM(edge_rows, bf16),
        s_buf=pltpu.VMEM((2, count, 2 * TILE), bf16),
        z_buf=pltpu.VMEM((2, count, 3 * TILE), bf16),
        u_buf=pltpu.VMEM((2, 2, 2 * count, TILE), bf16),
        c_buf=pltpu.VMEM((2, count, TILE), bf16),
        k_buf=pltpu.VMEM((2, 2 * count, TILE), bf16),
        load_sems=dma((2, 4)),
        kernel_sem=dma((1,)),
        gc_sem=dma((2, tiles)),
        edge_sem=dma((2, tiles)),
        copy_sems=dma((16,)),
        up_stage=pltpu.VMEM((2, rows, wide), bf16),
        down_stage=pltpu.VMEM((2, down_rows, width), bf16),
        up_stage_sems=dma((2,)),
        down_stage_sems=dma((2,)),
    )
    ups, downs = chips // 2, (chips - 1) // 2
    for name, lead, dims in (
        ("up", (), (rows, wide)), ("down", (), (down_rows, width)), ("out", (), (rows, width)),
        ("in", (tiles,), (rows, 3 * TILE)),
    ):
        made = [pltpu.VMEM(lead + (count,) + dims, bf16) for count in (chips, ups, downs)]
        made += [pltpu.VMEM(lead + dims, bf16)] * 2 + [dma(lead + (2, 2 + ups + downs))]
        for k, part in enumerate(made):
            scratch[name + str(k)] = part
    for name in ("v", "n"):
        for k, part in enumerate(small_scratch(size, *outs[name + "_out"][0])):
            scratch[name + str(k)] = part
    names = tuple(arrays) + tuple(outs) + tuple(scratch)
    return pl.pallas_call(
        functools.partial(back_kernel, size, names),
        out_shape=[jax.ShapeDtypeStruct(*kind) for kind in outs.values()],
        in_specs=[
            smem if name == "lens" else vmem if name in near else anywhere for name in arrays
        ],
        out_specs=[anywhere] + [vmem] * (len(outs) - 1),
        scratch_shapes=list(scratch.values()),
        compiler_params=pltpu.CompilerParams(
            collective_id=1, has_side_effects=True, vmem_limit_bytes=63 * 1024 * 1024
        ),
        name="back",
    )(*arrays.values())


def fits(size, groups, tokens, proj_weights, down_weights):
    micro, _, count, width = tokens.shape
    wide = down_weights.shape[0] * size
    return (
        groups == 2
        and size % 4 == 0
        and size == 16
        and proj_weights.shape[0] % 16 == 0
        and down_weights.shape[0] % 16 == 0
        and count % TILE == 0
        and width == 3 * TILE
        and micro >= groups
        and micro * count <= 1024
        and wide == 4 * width
        and proj_weights.shape[1] == 4 * width + wide
    )


def on_device_tuned(
    block_input,
    out_grad,
    lengths,
    decay_rates,
    proj_weights,
    proj_moment,
    proj_average,
    down_weights,
    down_moment,
    down_average,
    vectors,
    vector_moment,
    vector_average,
    filter_net,
    net_moment,
    net_average,
    filter_out,
    final_moment,
    final_average,
):
    micro, _, count, width = block_input.shape
    size = lax.axis_size("seq")
    tokens = block_input.reshape(micro, count, width)
    plain_table = transform_table(count)
    table = jnp.asarray(plain_table, dtype=bf16)
    table_back = jnp.asarray(plain_table.T, dtype=bf16)
    feature = jnp.asarray(feature_table(count * lax.axis_size("pos")))
    shared = dict(
        x=tokens, lens=lengths.T, vec=vectors, net=filter_net.T, final=filter_out,
        rate=decay_rates, table=table, back=table_back, feature=feature,
    )
    made = types.SimpleNamespace(**front(size, dict(shared, proj=proj_weights, down=down_weights)))
    block_output, branch_grad, up_step, down_step, small = mlp(
        made.hid, made.slope, made.n2t, out_grad.reshape(micro, count, width), made.res, vectors,
        made.wup, made.wdown,
    )
    chips = size // 2
    input_grad, proj_sum, down_sum, rest, _, net_sum = back(
        size,
        dict(
            shared, win=made.win, wout=made.wout, z=made.z, zh=made.zh, s=made.s, conv=made.conv,
            uhat=made.uhat, kern=made.kern, nt=made.nt, yt=made.yt, pre=made.pre,
            gb=branch_grad, small=small,
            dup=up_step.reshape(chips, 2, -1, up_step.shape[1]),
            ddown=down_step.reshape(chips, 2, -1, width),
        ),
    )
    input_grad, steps = update(
        input_grad,
        [
            (proj_sum, proj_weights, proj_moment, proj_average, 0.0001, 0, 1),
            (down_sum, down_weights, down_moment, down_average, 0.0001, 0, 0),
            (rest, vectors, vector_moment, vector_average, 0.001, 0, None),
            (net_sum, filter_net.T, net_moment.T, net_average.T, 0.0001, 0, None),
            (rest, filter_out, final_moment, final_average, 2e-06, FINAL_ROW, None),
        ]
    )
    steps[3] = [array.T for array in steps[3]]
    return (
        block_output.reshape(block_input.shape),
        input_grad.reshape(block_input.shape),
        *steps[0], *steps[1], *steps[2], *steps[3], *steps[4],
    )


def on_device_plain(
    block_input,
    out_grad,
    lengths,
    decay_rates,
    proj_weights,
    proj_moment,
    proj_average,
    down_weights,
    down_moment,
    down_average,
    vectors,
    vector_moment,
    vector_average,
    filter_net,
    net_moment,
    net_average,
    filter_out,
    final_moment,
    final_average,
):
    micro = block_input.shape[0]
    count = block_input.shape[2]
    width = block_input.shape[3]
    groups = lax.axis_size("pos")
    slot_length = count * groups
    tokens_all = micro * count
    group = lax.axis_index("pos")
    tap = vectors[13:22].reshape(3, 3 * width)
    short_bias = vectors[22:25].reshape(-1)
    in_bias = vectors[4:7].reshape(-1)
    up_bias = vectors[8:12].reshape(-1)
    skip = vectors[25]

    low_rows = proj_weights.astype(bf16)
    in_weight = lax.all_gather(low_rows[:, : 3 * width], "seq", axis=0, tiled=True)
    out_weight = lax.all_gather(low_rows[:, 3 * width : 4 * width], "seq", axis=0, tiled=True)
    up_weight = lax.all_gather(low_rows[:, 4 * width :], "seq", axis=0, tiled=True)
    down_weight = lax.all_gather(down_weights.astype(bf16), "seq", axis=0, tiled=True)

    table = jnp.asarray(transform_table(count))
    table_low = table.astype(bf16)
    every = jnp.arange(slot_length, dtype=jnp.int32)

    def make_filter(net_values, final_values):
        return filter_fn(net_values, final_values, decay_rates, every, slot_length)

    filters, filter_back = jax.vjp(make_filter, filter_net, filter_out)
    pieces = filters.reshape(groups, count, width)
    spectra = [
        jnp.dot(table, pieces[d], precision=lax.Precision.HIGH, preferred_element_type=f32)
        for d in range(groups)
    ]
    kernels = [spectra[0]] + [spectra[d] + turned(spectra[d - 1], 1.0) for d in range(1, groups)]

    def transform(values):
        return jnp.stack([dot(table_low, values[m]) for m in range(micro)])

    def transform_back(spectrum):
        low = spectrum.astype(bf16)
        return jnp.stack([dot_tn(table_low, low[m]) for m in range(micro)]) * (1.0 / count)

    tokens_low = block_input[:, 0]
    before = passed_along(tokens_low[:, -2:], "pos", 1)
    tokens = tokens_low.astype(f32).reshape(tokens_all, width)
    xh_one, scale_one = norm_parts(tokens)
    normed = (xh_one * vectors[0] + vectors[1]).astype(bf16)
    xh_before, _ = norm_parts(before.astype(f32).reshape(micro * 2, width))
    normed_before = (xh_before * vectors[0] + vectors[1]).astype(bf16)
    z = (dot(normed, in_weight) + in_bias).reshape(micro, count, 3 * width)
    z_before = (dot(normed_before, in_weight) + in_bias).reshape(micro, 2, 3 * width)
    z_before = jnp.where(group > 0, z_before, 0.0)
    z_long = jnp.concatenate([z_before, z], axis=1)
    short = (
        tap[0] * z_long[:, 2:] + tap[1] * z_long[:, 1:-1] + tap[2] * z_long[:, :-2] + short_bias
    ).astype(bf16)
    x0 = short[:, :, :width].astype(f32)
    x1 = short[:, :, width : 2 * width].astype(f32)
    v = short[:, :, 2 * width :].astype(f32)

    u = x1 * v
    u_low = u.astype(bf16)
    u_hat = [transform(u_low)]
    for d in range(1, groups):
        u_hat.append(transform(passed_along(u_low, "pos", d)))
    total = product(kernels[0], u_hat[0])
    for d in range(1, groups):
        total = total + product(kernels[d], u_hat[d])
    conv = transform_back(total) + skip * u
    here = group * count + jnp.arange(count, dtype=jnp.int32)
    mask = (here[None, :] < lengths[:, 0][:, None]).astype(f32)[:, :, None]
    y = (mask * x0 * conv).astype(bf16).reshape(tokens_all, width)
    residual = tokens + dot(y, out_weight) + vectors[7]
    xh_two, scale_two = norm_parts(residual)
    normed_two = (xh_two * vectors[2] + vectors[3]).astype(bf16)

    cot_low = out_grad[:, 0].reshape(tokens_all, width)
    cot = cot_low.astype(f32)
    pre = dot(normed_two, up_weight) + up_bias
    hidden, gelu_back = jax.vjp(jax.nn.gelu, pre)
    hidden_low = hidden.astype(bf16)
    block_output = (residual + dot(hidden_low, down_weight) + vectors[12]).astype(bf16)
    pre_grad = gelu_back(dot_nt(cot_low, down_weight))[0].astype(bf16)
    down_step = dot_tn(hidden_low, cot_low)
    up_step = dot_tn(normed_two, pre_grad)
    normed_two_grad = dot_nt(pre_grad, up_weight)
    part, gain_two, shift_two = norm_back(normed_two_grad, xh_two, scale_two, vectors[2])
    residual_grad = cot + part
    branch_low = residual_grad.astype(bf16)
    out_step = dot_tn(y, branch_low)
    y_grad = dot_nt(branch_low, out_weight).astype(bf16).astype(f32).reshape(micro, count, width)

    gw = mask * y_grad
    gx0 = gw * conv
    gc = gw * x0
    gc_low = gc.astype(bf16)
    skip_grad = jnp.sum(gc * u, axis=(0, 1))
    gc_hat = [transform(gc_low)]
    for d in range(1, groups):
        gc_hat.append(transform(passed_along(gc_low, "pos", -d)))
    back = product_conj(kernels[0], gc_hat[0])
    for d in range(1, groups):
        back = back + product_conj(kernels[d], gc_hat[d])
    gu = transform_back(back) + skip * gc
    kernel_grads = [jnp.sum(product_conj(u_hat[d], gc_hat[0]), axis=0) for d in range(groups)]
    filter_grads = []
    for d in range(groups):
        got = kernel_grads[d]
        if d + 1 < groups:
            got = got + turned(kernel_grads[d + 1], -1.0)
        filter_grads.append(dot_tn(table_low, got.astype(bf16)) * (1.0 / count))
    net_local, final_local = filter_back(jnp.concatenate(filter_grads, axis=0))
    short_grad = jnp.concatenate([gx0, gu * v, gu * x1], axis=-1).astype(bf16)
    after = passed_along(short_grad[:, :2], "pos", -1)
    short_long = jnp.concatenate([short_grad, after], axis=1).astype(f32)
    z_grad = (
        tap[0] * short_long[:, :-2] + tap[1] * short_long[:, 1:-1] + tap[2] * short_long[:, 2:]
    ).astype(bf16)
    here_grad = short_long[:, :-2]
    tap_grads = [
        jnp.sum(here_grad * z_long[:, 2 - k : 2 - k + count], axis=(0, 1)) for k in range(3)
    ]
    short_bias_grad = jnp.sum(here_grad, axis=(0, 1))
    z_grad = z_grad.reshape(tokens_all, 3 * width)
    in_step = dot_tn(normed, z_grad)
    in_bias_grad = jnp.sum(z_grad.astype(f32), axis=0)
    normed_grad = dot_nt(z_grad, in_weight)
    part, gain_one, shift_one = norm_back(normed_grad, xh_one, scale_one, vectors[0])
    input_grad = (residual_grad + part).astype(bf16)

    vector_local = jnp.concatenate(
        [
            gain_one[None],
            shift_one[None],
            gain_two[None],
            shift_two[None],
            in_bias_grad.reshape(3, width),
            jnp.sum(branch_low.astype(f32), axis=0)[None],
            jnp.sum(pre_grad.astype(f32), axis=0).reshape(4, width),
            jnp.sum(cot, axis=0)[None],
            jnp.stack(tap_grads).reshape(9, width),
            short_bias_grad.reshape(3, width),
            skip_grad[None],
        ],
        axis=0,
    )
    proj_local = jnp.concatenate([in_step, out_step, up_step], axis=1).astype(bf16)
    proj_shard = lax.psum_scatter(proj_local, "seq", scatter_dimension=0, tiled=True)
    down_shard = lax.psum_scatter(down_step.astype(bf16), "seq", scatter_dimension=0, tiled=True)
    proj_sum = lax.psum(proj_shard, "pos").astype(f32)
    down_sum = lax.psum(down_shard, "pos").astype(f32)
    vector_sum, net_sum, final_sum = lax.psum(
        (vector_local, net_local, final_local), ("seq", "pos")
    )
    return (
        block_output.reshape(micro, 1, count, width),
        input_grad.reshape(micro, 1, count, width),
        *nesterov(proj_weights, proj_moment, proj_average, proj_sum, 0.0001),
        *nesterov(down_weights, down_moment, down_average, down_sum, 0.0001),
        *nesterov(vectors, vector_moment, vector_average, vector_sum, 0.001),
        *nesterov(filter_net, net_moment, net_average, net_sum, 0.0001),
        *nesterov(filter_out, final_moment, final_average, final_sum, 2e-06),
    )


def on_device(*arrays):
    tuned = fits(
        lax.axis_size("seq"), lax.axis_size("pos"), arrays[0], arrays[4], arrays[7]
    )
    return (on_device_tuned if tuned else on_device_plain)(*arrays)


def solution(mesh):
    tokens = P(None, "seq", "pos", None)
    rows = P("seq", None)
    whole = P()
    return jax.shard_map(
        on_device,
        mesh=mesh,
        in_specs=(tokens, tokens, P(None, "seq"), whole) + (rows,) * 6 + (whole,) * 9,
        out_specs=(tokens, tokens) + (rows,) * 8 + (whole,) * 12,
        check_vma=False,
    )
```

```python
import functools
import math
import types

import jax
import jax.numpy as jnp
import numpy as np
from jax import lax
from jax.experimental import pallas as pl
from jax.experimental.pallas import tpu as pltpu
from jax.sharding import PartitionSpec as P

HID = 64
EMB = 33

highest = lax.Precision.HIGHEST
f32 = jnp.float32
bf16 = jnp.bfloat16


def passed_along(block, axis, distance):
    devices = range(lax.axis_size(axis))
    route = [(i - distance, i) for i in devices if i - distance in devices]
    return lax.ppermute(block, axis, route)


def dot(a, b):
    return lax.dot_general(a, b, (((1,), (0,)), ((), ())), preferred_element_type=f32)


def dot_tn(a, b):
    return lax.dot_general(a, b, (((0,), (0,)), ((), ())), preferred_element_type=f32)


def dot_nt(a, b):
    return lax.dot_general(a, b, (((1,), (1,)), ((), ())), preferred_element_type=f32)


def features(positions, slot_length):
    band_count = (EMB - 1) // 2
    scaled = positions.astype(f32) / slot_length
    bands = 0.0001 + jnp.arange(band_count, dtype=f32) * (
        (band_count - 1 - 0.0001) / (band_count - 1)
    )
    angles = 2.0 * math.pi * scaled[:, None] * bands[None, :]
    return jnp.concatenate([scaled[:, None], jnp.cos(angles), -jnp.sin(angles)], axis=1)


def filter_fn(net_values, final_values, rates, positions, slot_length):
    embedded = features(positions, slot_length)
    frequency = net_values[EMB + 3 + 2 * HID]
    layer_one = jnp.sin(
        frequency * (jnp.dot(embedded, net_values[:EMB], precision=highest) + net_values[EMB])
    )
    layer_two = jnp.sin(
        frequency
        * (
            jnp.dot(layer_one, net_values[EMB + 1 : EMB + 1 + HID], precision=highest)
            + net_values[EMB + 1 + HID]
        )
    )
    layer_three = jnp.sin(
        frequency
        * (
            jnp.dot(layer_two, net_values[EMB + 2 + HID : EMB + 2 + 2 * HID], precision=highest)
            + net_values[EMB + 2 + 2 * HID]
        )
    )
    shaped = jnp.dot(layer_three, final_values, precision=highest)
    scaled = positions.astype(f32) / slot_length
    window = jnp.exp(-scaled[:, None] * rates[None, :]) + 0.05
    return shaped * window


def transform_table(length):
    product = np.outer(2 * np.arange(length) + 1, np.arange(length)) % (4 * length)
    angle = product.astype(np.float64) * (math.pi / (2 * length))
    return np.concatenate([np.cos(angle), -np.sin(angle)], axis=0).astype(np.float32)


def feature_table(slot_length):
    scaled = np.arange(slot_length, dtype=np.float32) / np.float32(slot_length)
    band_count = (EMB - 1) // 2
    bands = np.float32(0.0001) + np.arange(band_count, dtype=np.float32) * np.float32(
        (band_count - 1 - 0.0001) / (band_count - 1)
    )
    angles = (np.float32(2.0 * math.pi) * scaled[:, None]) * bands[None, :]
    table = np.zeros((40, slot_length), np.float32)
    table[0] = scaled
    table[1 : 1 + band_count] = np.cos(angles).T
    table[1 + band_count : EMB] = -np.sin(angles).T
    table[EMB] = 1.0
    return table


def halves(spectrum):
    half = spectrum.shape[-2] // 2
    return spectrum[..., :half, :], spectrum[..., half:, :]


def turned(spectrum, sign):
    re, im = halves(spectrum)
    parity = (1.0 - 2.0 * (jnp.arange(re.shape[-2]) % 2).astype(f32))[:, None] * sign
    return jnp.concatenate([-parity * im, parity * re], axis=-2)


def product(kernel, signal):
    kr, ki = halves(kernel)
    sr, si = halves(signal)
    return jnp.concatenate([kr * sr - ki * si, kr * si + ki * sr], axis=-2)


def product_conj(kernel, signal):
    kr, ki = halves(kernel)
    sr, si = halves(signal)
    return jnp.concatenate([kr * sr + ki * si, kr * si - ki * sr], axis=-2)


def nesterov(weight, moment, average, gradient, rate):
    moment_next = 0.9 * moment + gradient
    weight_next = weight - rate * (gradient + 0.9 * moment_next)
    average_next = 0.9 * average + 0.1 * weight_next
    return (gradient, weight_next, moment_next, average_next)


def norm_parts(values):
    center = jnp.mean(values, axis=-1, keepdims=True)
    centred = values - center
    variance = jnp.mean(centred * centred, axis=-1, keepdims=True)
    scale = lax.rsqrt(variance + 1e-05)
    return centred * scale, scale


def norm_back(grad, xh, scale, gain):
    q = grad * gain
    return (
        (q - jnp.mean(q, -1, keepdims=True) - xh * jnp.mean(q * xh, -1, keepdims=True)) * scale,
        jnp.sum(grad * xh, axis=0),
        jnp.sum(grad, axis=0),
    )


MESH = pl.DeviceIdType.MESH


class Ring:
    def __init__(self, size):
        self.size = size
        self.count = size // 2
        self.seq = lax.axis_index("seq")
        self.pos = lax.axis_index("pos")
        self.core = lax.rem(self.seq, 2)
        chip = self.seq // 2
        odd = lax.rem(chip, 2)
        self.place = (1 - odd) * (chip // 2) + odd * (self.count - 1 - chip // 2)

    def chip(self, shift):
        place = lax.rem(self.place + (shift + self.count), self.count)
        low = jnp.where(place < self.count // 2, 1, 0)
        return low * (2 * place) + (1 - low) * (2 * (self.count - 1 - place) + 1)

    def device(self, shift):
        return {"seq": 2 * self.chip(shift) + self.core}

    @property
    def sibling(self):
        return {"seq": self.seq + 1 - 2 * self.core}

    @property
    def across(self):
        return {"pos": 1 - self.pos}


def greet_all(ring):
    barrier = pltpu.get_barrier_semaphore()
    for step in range(1, ring.size):
        other = lax.rem(ring.seq + step, ring.size)
        pl.semaphore_signal(barrier, inc=1, device_id={"seq": other}, device_id_type=MESH)
    pl.semaphore_signal(barrier, inc=1, device_id=ring.across, device_id_type=MESH)
    pl.semaphore_wait(barrier, ring.size)


def remote(src, dst, send, recv, device):
    return pltpu.make_async_remote_copy(
        src_ref=src, dst_ref=dst, send_sem=send, recv_sem=recv, device_id=device,
        device_id_type=MESH,
    )


class Reduction:
    def __init__(
        self, ring, turn, grad, twin, up, down, own, other, sems, stage=None, stage_sems=None
    ):
        self.ring, self.turn = ring, turn
        self.grad, self.twin, self.up, self.down = grad, twin, up, down
        self.own, self.other = own, other
        self.sems = sems
        self.stage, self.stage_sems = stage, stage_sems
        self.ups = ring.count // 2
        self.downs = (ring.count - 1) // 2

    def chip(self, shift):
        return self.ring.chip(shift * self.turn)

    def copies(self):
        ring = self.ring
        made = [(self.grad.at[:, 1 - ring.core], self.twin, ring.sibling)]
        for step in range(self.ups):
            block = self.twin.at[self.chip(self.ups - step)]
            made.append((block, self.up.at[step], ring.device(self.turn)))
        for step in range(self.downs):
            block = self.twin.at[self.chip(step - self.downs)]
            made.append((block, self.down.at[step], ring.device(-self.turn)))
        made.append((self.own, self.other, ring.across))
        return made

    def copy(self, index):
        src, dst, device = self.copies()[index]
        return remote(src, dst, self.sems.at[0, index], self.sems.at[1, index], device)

    def begin(self):
        self.copy(0).start()

    def fetch(self, chip, slot):
        return pltpu.make_async_copy(
            self.grad.at[chip, self.ring.core], self.stage.at[slot], self.stage_sems.at[slot]
        )

    def merge(self):
        core = self.ring.core
        count = self.ring.count
        if self.stage is None:
            self.copy(0).wait_recv()

            @pl.loop(0, count)
            def _(chip):
                self.twin[chip] = self.twin[chip] + self.grad[chip, core]

        else:
            self.fetch(0, 0).start()
            self.copy(0).wait_recv()

            @pl.loop(0, count)
            def _(chip):
                slot = lax.rem(chip, 2)

                @pl.when(chip + 1 < count)
                def _():
                    self.fetch(chip + 1, 1 - slot).start()

                self.fetch(chip, slot).wait()
                self.twin[chip] = self.twin[chip] + self.stage[slot]

        self.copy(1).start()
        self.copy(1 + self.ups).start()

    def advance(self, step):
        self.copy(step).wait_recv()
        owner = self.chip(self.ups - step)
        self.twin[owner] = self.twin[owner] + self.up[step - 1]
        self.copy(1 + step).start()
        if step < self.downs:
            self.copy(self.ups + step).wait_recv()
            owner = self.chip(step - self.downs)
            self.twin[owner] = self.twin[owner] + self.down[step - 1]
            self.copy(1 + self.ups + step).start()

    def collect(self):
        self.copy(self.ups).wait_recv()
        self.copy(self.ups + self.downs).wait_recv()
        mine = self.chip(0)
        total = (
            self.twin[mine].astype(f32)
            + self.up[self.ups - 1].astype(f32)
            + self.down[self.downs - 1].astype(f32)
        )
        self.own[...] = total.astype(bf16)
        self.copy(1 + self.ups + self.downs).start()

    def result(self):
        self.copy(1 + self.ups + self.downs).wait_recv()
        return self.own[...].astype(f32) + self.other[...].astype(f32)

    def finish(self):
        for index in range(2 + self.ups + self.downs):
            self.copy(index).wait_send()


class SmallSum:
    def __init__(self, ring, values, parts, mine, other, sums, sems):
        self.ring, self.values, self.parts = ring, values, parts
        self.mine, self.other, self.sums = mine, other, sums
        self.sems = sems
        self.rows = parts.shape[1]
        self.waiting = []

    def block(self, index):
        return pl.ds(pl.multiple_of(index * self.rows, 8), self.rows)

    def begin(self):
        ring = self.ring
        self.arriving = []
        for step in range(1, ring.size):
            other = lax.rem(ring.seq + step, ring.size)
            copy = remote(
                self.values.at[self.block(other)], self.parts.at[step],
                self.sems.at[0, step], self.sems.at[1, step], {"seq": other},
            )
            copy.start()
            self.arriving.append(copy)
            self.waiting.append(copy)

    def add_up(self):
        for copy in self.arriving:
            copy.wait_recv()
        total = self.values[self.block(self.ring.seq)]
        for step in range(1, self.ring.size):
            total = total + self.parts[step]
        self.mine[...] = total
        self.crossing = remote(
            self.mine, self.other, self.sems.at[0, 0], self.sems.at[1, 0], self.ring.across
        )
        self.crossing.start()
        self.waiting.append(self.crossing)

    def spread(self):
        self.crossing.wait_recv()
        block = self.block(self.ring.seq)
        self.sums[block] = self.mine[...] + self.other[...]
        self.arriving = []
        for step in range(1, self.ring.size):
            other = lax.rem(self.ring.seq + step, self.ring.size)
            copy = remote(
                self.sums.at[block], self.sums.at[block],
                self.sems.at[2, step], self.sems.at[3, step], {"seq": other},
            )
            copy.start()
            self.waiting.append(copy)
            back = lax.rem(self.ring.seq + (self.ring.size - step), self.ring.size)
            self.arriving.append(
                remote(
                    self.sums.at[self.block(back)], self.sums.at[self.block(back)],
                    self.sems.at[2, step], self.sems.at[3, step], {"seq": other},
                )
            )

    def finish(self):
        for copy in self.arriving:
            copy.wait_recv()
        for copy in self.waiting:
            copy.wait_send()


def reduction_scratch(size, rows, columns):
    chips = size // 2
    ups, downs = chips // 2, (chips - 1) // 2
    return [
        pltpu.VMEM((chips, rows, columns), bf16),
        pltpu.VMEM((ups, rows, columns), bf16),
        pltpu.VMEM((downs, rows, columns), bf16),
        pltpu.VMEM((rows, columns), bf16),
        pltpu.VMEM((rows, columns), bf16),
        pltpu.SemaphoreType.DMA((2, 2 + ups + downs)),
    ]


def small_scratch(size, rows, columns):
    return [
        pltpu.VMEM((size, rows // size, columns), f32),
        pltpu.VMEM((rows // size, columns), f32),
        pltpu.VMEM((rows // size, columns), f32),
        pltpu.SemaphoreType.DMA((4, size)),
    ]


class Gather:
    def __init__(self, ring, turn, mine, full, sems):
        self.ring, self.turn = ring, turn
        self.mine, self.full, self.sems = mine, full, sems
        self.ups = ring.count // 2
        self.downs = (ring.count - 1) // 2
        self.waiting, self.arriving = [], []

    def send(self, src, place, index, device):
        copy = remote(
            src, self.full.at[self.ring.chip(place * self.turn), self.ring.core],
            self.sems.at[0, index], self.sems.at[1, index], device,
        )
        copy.start()
        self.waiting.append(copy)
        return copy

    def share(self, src, place, index):
        index = self.ups + self.downs + index
        self.send(src, place, index, self.ring.sibling)
        block = self.full.at[self.ring.chip(place * self.turn), 1 - self.ring.core]
        self.arriving.append(
            remote(block, block, self.sems.at[0, index], self.sems.at[1, index], self.ring.sibling)
        )

    def wait_block(self, place, index, device):
        block = self.full.at[self.ring.chip(place * self.turn), self.ring.core]
        remote(block, block, self.sems.at[0, index], self.sems.at[1, index], device).wait_recv()
        return block

    def begin(self):
        ring = self.ring
        self.send(self.mine, 0, 0, ring.device(self.turn))
        self.send(self.mine, 0, self.ups, ring.device(-self.turn))
        self.share(self.mine, 0, 0)
        self.local = pltpu.make_async_copy(
            self.mine, self.full.at[ring.chip(0), ring.core], self.sems.at[2, 0]
        )
        self.local.start()

    def advance(self, step):
        ring = self.ring
        block = self.wait_block(-step, step - 1, ring.device(self.turn))
        if step < self.ups:
            self.send(block, -step, step, ring.device(self.turn))
        self.share(block, -step, step)
        if step <= self.downs:
            block = self.wait_block(step, self.ups + step - 1, ring.device(-self.turn))
            if step < self.downs:
                self.send(block, step, self.ups + step, ring.device(-self.turn))
            self.share(block, step, self.ups + step)

    def arrive(self):
        self.local.wait()
        for copy in self.arriving:
            copy.wait_recv()

    def finish(self):
        for copy in self.waiting:
            copy.wait_send()


def gather_sems(size):
    chips = size // 2
    return pltpu.SemaphoreType.DMA((3, 2 * chips))


PI_PARTS = (3.140625, 9.676535897932384e-4)


def sin_cos(x):
    turns = jnp.floor(x * (1.0 / math.pi) + 0.5)
    rest = (x - turns * PI_PARTS[0]) - turns * PI_PARTS[1]
    half = turns * 0.5
    sign = 1.0 - 4.0 * (half - jnp.floor(half))
    square = rest * rest
    odd = 1.0 / 6227020800.0
    for factor in (-1.0 / 39916800.0, 1.0 / 362880.0, -1.0 / 5040.0, 1.0 / 120.0, -1.0 / 6.0):
        odd = odd * square + factor
    even = 1.0 / 479001600.0
    for factor in (-1.0 / 3628800.0, 1.0 / 40320.0, -1.0 / 720.0, 1.0 / 24.0, -0.5):
        even = even * square + factor
    signed = sign * rest
    return signed + signed * square * odd, sign + sign * square * even


def norm_rows(values):
    center = jnp.mean(values, axis=1, keepdims=True)
    centred = values - center
    variance = jnp.mean(centred * centred, axis=1, keepdims=True)
    return centred * lax.rsqrt(variance + 1e-05)


TILE = 256


class Copies:
    def __init__(self, sems):
        self.sems, self.used, self.open = sems, 0, []

    def start(self, src, dst):
        copy = pltpu.make_async_copy(src, dst, self.sems.at[self.used])
        self.used += 1
        copy.start()
        return copy

    def out(self, src, dst):
        copy = self.start(src, dst)
        self.open.append(copy)
        return copy

    def settle(self, copy):
        copy.wait()
        self.open = [other for other in self.open if other is not copy]

    def finish(self):
        for copy in self.open:
            copy.wait()


def valid_rows(length, first, rows, columns):
    at = lax.broadcasted_iota(jnp.int32, (rows, columns), 0) + first
    return jnp.where(at < length, 1.0, 0.0).astype(f32)


def blocks(rows, step):
    return [slice(at, at + step) for at in range(0, rows, step)]


def folded(values):
    return jnp.sum(values.reshape(-1, 8, values.shape[1]), axis=0)


def front_kernel(size, names, *refs):
    ref = types.SimpleNamespace(**dict(zip(names, refs)))
    x, vec, net = ref.x_in, ref.vec, ref.net
    micro, count, width = x.shape
    slot = 2 * count
    tiles = width // TILE
    ring = Ring(size)
    copies = Copies(ref.copy_sems)
    proj_copy = copies.start(ref.proj, ref.proj_in)
    x_copy = copies.start(ref.x, x)
    down_copy = copies.start(ref.down, ref.down_in)
    feature_copy = copies.start(ref.feature, ref.feature_in)
    table_copy = copies.start(ref.table, ref.table_in)
    back_copy = copies.start(ref.back, ref.back_in)
    table, table_back = ref.table_in, ref.back_in
    inside = jnp.where(ring.pos > 0, 1.0, 0.0).astype(f32)

    proj_copy.wait()
    own = ref.in_own
    for j in range(tiles):
        for p in range(3):
            first = p * width + j * TILE
            own[j, :, p * TILE : (p + 1) * TILE] = ref.proj_in[:, first : first + TILE].astype(bf16)
    greet_all(ring)
    gather = [Gather(ring, 1 - 2 * (j % 2), own.at[j], ref.win_in.at[j], ref.win_sem.at[j]) for j in range(tiles)]
    gather_out = Gather(ring, -1, ref.out_own, ref.wout_in, ref.wout_sem)
    gather_up = Gather(ring, 1, ref.up_own, ref.wup, ref.wup_sem)
    gather_down = Gather(ring, -1, ref.down_own, ref.wdown, ref.wdown_sem)
    gather[0].begin()
    gather[1].begin()
    x_copy.wait()
    edge = remote(
        x.at[:, pl.ds(count - 16, 16)], ref.halo, ref.halo_sem.at[0],
        ref.halo_sem.at[1], ring.across,
    )
    edge.start()

    gain, shift = vec[0:1], vec[1:2]
    normed_ref, turned_ref = ref.n_in, ref.nt_in

    def first_norm(m):
        for rows in blocks(count, 16):
            normed_ref[m, rows] = (norm_rows(x[m, rows].astype(f32)) * gain + shift).astype(bf16)
        for rows in blocks(count, TILE):
            turned_ref[m, :, rows] = normed_ref[m, rows].T

    first_norm(0)
    gather[0].advance(1)
    gather[1].advance(1)
    gather[2].begin()
    for m in range(1, micro):
        first_norm(m)
    copies.out(turned_ref, ref.nt)
    ref.out_own[...] = ref.proj_in[:, 3 * width : 4 * width].astype(bf16)
    gather[0].advance(2)
    gather[1].advance(2)
    edge.wait_recv()
    for m in range(micro):
        ref.halo_n[m] = (norm_rows(ref.halo[m].astype(f32)) * gain + shift).astype(bf16)
    feature_copy.wait()

    frequency = net[:, EMB + 3 + 2 * HID : EMB + 4 + 2 * HID]
    pre = ref.pre_in

    def layer(i, weights, values):
        made = jnp.dot(weights, values, precision=highest, preferred_element_type=f32)
        if i > 0:
            first = EMB + 1 + (i - 1) * (HID + 1) + HID
            made = made + net[:, first : first + 1]
        pre[i * HID : (i + 1) * HID] = made
        return jnp.concatenate(
            [sin_cos(frequency[part] * made[part])[0] for part in blocks(HID, 16)], axis=0
        )

    hidden = layer(0, net[:, : ref.feature_in.shape[0]], ref.feature_in[...])
    for i in (1, 2):
        first = EMB + 1 + (i - 1) * (HID + 1)
        hidden = layer(i, net[:, first : first + HID], hidden)
    ref.act_in[...] = hidden.astype(bf16)
    copies.out(pre, ref.pre)
    rates = ref.rate[...].reshape(1, width)

    def filter_rows(at):
        shaped = dot_tn(
            ref.act_in[:, at * TILE : (at + 1) * TILE], ref.final[...].astype(bf16)
        )
        for part in blocks(TILE, 16):
            at_row = lax.broadcasted_iota(jnp.int32, (16, width), 0) + (at * TILE + part.start)
            window = jnp.exp(at_row.astype(f32) * (rates * (-1.0 / slot))) + 0.05
            first = at * TILE + part.start
            ref.filt[first : first + 16] = (shaped[part] * window).astype(bf16)

    row_blocks = slot // TILE
    gather[0].advance(3)
    gather[1].advance(3)
    gather[2].advance(1)
    for at in range(row_blocks // 2):
        filter_rows(at)
    down_copy.wait()
    ref.up_own[...] = ref.proj_in[:, 4 * width :].astype(bf16)
    ref.down_own[...] = ref.down_in[...].astype(bf16)
    gather[0].advance(4)
    gather[2].advance(2)
    gather_out.begin()
    gather[1].advance(4)
    gather[0].arrive()

    z_in, s_in, ulow, urecv = ref.z_in, ref.s_in, ref.ulow, ref.urecv
    zbuf, spec = ref.zbuf, ref.spec
    crossing = []

    def project(j):
        weight = ref.win_in[j].reshape(width, 3 * TILE)
        bias = jnp.concatenate(
            [vec[4 + p : 5 + p, j * TILE : (j + 1) * TILE] for p in range(3)], axis=1
        )
        lane = slice(j * TILE, (j + 1) * TILE)
        taps = [[vec[13 + 3 * k + p : 14 + 3 * k + p, lane] for p in range(3)] for k in range(3)]
        constant = [
            (taps[0][p] + taps[1][p] + taps[2][p]) * vec[4 + p : 5 + p, lane]
            + vec[22 + p : 23 + p, lane]
            for p in range(3)
        ]

        @pl.loop(0, micro)
        def _(m):
            zbuf[16:] = dot(normed_ref[m], weight)
            zbuf[:16] = dot(ref.halo_n[m], weight) * inside + bias * (inside - 1.0)
            ref.zh_in[j, m] = (zbuf[:16] + bias).astype(bf16)
            for rows in blocks(count, 32):
                parts = []
                for p in range(3):
                    cols = slice(p * TILE, (p + 1) * TILE)
                    first = rows.start
                    z = zbuf[first + 16 : first + 48, cols]
                    z_in[j, m, rows, cols] = (z + bias[:, cols]).astype(bf16)
                    short = (
                        taps[0][p] * z
                        + taps[1][p] * zbuf[first + 15 : first + 47, cols]
                        + taps[2][p] * zbuf[first + 14 : first + 46, cols]
                        + constant[p]
                    ).astype(bf16)
                    s_in[j, m, rows, cols] = short
                    parts.append(short.astype(f32))
                ulow[j, m, rows] = (parts[1] * parts[2]).astype(bf16)

        copy = remote(
            ulow.at[j], urecv.at[j], ref.u_sem.at[0, j], ref.u_sem.at[1, j], ring.across
        )
        copy.start()
        crossing.append(copy)
        copies.out(z_in.at[j], ref.z.at[j])
        copies.out(s_in.at[j], ref.s.at[j])

    project(0)
    gather[2].advance(3)
    gather_up.begin()
    gather[1].arrive()
    project(1)
    gather[2].advance(4)
    gather_down.begin()
    gather_out.advance(1)
    gather[2].arrive()
    project(2)
    copies.out(ref.zh_in, ref.zh)
    copies.out(ref.win_in, ref.win)
    gather_out.advance(2)
    gather_up.advance(1)
    gather_out.advance(3)
    for at in range(row_blocks // 2, row_blocks):
        filter_rows(at)
    gather_down.advance(1)
    gather_out.advance(4)
    gather_out.arrive()
    copies.out(ref.wout_in, ref.wout)
    table_copy.wait()
    back_copy.wait()

    parity = 1.0 - 2.0 * (lax.broadcasted_iota(jnp.int32, (16, TILE), 0) % 2).astype(f32)
    kern, uhat = ref.kern_in, ref.uhat_in
    one, two = ref.one, ref.two

    @pl.loop(0, tiles)
    def _(j):
        cols = pl.ds(pl.multiple_of(j * TILE, TILE), TILE)
        one[...] = dot(table[...], ref.filt[:count, cols])
        two[...] = dot(table[...], ref.filt[count:, cols])
        for re in blocks(count, 16):
            im = slice(re.start + count, re.stop + count)
            kern[j, 0, re] = one[re].astype(bf16)
            kern[j, 0, im] = one[im].astype(bf16)
            kern[j, 1, re] = (two[re] - parity * one[im]).astype(bf16)
            kern[j, 1, im] = (two[im] + parity * one[re]).astype(bf16)
        for m in range(micro):
            uhat[j, m, 0] = dot(table[...], ulow[j, m]).astype(bf16)

    copies.out(kern, ref.kern)
    gather_up.advance(2)

    def mix(j):
        crossing[j].wait_recv()
        lane = slice(j * TILE, (j + 1) * TILE)

        @pl.loop(0, micro)
        def _(m):
            one[...] = dot(table[...], urecv[j, m])
            for re in blocks(count, 16):
                im = slice(re.start + count, re.stop + count)
                k0r, k0i = kern[j, 0, re].astype(f32), kern[j, 0, im].astype(f32)
                k1r, k1i = kern[j, 1, re].astype(f32), kern[j, 1, im].astype(f32)
                ur, ui = uhat[j, m, 0, re].astype(f32), uhat[j, m, 0, im].astype(f32)
                vr, vi = one[re] * inside, one[im] * inside
                uhat[j, m, 1, re] = vr.astype(bf16)
                uhat[j, m, 1, im] = vi.astype(bf16)
                spec[re] = (k0r * ur - k0i * ui + k1r * vr - k1i * vi).astype(bf16)
                spec[im] = (k0r * ui + k0i * ur + k1r * vi + k1i * vr).astype(bf16)
            two[:count] = dot(table_back[...], spec[...])
            length = ref.lens[0, m] - ring.pos * count
            for rows in blocks(count, 32):
                gated = s_in[j, m, rows, TILE : 2 * TILE].astype(f32) * s_in[
                    j, m, rows, 2 * TILE :
                ].astype(f32)
                conv = two[rows] * (1.0 / count) + vec[25:26, lane] * gated
                ref.conv_in[j, m, rows] = conv.astype(bf16)
                mask = valid_rows(length, rows.start, 32, TILE)
                ref.y_in[m, rows, lane] = (
                    mask * s_in[j, m, rows, :TILE].astype(f32) * conv
                ).astype(bf16)

        copies.out(ref.conv_in.at[j], ref.conv.at[j])
        copies.out(uhat.at[j], ref.uhat.at[j])

    for j in range(tiles):
        mix(j)
        if j == 0:
            gather_down.advance(2)
        if j == 1:
            gather_up.advance(3)

    for m in range(micro):
        ref.res_in[m] = dot(ref.y_in[m], ref.wout_in[...].reshape(width, width))
        for rows in blocks(count, TILE):
            ref.yt_in[m, :, rows] = ref.y_in[m, rows].T
        for rows in blocks(count, 16):
            residual = x[m, rows].astype(f32) + ref.res_in[m, rows] + vec[7:8]
            ref.res_in[m, rows] = residual
            ref.n2_in[m, rows] = (norm_rows(residual) * vec[2:3] + vec[3:4]).astype(bf16)
        for rows in blocks(count, TILE):
            ref.n2t_in[m, :, rows] = ref.n2_in[m, rows].T
        for src, dst in (
            (ref.yt_in, ref.yt), (ref.res_in, ref.res), (ref.n2_in, ref.n2), (ref.n2t_in, ref.n2t)
        ):
            copies.out(src.at[m], dst.at[m])
        if m == 0:
            gather_down.advance(3)
    gather_up.advance(4)
    gather_up.arrive()

    gather_down.advance(4)
    gather_down.arrive()
    for work in gather:
        work.finish()
    for work in (gather_out, gather_up, gather_down):
        work.finish()
    edge.wait_send()
    for copy in crossing:
        copy.wait_send()
    copies.finish()


def front(size, arrays):
    chips = size // 2
    micro, count, width = arrays["x"].shape
    rows, down_rows = arrays["proj"].shape[0], arrays["down"].shape[0]
    wide = down_rows * size
    tiles = width // TILE
    vmem = pl.BlockSpec(memory_space=pltpu.VMEM)
    anywhere = pl.BlockSpec(memory_space=pl.ANY)
    smem = pl.BlockSpec(memory_space=pltpu.SMEM)
    near = ("vec", "net", "final", "rate")
    kinds = dict(
        win=((tiles, chips, 2, rows, 3 * TILE), bf16),
        wout=((chips, 2, rows, width), bf16),
        z=((tiles, micro, count, 3 * TILE), bf16),
        zh=((tiles, micro, 16, 3 * TILE), bf16),
        s=((tiles, micro, count, 3 * TILE), bf16),
        conv=((tiles, micro, count, TILE), bf16),
        uhat=((tiles, micro, 2, 2 * count, TILE), bf16),
        kern=((tiles, 2, 2 * count, TILE), bf16),
        res=((micro, count, width), f32),
        nt=((micro, width, count), bf16),
        n2=((micro, count, width), bf16),
        n2t=((micro, width, count), bf16),
        yt=((micro, width, count), bf16),
        pre=((3 * HID, 2 * count), f32),
    )
    outs = dict(
        kinds,
        wup=((chips, 2, rows, wide), bf16),
        wdown=((chips, 2, down_rows, width), bf16),
    )
    dma = pltpu.SemaphoreType.DMA
    scratch = {
        name + "_in": pltpu.VMEM(*kind) for name, kind in kinds.items()
    }
    for name, array in arrays.items():
        if name not in near and name != "lens":
            scratch[name + "_in"] = pltpu.VMEM(array.shape, array.dtype)
    scratch.update(
        dict(
            n_in=pltpu.VMEM((micro, count, width), bf16),
            one=pltpu.VMEM((2 * count, TILE), f32),
            two=pltpu.VMEM((2 * count, TILE), f32),
            act_in=pltpu.VMEM((HID, 2 * count), bf16),
            y_in=pltpu.VMEM((micro, count, width), bf16),
            in_own=pltpu.VMEM((tiles, rows, 3 * TILE), bf16),
            out_own=pltpu.VMEM((rows, width), bf16),
            up_own=pltpu.VMEM((rows, wide), bf16),
            down_own=pltpu.VMEM((down_rows, width), bf16),
            halo=pltpu.VMEM((micro, 16, width), bf16),
            halo_n=pltpu.VMEM((micro, 16, width), bf16),
            filt=pltpu.VMEM((2 * count, width), bf16),
            zbuf=pltpu.VMEM((16 + count, 3 * TILE), f32),
            ulow=pltpu.VMEM((tiles, micro, count, TILE), bf16),
            urecv=pltpu.VMEM((tiles, micro, count, TILE), bf16),
            spec=pltpu.VMEM((2 * count, TILE), bf16),
            win_sem=dma((tiles, 3, 2 * chips)),
            wout_sem=gather_sems(size),
            wup_sem=gather_sems(size),
            wdown_sem=gather_sems(size),
            halo_sem=dma((2,)),
            u_sem=dma((2, tiles)),
            copy_sems=dma((56,)),
        )
    )
    names = tuple(arrays) + tuple(outs) + tuple(scratch)
    made = pl.pallas_call(
        functools.partial(front_kernel, size, names),
        out_shape=[jax.ShapeDtypeStruct(*kind) for kind in outs.values()],
        in_specs=[
            smem if name == "lens" else vmem if name in near else anywhere for name in arrays
        ],
        out_specs=[anywhere] * len(outs),
        scratch_shapes=list(scratch.values()),
        compiler_params=pltpu.CompilerParams(
            collective_id=0, has_side_effects=True, vmem_limit_bytes=63 * 1024 * 1024
        ),
        name="front",
    )(*arrays.values())
    return dict(zip(outs, made))


GELU_SCALE = math.sqrt(2.0 / math.pi)


def gelu_pair(a):
    square = a * a
    half = 0.5 + 0.5 * jnp.tanh(a * (GELU_SCALE + (GELU_SCALE * 0.044715) * square))
    hidden = a * half
    bend = 2.0 * GELU_SCALE + (2.0 * GELU_SCALE * 0.134145) * square
    return hidden, half + (hidden - hidden * half) * bend


def mlp_kernel(
    n2_ref, n2t_ref, gm_ref, res_ref, vec_ref, wup_ref, wdown_ref,
    out_ref, gb_ref, dup_ref, ddown_ref, small_ref,
    acc_out, acc_gn, hid_ref, ga_ref,
):
    step, last = pl.program_id(0), pl.num_programs(0) - 1
    micro, count, width = n2_ref.shape
    chunk = width
    wup = wup_ref[...].reshape(width, chunk)
    wdown = wdown_ref[...].reshape(chunk, width)
    bias = vec_ref[pl.ds(8 + step, 1)]

    @pl.when(step == 0)
    def _():
        acc_out[...] = jnp.zeros_like(acc_out)
        acc_gn[...] = jnp.zeros_like(acc_gn)
        small_ref[...] = jnp.zeros_like(small_ref)

    bias_sum = jnp.zeros((8, chunk), f32)
    for m in range(micro):
        for rows in blocks(count, TILE):
            hidden, slope = gelu_pair(dot(n2_ref[m, rows], wup) + bias)
            hidden = hidden.astype(bf16)
            ga = (dot_nt(gm_ref[m, rows], wdown) * slope).astype(bf16)
            hid_ref[m, rows] = hidden
            ga_ref[m, rows] = ga
            bias_sum = bias_sum + folded(ga.astype(f32))
            acc_out[m, rows] += dot(hidden, wdown)
            acc_gn[m, rows] += dot_nt(ga, wup)
    small_ref[pl.ds(4 + step, 1)] = jnp.sum(bias_sum, axis=0, keepdims=True)
    down_total = dot_tn(hid_ref[0], gm_ref[0])
    up_total = dot(n2t_ref[0], ga_ref[0])
    for m in range(1, micro):
        down_total = down_total + dot_tn(hid_ref[m], gm_ref[m])
        up_total = up_total + dot(n2t_ref[m], ga_ref[m])
    ddown_ref[...] = down_total.astype(bf16)
    dup_ref[...] = up_total.astype(bf16)

    @pl.when(step == last)
    def _():
        sums = [jnp.zeros((8, width), f32)] * 4
        for m in range(micro):
            for rows in blocks(count, 16):
                residual = res_ref[m, rows]
                out_ref[m, rows] = (residual + acc_out[m, rows] + vec_ref[12:13]).astype(bf16)
                gx, gain_part, grad = norm_rows_back(acc_gn[m, rows], residual, vec_ref[2:3])
                gm = gm_ref[m, rows].astype(f32)
                low = (gm + gx).astype(bf16)
                gb_ref[m, rows] = low
                parts = (gain_part, grad, low.astype(f32), gm)
                sums = [total + folded(part) for total, part in zip(sums, parts)]
        for k in range(4):
            small_ref[k : k + 1] = jnp.sum(sums[k], axis=0, keepdims=True)


def norm_rows_back(grad, values, gain):
    center = jnp.mean(values, axis=1, keepdims=True)
    centred = values - center
    variance = jnp.mean(centred * centred, axis=1, keepdims=True)
    scale = lax.rsqrt(variance + 1e-05)
    xh = centred * scale
    q = grad * gain
    gx = scale * (
        q - jnp.mean(q, axis=1, keepdims=True) - xh * jnp.mean(q * xh, axis=1, keepdims=True)
    )
    return gx, grad * xh, grad


def mlp(n2, n2t, gm, res, vectors, wup, wdown):
    micro, count, width = gm.shape
    chips, cores, rows, wide = wup.shape
    steps = wide // width
    per = chips // steps

    def whole(array):
        return pl.BlockSpec(array.shape, lambda i: (0,) * array.ndim)

    def shape(dims, kind=bf16):
        return jax.ShapeDtypeStruct(dims, kind)

    tokens = pl.BlockSpec((micro, count, width), lambda i: (0, 0, 0))
    return pl.pallas_call(
        mlp_kernel,
        grid=(steps,),
        in_specs=[
            whole(n2), whole(n2t), whole(gm), whole(res), whole(vectors),
            pl.BlockSpec((chips, cores, rows, width), lambda i: (0, 0, 0, i)),
            pl.BlockSpec((per, cores, wdown.shape[2], width), lambda i: (i, 0, 0, 0)),
        ],
        out_specs=[
            tokens, tokens,
            pl.BlockSpec((width, width), lambda i: (0, i)),
            pl.BlockSpec((width, width), lambda i: (i, 0)),
            pl.BlockSpec((4 + steps, width), lambda i: (0, 0)),
        ],
        out_shape=[
            shape((micro, count, width)),
            shape((micro, count, width)),
            shape((width, wide)),
            shape((wide, width)),
            shape((4 + steps, width), f32),
        ],
        scratch_shapes=[
            pltpu.VMEM((micro, count, width), f32),
            pltpu.VMEM((micro, count, width), f32),
            pltpu.VMEM((micro, count, width), bf16),
            pltpu.VMEM((micro, count, width), bf16),
        ],
        compiler_params=pltpu.CompilerParams(vmem_limit_bytes=63 * 1024 * 1024),
        name="mlp",
    )(n2, n2t, gm, res, vectors, wup, wdown)


def update_kernel(rates, firsts, *refs):
    count = len(rates)
    kept_in, kept_out, refs = refs[0], refs[4 * count + 1], refs[1 : 4 * count + 1] + refs[4 * count + 2 :]
    kept_out[...] = kept_in[...]
    ins, outs = refs[: 4 * count], refs[4 * count :]
    for i, (rate, first) in enumerate(zip(rates, firsts)):
        grad_ref, weight_ref, moment_ref, average_ref = ins[4 * i : 4 * i + 4]
        rows, columns = weight_ref.shape
        stepped = nesterov(
            weight_ref[...], moment_ref[...], average_ref[...],
            grad_ref[first : first + rows, :columns], rate,
        )
        for out, value in zip(outs[4 * i : 4 * i + 4], stepped):
            out[...] = value


def update(kept, sets):
    steps = 4
    held = pl.BlockSpec(
        (kept.shape[0], kept.shape[1] // steps, kept.shape[2]), lambda i: (0, i, 0)
    )
    arrays, in_specs, out_specs = [kept], [held], [held]
    shapes = [jax.ShapeDtypeStruct(kept.shape, kept.dtype)]

    def spec(shape, cut):
        if cut is None:
            return pl.BlockSpec(shape, lambda i: (0, 0))
        if cut:
            return pl.BlockSpec((shape[0], shape[1] // steps), lambda i: (0, i))
        return pl.BlockSpec((shape[0] // steps, shape[1]), lambda i: (i, 0))

    for grad, weight, moment, average, rate, first, cut in sets:
        arrays += [grad, weight, moment, average]
        in_specs += [spec(grad.shape, cut)] + [spec(weight.shape, cut)] * 3
        out_specs += [spec(weight.shape, cut)] * 4
        shapes += [jax.ShapeDtypeStruct(weight.shape, f32)] * 4
    made = pl.pallas_call(
        functools.partial(update_kernel, [s[4] for s in sets], [s[5] for s in sets]),
        grid=(steps,),
        in_specs=in_specs,
        out_specs=out_specs,
        out_shape=shapes,
        compiler_params=pltpu.CompilerParams(vmem_limit_bytes=63 * 1024 * 1024),
        name="update",
    )(*arrays)
    return made[0], [made[4 * i + 1 : 4 * i + 5] for i in range(len(sets))]


GROUP = 32
HALF = 384


def back_kernel(size, names, *refs):
    ref = types.SimpleNamespace(**dict(zip(names, refs)))
    gb, vec, table, table_back = ref.gb, ref.vec, ref.table, ref.back
    micro, count, width = gb.shape
    slot = 2 * count
    tiles = width // TILE
    ring = Ring(size)
    gw, gc, gcr, gz = ref.gw, ref.gc, ref.gcr, ref.gz
    vsum, nsum, fsum = ref.vsum, ref.nsum, ref.fsum
    one, two = ref.one, ref.two
    gate, turned = ref.gate, ref.turned
    inside = jnp.where(ring.pos < 1, 1.0, 0.0).astype(f32)
    first_half, second_half = ring.pos == 0, ring.pos == 1
    copies = Copies(ref.copy_sems)
    gate_copies = [
        copies.start(ref.s.at[j, :, :, pl.ds(0, TILE)], gate.at[j]) for j in range(tiles)
    ]
    wout = ref.din.at[0]
    wout_copy = copies.start(ref.wout, wout)
    turned_copy = copies.start(ref.yt, turned)

    greet_all(ring)
    red = {}

    def parts_of(name):
        return [getattr(ref, name + str(k)) for k in range(6)]

    down = Reduction(ring, -1, ref.ddown, *parts_of("down"), ref.down_stage, ref.down_stage_sems)
    up = Reduction(ring, 1, ref.dup, *parts_of("up"), ref.up_stage, ref.up_stage_sems)
    out = Reduction(ring, -1, ref.dout, *parts_of("out"))
    inner = [
        Reduction(ring, 1 - 2 * (j % 2), ref.din.at[j], *[part.at[j] for part in parts_of("in")])
        for j in range(tiles)
    ]
    down.begin()
    up.begin()
    vsum[...] = jnp.zeros_like(vsum)
    nsum[...] = jnp.zeros_like(nsum)
    small = ref.small
    for j in range(tiles):
        lane, base = slice(j * TILE, (j + 1) * TILE), j * GROUP
        vsum[base + 2 : base + 4] = small[0:2, lane]
        vsum[base + 7 : base + 8] = small[2:3, lane]
        vsum[base + 12 : base + 13] = small[3:4, lane]
        vsum[base + 8 : base + 12] = small[4:8, lane]

    crossing = []
    wout_copy.wait()
    for j in range(tiles):
        gate_copies[j].wait()
        weight = wout[...].reshape(width, width)[j * TILE : (j + 1) * TILE]

        @pl.loop(0, micro)
        def _(m):
            one[:count] = dot_nt(gb[m], weight)
            length = ref.lens[0, m] - ring.pos * count
            for rows in blocks(count, 32):
                mask = valid_rows(length, rows.start, 32, TILE)
                grad = mask * one[rows].astype(bf16).astype(f32)
                gw[j, m, rows] = grad.astype(bf16)
                gc[j, m, rows] = (grad * gate[j, m, rows].astype(f32)).astype(bf16)

        copy = remote(
            gc.at[j], gcr.at[j], ref.gc_sem.at[0, j], ref.gc_sem.at[1, j], ring.across
        )
        copy.start()
        crossing.append(copy)
    turned_copy.wait()

    @pl.loop(0, tiles)
    def _(j):
        cols = pl.ds(pl.multiple_of(j * TILE, TILE), TILE)
        total = dot(turned[0], gb[0, :, cols])
        for m in range(1, micro):
            total = total + dot(turned[m], gb[m, :, cols])
        dout = ref.dout
        dout[:, :, :, cols] = total.astype(bf16).reshape(dout.shape[:3] + (TILE,))

    turned_copy = copies.start(ref.nt, turned)
    out.begin()
    down.merge()
    up.merge()

    parity = 1.0 - 2.0 * (lax.broadcasted_iota(jnp.int32, (16, TILE), 0) % 2).astype(f32)
    gk = ref.gk
    gbuf, zbuf, spec = ref.gbuf, ref.zbuf, ref.spec
    first_rows, next_rows = ref.first_rows, ref.next_rows

    def loads(j, m, at):
        made = [
            (ref.s.at[j, m, :, pl.ds(TILE, 2 * TILE)], ref.s_buf.at[at]),
            (ref.z.at[j, m], ref.z_buf.at[at]),
            (ref.uhat.at[j, m], ref.u_buf.at[at]),
            (ref.conv.at[j, m], ref.c_buf.at[at]),
        ]
        return [
            pltpu.make_async_copy(src, dst, ref.load_sems.at[at, i])
            for i, (src, dst) in enumerate(made)
        ]

    def load_kernel(j):
        return pltpu.make_async_copy(ref.kern.at[j], ref.k_buf, ref.kernel_sem.at[0])

    def start_loads(j, m, at):
        for copy in loads(j, m, at):
            copy.start()

    start_loads(0, 0, 0)
    load_kernel(0).start()
    gbuf[:, count:] = jnp.zeros_like(gbuf[:, count:])

    def unmix(j):
        crossing[j].wait_recv()
        load_kernel(j).wait()
        lane = slice(j * TILE, (j + 1) * TILE)
        kn = ref.k_buf

        @pl.loop(0, micro)
        def _(m):
            at = lax.rem(j * micro + m, 2)
            for copy in loads(j, m, at):
                copy.wait()

            @pl.when(m + 1 < micro)
            def _():
                start_loads(j, m + 1, 1 - at)

            if j + 1 < tiles:

                @pl.when(m + 1 == micro)
                def _():
                    start_loads(j + 1, 0, 1 - at)

            one[...] = dot(table[...], gc[j, m])
            keep = jnp.where(m > 0, 1.0, 0.0).astype(f32)
            uh = ref.u_buf

            def filter_grad(d, re, im, gr, gi):
                ur, ui = uh[at, d, re].astype(f32), uh[at, d, im].astype(f32)
                gk[d, re] = gk[d, re] * keep + (ur * gr + ui * gi)
                gk[d, im] = gk[d, im] * keep + (ur * gi - ui * gr)

            @pl.when(first_half)
            def _():
                two[...] = dot(table[...], gcr[j, m])
                for re in blocks(count, 16):
                    im = slice(re.start + count, re.stop + count)
                    gr, gi, hr, hi = one[re], one[im], two[re], two[im]
                    k0r, k0i = kn[0, re].astype(f32), kn[0, im].astype(f32)
                    k1r, k1i = kn[1, re].astype(f32), kn[1, im].astype(f32)
                    spec[re] = (k0r * gr + k0i * gi + k1r * hr + k1i * hi).astype(bf16)
                    spec[im] = (k0r * gi - k0i * gr + k1r * hi - k1i * hr).astype(bf16)
                    filter_grad(0, re, im, gr, gi)

            @pl.when(second_half)
            def _():
                for re in blocks(count, 16):
                    im = slice(re.start + count, re.stop + count)
                    gr, gi = one[re], one[im]
                    k0r, k0i = kn[0, re].astype(f32), kn[0, im].astype(f32)
                    spec[re] = (k0r * gr + k0i * gi).astype(bf16)
                    spec[im] = (k0r * gi - k0i * gr).astype(bf16)
                    filter_grad(0, re, im, gr, gi)
                    filter_grad(1, re, im, gr, gi)

            two[:count] = dot(table_back[...], spec[...])
            skip_sum = jnp.zeros((8, TILE), f32)
            for rows in blocks(count, 32):
                x1 = ref.s_buf[at, rows, :TILE].astype(f32)
                v = ref.s_buf[at, rows, TILE:].astype(f32)
                grad_w = gw[j, m, rows].astype(f32)
                gc_full = grad_w * gate[j, m, rows].astype(f32)
                gu = two[rows] * (1.0 / count) + vec[25:26, lane] * gc_full
                skip_sum = skip_sum + folded(gc_full * (x1 * v))
                grads = (grad_w * ref.c_buf[at, rows].astype(f32), gu * v, gu * x1)
                for p in range(3):
                    low = grads[p].astype(bf16)
                    gbuf[p, rows] = low.astype(f32)
                    if rows.start == 0:
                        first_rows[j, m, :, p * TILE : (p + 1) * TILE] = low[:16]
            vsum[j * GROUP + 25 : j * GROUP + 26] += jnp.sum(skip_sum, axis=0, keepdims=True)
            for p in range(3):
                cols = slice(p * TILE, (p + 1) * TILE)
                zbuf[:16] = ref.zh[j, m, :, cols].astype(f32)
                for rows in blocks(count, 32):
                    zbuf[rows.start + 16 : rows.stop + 16] = ref.z_buf[at, rows, cols].astype(f32)
                taps = [vec[13 + 3 * k + p : 14 + 3 * k + p, lane] for k in range(3)]
                sums = [jnp.zeros((8, TILE), f32) for _ in range(4)]
                for rows in blocks(count, 32):
                    first = rows.start
                    grad = gbuf[p, rows]
                    gz[j, m, rows, cols] = (
                        taps[0] * grad
                        + taps[1] * gbuf[p, first + 1 : first + 33]
                        + taps[2] * gbuf[p, first + 2 : first + 34]
                    ).astype(bf16)
                    for k in range(3):
                        sums[k] = sums[k] + folded(grad * zbuf[first + 16 - k : first + 48 - k])
                    sums[3] = sums[3] + folded(grad)
                gz[j, m, count - 16 :, cols] = gbuf[p, count - 16 : count].astype(bf16)
                for k in range(4):
                    row = j * GROUP + 13 + 3 * k + p
                    vsum[row : row + 1] += jnp.sum(sums[k], axis=0, keepdims=True)

        if j + 1 < tiles:
            load_kernel(j + 1).start()
        edge = remote(
            first_rows.at[j], next_rows.at[j], ref.edge_sem.at[0, j],
            ref.edge_sem.at[1, j], ring.across,
        )
        edge.start()
        @pl.when(first_half)
        def _():
            for re in blocks(2 * count, 16):
                spec[re] = gk[0, re].astype(bf16)
            gate[j, 1] = jnp.zeros_like(gate[j, 1])

        @pl.when(second_half)
        def _():
            for re in blocks(2 * count, 16):
                spec[re] = gk[1, re].astype(bf16)
            two[count:] = dot(table_back[...], spec[...])
            for rows in blocks(count, 16):
                second = two[rows.start + count : rows.stop + count]
                gate[j, 1, rows] = (second * (1.0 / count)).astype(bf16)
            for re in blocks(count, 16):
                im = slice(re.start + count, re.stop + count)
                spec[re] = (gk[0, re] + parity * gk[1, im]).astype(bf16)
                spec[im] = (gk[0, im] - parity * gk[1, re]).astype(bf16)

        two[:count] = dot(table_back[...], spec[...])
        for rows in blocks(count, 16):
            gate[j, 0, rows] = (two[rows] * (1.0 / count)).astype(bf16)
        return edge

    def project_back(j, edge):
        edge.wait_recv()
        lane = slice(j * TILE, (j + 1) * TILE)
        ebuf = ref.ebuf
        for m in range(micro):
            for p in range(3):
                cols = slice(p * TILE, (p + 1) * TILE)
                own = gz[j, m, count - 16 :, cols].astype(f32)
                ebuf[:16] = own
                ebuf[16:] = next_rows[j, m, :, cols].astype(f32) * inside
                gz[j, m, count - 16 :, cols] = (
                    vec[13 + p : 14 + p, lane] * own
                    + vec[16 + p : 17 + p, lane] * ebuf[1:17]
                    + vec[19 + p : 20 + p, lane] * ebuf[2:18]
                ).astype(bf16)
        for p in range(3):
            cols = slice(p * TILE, (p + 1) * TILE)
            total = dot(turned[0], gz[j, 0, :, cols])
            for m in range(1, micro):
                total = total + dot(turned[m], gz[j, m, :, cols])
            din = ref.din
            din[j, :, :, :, cols] = total.astype(bf16).reshape(din.shape[1:4] + (TILE,))
            bias = jnp.zeros((8, TILE), f32)
            for m in range(micro):
                for rows in blocks(count, 32):
                    bias = bias + folded(gz[j, m, rows, cols].astype(f32))
            row = j * GROUP + 4 + p
            vsum[row : row + 1] = jnp.sum(bias, axis=0, keepdims=True)
        inner[j].begin()

    edges = [unmix(0)]
    down.advance(1)
    up.advance(1)
    out.merge()
    edges.append(unmix(1))
    turned_copy.wait()
    project_back(0, edges[0])
    down.advance(2)
    up.advance(2)
    out.advance(1)
    inner[0].merge()
    edges.append(unmix(2))
    project_back(1, edges[1])
    x_copies = [
        copies.start(ref.x.at[:, :, pl.ds(j * TILE, TILE)], gcr.at[j]) for j in range(tiles)
    ]
    pre_copies = [
        copies.start(
            ref.pre.at[:, pl.ds(t * TILE, TILE)], one.at[pl.ds(t * 3 * HID, 3 * HID)]
        )
        for t in range(slot // TILE)
    ]
    down.advance(3)
    up.advance(3)
    inner[1].merge()
    project_back(2, edges[2])
    out.advance(2)
    inner[0].advance(1)
    inner[1].advance(1)
    for copy in x_copies:
        copy.wait()
    for copy in crossing:
        copy.wait_send()

    def first_norm(m):
        for t in range(tiles):
            total = 0.0
            for j in range(tiles):
                weight = ref.win[j].reshape(width, 3 * TILE)[t * TILE : (t + 1) * TILE]
                total = total + dot_nt(gz[j, m], weight)
            gbuf[t, :count] = total
        sums = [jnp.zeros((8, width), f32)] * 2
        for rows in blocks(count, 16):
            tokens = jnp.concatenate([gcr[j, m, rows] for j in range(tiles)], axis=1)
            grad = jnp.concatenate([gbuf[t, rows] for t in range(tiles)], axis=1)
            gx, gain_part, shift_part = norm_rows_back(grad, tokens.astype(f32), vec[0:1])
            sums = [sums[0] + folded(gain_part), sums[1] + folded(shift_part)]
            total = (gb[m, rows].astype(f32) + gx).astype(bf16)
            for j in range(tiles):
                gc[j, m, rows] = total[:, j * TILE : (j + 1) * TILE]
        for k in range(2):
            total = jnp.sum(sums[k], axis=0, keepdims=True)
            for j in range(tiles):
                row = j * GROUP + k
                vsum[row : row + 1] += total[:, j * TILE : (j + 1) * TILE]

    def filter_back():
        ref.net_sum[...] = jnp.zeros_like(ref.net_sum)
        net = ref.net
        for copy in pre_copies:
            copy.wait()

        def pre(first, last):
            return jnp.concatenate(
                [
                    one[t * 3 * HID + first : t * 3 * HID + last]
                    for t in range(slot // TILE)
                ],
                axis=1,
            )

        frequency = net[:, EMB + 3 + 2 * HID : EMB + 4 + 2 * HID]
        rates = ref.rate[...].reshape(1, width)
        final_low = ref.final[...].astype(bf16)
        acts, slopes = [], []
        for i in range(3):
            pairs = [
                sin_cos(frequency[part] * pre(i * HID + part.start, i * HID + part.stop))
                for part in blocks(HID, 16)
            ]
            acts.append(jnp.concatenate([pair[0] for pair in pairs], axis=0))
            slopes.append(jnp.concatenate([pair[1] for pair in pairs], axis=0))
        last = acts[2].astype(bf16)
        grad = jnp.zeros((HID, slot), f32)
        for j in range(tiles):
            lane = slice(j * TILE, (j + 1) * TILE)
            for half in range(2):
                for rows in blocks(count, 32):
                    first = half * count + rows.start
                    at_row = lax.broadcasted_iota(jnp.int32, (32, TILE), 0) + first
                    window = jnp.exp(at_row.astype(f32) * (rates[:, lane] * (-1.0 / slot))) + 0.05
                    spec[first : first + 32] = (gate[j, half, rows].astype(f32) * window).astype(bf16)
            total = dot(last, spec[...])
            for part in blocks(TILE, 128):
                at = j * TILE + part.start
                row, column = at // HALF * HID, at % HALF
                fsum[row : row + HID, column : column + 128] = total[:, part]
            grad = grad + dot_nt(final_low[:, lane], spec[...])
        freq_sum = jnp.zeros((HID, 1), f32)

        def put(first, values):
            ref.net_sum[:, first : first + values.shape[1]] = values

        for i in (2, 1, 0):
            turn = grad * slopes[i]
            freq_sum = freq_sum + jnp.sum(turn * pre(i * HID, (i + 1) * HID), axis=1, keepdims=True)
            grad = turn * frequency
            below = ref.feature[...] if i == 0 else acts[i - 1]
            made = lax.dot_general(
                grad, below, (((1,), (1,)), ((), ())), precision=highest,
                preferred_element_type=f32,
            )
            if i == 0:
                put(0, made[:, : EMB + 1])
            else:
                first = EMB + 1 + (i - 1) * (HID + 1)
                put(first, made)
                put(first + HID, jnp.sum(grad, axis=1, keepdims=True))
                grad = lax.dot_general(
                    net[:, first : first + HID], grad, (((0,), (0,)), ((), ())),
                    precision=highest, preferred_element_type=f32,
                )
        put(EMB + 3 + 2 * HID, freq_sum)
        nsum[:HID] = ref.net_sum[:, :128]
        nsum[HID:] = ref.net_sum[:, 128:]

    smalls = []
    for values, name in ((fsum, "f"), (nsum, "n"), (vsum, "v")):
        parts = [getattr(ref, name + str(k)) for k in range(5)]
        smalls.append(SmallSum(ring, values, *parts))
    first_norm(0)
    inner[2].merge()
    down.collect()
    up.collect()
    out.advance(3)
    inner[0].advance(2)
    inner[1].advance(2)
    filter_back()
    for work in smalls[:2]:
        work.begin()
    inner[2].advance(1)
    inner[0].advance(3)
    inner[1].advance(3)
    out.collect()
    for m in range(1, micro):
        first_norm(m)
    smalls[2].begin()
    for j in range(tiles):
        copies.out(gc.at[j], ref.input_grad.at[:, :, pl.ds(j * TILE, TILE)])
    for work in smalls[:2]:
        work.add_up()
    inner[2].advance(2)
    inner[0].collect()
    inner[1].collect()
    psum = ref.proj_sum
    wide = psum.shape[1] - 4 * width
    ref.down_sum[...] = down.result()
    smalls[2].add_up()
    for work in smalls[:2]:
        work.spread()
    psum[:, 4 * width : 4 * width + wide] = up.result()
    psum[:, 3 * width : 4 * width] = out.result()
    inner[2].advance(3)
    smalls[2].spread()
    inner[2].collect()
    for j in range(tiles):
        total = inner[j].result()
        for p in range(3):
            first = p * width + j * TILE
            psum[:, first : first + TILE] = total[:, p * TILE : (p + 1) * TILE]
    for work in smalls:
        work.finish()
    for part in blocks(width, 128):
        row, column = part.start // HALF * HID, part.start % HALF
        ref.final_sum[:, part] = smalls[0].sums[row : row + HID, column : column + 128]
    ref.net_sum[:, :128] = smalls[1].sums[:HID]
    ref.net_sum[:, 128:] = smalls[1].sums[HID:]
    for j in range(tiles):
        ref.vec_sum[:, j * TILE : (j + 1) * TILE] = smalls[2].sums[j * GROUP : (j + 1) * GROUP]
    for work in [down, up, out] + inner:
        work.finish()
    for edge in edges:
        edge.wait_send()
    copies.finish()


def back(size, arrays):
    chips = size // 2
    micro, count, width = arrays["gb"].shape
    rows, wide = arrays["dup"].shape[2:]
    down_rows = arrays["ddown"].shape[2]
    tiles = width // TILE
    vmem = pl.BlockSpec(memory_space=pltpu.VMEM)
    anywhere = pl.BlockSpec(memory_space=pl.ANY)
    smem = pl.BlockSpec(memory_space=pltpu.SMEM)
    near = ("gb", "vec", "net", "final", "rate", "table", "back", "win", "zh", "small", "feature")
    small_rows = 8 * size
    outs = dict(
        input_grad=((micro, count, width), bf16),
        proj_sum=((rows, 4 * width + wide), f32),
        down_sum=((down_rows, width), f32),
        vec_sum=((GROUP, width), f32),
        final_sum=((HID, width), f32),
        net_sum=((HID, 256), f32),
    )
    dma = pltpu.SemaphoreType.DMA
    tile_tokens = (tiles, micro, count, TILE)
    edge_rows = (tiles, micro, 16, 3 * TILE)
    scratch = dict(
        din=pltpu.VMEM((tiles, chips, 2, rows, 3 * TILE), bf16),
        dout=pltpu.VMEM((chips, 2, rows, width), bf16),
        gw=pltpu.VMEM(tile_tokens, bf16),
        gc=pltpu.VMEM(tile_tokens, bf16),
        gcr=pltpu.VMEM(tile_tokens, bf16),
        gate=pltpu.VMEM(tile_tokens, bf16),
        gz=pltpu.VMEM((tiles, micro, count, 3 * TILE), bf16),
        turned=pltpu.VMEM((micro, width, count), bf16),
        vsum=pltpu.VMEM((small_rows, TILE), f32),
        nsum=pltpu.VMEM((small_rows, 128), f32),
        fsum=pltpu.VMEM((small_rows, HALF), f32),
        gk=pltpu.VMEM((2, 2 * count, TILE), f32),
        gbuf=pltpu.VMEM((3, count + 16, TILE), f32),
        one=pltpu.VMEM((2 * count, TILE), f32),
        two=pltpu.VMEM((2 * count, TILE), f32),
        zbuf=pltpu.VMEM((count + 16, TILE), f32),
        ebuf=pltpu.VMEM((32, TILE), f32),
        spec=pltpu.VMEM((2 * count, TILE), bf16),
        first_rows=pltpu.VMEM(edge_rows, bf16),
        next_rows=pltpu.VMEM(edge_rows, bf16),
        s_buf=pltpu.VMEM((2, count, 2 * TILE), bf16),
        z_buf=pltpu.VMEM((2, count, 3 * TILE), bf16),
        u_buf=pltpu.VMEM((2, 2, 2 * count, TILE), bf16),
        c_buf=pltpu.VMEM((2, count, TILE), bf16),
        k_buf=pltpu.VMEM((2, 2 * count, TILE), bf16),
        load_sems=dma((2, 4)),
        kernel_sem=dma((1,)),
        gc_sem=dma((2, tiles)),
        edge_sem=dma((2, tiles)),
        copy_sems=dma((24,)),
        up_stage=pltpu.VMEM((2, rows, wide), bf16),
        down_stage=pltpu.VMEM((2, down_rows, width), bf16),
        up_stage_sems=dma((2,)),
        down_stage_sems=dma((2,)),
    )
    ups, downs = chips // 2, (chips - 1) // 2
    for name, lead, dims in (
        ("up", (), (rows, wide)), ("down", (), (down_rows, width)), ("out", (), (rows, width)),
        ("in", (tiles,), (rows, 3 * TILE)),
    ):
        made = [pltpu.VMEM(lead + (count,) + dims, bf16) for count in (chips, ups, downs)]
        made += [pltpu.VMEM(lead + dims, bf16)] * 2 + [dma(lead + (2, 2 + ups + downs))]
        for k, part in enumerate(made):
            scratch[name + str(k)] = part
    for name, columns in (("v", TILE), ("n", 128), ("f", HALF)):
        made = small_scratch(size, small_rows, columns)
        made.insert(3, pltpu.VMEM((small_rows, columns), f32))
        for k, part in enumerate(made):
            scratch[name + str(k)] = part
    names = tuple(arrays) + tuple(outs) + tuple(scratch)
    return pl.pallas_call(
        functools.partial(back_kernel, size, names),
        out_shape=[jax.ShapeDtypeStruct(*kind) for kind in outs.values()],
        in_specs=[
            smem if name == "lens" else vmem if name in near else anywhere for name in arrays
        ],
        out_specs=[anywhere] + [vmem] * (len(outs) - 1),
        scratch_shapes=list(scratch.values()),
        compiler_params=pltpu.CompilerParams(
            collective_id=1, has_side_effects=True, vmem_limit_bytes=255 * 1024 * 256
        ),
        name="back",
    )(*arrays.values())


def fits(size, groups, tokens, proj_weights, down_weights):
    micro, _, count, width = tokens.shape
    wide = down_weights.shape[0] * size
    return (
        groups == 2
        and size % 4 == 0
        and size == 16
        and proj_weights.shape[0] % 16 == 0
        and down_weights.shape[0] % 16 == 0
        and count % TILE == 0
        and width == 3 * TILE
        and micro >= groups
        and 3 * HID <= TILE
        and micro * count <= 1024
        and wide == 4 * width
        and proj_weights.shape[1] == 4 * width + wide
    )


def on_device_tuned(
    block_input,
    out_grad,
    lengths,
    decay_rates,
    proj_weights,
    proj_moment,
    proj_average,
    down_weights,
    down_moment,
    down_average,
    vectors,
    vector_moment,
    vector_average,
    filter_net,
    net_moment,
    net_average,
    filter_out,
    final_moment,
    final_average,
):
    micro, _, count, width = block_input.shape
    size = lax.axis_size("seq")
    tokens = block_input.reshape(micro, count, width)
    plain_table = transform_table(count)
    table = jnp.asarray(plain_table, dtype=bf16)
    table_back = jnp.asarray(plain_table.T, dtype=bf16)
    feature = jnp.asarray(feature_table(count * lax.axis_size("pos")))
    shared = dict(
        x=tokens, lens=lengths.T, vec=vectors, net=filter_net.T, final=filter_out,
        rate=decay_rates, table=table, back=table_back, feature=feature,
    )
    made = types.SimpleNamespace(**front(size, dict(shared, proj=proj_weights, down=down_weights)))
    block_output, branch_grad, up_step, down_step, small = mlp(
        made.n2, made.n2t, out_grad.reshape(micro, count, width), made.res, vectors,
        made.wup, made.wdown,
    )
    chips = size // 2
    input_grad, proj_sum, down_sum, vector_sum, final_sum, net_sum = back(
        size,
        dict(
            shared, win=made.win, wout=made.wout, z=made.z, zh=made.zh, s=made.s, conv=made.conv,
            uhat=made.uhat, kern=made.kern, nt=made.nt, yt=made.yt, pre=made.pre,
            gb=branch_grad, small=small,
            dup=up_step.reshape(chips, 2, -1, up_step.shape[1]),
            ddown=down_step.reshape(chips, 2, -1, width),
        ),
    )
    input_grad, steps = update(
        input_grad,
        [
            (proj_sum, proj_weights, proj_moment, proj_average, 0.0001, 0, 1),
            (down_sum, down_weights, down_moment, down_average, 0.0001, 0, 0),
            (vector_sum, vectors, vector_moment, vector_average, 0.001, 0, None),
            (net_sum, filter_net.T, net_moment.T, net_average.T, 0.0001, 0, None),
            (final_sum, filter_out, final_moment, final_average, 2e-06, 0, None),
        ]
    )
    steps[3] = [array.T for array in steps[3]]
    return (
        block_output.reshape(block_input.shape),
        input_grad.reshape(block_input.shape),
        *steps[0], *steps[1], *steps[2], *steps[3], *steps[4],
    )


def on_device_plain(
    block_input,
    out_grad,
    lengths,
    decay_rates,
    proj_weights,
    proj_moment,
    proj_average,
    down_weights,
    down_moment,
    down_average,
    vectors,
    vector_moment,
    vector_average,
    filter_net,
    net_moment,
    net_average,
    filter_out,
    final_moment,
    final_average,
):
    micro = block_input.shape[0]
    count = block_input.shape[2]
    width = block_input.shape[3]
    groups = lax.axis_size("pos")
    slot_length = count * groups
    tokens_all = micro * count
    group = lax.axis_index("pos")
    tap = vectors[13:22].reshape(3, 3 * width)
    short_bias = vectors[22:25].reshape(-1)
    in_bias = vectors[4:7].reshape(-1)
    up_bias = vectors[8:12].reshape(-1)
    skip = vectors[25]

    low_rows = proj_weights.astype(bf16)
    in_weight = lax.all_gather(low_rows[:, : 3 * width], "seq", axis=0, tiled=True)
    out_weight = lax.all_gather(low_rows[:, 3 * width : 4 * width], "seq", axis=0, tiled=True)
    up_weight = lax.all_gather(low_rows[:, 4 * width :], "seq", axis=0, tiled=True)
    down_weight = lax.all_gather(down_weights.astype(bf16), "seq", axis=0, tiled=True)

    table = jnp.asarray(transform_table(count))
    table_low = table.astype(bf16)
    every = jnp.arange(slot_length, dtype=jnp.int32)

    def make_filter(net_values, final_values):
        return filter_fn(net_values, final_values, decay_rates, every, slot_length)

    filters, filter_back = jax.vjp(make_filter, filter_net, filter_out)
    pieces = filters.reshape(groups, count, width)
    spectra = [
        jnp.dot(table, pieces[d], precision=lax.Precision.HIGH, preferred_element_type=f32)
        for d in range(groups)
    ]
    kernels = [spectra[0]] + [spectra[d] + turned(spectra[d - 1], 1.0) for d in range(1, groups)]

    def transform(values):
        return jnp.stack([dot(table_low, values[m]) for m in range(micro)])

    def transform_back(spectrum):
        low = spectrum.astype(bf16)
        return jnp.stack([dot_tn(table_low, low[m]) for m in range(micro)]) * (1.0 / count)

    tokens_low = block_input[:, 0]
    before = passed_along(tokens_low[:, -2:], "pos", 1)
    tokens = tokens_low.astype(f32).reshape(tokens_all, width)
    xh_one, scale_one = norm_parts(tokens)
    normed = (xh_one * vectors[0] + vectors[1]).astype(bf16)
    xh_before, _ = norm_parts(before.astype(f32).reshape(micro * 2, width))
    normed_before = (xh_before * vectors[0] + vectors[1]).astype(bf16)
    z = (dot(normed, in_weight) + in_bias).reshape(micro, count, 3 * width)
    z_before = (dot(normed_before, in_weight) + in_bias).reshape(micro, 2, 3 * width)
    z_before = jnp.where(group > 0, z_before, 0.0)
    z_long = jnp.concatenate([z_before, z], axis=1)
    short = (
        tap[0] * z_long[:, 2:] + tap[1] * z_long[:, 1:-1] + tap[2] * z_long[:, :-2] + short_bias
    ).astype(bf16)
    x0 = short[:, :, :width].astype(f32)
    x1 = short[:, :, width : 2 * width].astype(f32)
    v = short[:, :, 2 * width :].astype(f32)

    u = x1 * v
    u_low = u.astype(bf16)
    u_hat = [transform(u_low)]
    for d in range(1, groups):
        u_hat.append(transform(passed_along(u_low, "pos", d)))
    total = product(kernels[0], u_hat[0])
    for d in range(1, groups):
        total = total + product(kernels[d], u_hat[d])
    conv = transform_back(total) + skip * u
    here = group * count + jnp.arange(count, dtype=jnp.int32)
    mask = (here[None, :] < lengths[:, 0][:, None]).astype(f32)[:, :, None]
    y = (mask * x0 * conv).astype(bf16).reshape(tokens_all, width)
    residual = tokens + dot(y, out_weight) + vectors[7]
    xh_two, scale_two = norm_parts(residual)
    normed_two = (xh_two * vectors[2] + vectors[3]).astype(bf16)

    cot_low = out_grad[:, 0].reshape(tokens_all, width)
    cot = cot_low.astype(f32)
    pre = dot(normed_two, up_weight) + up_bias
    hidden, gelu_back = jax.vjp(jax.nn.gelu, pre)
    hidden_low = hidden.astype(bf16)
    block_output = (residual + dot(hidden_low, down_weight) + vectors[12]).astype(bf16)
    pre_grad = gelu_back(dot_nt(cot_low, down_weight))[0].astype(bf16)
    down_step = dot_tn(hidden_low, cot_low)
    up_step = dot_tn(normed_two, pre_grad)
    normed_two_grad = dot_nt(pre_grad, up_weight)
    part, gain_two, shift_two = norm_back(normed_two_grad, xh_two, scale_two, vectors[2])
    residual_grad = cot + part
    branch_low = residual_grad.astype(bf16)
    out_step = dot_tn(y, branch_low)
    y_grad = dot_nt(branch_low, out_weight).astype(bf16).astype(f32).reshape(micro, count, width)

    gw = mask * y_grad
    gx0 = gw * conv
    gc = gw * x0
    gc_low = gc.astype(bf16)
    skip_grad = jnp.sum(gc * u, axis=(0, 1))
    gc_hat = [transform(gc_low)]
    for d in range(1, groups):
        gc_hat.append(transform(passed_along(gc_low, "pos", -d)))
    back = product_conj(kernels[0], gc_hat[0])
    for d in range(1, groups):
        back = back + product_conj(kernels[d], gc_hat[d])
    gu = transform_back(back) + skip * gc
    kernel_grads = [jnp.sum(product_conj(u_hat[d], gc_hat[0]), axis=0) for d in range(groups)]
    filter_grads = []
    for d in range(groups):
        got = kernel_grads[d]
        if d + 1 < groups:
            got = got + turned(kernel_grads[d + 1], -1.0)
        filter_grads.append(dot_tn(table_low, got.astype(bf16)) * (1.0 / count))
    net_local, final_local = filter_back(jnp.concatenate(filter_grads, axis=0))
    short_grad = jnp.concatenate([gx0, gu * v, gu * x1], axis=-1).astype(bf16)
    after = passed_along(short_grad[:, :2], "pos", -1)
    short_long = jnp.concatenate([short_grad, after], axis=1).astype(f32)
    z_grad = (
        tap[0] * short_long[:, :-2] + tap[1] * short_long[:, 1:-1] + tap[2] * short_long[:, 2:]
    ).astype(bf16)
    here_grad = short_long[:, :-2]
    tap_grads = [
        jnp.sum(here_grad * z_long[:, 2 - k : 2 - k + count], axis=(0, 1)) for k in range(3)
    ]
    short_bias_grad = jnp.sum(here_grad, axis=(0, 1))
    z_grad = z_grad.reshape(tokens_all, 3 * width)
    in_step = dot_tn(normed, z_grad)
    in_bias_grad = jnp.sum(z_grad.astype(f32), axis=0)
    normed_grad = dot_nt(z_grad, in_weight)
    part, gain_one, shift_one = norm_back(normed_grad, xh_one, scale_one, vectors[0])
    input_grad = (residual_grad + part).astype(bf16)

    vector_local = jnp.concatenate(
        [
            gain_one[None],
            shift_one[None],
            gain_two[None],
            shift_two[None],
            in_bias_grad.reshape(3, width),
            jnp.sum(branch_low.astype(f32), axis=0)[None],
            jnp.sum(pre_grad.astype(f32), axis=0).reshape(4, width),
            jnp.sum(cot, axis=0)[None],
            jnp.stack(tap_grads).reshape(9, width),
            short_bias_grad.reshape(3, width),
            skip_grad[None],
        ],
        axis=0,
    )
    proj_local = jnp.concatenate([in_step, out_step, up_step], axis=1).astype(bf16)
    proj_shard = lax.psum_scatter(proj_local, "seq", scatter_dimension=0, tiled=True)
    down_shard = lax.psum_scatter(down_step.astype(bf16), "seq", scatter_dimension=0, tiled=True)
    proj_sum = lax.psum(proj_shard, "pos").astype(f32)
    down_sum = lax.psum(down_shard, "pos").astype(f32)
    vector_sum, net_sum, final_sum = lax.psum(
        (vector_local, net_local, final_local), ("seq", "pos")
    )
    return (
        block_output.reshape(micro, 1, count, width),
        input_grad.reshape(micro, 1, count, width),
        *nesterov(proj_weights, proj_moment, proj_average, proj_sum, 0.0001),
        *nesterov(down_weights, down_moment, down_average, down_sum, 0.0001),
        *nesterov(vectors, vector_moment, vector_average, vector_sum, 0.001),
        *nesterov(filter_net, net_moment, net_average, net_sum, 0.0001),
        *nesterov(filter_out, final_moment, final_average, final_sum, 2e-06),
    )


def on_device(*arrays):
    tuned = fits(
        lax.axis_size("seq"), lax.axis_size("pos"), arrays[0], arrays[4], arrays[7]
    )
    return (on_device_tuned if tuned else on_device_plain)(*arrays)


def solution(mesh):
    tokens = P(None, "seq", "pos", None)
    rows = P("seq", None)
    whole = P()
    return jax.shard_map(
        on_device,
        mesh=mesh,
        in_specs=(tokens, tokens, P(None, "seq"), whole) + (rows,) * 6 + (whole,) * 9,
        out_specs=(tokens, tokens) + (rows,) * 8 + (whole,) * 12,
        check_vma=False,
    )
```

```python
import functools
import math
import types

import jax
import jax.numpy as jnp
import numpy as np
from jax import lax
from jax.experimental import pallas as pl
from jax.experimental.pallas import tpu as pltpu
from jax.sharding import PartitionSpec as P

HID = 64
EMB = 33

highest = lax.Precision.HIGHEST
f32 = jnp.float32
bf16 = jnp.bfloat16


def passed_along(block, axis, distance):
    devices = range(lax.axis_size(axis))
    route = [(i - distance, i) for i in devices if i - distance in devices]
    return lax.ppermute(block, axis, route)


def dot(a, b):
    return lax.dot_general(a, b, (((1,), (0,)), ((), ())), preferred_element_type=f32)


def dot_tn(a, b):
    return lax.dot_general(a, b, (((0,), (0,)), ((), ())), preferred_element_type=f32)


def dot_nt(a, b):
    return lax.dot_general(a, b, (((1,), (1,)), ((), ())), preferred_element_type=f32)


def features(positions, slot_length):
    band_count = (EMB - 1) // 2
    scaled = positions.astype(f32) / slot_length
    bands = 0.0001 + jnp.arange(band_count, dtype=f32) * (
        (band_count - 1 - 0.0001) / (band_count - 1)
    )
    angles = 2.0 * math.pi * scaled[:, None] * bands[None, :]
    return jnp.concatenate([scaled[:, None], jnp.cos(angles), -jnp.sin(angles)], axis=1)


def filter_fn(net_values, final_values, rates, positions, slot_length):
    embedded = features(positions, slot_length)
    frequency = net_values[EMB + 3 + 2 * HID]
    layer_one = jnp.sin(
        frequency * (jnp.dot(embedded, net_values[:EMB], precision=highest) + net_values[EMB])
    )
    layer_two = jnp.sin(
        frequency
        * (
            jnp.dot(layer_one, net_values[EMB + 1 : EMB + 1 + HID], precision=highest)
            + net_values[EMB + 1 + HID]
        )
    )
    layer_three = jnp.sin(
        frequency
        * (
            jnp.dot(layer_two, net_values[EMB + 2 + HID : EMB + 2 + 2 * HID], precision=highest)
            + net_values[EMB + 2 + 2 * HID]
        )
    )
    shaped = jnp.dot(layer_three, final_values, precision=highest)
    scaled = positions.astype(f32) / slot_length
    window = jnp.exp(-scaled[:, None] * rates[None, :]) + 0.05
    return shaped * window


def transform_table(length):
    product = np.outer(2 * np.arange(length) + 1, np.arange(length)) % (4 * length)
    angle = product.astype(np.float64) * (math.pi / (2 * length))
    return np.concatenate([np.cos(angle), -np.sin(angle)], axis=0).astype(np.float32)


def feature_table(slot_length):
    scaled = np.arange(slot_length, dtype=np.float32) / np.float32(slot_length)
    band_count = (EMB - 1) // 2
    bands = np.float32(0.0001) + np.arange(band_count, dtype=np.float32) * np.float32(
        (band_count - 1 - 0.0001) / (band_count - 1)
    )
    angles = (np.float32(2.0 * math.pi) * scaled[:, None]) * bands[None, :]
    table = np.zeros((40, slot_length), np.float32)
    table[0] = scaled
    table[1 : 1 + band_count] = np.cos(angles).T
    table[1 + band_count : EMB] = -np.sin(angles).T
    table[EMB] = 1.0
    return table


def halves(spectrum):
    half = spectrum.shape[-2] // 2
    return spectrum[..., :half, :], spectrum[..., half:, :]


def turned(spectrum, sign):
    re, im = halves(spectrum)
    parity = (1.0 - 2.0 * (jnp.arange(re.shape[-2]) % 2).astype(f32))[:, None] * sign
    return jnp.concatenate([-parity * im, parity * re], axis=-2)


def product(kernel, signal):
    kr, ki = halves(kernel)
    sr, si = halves(signal)
    return jnp.concatenate([kr * sr - ki * si, kr * si + ki * sr], axis=-2)


def product_conj(kernel, signal):
    kr, ki = halves(kernel)
    sr, si = halves(signal)
    return jnp.concatenate([kr * sr + ki * si, kr * si - ki * sr], axis=-2)


def nesterov(weight, moment, average, gradient, rate):
    moment_next = 0.9 * moment + gradient
    weight_next = weight - rate * (gradient + 0.9 * moment_next)
    average_next = 0.9 * average + 0.1 * weight_next
    return (gradient, weight_next, moment_next, average_next)


def norm_parts(values):
    center = jnp.mean(values, axis=-1, keepdims=True)
    centred = values - center
    variance = jnp.mean(centred * centred, axis=-1, keepdims=True)
    scale = lax.rsqrt(variance + 1e-05)
    return centred * scale, scale


def norm_back(grad, xh, scale, gain):
    q = grad * gain
    return (
        (q - jnp.mean(q, -1, keepdims=True) - xh * jnp.mean(q * xh, -1, keepdims=True)) * scale,
        jnp.sum(grad * xh, axis=0),
        jnp.sum(grad, axis=0),
    )


MESH = pl.DeviceIdType.MESH


class Ring:
    def __init__(self, size):
        self.size = size
        self.count = size // 2
        self.seq = lax.axis_index("seq")
        self.pos = lax.axis_index("pos")
        self.core = lax.rem(self.seq, 2)
        chip = self.seq // 2
        odd = lax.rem(chip, 2)
        self.place = (1 - odd) * (chip // 2) + odd * (self.count - 1 - chip // 2)

    def chip(self, shift):
        place = lax.rem(self.place + (shift + self.count), self.count)
        low = jnp.where(place < self.count // 2, 1, 0)
        return low * (2 * place) + (1 - low) * (2 * (self.count - 1 - place) + 1)

    def device(self, shift):
        return {"seq": 2 * self.chip(shift) + self.core}

    @property
    def sibling(self):
        return {"seq": self.seq + 1 - 2 * self.core}

    @property
    def across(self):
        return {"pos": 1 - self.pos}


def greet_all(ring):
    barrier = pltpu.get_barrier_semaphore()
    for step in range(1, ring.size):
        other = lax.rem(ring.seq + step, ring.size)
        pl.semaphore_signal(barrier, inc=1, device_id={"seq": other}, device_id_type=MESH)
    pl.semaphore_signal(barrier, inc=1, device_id=ring.across, device_id_type=MESH)
    pl.semaphore_wait(barrier, ring.size)


def remote(src, dst, send, recv, device):
    return pltpu.make_async_remote_copy(
        src_ref=src, dst_ref=dst, send_sem=send, recv_sem=recv, device_id=device,
        device_id_type=MESH,
    )


class Reduction:
    def __init__(self, ring, turn, grad, twin, up, down, own, other, sems, block=None):
        self.ring, self.turn = ring, turn
        self.grad, self.twin, self.up, self.down = grad, twin, up, down
        self.own, self.other = own, other
        self.sems = sems
        self.block = block or (lambda chip: self.grad[chip, ring.core])
        self.ups = ring.count // 2
        self.downs = (ring.count - 1) // 2

    def chip(self, shift):
        return self.ring.chip(shift * self.turn)

    def copies(self):
        ring = self.ring
        made = [(self.grad.at[:, 1 - ring.core], self.twin, ring.sibling)]
        for step in range(self.ups):
            block = self.twin.at[self.chip(self.ups - step)]
            made.append((block, self.up.at[step], ring.device(self.turn)))
        for step in range(self.downs):
            block = self.twin.at[self.chip(step - self.downs)]
            made.append((block, self.down.at[step], ring.device(-self.turn)))
        made.append((self.own, self.other, ring.across))
        return made

    def copy(self, index):
        src, dst, device = self.copies()[index]
        return remote(src, dst, self.sems.at[0, index], self.sems.at[1, index], device)

    def begin(self):
        self.copy(0).start()

    def merge(self):
        self.copy(0).wait_recv()

        def add(shift):
            chip = self.chip(shift)
            self.twin[chip] = self.twin[chip] + self.block(chip)

        add(self.ups)
        self.copy(1).start()
        add(-self.downs)
        self.copy(1 + self.ups).start()
        for shift in range(1 - self.downs, self.ups):
            add(shift)

    def advance(self, step):
        self.copy(step).wait_recv()
        owner = self.chip(self.ups - step)
        self.twin[owner] = self.twin[owner] + self.up[step - 1]
        self.copy(1 + step).start()
        if step < self.downs:
            self.copy(self.ups + step).wait_recv()
            owner = self.chip(step - self.downs)
            self.twin[owner] = self.twin[owner] + self.down[step - 1]
            self.copy(1 + self.ups + step).start()

    def collect(self):
        self.copy(self.ups).wait_recv()
        self.copy(self.ups + self.downs).wait_recv()
        mine = self.chip(0)
        total = (
            self.twin[mine].astype(f32)
            + self.up[self.ups - 1].astype(f32)
            + self.down[self.downs - 1].astype(f32)
        )
        self.own[...] = total.astype(bf16)
        self.copy(1 + self.ups + self.downs).start()

    def result(self):
        self.copy(1 + self.ups + self.downs).wait_recv()
        return self.own[...].astype(f32) + self.other[...].astype(f32)

    def finish(self):
        for index in range(2 + self.ups + self.downs):
            self.copy(index).wait_send()


class SmallSum:
    def __init__(self, ring, values, parts, mine, other, sums, sems):
        self.ring, self.values, self.parts = ring, values, parts
        self.mine, self.other, self.sums = mine, other, sums
        self.sems = sems
        self.rows = parts.shape[1]
        self.waiting = []

    def block(self, index):
        return pl.ds(pl.multiple_of(index * self.rows, 8), self.rows)

    def begin(self):
        ring = self.ring
        self.arriving = []
        for step in range(1, ring.size):
            other = lax.rem(ring.seq + step, ring.size)
            copy = remote(
                self.values.at[self.block(other)], self.parts.at[step],
                self.sems.at[0, step], self.sems.at[1, step], {"seq": other},
            )
            copy.start()
            self.arriving.append(copy)
            self.waiting.append(copy)

    def add_up(self):
        for copy in self.arriving:
            copy.wait_recv()
        total = self.values[self.block(self.ring.seq)]
        for step in range(1, self.ring.size):
            total = total + self.parts[step]
        self.mine[...] = total
        self.crossing = remote(
            self.mine, self.other, self.sems.at[0, 0], self.sems.at[1, 0], self.ring.across
        )
        self.crossing.start()
        self.waiting.append(self.crossing)

    def spread(self):
        self.crossing.wait_recv()
        block = self.block(self.ring.seq)
        self.sums[block] = self.mine[...] + self.other[...]
        self.arriving = []
        for step in range(1, self.ring.size):
            other = lax.rem(self.ring.seq + step, self.ring.size)
            copy = remote(
                self.sums.at[block], self.sums.at[block],
                self.sems.at[2, step], self.sems.at[3, step], {"seq": other},
            )
            copy.start()
            self.waiting.append(copy)
            back = lax.rem(self.ring.seq + (self.ring.size - step), self.ring.size)
            self.arriving.append(
                remote(
                    self.sums.at[self.block(back)], self.sums.at[self.block(back)],
                    self.sems.at[2, step], self.sems.at[3, step], {"seq": other},
                )
            )

    def finish(self):
        for copy in self.arriving:
            copy.wait_recv()
        for copy in self.waiting:
            copy.wait_send()


def reduction_scratch(size, rows, columns):
    chips = size // 2
    ups, downs = chips // 2, (chips - 1) // 2
    return [
        pltpu.VMEM((chips, rows, columns), bf16),
        pltpu.VMEM((ups, rows, columns), bf16),
        pltpu.VMEM((downs, rows, columns), bf16),
        pltpu.VMEM((rows, columns), bf16),
        pltpu.VMEM((rows, columns), bf16),
        pltpu.SemaphoreType.DMA((2, 2 + ups + downs)),
    ]


def small_scratch(size, rows, columns):
    return [
        pltpu.VMEM((size, rows // size, columns), f32),
        pltpu.VMEM((rows // size, columns), f32),
        pltpu.VMEM((rows // size, columns), f32),
        pltpu.SemaphoreType.DMA((4, size)),
    ]


class Gather:
    def __init__(self, ring, turn, mine, full, sems):
        self.ring, self.turn = ring, turn
        self.mine, self.full, self.sems = mine, full, sems
        self.ups = ring.count // 2
        self.downs = (ring.count - 1) // 2
        self.waiting, self.arriving = [], []

    def send(self, src, place, index, device):
        copy = remote(
            src, self.full.at[self.ring.chip(place * self.turn), self.ring.core],
            self.sems.at[0, index], self.sems.at[1, index], device,
        )
        copy.start()
        self.waiting.append(copy)
        return copy

    def share(self, src, place, index):
        index = self.ups + self.downs + index
        self.send(src, place, index, self.ring.sibling)
        block = self.full.at[self.ring.chip(place * self.turn), 1 - self.ring.core]
        self.arriving.append(
            remote(block, block, self.sems.at[0, index], self.sems.at[1, index], self.ring.sibling)
        )

    def wait_block(self, place, index, device):
        block = self.full.at[self.ring.chip(place * self.turn), self.ring.core]
        remote(block, block, self.sems.at[0, index], self.sems.at[1, index], device).wait_recv()
        return block

    def begin(self):
        ring = self.ring
        self.send(self.mine, 0, 0, ring.device(self.turn))
        self.send(self.mine, 0, self.ups, ring.device(-self.turn))
        self.share(self.mine, 0, 0)
        self.local = pltpu.make_async_copy(
            self.mine, self.full.at[ring.chip(0), ring.core], self.sems.at[2, 0]
        )
        self.local.start()

    def advance(self, step):
        ring = self.ring
        block = self.wait_block(-step, step - 1, ring.device(self.turn))
        if step < self.ups:
            self.send(block, -step, step, ring.device(self.turn))
        self.share(block, -step, step)
        if step <= self.downs:
            block = self.wait_block(step, self.ups + step - 1, ring.device(-self.turn))
            if step < self.downs:
                self.send(block, step, self.ups + step, ring.device(-self.turn))
            self.share(block, step, self.ups + step)

    def arrive(self):
        self.local.wait()
        for copy in self.arriving:
            copy.wait_recv()

    def finish(self):
        for copy in self.waiting:
            copy.wait_send()


def gather_sems(size):
    chips = size // 2
    return pltpu.SemaphoreType.DMA((3, 2 * chips))


PI_PARTS = (3.140625, 9.676535897932384e-4)


def sin_cos(x):
    turns = jnp.floor(x * (1.0 / math.pi) + 0.5)
    rest = (x - turns * PI_PARTS[0]) - turns * PI_PARTS[1]
    half = turns * 0.5
    sign = 1.0 - 4.0 * (half - jnp.floor(half))
    square = rest * rest
    odd = 1.0 / 6227020800.0
    for factor in (-1.0 / 39916800.0, 1.0 / 362880.0, -1.0 / 5040.0, 1.0 / 120.0, -1.0 / 6.0):
        odd = odd * square + factor
    even = 1.0 / 479001600.0
    for factor in (-1.0 / 3628800.0, 1.0 / 40320.0, -1.0 / 720.0, 1.0 / 24.0, -0.5):
        even = even * square + factor
    signed = sign * rest
    return signed + signed * square * odd, sign + sign * square * even


def norm_rows(values):
    center = jnp.mean(values, axis=1, keepdims=True)
    centred = values - center
    variance = jnp.mean(centred * centred, axis=1, keepdims=True)
    return centred * lax.rsqrt(variance + 1e-05)


TILE = 256


class Copies:
    def __init__(self, sems):
        self.sems, self.used, self.open = sems, 0, []

    def start(self, src, dst):
        copy = pltpu.make_async_copy(src, dst, self.sems.at[self.used])
        self.used += 1
        copy.start()
        return copy

    def out(self, src, dst):
        copy = self.start(src, dst)
        self.open.append(copy)
        return copy

    def settle(self, copy):
        copy.wait()
        self.open = [other for other in self.open if other is not copy]

    def finish(self):
        for copy in self.open:
            copy.wait()


def valid_rows(length, first, rows, columns):
    at = lax.broadcasted_iota(jnp.int32, (rows, columns), 0) + first
    return jnp.where(at < length, 1.0, 0.0).astype(f32)


def blocks(rows, step):
    return [slice(at, at + step) for at in range(0, rows, step)]


def folded(values):
    return jnp.sum(values.reshape(-1, 8, values.shape[1]), axis=0)


def front_kernel(size, names, *refs):
    ref = types.SimpleNamespace(**dict(zip(names, refs)))
    x, vec, net = ref.x_in, ref.vec, ref.net
    micro, count, width = x.shape
    slot = 2 * count
    tiles = width // TILE
    ring = Ring(size)
    copies = Copies(ref.copy_sems)
    proj_copy = copies.start(ref.proj, ref.proj_in)
    x_copy = copies.start(ref.x, x)
    down_copy = copies.start(ref.down, ref.down_in)
    feature_copy = copies.start(ref.feature, ref.feature_in)
    table_copy = copies.start(ref.table, ref.table_in)
    back_copy = copies.start(ref.back, ref.back_in)
    table, table_back = ref.table_in, ref.back_in
    inside = jnp.where(ring.pos > 0, 1.0, 0.0).astype(f32)

    proj_copy.wait()
    own = ref.in_own
    for j in range(tiles):
        for p in range(3):
            first = p * width + j * TILE
            own[j, :, p * TILE : (p + 1) * TILE] = ref.proj_in[:, first : first + TILE].astype(bf16)
    greet_all(ring)
    gather = [Gather(ring, 1 - 2 * (j % 2), own.at[j], ref.win_in.at[j], ref.win_sem.at[j]) for j in range(tiles)]
    gather_out = Gather(ring, -1, ref.out_own, ref.wout_in, ref.wout_sem)
    gather_up = Gather(ring, 1, ref.up_own, ref.wup, ref.wup_sem)
    gather_down = Gather(ring, -1, ref.down_own, ref.wdown, ref.wdown_sem)
    gather[0].begin()
    gather[1].begin()
    x_copy.wait()
    edge = remote(
        x.at[:, pl.ds(count - 16, 16)], ref.halo, ref.halo_sem.at[0],
        ref.halo_sem.at[1], ring.across,
    )
    edge.start()

    gain, shift = vec[0:1], vec[1:2]
    normed_ref, turned_ref = ref.n_in, ref.nt_in

    def first_norm(m):
        for rows in blocks(count, 16):
            normed_ref[m, rows] = (norm_rows(x[m, rows].astype(f32)) * gain + shift).astype(bf16)
        for rows in blocks(count, TILE):
            turned_ref[m, :, rows] = normed_ref[m, rows].T

    first_norm(0)
    gather[0].advance(1)
    gather[1].advance(1)
    gather[2].begin()
    for m in range(1, micro):
        first_norm(m)
    copies.out(turned_ref, ref.nt)
    ref.out_own[...] = ref.proj_in[:, 3 * width : 4 * width].astype(bf16)
    gather[0].advance(2)
    gather[1].advance(2)
    edge.wait_recv()
    for m in range(micro):
        ref.halo_n[m] = (norm_rows(ref.halo[m].astype(f32)) * gain + shift).astype(bf16)
    feature_copy.wait()

    frequency = net[:, EMB + 3 + 2 * HID : EMB + 4 + 2 * HID]
    pre = ref.pre_in

    def layer(i, weights, values):
        made = jnp.dot(weights, values, precision=highest, preferred_element_type=f32)
        if i > 0:
            first = EMB + 1 + (i - 1) * (HID + 1) + HID
            made = made + net[:, first : first + 1]
        pre[i * HID : (i + 1) * HID] = made
        return jnp.concatenate(
            [sin_cos(frequency[part] * made[part])[0] for part in blocks(HID, 16)], axis=0
        )

    hidden = layer(0, net[:, : ref.feature_in.shape[0]], ref.feature_in[...])
    for i in (1, 2):
        first = EMB + 1 + (i - 1) * (HID + 1)
        hidden = layer(i, net[:, first : first + HID], hidden)
    ref.act_in[...] = hidden.astype(bf16)
    copies.out(pre, ref.pre)
    rates = ref.rate[...].reshape(1, width)

    def filter_rows(at):
        shaped = dot_tn(
            ref.act_in[:, at * TILE : (at + 1) * TILE], ref.final[...].astype(bf16)
        )
        for part in blocks(TILE, 16):
            at_row = lax.broadcasted_iota(jnp.int32, (16, width), 0) + (at * TILE + part.start)
            window = jnp.exp(at_row.astype(f32) * (rates * (-1.0 / slot))) + 0.05
            first = at * TILE + part.start
            ref.filt[first : first + 16] = (shaped[part] * window).astype(bf16)

    row_blocks = slot // TILE
    gather[0].advance(3)
    gather[1].advance(3)
    gather[2].advance(1)
    for at in range(row_blocks // 2):
        filter_rows(at)
    down_copy.wait()
    ref.up_own[...] = ref.proj_in[:, 4 * width :].astype(bf16)
    ref.down_own[...] = ref.down_in[...].astype(bf16)
    gather[0].advance(4)
    gather[2].advance(2)
    gather_out.begin()
    gather[1].advance(4)
    gather[0].arrive()

    z_in, s_in, ulow, urecv = ref.z_in, ref.s_in, ref.ulow, ref.urecv
    zbuf, spec = ref.zbuf, ref.spec
    crossing = []

    def project(j):
        weight = ref.win_in[j].reshape(width, 3 * TILE)
        bias = jnp.concatenate(
            [vec[4 + p : 5 + p, j * TILE : (j + 1) * TILE] for p in range(3)], axis=1
        )
        lane = slice(j * TILE, (j + 1) * TILE)
        taps = [[vec[13 + 3 * k + p : 14 + 3 * k + p, lane] for p in range(3)] for k in range(3)]
        constant = [
            (taps[0][p] + taps[1][p] + taps[2][p]) * vec[4 + p : 5 + p, lane]
            + vec[22 + p : 23 + p, lane]
            for p in range(3)
        ]

        @pl.loop(0, micro)
        def _(m):
            zbuf[16:] = dot(normed_ref[m], weight)
            zbuf[:16] = dot(ref.halo_n[m], weight) * inside + bias * (inside - 1.0)
            ref.zh_in[j, m] = (zbuf[:16] + bias).astype(bf16)
            for rows in blocks(count, 32):
                parts = []
                for p in range(3):
                    cols = slice(p * TILE, (p + 1) * TILE)
                    first = rows.start
                    z = zbuf[first + 16 : first + 48, cols]
                    z_in[j, m, rows, cols] = (z + bias[:, cols]).astype(bf16)
                    short = (
                        taps[0][p] * z
                        + taps[1][p] * zbuf[first + 15 : first + 47, cols]
                        + taps[2][p] * zbuf[first + 14 : first + 46, cols]
                        + constant[p]
                    ).astype(bf16)
                    s_in[j, m, rows, cols] = short
                    parts.append(short.astype(f32))
                ulow[j, m, rows] = (parts[1] * parts[2]).astype(bf16)

        copy = remote(
            ulow.at[j], urecv.at[j], ref.u_sem.at[0, j], ref.u_sem.at[1, j], ring.across
        )
        copy.start()
        crossing.append(copy)
        copies.out(z_in.at[j], ref.z.at[j])
        copies.out(s_in.at[j], ref.s.at[j])

    project(0)
    gather[2].advance(3)
    gather_up.begin()
    gather[1].arrive()
    project(1)
    gather[2].advance(4)
    gather_down.begin()
    gather_out.advance(1)
    gather[2].arrive()
    project(2)
    copies.out(ref.zh_in, ref.zh)
    copies.out(ref.win_in, ref.win)
    gather_out.advance(2)
    gather_up.advance(1)
    gather_out.advance(3)
    for at in range(row_blocks // 2, row_blocks):
        filter_rows(at)
    gather_down.advance(1)
    gather_out.advance(4)
    gather_out.arrive()
    copies.out(ref.wout_in, ref.wout)
    table_copy.wait()
    back_copy.wait()

    parity = 1.0 - 2.0 * (lax.broadcasted_iota(jnp.int32, (16, TILE), 0) % 2).astype(f32)
    kern, uhat = ref.kern_in, ref.uhat_in
    one, two = ref.one, ref.two

    @pl.loop(0, tiles)
    def _(j):
        cols = pl.ds(pl.multiple_of(j * TILE, TILE), TILE)
        one[...] = dot(table[...], ref.filt[:count, cols])
        two[...] = dot(table[...], ref.filt[count:, cols])
        for re in blocks(count, 16):
            im = slice(re.start + count, re.stop + count)
            kern[j, 0, re] = one[re].astype(bf16)
            kern[j, 0, im] = one[im].astype(bf16)
            kern[j, 1, re] = (two[re] - parity * one[im]).astype(bf16)
            kern[j, 1, im] = (two[im] + parity * one[re]).astype(bf16)
        for m in range(micro):
            uhat[j, m, 0] = dot(table[...], ulow[j, m]).astype(bf16)

    copies.out(kern, ref.kern)
    gather_up.advance(2)

    def mix(j):
        crossing[j].wait_recv()
        lane = slice(j * TILE, (j + 1) * TILE)

        @pl.loop(0, micro)
        def _(m):
            one[...] = dot(table[...], urecv[j, m])
            for re in blocks(count, 16):
                im = slice(re.start + count, re.stop + count)
                k0r, k0i = kern[j, 0, re].astype(f32), kern[j, 0, im].astype(f32)
                k1r, k1i = kern[j, 1, re].astype(f32), kern[j, 1, im].astype(f32)
                ur, ui = uhat[j, m, 0, re].astype(f32), uhat[j, m, 0, im].astype(f32)
                vr, vi = one[re] * inside, one[im] * inside
                uhat[j, m, 1, re] = vr.astype(bf16)
                uhat[j, m, 1, im] = vi.astype(bf16)
                spec[re] = (k0r * ur - k0i * ui + k1r * vr - k1i * vi).astype(bf16)
                spec[im] = (k0r * ui + k0i * ur + k1r * vi + k1i * vr).astype(bf16)
            two[:count] = dot(table_back[...], spec[...])
            length = ref.lens[0, m] - ring.pos * count
            for rows in blocks(count, 32):
                gated = s_in[j, m, rows, TILE : 2 * TILE].astype(f32) * s_in[
                    j, m, rows, 2 * TILE :
                ].astype(f32)
                conv = two[rows] * (1.0 / count) + vec[25:26, lane] * gated
                ref.conv_in[j, m, rows] = conv.astype(bf16)
                mask = valid_rows(length, rows.start, 32, TILE)
                ref.y_in[m, rows, lane] = (
                    mask * s_in[j, m, rows, :TILE].astype(f32) * conv
                ).astype(bf16)

        copies.out(ref.conv_in.at[j], ref.conv.at[j])
        copies.out(uhat.at[j], ref.uhat.at[j])

    for j in range(tiles):
        mix(j)
        if j == 0:
            gather_down.advance(2)
        if j == 1:
            gather_up.advance(3)

    for m in range(micro):
        ref.res_in[m] = dot(ref.y_in[m], ref.wout_in[...].reshape(width, width))
        for rows in blocks(count, TILE):
            ref.yt_in[m, :, rows] = ref.y_in[m, rows].T
        for rows in blocks(count, 16):
            residual = x[m, rows].astype(f32) + ref.res_in[m, rows] + vec[7:8]
            ref.res_in[m, rows] = residual
            ref.n2_in[m, rows] = (norm_rows(residual) * vec[2:3] + vec[3:4]).astype(bf16)
        for rows in blocks(count, TILE):
            ref.n2t_in[m, :, rows] = ref.n2_in[m, rows].T
        for src, dst in (
            (ref.yt_in, ref.yt), (ref.res_in, ref.res), (ref.n2_in, ref.n2), (ref.n2t_in, ref.n2t)
        ):
            copies.out(src.at[m], dst.at[m])
        if m == 0:
            gather_down.advance(3)
    gather_up.advance(4)
    gather_up.arrive()

    gather_down.advance(4)
    gather_down.arrive()
    for work in gather:
        work.finish()
    for work in (gather_out, gather_up, gather_down):
        work.finish()
    edge.wait_send()
    for copy in crossing:
        copy.wait_send()
    copies.finish()


def front(size, arrays):
    chips = size // 2
    micro, count, width = arrays["x"].shape
    rows, down_rows = arrays["proj"].shape[0], arrays["down"].shape[0]
    wide = down_rows * size
    tiles = width // TILE
    vmem = pl.BlockSpec(memory_space=pltpu.VMEM)
    anywhere = pl.BlockSpec(memory_space=pl.ANY)
    smem = pl.BlockSpec(memory_space=pltpu.SMEM)
    near = ("vec", "net", "final", "rate")
    kinds = dict(
        win=((tiles, chips, 2, rows, 3 * TILE), bf16),
        wout=((chips, 2, rows, width), bf16),
        z=((tiles, micro, count, 3 * TILE), bf16),
        zh=((tiles, micro, 16, 3 * TILE), bf16),
        s=((tiles, micro, count, 3 * TILE), bf16),
        conv=((tiles, micro, count, TILE), bf16),
        uhat=((tiles, micro, 2, 2 * count, TILE), bf16),
        kern=((tiles, 2, 2 * count, TILE), bf16),
        res=((micro, count, width), f32),
        nt=((micro, width, count), bf16),
        n2=((micro, count, width), bf16),
        n2t=((micro, width, count), bf16),
        yt=((micro, width, count), bf16),
        pre=((3 * HID, 2 * count), f32),
    )
    outs = dict(
        kinds,
        wup=((chips, 2, rows, wide), bf16),
        wdown=((chips, 2, down_rows, width), bf16),
    )
    dma = pltpu.SemaphoreType.DMA
    scratch = {
        name + "_in": pltpu.VMEM(*kind) for name, kind in kinds.items()
    }
    for name, array in arrays.items():
        if name not in near and name != "lens":
            scratch[name + "_in"] = pltpu.VMEM(array.shape, array.dtype)
    scratch.update(
        dict(
            n_in=pltpu.VMEM((micro, count, width), bf16),
            one=pltpu.VMEM((2 * count, TILE), f32),
            two=pltpu.VMEM((2 * count, TILE), f32),
            act_in=pltpu.VMEM((HID, 2 * count), bf16),
            y_in=pltpu.VMEM((micro, count, width), bf16),
            in_own=pltpu.VMEM((tiles, rows, 3 * TILE), bf16),
            out_own=pltpu.VMEM((rows, width), bf16),
            up_own=pltpu.VMEM((rows, wide), bf16),
            down_own=pltpu.VMEM((down_rows, width), bf16),
            halo=pltpu.VMEM((micro, 16, width), bf16),
            halo_n=pltpu.VMEM((micro, 16, width), bf16),
            filt=pltpu.VMEM((2 * count, width), bf16),
            zbuf=pltpu.VMEM((16 + count, 3 * TILE), f32),
            ulow=pltpu.VMEM((tiles, micro, count, TILE), bf16),
            urecv=pltpu.VMEM((tiles, micro, count, TILE), bf16),
            spec=pltpu.VMEM((2 * count, TILE), bf16),
            win_sem=dma((tiles, 3, 2 * chips)),
            wout_sem=gather_sems(size),
            wup_sem=gather_sems(size),
            wdown_sem=gather_sems(size),
            halo_sem=dma((2,)),
            u_sem=dma((2, tiles)),
            copy_sems=dma((56,)),
        )
    )
    names = tuple(arrays) + tuple(outs) + tuple(scratch)
    made = pl.pallas_call(
        functools.partial(front_kernel, size, names),
        out_shape=[jax.ShapeDtypeStruct(*kind) for kind in outs.values()],
        in_specs=[
            smem if name == "lens" else vmem if name in near else anywhere for name in arrays
        ],
        out_specs=[anywhere] * len(outs),
        scratch_shapes=list(scratch.values()),
        compiler_params=pltpu.CompilerParams(
            collective_id=0, has_side_effects=True, vmem_limit_bytes=63 * 1024 * 1024
        ),
        name="front",
    )(*arrays.values())
    return dict(zip(outs, made))


GELU_SCALE = math.sqrt(2.0 / math.pi)


def gelu_pair(a):
    square = a * a
    half = 0.5 + 0.5 * jnp.tanh(a * (GELU_SCALE + (GELU_SCALE * 0.044715) * square))
    hidden = a * half
    bend = 2.0 * GELU_SCALE + (2.0 * GELU_SCALE * 0.134145) * square
    return hidden, half + (hidden - hidden * half) * bend


def mlp_kernel(
    n2_ref, n2t_ref, gm_ref, res_ref, vec_ref, wup_ref, wdown_ref,
    out_ref, gb_ref, dup_ref, ddown_ref, small_ref,
    acc_out, acc_gn, hid_ref, ga_ref,
):
    step, last = pl.program_id(0), pl.num_programs(0) - 1
    micro, count, width = n2_ref.shape
    chunk = width
    wup = wup_ref[...].reshape(width, chunk)
    wdown = wdown_ref[...].reshape(chunk, width)
    bias = vec_ref[pl.ds(8 + step, 1)]

    @pl.when(step == 0)
    def _():
        acc_out[...] = jnp.zeros_like(acc_out)
        acc_gn[...] = jnp.zeros_like(acc_gn)
        small_ref[...] = jnp.zeros_like(small_ref)

    bias_sum = jnp.zeros((8, chunk), f32)
    for m in range(micro):
        for rows in blocks(count, TILE):
            hidden, slope = gelu_pair(dot(n2_ref[m, rows], wup) + bias)
            hidden = hidden.astype(bf16)
            ga = (dot_nt(gm_ref[m, rows], wdown) * slope).astype(bf16)
            hid_ref[m, rows] = hidden
            ga_ref[m, rows] = ga
            bias_sum = bias_sum + folded(ga.astype(f32))
            acc_out[m, rows] += dot(hidden, wdown)
            acc_gn[m, rows] += dot_nt(ga, wup)
    small_ref[pl.ds(4 + step, 1)] = jnp.sum(bias_sum, axis=0, keepdims=True)
    down_total = dot_tn(hid_ref[0], gm_ref[0])
    up_total = dot(n2t_ref[0], ga_ref[0])
    for m in range(1, micro):
        down_total = down_total + dot_tn(hid_ref[m], gm_ref[m])
        up_total = up_total + dot(n2t_ref[m], ga_ref[m])
    ddown_ref[...] = down_total.astype(bf16)
    dup_ref[...] = up_total.astype(bf16).reshape(dup_ref.shape)

    @pl.when(step == last)
    def _():
        sums = [jnp.zeros((8, width), f32)] * 4
        for m in range(micro):
            for rows in blocks(count, 16):
                residual = res_ref[m, rows]
                out_ref[m, rows] = (residual + acc_out[m, rows] + vec_ref[12:13]).astype(bf16)
                gx, gain_part, grad = norm_rows_back(acc_gn[m, rows], residual, vec_ref[2:3])
                gm = gm_ref[m, rows].astype(f32)
                low = (gm + gx).astype(bf16)
                gb_ref[m, rows] = low
                parts = (gain_part, grad, low.astype(f32), gm)
                sums = [total + folded(part) for total, part in zip(sums, parts)]
        for k in range(4):
            small_ref[k : k + 1] = jnp.sum(sums[k], axis=0, keepdims=True)


def norm_rows_back(grad, values, gain):
    center = jnp.mean(values, axis=1, keepdims=True)
    centred = values - center
    variance = jnp.mean(centred * centred, axis=1, keepdims=True)
    scale = lax.rsqrt(variance + 1e-05)
    xh = centred * scale
    q = grad * gain
    gx = scale * (
        q - jnp.mean(q, axis=1, keepdims=True) - xh * jnp.mean(q * xh, axis=1, keepdims=True)
    )
    return gx, grad * xh, grad


def mlp(n2, n2t, gm, res, vectors, wup, wdown):
    micro, count, width = gm.shape
    chips, cores, rows, wide = wup.shape
    steps = wide // width
    per = chips // steps

    def whole(array):
        return pl.BlockSpec(array.shape, lambda i: (0,) * array.ndim)

    def shape(dims, kind=bf16):
        return jax.ShapeDtypeStruct(dims, kind)

    tokens = pl.BlockSpec((micro, count, width), lambda i: (0, 0, 0))
    return pl.pallas_call(
        mlp_kernel,
        grid=(steps,),
        in_specs=[
            whole(n2), whole(n2t), whole(gm), whole(res), whole(vectors),
            pl.BlockSpec((chips, cores, rows, width), lambda i: (0, 0, 0, i)),
            pl.BlockSpec((per, cores, wdown.shape[2], width), lambda i: (i, 0, 0, 0)),
        ],
        out_specs=[
            tokens, tokens,
            pl.BlockSpec((chips, cores, 1, rows, width), lambda i: (0, 0, i, 0, 0)),
            pl.BlockSpec((width, width), lambda i: (i, 0)),
            pl.BlockSpec((4 + steps, width), lambda i: (0, 0)),
        ],
        out_shape=[
            shape((micro, count, width)),
            shape((micro, count, width)),
            shape((chips, cores, steps, rows, width)),
            shape((wide, width)),
            shape((4 + steps, width), f32),
        ],
        scratch_shapes=[
            pltpu.VMEM((micro, count, width), f32),
            pltpu.VMEM((micro, count, width), f32),
            pltpu.VMEM((micro, count, width), bf16),
            pltpu.VMEM((micro, count, width), bf16),
        ],
        compiler_params=pltpu.CompilerParams(vmem_limit_bytes=63 * 1024 * 1024),
        name="mlp",
    )(n2, n2t, gm, res, vectors, wup, wdown)


def update_kernel(rates, firsts, *refs):
    count = len(rates)
    kept_in, kept_out, refs = refs[0], refs[4 * count + 1], refs[1 : 4 * count + 1] + refs[4 * count + 2 :]
    kept_out[...] = kept_in[...]
    ins, outs = refs[: 4 * count], refs[4 * count :]
    for i, (rate, first) in enumerate(zip(rates, firsts)):
        grad_ref, weight_ref, moment_ref, average_ref = ins[4 * i : 4 * i + 4]
        rows, columns = weight_ref.shape
        stepped = nesterov(
            weight_ref[...], moment_ref[...], average_ref[...],
            grad_ref[first : first + rows, :columns], rate,
        )
        for out, value in zip(outs[4 * i : 4 * i + 4], stepped):
            out[...] = value


def update(kept, sets):
    steps = 4
    held = pl.BlockSpec(
        (kept.shape[0], kept.shape[1] // steps, kept.shape[2]), lambda i: (0, i, 0)
    )
    arrays, in_specs, out_specs = [kept], [held], [held]
    shapes = [jax.ShapeDtypeStruct(kept.shape, kept.dtype)]

    def spec(shape, cut):
        if cut is None:
            return pl.BlockSpec(shape, lambda i: (0, 0))
        if cut:
            return pl.BlockSpec((shape[0], shape[1] // steps), lambda i: (0, i))
        return pl.BlockSpec((shape[0] // steps, shape[1]), lambda i: (i, 0))

    for grad, weight, moment, average, rate, first, cut in sets:
        arrays += [grad, weight, moment, average]
        in_specs += [spec(grad.shape, cut)] + [spec(weight.shape, cut)] * 3
        out_specs += [spec(weight.shape, cut)] * 4
        shapes += [jax.ShapeDtypeStruct(weight.shape, f32)] * 4
    made = pl.pallas_call(
        functools.partial(update_kernel, [s[4] for s in sets], [s[5] for s in sets]),
        grid=(steps,),
        in_specs=in_specs,
        out_specs=out_specs,
        out_shape=shapes,
        compiler_params=pltpu.CompilerParams(vmem_limit_bytes=63 * 1024 * 1024),
        name="update",
    )(*arrays)
    return made[0], [made[4 * i + 1 : 4 * i + 5] for i in range(len(sets))]


GROUP = 32
HALF = 384


def back_kernel(size, names, *refs):
    ref = types.SimpleNamespace(**dict(zip(names, refs)))
    gb, vec, table, table_back = ref.gb, ref.vec, ref.table, ref.back
    micro, count, width = gb.shape
    slot = 2 * count
    tiles = width // TILE
    ring = Ring(size)
    gw, gc, gcr, gz = ref.gw, ref.gc, ref.gcr, ref.gz
    vsum, nsum, fsum = ref.vsum, ref.nsum, ref.fsum
    one, two = ref.one, ref.two
    gate, turned = ref.gate, ref.turned
    inside = jnp.where(ring.pos < 1, 1.0, 0.0).astype(f32)
    first_half, second_half = ring.pos == 0, ring.pos == 1
    copies = Copies(ref.copy_sems)
    gate_copies = [
        copies.start(ref.s.at[j, :, :, pl.ds(0, TILE)], gate.at[j]) for j in range(tiles)
    ]
    wout = ref.din.at[0]
    wout_copy = copies.start(ref.wout, wout)
    turned_copy = copies.start(ref.yt, turned)
    win_copy = copies.start(ref.win, ref.win_in)

    greet_all(ring)
    red = {}

    def parts_of(name):
        return [getattr(ref, name + str(k)) for k in range(6)]

    deep, blocks_up = ref.ddown.shape[2], ref.dup.shape[2]
    fit = count // deep
    staged = []
    for chip in range(ring.count):
        at, row = chip // fit, chip % fit * deep
        staged.append(
            copies.start(
                ref.ddown.at[chip, ring.core], gz.at[at // micro, at % micro, pl.ds(row, deep)]
            )
        )
    for c in range(blocks_up):
        staged.append(
            copies.start(ref.dup.at[:, ring.core, c], ref.din.at[1 + c // 2, :, c % 2])
        )

    def down_block(chip):
        at, row = chip // fit, pl.multiple_of(lax.rem(chip, fit) * deep, 16)
        return gz[at // micro, lax.rem(at, micro), pl.ds(row, deep)]

    def up_block(chip):
        return jnp.stack([ref.din[1 + c // 2, chip, c % 2] for c in range(blocks_up)])

    down = Reduction(ring, -1, ref.ddown, *parts_of("down"), down_block)
    up = Reduction(ring, 1, ref.dup, *parts_of("up"), up_block)
    out = Reduction(ring, -1, ref.dout, *parts_of("out"))
    inner = [
        Reduction(ring, 1 - 2 * (j % 2), ref.din.at[j], *[part.at[j] for part in parts_of("in")])
        for j in range(tiles)
    ]
    down.begin()
    up.begin()
    vsum[...] = jnp.zeros_like(vsum)
    nsum[...] = jnp.zeros_like(nsum)
    small = ref.small
    for j in range(tiles):
        lane, base = slice(j * TILE, (j + 1) * TILE), j * GROUP
        vsum[base + 2 : base + 4] = small[0:2, lane]
        vsum[base + 7 : base + 8] = small[2:3, lane]
        vsum[base + 12 : base + 13] = small[3:4, lane]
        vsum[base + 8 : base + 12] = small[4:8, lane]

    crossing = []
    wout_copy.wait()
    for j in range(tiles):
        gate_copies[j].wait()
        weight = wout[...].reshape(width, width)[j * TILE : (j + 1) * TILE]

        @pl.loop(0, micro)
        def _(m):
            one[:count] = dot_nt(gb[m], weight)
            length = ref.lens[0, m] - ring.pos * count
            for rows in blocks(count, 32):
                mask = valid_rows(length, rows.start, 32, TILE)
                grad = mask * one[rows].astype(bf16).astype(f32)
                gw[j, m, rows] = grad.astype(bf16)
                gc[j, m, rows] = (grad * gate[j, m, rows].astype(f32)).astype(bf16)

        copy = remote(
            gc.at[j], gcr.at[j], ref.gc_sem.at[0, j], ref.gc_sem.at[1, j], ring.across
        )
        copy.start()
        crossing.append(copy)
    turned_copy.wait()

    @pl.loop(0, tiles)
    def _(j):
        cols = pl.ds(pl.multiple_of(j * TILE, TILE), TILE)
        total = dot(turned[0], gb[0, :, cols])
        for m in range(1, micro):
            total = total + dot(turned[m], gb[m, :, cols])
        dout = ref.dout
        dout[:, :, :, cols] = total.astype(bf16).reshape(dout.shape[:3] + (TILE,))

    turned_copy = copies.start(ref.nt, turned)
    out.begin()
    for copy in staged:
        copy.wait()
    down.merge()
    up.merge()

    parity = 1.0 - 2.0 * (lax.broadcasted_iota(jnp.int32, (16, TILE), 0) % 2).astype(f32)
    gk = ref.gk
    gbuf, zbuf, spec = ref.gbuf, ref.zbuf, ref.spec
    first_rows, next_rows = ref.first_rows, ref.next_rows

    def loads(j, m, at):
        made = [
            (ref.s.at[j, m, :, pl.ds(TILE, 2 * TILE)], ref.s_buf.at[at]),
            (ref.z.at[j, m], ref.z_buf.at[at]),
            (ref.uhat.at[j, m], ref.u_buf.at[at]),
            (ref.conv.at[j, m], ref.c_buf.at[at]),
        ]
        return [
            pltpu.make_async_copy(src, dst, ref.load_sems.at[at, i])
            for i, (src, dst) in enumerate(made)
        ]

    def load_kernel(j):
        return pltpu.make_async_copy(ref.kern.at[j], ref.k_buf, ref.kernel_sem.at[0])

    def start_loads(j, m, at):
        for copy in loads(j, m, at):
            copy.start()

    start_loads(0, 0, 0)
    load_kernel(0).start()
    gbuf[:, count:] = jnp.zeros_like(gbuf[:, count:])

    def unmix(j):
        crossing[j].wait_recv()
        load_kernel(j).wait()
        lane = slice(j * TILE, (j + 1) * TILE)
        kn = ref.k_buf

        @pl.loop(0, micro)
        def _(m):
            at = lax.rem(j * micro + m, 2)
            for copy in loads(j, m, at):
                copy.wait()

            @pl.when(m + 1 < micro)
            def _():
                start_loads(j, m + 1, 1 - at)

            if j + 1 < tiles:

                @pl.when(m + 1 == micro)
                def _():
                    start_loads(j + 1, 0, 1 - at)

            one[...] = dot(table[...], gc[j, m])
            keep = jnp.where(m > 0, 1.0, 0.0).astype(f32)
            uh = ref.u_buf

            def filter_grad(d, re, im, gr, gi):
                ur, ui = uh[at, d, re].astype(f32), uh[at, d, im].astype(f32)
                gk[d, re] = gk[d, re] * keep + (ur * gr + ui * gi)
                gk[d, im] = gk[d, im] * keep + (ur * gi - ui * gr)

            @pl.when(first_half)
            def _():
                two[...] = dot(table[...], gcr[j, m])
                for re in blocks(count, 16):
                    im = slice(re.start + count, re.stop + count)
                    gr, gi, hr, hi = one[re], one[im], two[re], two[im]
                    k0r, k0i = kn[0, re].astype(f32), kn[0, im].astype(f32)
                    k1r, k1i = kn[1, re].astype(f32), kn[1, im].astype(f32)
                    spec[re] = (k0r * gr + k0i * gi + k1r * hr + k1i * hi).astype(bf16)
                    spec[im] = (k0r * gi - k0i * gr + k1r * hi - k1i * hr).astype(bf16)
                    filter_grad(0, re, im, gr, gi)

            @pl.when(second_half)
            def _():
                for re in blocks(count, 16):
                    im = slice(re.start + count, re.stop + count)
                    gr, gi = one[re], one[im]
                    k0r, k0i = kn[0, re].astype(f32), kn[0, im].astype(f32)
                    spec[re] = (k0r * gr + k0i * gi).astype(bf16)
                    spec[im] = (k0r * gi - k0i * gr).astype(bf16)
                    filter_grad(0, re, im, gr, gi)
                    filter_grad(1, re, im, gr, gi)

            two[:count] = dot(table_back[...], spec[...])
            skip_sum = jnp.zeros((8, TILE), f32)
            for rows in blocks(count, 32):
                x1 = ref.s_buf[at, rows, :TILE].astype(f32)
                v = ref.s_buf[at, rows, TILE:].astype(f32)
                grad_w = gw[j, m, rows].astype(f32)
                gc_full = grad_w * gate[j, m, rows].astype(f32)
                gu = two[rows] * (1.0 / count) + vec[25:26, lane] * gc_full
                skip_sum = skip_sum + folded(gc_full * (x1 * v))
                grads = (grad_w * ref.c_buf[at, rows].astype(f32), gu * v, gu * x1)
                for p in range(3):
                    low = grads[p].astype(bf16)
                    gbuf[p, rows] = low.astype(f32)
                    if rows.start == 0:
                        first_rows[j, m, :, p * TILE : (p + 1) * TILE] = low[:16]
            vsum[j * GROUP + 25 : j * GROUP + 26] += jnp.sum(skip_sum, axis=0, keepdims=True)
            for p in range(3):
                cols = slice(p * TILE, (p + 1) * TILE)
                zbuf[:16] = ref.zh[j, m, :, cols].astype(f32)
                for rows in blocks(count, 32):
                    zbuf[rows.start + 16 : rows.stop + 16] = ref.z_buf[at, rows, cols].astype(f32)
                taps = [vec[13 + 3 * k + p : 14 + 3 * k + p, lane] for k in range(3)]
                sums = [jnp.zeros((8, TILE), f32) for _ in range(4)]
                for rows in blocks(count, 32):
                    first = rows.start
                    grad = gbuf[p, rows]
                    gz[j, m, rows, cols] = (
                        taps[0] * grad
                        + taps[1] * gbuf[p, first + 1 : first + 33]
                        + taps[2] * gbuf[p, first + 2 : first + 34]
                    ).astype(bf16)
                    for k in range(3):
                        sums[k] = sums[k] + folded(grad * zbuf[first + 16 - k : first + 48 - k])
                    sums[3] = sums[3] + folded(grad)
                gz[j, m, count - 16 :, cols] = gbuf[p, count - 16 : count].astype(bf16)
                for k in range(4):
                    row = j * GROUP + 13 + 3 * k + p
                    vsum[row : row + 1] += jnp.sum(sums[k], axis=0, keepdims=True)

        if j + 1 < tiles:
            load_kernel(j + 1).start()
        edge = remote(
            first_rows.at[j], next_rows.at[j], ref.edge_sem.at[0, j],
            ref.edge_sem.at[1, j], ring.across,
        )
        edge.start()
        @pl.when(first_half)
        def _():
            for re in blocks(2 * count, 16):
                spec[re] = gk[0, re].astype(bf16)
            gate[j, 1] = jnp.zeros_like(gate[j, 1])

        @pl.when(second_half)
        def _():
            for re in blocks(2 * count, 16):
                spec[re] = gk[1, re].astype(bf16)
            two[count:] = dot(table_back[...], spec[...])
            for rows in blocks(count, 16):
                second = two[rows.start + count : rows.stop + count]
                gate[j, 1, rows] = (second * (1.0 / count)).astype(bf16)
            for re in blocks(count, 16):
                im = slice(re.start + count, re.stop + count)
                spec[re] = (gk[0, re] + parity * gk[1, im]).astype(bf16)
                spec[im] = (gk[0, im] - parity * gk[1, re]).astype(bf16)

        two[:count] = dot(table_back[...], spec[...])
        for rows in blocks(count, 16):
            gate[j, 0, rows] = (two[rows] * (1.0 / count)).astype(bf16)
        return edge

    def project_back(j, edge):
        edge.wait_recv()
        lane = slice(j * TILE, (j + 1) * TILE)
        ebuf = ref.ebuf
        for m in range(micro):
            for p in range(3):
                cols = slice(p * TILE, (p + 1) * TILE)
                own = gz[j, m, count - 16 :, cols].astype(f32)
                ebuf[:16] = own
                ebuf[16:] = next_rows[j, m, :, cols].astype(f32) * inside
                gz[j, m, count - 16 :, cols] = (
                    vec[13 + p : 14 + p, lane] * own
                    + vec[16 + p : 17 + p, lane] * ebuf[1:17]
                    + vec[19 + p : 20 + p, lane] * ebuf[2:18]
                ).astype(bf16)
        for p in range(3):
            cols = slice(p * TILE, (p + 1) * TILE)
            total = dot(turned[0], gz[j, 0, :, cols])
            for m in range(1, micro):
                total = total + dot(turned[m], gz[j, m, :, cols])
            din = ref.din
            din[j, :, :, :, cols] = total.astype(bf16).reshape(din.shape[1:4] + (TILE,))
            bias = jnp.zeros((8, TILE), f32)
            for m in range(micro):
                for rows in blocks(count, 32):
                    bias = bias + folded(gz[j, m, rows, cols].astype(f32))
            row = j * GROUP + 4 + p
            vsum[row : row + 1] = jnp.sum(bias, axis=0, keepdims=True)
        inner[j].begin()

    edges = [unmix(0)]
    down.advance(1)
    up.advance(1)
    out.merge()
    edges.append(unmix(1))
    turned_copy.wait()
    project_back(0, edges[0])
    down.advance(2)
    up.advance(2)
    out.advance(1)
    inner[0].merge()
    edges.append(unmix(2))
    project_back(1, edges[1])
    x_copies = [
        copies.start(ref.x.at[:, :, pl.ds(j * TILE, TILE)], gcr.at[j]) for j in range(tiles)
    ]
    pre_copies = [
        copies.start(
            ref.pre.at[:, pl.ds(t * TILE, TILE)], one.at[pl.ds(t * 3 * HID, 3 * HID)]
        )
        for t in range(slot // TILE)
    ]
    down.advance(3)
    up.advance(3)
    inner[1].merge()
    project_back(2, edges[2])
    out.advance(2)
    inner[0].advance(1)
    inner[1].advance(1)
    for copy in x_copies:
        copy.wait()
    for copy in crossing:
        copy.wait_send()

    def first_norm(m, part):
        piece = slice(part * TILE, (part + 1) * TILE)
        for t in range(tiles):
            total = 0.0
            for j in range(tiles):
                weight = ref.win_in[j].reshape(width, 3 * TILE)[t * TILE : (t + 1) * TILE]
                total = total + dot_nt(gz[j, m, piece], weight)
            gbuf[t, piece] = total
        sums = [jnp.zeros((8, width), f32)] * 2
        for rows in blocks(count, 16)[part * TILE // 16 : (part + 1) * TILE // 16]:
            tokens = jnp.concatenate([gcr[j, m, rows] for j in range(tiles)], axis=1)
            grad = jnp.concatenate([gbuf[t, rows] for t in range(tiles)], axis=1)
            gx, gain_part, shift_part = norm_rows_back(grad, tokens.astype(f32), vec[0:1])
            sums = [sums[0] + folded(gain_part), sums[1] + folded(shift_part)]
            total = (gb[m, rows].astype(f32) + gx).astype(bf16)
            for j in range(tiles):
                gc[j, m, rows] = total[:, j * TILE : (j + 1) * TILE]
        for k in range(2):
            total = jnp.sum(sums[k], axis=0, keepdims=True)
            for j in range(tiles):
                row = j * GROUP + k
                vsum[row : row + 1] += total[:, j * TILE : (j + 1) * TILE]

    def filter_back():
        ref.net_sum[...] = jnp.zeros_like(ref.net_sum)
        net = ref.net
        for copy in pre_copies:
            copy.wait()

        def pre(first, last):
            return jnp.concatenate(
                [
                    one[t * 3 * HID + first : t * 3 * HID + last]
                    for t in range(slot // TILE)
                ],
                axis=1,
            )

        frequency = net[:, EMB + 3 + 2 * HID : EMB + 4 + 2 * HID]
        rates = ref.rate[...].reshape(1, width)
        final_low = ref.final[...].astype(bf16)
        acts, slopes = [], []
        for i in range(3):
            pairs = [
                sin_cos(frequency[part] * pre(i * HID + part.start, i * HID + part.stop))
                for part in blocks(HID, 16)
            ]
            acts.append(jnp.concatenate([pair[0] for pair in pairs], axis=0))
            slopes.append(jnp.concatenate([pair[1] for pair in pairs], axis=0))
        last = acts[2].astype(bf16)
        grad = jnp.zeros((HID, slot), f32)
        for j in range(tiles):
            lane = slice(j * TILE, (j + 1) * TILE)
            for half in range(2):
                for rows in blocks(count, 32):
                    first = half * count + rows.start
                    at_row = lax.broadcasted_iota(jnp.int32, (32, TILE), 0) + first
                    window = jnp.exp(at_row.astype(f32) * (rates[:, lane] * (-1.0 / slot))) + 0.05
                    spec[first : first + 32] = (gate[j, half, rows].astype(f32) * window).astype(bf16)
            total = dot(last, spec[...])
            for part in blocks(TILE, 128):
                at = j * TILE + part.start
                row, column = at // HALF * HID, at % HALF
                fsum[row : row + HID, column : column + 128] = total[:, part]
            grad = grad + dot_nt(final_low[:, lane], spec[...])
        freq_sum = jnp.zeros((HID, 1), f32)

        def put(first, values):
            ref.net_sum[:, first : first + values.shape[1]] = values

        for i in (2, 1, 0):
            turn = grad * slopes[i]
            freq_sum = freq_sum + jnp.sum(turn * pre(i * HID, (i + 1) * HID), axis=1, keepdims=True)
            grad = turn * frequency
            below = ref.feature[...] if i == 0 else acts[i - 1]
            made = lax.dot_general(
                grad, below, (((1,), (1,)), ((), ())), precision=highest,
                preferred_element_type=f32,
            )
            if i == 0:
                put(0, made[:, : EMB + 1])
            else:
                first = EMB + 1 + (i - 1) * (HID + 1)
                put(first, made)
                put(first + HID, jnp.sum(grad, axis=1, keepdims=True))
                grad = lax.dot_general(
                    net[:, first : first + HID], grad, (((0,), (0,)), ((), ())),
                    precision=highest, preferred_element_type=f32,
                )
        put(EMB + 3 + 2 * HID, freq_sum)
        nsum[:HID] = ref.net_sum[:, :128]
        nsum[HID:] = ref.net_sum[:, 128:]

    smalls = []
    for values, name in ((fsum, "f"), (nsum, "n"), (vsum, "v")):
        parts = [getattr(ref, name + str(k)) for k in range(5)]
        smalls.append(SmallSum(ring, values, *parts))
    win_copy.wait()
    pieces = [(m, part) for m in range(micro) for part in range(count // TILE)]
    quarter = max(1, len(pieces) // 4)

    def norms(at):
        last = len(pieces) if at == 3 else (at + 1) * quarter
        for m, part in pieces[at * quarter : last]:
            first_norm(m, part)

    norms(0)
    inner[2].merge()
    inner[0].advance(2)
    inner[1].advance(2)
    down.collect()
    norms(1)
    inner[2].advance(1)
    up.collect()
    out.advance(3)
    filter_back()
    for work in smalls[:2]:
        work.begin()
    inner[2].advance(2)
    inner[0].advance(3)
    inner[1].advance(3)
    norms(2)
    inner[2].advance(3)
    out.collect()
    inner[0].collect()
    inner[1].collect()
    for work in smalls[:2]:
        work.add_up()
    norms(3)
    smalls[2].begin()
    inner[2].collect()
    for work in smalls[:2]:
        work.spread()
    for j in range(tiles):
        copies.out(gc.at[j], ref.input_grad.at[:, :, pl.ds(j * TILE, TILE)])
    psum = ref.proj_sum
    ref.down_sum[...] = down.result()
    total = up.result()
    for c in range(blocks_up):
        psum[:, (4 + c) * width : (5 + c) * width] = total[c]
    psum[:, 3 * width : 4 * width] = out.result()
    smalls[2].add_up()
    smalls[2].spread()
    for j in range(tiles):
        total = inner[j].result()
        for p in range(3):
            first = p * width + j * TILE
            psum[:, first : first + TILE] = total[:, p * TILE : (p + 1) * TILE]
    for work in smalls:
        work.finish()
    for part in blocks(width, 128):
        row, column = part.start // HALF * HID, part.start % HALF
        ref.final_sum[:, part] = smalls[0].sums[row : row + HID, column : column + 128]
    ref.net_sum[:, :128] = smalls[1].sums[:HID]
    ref.net_sum[:, 128:] = smalls[1].sums[HID:]
    for j in range(tiles):
        ref.vec_sum[:, j * TILE : (j + 1) * TILE] = smalls[2].sums[j * GROUP : (j + 1) * GROUP]
    for work in [down, up, out] + inner:
        work.finish()
    for edge in edges:
        edge.wait_send()
    copies.finish()


def back(size, arrays):
    chips = size // 2
    micro, count, width = arrays["gb"].shape
    blocks_up, rows = arrays["dup"].shape[2:4]
    wide = blocks_up * width
    down_rows = arrays["ddown"].shape[2]
    tiles = width // TILE
    vmem = pl.BlockSpec(memory_space=pltpu.VMEM)
    anywhere = pl.BlockSpec(memory_space=pl.ANY)
    smem = pl.BlockSpec(memory_space=pltpu.SMEM)
    near = ("gb", "vec", "net", "final", "rate", "table", "back", "zh", "small", "feature")
    small_rows = 8 * size
    outs = dict(
        input_grad=((micro, count, width), bf16),
        proj_sum=((rows, 4 * width + wide), f32),
        down_sum=((down_rows, width), f32),
        vec_sum=((GROUP, width), f32),
        final_sum=((HID, width), f32),
        net_sum=((HID, 256), f32),
    )
    dma = pltpu.SemaphoreType.DMA
    tile_tokens = (tiles, micro, count, TILE)
    edge_rows = (tiles, micro, 16, 3 * TILE)
    scratch = dict(
        din=pltpu.VMEM((tiles, chips, 2, rows, 3 * TILE), bf16),
        dout=pltpu.VMEM((chips, 2, rows, width), bf16),
        gw=pltpu.VMEM(tile_tokens, bf16),
        gc=pltpu.VMEM(tile_tokens, bf16),
        gcr=pltpu.VMEM(tile_tokens, bf16),
        gate=pltpu.VMEM(tile_tokens, bf16),
        gz=pltpu.VMEM((tiles, micro, count, 3 * TILE), bf16),
        turned=pltpu.VMEM((micro, width, count), bf16),
        vsum=pltpu.VMEM((small_rows, TILE), f32),
        nsum=pltpu.VMEM((small_rows, 128), f32),
        fsum=pltpu.VMEM((small_rows, HALF), f32),
        gk=pltpu.VMEM((2, 2 * count, TILE), f32),
        gbuf=pltpu.VMEM((3, count + 16, TILE), f32),
        one=pltpu.VMEM((2 * count, TILE), f32),
        two=pltpu.VMEM((2 * count, TILE), f32),
        zbuf=pltpu.VMEM((count + 16, TILE), f32),
        ebuf=pltpu.VMEM((32, TILE), f32),
        spec=pltpu.VMEM((2 * count, TILE), bf16),
        first_rows=pltpu.VMEM(edge_rows, bf16),
        next_rows=pltpu.VMEM(edge_rows, bf16),
        s_buf=pltpu.VMEM((2, count, 2 * TILE), bf16),
        z_buf=pltpu.VMEM((2, count, 3 * TILE), bf16),
        u_buf=pltpu.VMEM((2, 2, 2 * count, TILE), bf16),
        c_buf=pltpu.VMEM((2, count, TILE), bf16),
        k_buf=pltpu.VMEM((2, 2 * count, TILE), bf16),
        load_sems=dma((2, 4)),
        kernel_sem=dma((1,)),
        gc_sem=dma((2, tiles)),
        edge_sem=dma((2, tiles)),
        copy_sems=dma((40,)),
        win_in=pltpu.VMEM(arrays["win"].shape, bf16),
    )
    ups, downs = chips // 2, (chips - 1) // 2
    for name, lead, dims in (
        ("up", (), (blocks_up, rows, width)), ("down", (), (down_rows, width)), ("out", (), (rows, width)),
        ("in", (tiles,), (rows, 3 * TILE)),
    ):
        made = [pltpu.VMEM(lead + (count,) + dims, bf16) for count in (chips, ups, downs)]
        made += [pltpu.VMEM(lead + dims, bf16)] * 2 + [dma(lead + (2, 2 + ups + downs))]
        for k, part in enumerate(made):
            scratch[name + str(k)] = part
    for name, columns in (("v", TILE), ("n", 128), ("f", HALF)):
        made = small_scratch(size, small_rows, columns)
        made.insert(3, pltpu.VMEM((small_rows, columns), f32))
        for k, part in enumerate(made):
            scratch[name + str(k)] = part
    names = tuple(arrays) + tuple(outs) + tuple(scratch)
    return pl.pallas_call(
        functools.partial(back_kernel, size, names),
        out_shape=[jax.ShapeDtypeStruct(*kind) for kind in outs.values()],
        in_specs=[
            smem if name == "lens" else vmem if name in near else anywhere for name in arrays
        ],
        out_specs=[anywhere] + [vmem] * (len(outs) - 1),
        scratch_shapes=list(scratch.values()),
        compiler_params=pltpu.CompilerParams(
            collective_id=1, has_side_effects=True, vmem_limit_bytes=255 * 1024 * 256
        ),
        name="back",
    )(*arrays.values())


def fits(size, groups, tokens, proj_weights, down_weights):
    micro, _, count, width = tokens.shape
    wide = down_weights.shape[0] * size
    return (
        groups == 2
        and size % 4 == 0
        and size == 16
        and proj_weights.shape[0] % 16 == 0
        and down_weights.shape[0] % 16 == 0
        and count % TILE == 0
        and width == 3 * TILE
        and micro >= groups
        and 3 * HID <= TILE
        and down_weights.shape[0] <= count
        and micro * count <= 1024
        and wide == 4 * width
        and proj_weights.shape[1] == 4 * width + wide
    )


def on_device_tuned(
    block_input,
    out_grad,
    lengths,
    decay_rates,
    proj_weights,
    proj_moment,
    proj_average,
    down_weights,
    down_moment,
    down_average,
    vectors,
    vector_moment,
    vector_average,
    filter_net,
    net_moment,
    net_average,
    filter_out,
    final_moment,
    final_average,
):
    micro, _, count, width = block_input.shape
    size = lax.axis_size("seq")
    tokens = block_input.reshape(micro, count, width)
    plain_table = transform_table(count)
    table = jnp.asarray(plain_table, dtype=bf16)
    table_back = jnp.asarray(plain_table.T, dtype=bf16)
    feature = jnp.asarray(feature_table(count * lax.axis_size("pos")))
    shared = dict(
        x=tokens, lens=lengths.T, vec=vectors, net=filter_net.T, final=filter_out,
        rate=decay_rates, table=table, back=table_back, feature=feature,
    )
    made = types.SimpleNamespace(**front(size, dict(shared, proj=proj_weights, down=down_weights)))
    block_output, branch_grad, up_step, down_step, small = mlp(
        made.n2, made.n2t, out_grad.reshape(micro, count, width), made.res, vectors,
        made.wup, made.wdown,
    )
    chips = size // 2
    input_grad, proj_sum, down_sum, vector_sum, final_sum, net_sum = back(
        size,
        dict(
            shared, win=made.win, wout=made.wout, z=made.z, zh=made.zh, s=made.s, conv=made.conv,
            uhat=made.uhat, kern=made.kern, nt=made.nt, yt=made.yt, pre=made.pre,
            gb=branch_grad, small=small,
            dup=up_step,
            ddown=down_step.reshape(chips, 2, -1, width),
        ),
    )
    input_grad, steps = update(
        input_grad,
        [
            (proj_sum, proj_weights, proj_moment, proj_average, 0.0001, 0, 1),
            (down_sum, down_weights, down_moment, down_average, 0.0001, 0, 0),
            (vector_sum, vectors, vector_moment, vector_average, 0.001, 0, None),
            (net_sum, filter_net.T, net_moment.T, net_average.T, 0.0001, 0, None),
            (final_sum, filter_out, final_moment, final_average, 2e-06, 0, None),
        ]
    )
    steps[3] = [array.T for array in steps[3]]
    return (
        block_output.reshape(block_input.shape),
        input_grad.reshape(block_input.shape),
        *steps[0], *steps[1], *steps[2], *steps[3], *steps[4],
    )


def on_device_plain(
    block_input,
    out_grad,
    lengths,
    decay_rates,
    proj_weights,
    proj_moment,
    proj_average,
    down_weights,
    down_moment,
    down_average,
    vectors,
    vector_moment,
    vector_average,
    filter_net,
    net_moment,
    net_average,
    filter_out,
    final_moment,
    final_average,
):
    micro = block_input.shape[0]
    count = block_input.shape[2]
    width = block_input.shape[3]
    groups = lax.axis_size("pos")
    slot_length = count * groups
    tokens_all = micro * count
    group = lax.axis_index("pos")
    tap = vectors[13:22].reshape(3, 3 * width)
    short_bias = vectors[22:25].reshape(-1)
    in_bias = vectors[4:7].reshape(-1)
    up_bias = vectors[8:12].reshape(-1)
    skip = vectors[25]

    low_rows = proj_weights.astype(bf16)
    in_weight = lax.all_gather(low_rows[:, : 3 * width], "seq", axis=0, tiled=True)
    out_weight = lax.all_gather(low_rows[:, 3 * width : 4 * width], "seq", axis=0, tiled=True)
    up_weight = lax.all_gather(low_rows[:, 4 * width :], "seq", axis=0, tiled=True)
    down_weight = lax.all_gather(down_weights.astype(bf16), "seq", axis=0, tiled=True)

    table = jnp.asarray(transform_table(count))
    table_low = table.astype(bf16)
    every = jnp.arange(slot_length, dtype=jnp.int32)

    def make_filter(net_values, final_values):
        return filter_fn(net_values, final_values, decay_rates, every, slot_length)

    filters, filter_back = jax.vjp(make_filter, filter_net, filter_out)
    pieces = filters.reshape(groups, count, width)
    spectra = [
        jnp.dot(table, pieces[d], precision=lax.Precision.HIGH, preferred_element_type=f32)
        for d in range(groups)
    ]
    kernels = [spectra[0]] + [spectra[d] + turned(spectra[d - 1], 1.0) for d in range(1, groups)]

    def transform(values):
        return jnp.stack([dot(table_low, values[m]) for m in range(micro)])

    def transform_back(spectrum):
        low = spectrum.astype(bf16)
        return jnp.stack([dot_tn(table_low, low[m]) for m in range(micro)]) * (1.0 / count)

    tokens_low = block_input[:, 0]
    before = passed_along(tokens_low[:, -2:], "pos", 1)
    tokens = tokens_low.astype(f32).reshape(tokens_all, width)
    xh_one, scale_one = norm_parts(tokens)
    normed = (xh_one * vectors[0] + vectors[1]).astype(bf16)
    xh_before, _ = norm_parts(before.astype(f32).reshape(micro * 2, width))
    normed_before = (xh_before * vectors[0] + vectors[1]).astype(bf16)
    z = (dot(normed, in_weight) + in_bias).reshape(micro, count, 3 * width)
    z_before = (dot(normed_before, in_weight) + in_bias).reshape(micro, 2, 3 * width)
    z_before = jnp.where(group > 0, z_before, 0.0)
    z_long = jnp.concatenate([z_before, z], axis=1)
    short = (
        tap[0] * z_long[:, 2:] + tap[1] * z_long[:, 1:-1] + tap[2] * z_long[:, :-2] + short_bias
    ).astype(bf16)
    x0 = short[:, :, :width].astype(f32)
    x1 = short[:, :, width : 2 * width].astype(f32)
    v = short[:, :, 2 * width :].astype(f32)

    u = x1 * v
    u_low = u.astype(bf16)
    u_hat = [transform(u_low)]
    for d in range(1, groups):
        u_hat.append(transform(passed_along(u_low, "pos", d)))
    total = product(kernels[0], u_hat[0])
    for d in range(1, groups):
        total = total + product(kernels[d], u_hat[d])
    conv = transform_back(total) + skip * u
    here = group * count + jnp.arange(count, dtype=jnp.int32)
    mask = (here[None, :] < lengths[:, 0][:, None]).astype(f32)[:, :, None]
    y = (mask * x0 * conv).astype(bf16).reshape(tokens_all, width)
    residual = tokens + dot(y, out_weight) + vectors[7]
    xh_two, scale_two = norm_parts(residual)
    normed_two = (xh_two * vectors[2] + vectors[3]).astype(bf16)

    cot_low = out_grad[:, 0].reshape(tokens_all, width)
    cot = cot_low.astype(f32)
    pre = dot(normed_two, up_weight) + up_bias
    hidden, gelu_back = jax.vjp(jax.nn.gelu, pre)
    hidden_low = hidden.astype(bf16)
    block_output = (residual + dot(hidden_low, down_weight) + vectors[12]).astype(bf16)
    pre_grad = gelu_back(dot_nt(cot_low, down_weight))[0].astype(bf16)
    down_step = dot_tn(hidden_low, cot_low)
    up_step = dot_tn(normed_two, pre_grad)
    normed_two_grad = dot_nt(pre_grad, up_weight)
    part, gain_two, shift_two = norm_back(normed_two_grad, xh_two, scale_two, vectors[2])
    residual_grad = cot + part
    branch_low = residual_grad.astype(bf16)
    out_step = dot_tn(y, branch_low)
    y_grad = dot_nt(branch_low, out_weight).astype(bf16).astype(f32).reshape(micro, count, width)

    gw = mask * y_grad
    gx0 = gw * conv
    gc = gw * x0
    gc_low = gc.astype(bf16)
    skip_grad = jnp.sum(gc * u, axis=(0, 1))
    gc_hat = [transform(gc_low)]
    for d in range(1, groups):
        gc_hat.append(transform(passed_along(gc_low, "pos", -d)))
    back = product_conj(kernels[0], gc_hat[0])
    for d in range(1, groups):
        back = back + product_conj(kernels[d], gc_hat[d])
    gu = transform_back(back) + skip * gc
    kernel_grads = [jnp.sum(product_conj(u_hat[d], gc_hat[0]), axis=0) for d in range(groups)]
    filter_grads = []
    for d in range(groups):
        got = kernel_grads[d]
        if d + 1 < groups:
            got = got + turned(kernel_grads[d + 1], -1.0)
        filter_grads.append(dot_tn(table_low, got.astype(bf16)) * (1.0 / count))
    net_local, final_local = filter_back(jnp.concatenate(filter_grads, axis=0))
    short_grad = jnp.concatenate([gx0, gu * v, gu * x1], axis=-1).astype(bf16)
    after = passed_along(short_grad[:, :2], "pos", -1)
    short_long = jnp.concatenate([short_grad, after], axis=1).astype(f32)
    z_grad = (
        tap[0] * short_long[:, :-2] + tap[1] * short_long[:, 1:-1] + tap[2] * short_long[:, 2:]
    ).astype(bf16)
    here_grad = short_long[:, :-2]
    tap_grads = [
        jnp.sum(here_grad * z_long[:, 2 - k : 2 - k + count], axis=(0, 1)) for k in range(3)
    ]
    short_bias_grad = jnp.sum(here_grad, axis=(0, 1))
    z_grad = z_grad.reshape(tokens_all, 3 * width)
    in_step = dot_tn(normed, z_grad)
    in_bias_grad = jnp.sum(z_grad.astype(f32), axis=0)
    normed_grad = dot_nt(z_grad, in_weight)
    part, gain_one, shift_one = norm_back(normed_grad, xh_one, scale_one, vectors[0])
    input_grad = (residual_grad + part).astype(bf16)

    vector_local = jnp.concatenate(
        [
            gain_one[None],
            shift_one[None],
            gain_two[None],
            shift_two[None],
            in_bias_grad.reshape(3, width),
            jnp.sum(branch_low.astype(f32), axis=0)[None],
            jnp.sum(pre_grad.astype(f32), axis=0).reshape(4, width),
            jnp.sum(cot, axis=0)[None],
            jnp.stack(tap_grads).reshape(9, width),
            short_bias_grad.reshape(3, width),
            skip_grad[None],
        ],
        axis=0,
    )
    proj_local = jnp.concatenate([in_step, out_step, up_step], axis=1).astype(bf16)
    proj_shard = lax.psum_scatter(proj_local, "seq", scatter_dimension=0, tiled=True)
    down_shard = lax.psum_scatter(down_step.astype(bf16), "seq", scatter_dimension=0, tiled=True)
    proj_sum = lax.psum(proj_shard, "pos").astype(f32)
    down_sum = lax.psum(down_shard, "pos").astype(f32)
    vector_sum, net_sum, final_sum = lax.psum(
        (vector_local, net_local, final_local), ("seq", "pos")
    )
    return (
        block_output.reshape(micro, 1, count, width),
        input_grad.reshape(micro, 1, count, width),
        *nesterov(proj_weights, proj_moment, proj_average, proj_sum, 0.0001),
        *nesterov(down_weights, down_moment, down_average, down_sum, 0.0001),
        *nesterov(vectors, vector_moment, vector_average, vector_sum, 0.001),
        *nesterov(filter_net, net_moment, net_average, net_sum, 0.0001),
        *nesterov(filter_out, final_moment, final_average, final_sum, 2e-06),
    )


def on_device(*arrays):
    tuned = fits(
        lax.axis_size("seq"), lax.axis_size("pos"), arrays[0], arrays[4], arrays[7]
    )
    return (on_device_tuned if tuned else on_device_plain)(*arrays)


def solution(mesh):
    tokens = P(None, "seq", "pos", None)
    rows = P("seq", None)
    whole = P()
    return jax.shard_map(
        on_device,
        mesh=mesh,
        in_specs=(tokens, tokens, P(None, "seq"), whole) + (rows,) * 6 + (whole,) * 9,
        out_specs=(tokens, tokens) + (rows,) * 8 + (whole,) * 12,
        check_vma=False,
    )
```

```python
import functools
import math
import types

import jax
import jax.numpy as jnp
import numpy as np
from jax import lax
from jax.experimental import pallas as pl
from jax.experimental.pallas import tpu as pltpu
from jax.sharding import PartitionSpec as P

HID = 64
EMB = 33

highest = lax.Precision.HIGHEST
f32 = jnp.float32
bf16 = jnp.bfloat16


def passed_along(block, axis, distance):
    devices = range(lax.axis_size(axis))
    route = [(i - distance, i) for i in devices if i - distance in devices]
    return lax.ppermute(block, axis, route)


def dot(a, b):
    return lax.dot_general(a, b, (((1,), (0,)), ((), ())), preferred_element_type=f32)


def dot_tn(a, b):
    return lax.dot_general(a, b, (((0,), (0,)), ((), ())), preferred_element_type=f32)


def dot_nt(a, b):
    return lax.dot_general(a, b, (((1,), (1,)), ((), ())), preferred_element_type=f32)


def features(positions, slot_length):
    band_count = (EMB - 1) // 2
    scaled = positions.astype(f32) / slot_length
    bands = 0.0001 + jnp.arange(band_count, dtype=f32) * (
        (band_count - 1 - 0.0001) / (band_count - 1)
    )
    angles = 2.0 * math.pi * scaled[:, None] * bands[None, :]
    return jnp.concatenate([scaled[:, None], jnp.cos(angles), -jnp.sin(angles)], axis=1)


def filter_fn(net_values, final_values, rates, positions, slot_length):
    embedded = features(positions, slot_length)
    frequency = net_values[EMB + 3 + 2 * HID]
    layer_one = jnp.sin(
        frequency * (jnp.dot(embedded, net_values[:EMB], precision=highest) + net_values[EMB])
    )
    layer_two = jnp.sin(
        frequency
        * (
            jnp.dot(layer_one, net_values[EMB + 1 : EMB + 1 + HID], precision=highest)
            + net_values[EMB + 1 + HID]
        )
    )
    layer_three = jnp.sin(
        frequency
        * (
            jnp.dot(layer_two, net_values[EMB + 2 + HID : EMB + 2 + 2 * HID], precision=highest)
            + net_values[EMB + 2 + 2 * HID]
        )
    )
    shaped = jnp.dot(layer_three, final_values, precision=highest)
    scaled = positions.astype(f32) / slot_length
    window = jnp.exp(-scaled[:, None] * rates[None, :]) + 0.05
    return shaped * window


def transform_table(length):
    product = np.outer(2 * np.arange(length) + 1, np.arange(length)) % (4 * length)
    angle = product.astype(np.float64) * (math.pi / (2 * length))
    return np.concatenate([np.cos(angle), -np.sin(angle)], axis=0).astype(np.float32)


def feature_table(slot_length):
    scaled = np.arange(slot_length, dtype=np.float32) / np.float32(slot_length)
    band_count = (EMB - 1) // 2
    bands = np.float32(0.0001) + np.arange(band_count, dtype=np.float32) * np.float32(
        (band_count - 1 - 0.0001) / (band_count - 1)
    )
    angles = (np.float32(2.0 * math.pi) * scaled[:, None]) * bands[None, :]
    table = np.zeros((40, slot_length), np.float32)
    table[0] = scaled
    table[1 : 1 + band_count] = np.cos(angles).T
    table[1 + band_count : EMB] = -np.sin(angles).T
    table[EMB] = 1.0
    return table


def halves(spectrum):
    half = spectrum.shape[-2] // 2
    return spectrum[..., :half, :], spectrum[..., half:, :]


def turned(spectrum, sign):
    re, im = halves(spectrum)
    parity = (1.0 - 2.0 * (jnp.arange(re.shape[-2]) % 2).astype(f32))[:, None] * sign
    return jnp.concatenate([-parity * im, parity * re], axis=-2)


def product(kernel, signal):
    kr, ki = halves(kernel)
    sr, si = halves(signal)
    return jnp.concatenate([kr * sr - ki * si, kr * si + ki * sr], axis=-2)


def product_conj(kernel, signal):
    kr, ki = halves(kernel)
    sr, si = halves(signal)
    return jnp.concatenate([kr * sr + ki * si, kr * si - ki * sr], axis=-2)


def nesterov(weight, moment, average, gradient, rate):
    moment_next = 0.9 * moment + gradient
    weight_next = weight - rate * (gradient + 0.9 * moment_next)
    average_next = 0.9 * average + 0.1 * weight_next
    return (gradient, weight_next, moment_next, average_next)


def norm_parts(values):
    center = jnp.mean(values, axis=-1, keepdims=True)
    centred = values - center
    variance = jnp.mean(centred * centred, axis=-1, keepdims=True)
    scale = lax.rsqrt(variance + 1e-05)
    return centred * scale, scale


def norm_back(grad, xh, scale, gain):
    q = grad * gain
    return (
        (q - jnp.mean(q, -1, keepdims=True) - xh * jnp.mean(q * xh, -1, keepdims=True)) * scale,
        jnp.sum(grad * xh, axis=0),
        jnp.sum(grad, axis=0),
    )


MESH = pl.DeviceIdType.MESH


class Ring:
    def __init__(self, size):
        self.size = size
        self.count = size // 2
        self.seq = lax.axis_index("seq")
        self.pos = lax.axis_index("pos")
        self.core = lax.rem(self.seq, 2)
        chip = self.seq // 2
        odd = lax.rem(chip, 2)
        self.place = (1 - odd) * (chip // 2) + odd * (self.count - 1 - chip // 2)

    def chip(self, shift):
        place = lax.rem(self.place + (shift + self.count), self.count)
        low = jnp.where(place < self.count // 2, 1, 0)
        return low * (2 * place) + (1 - low) * (2 * (self.count - 1 - place) + 1)

    def device(self, shift):
        return {"seq": 2 * self.chip(shift) + self.core}

    @property
    def sibling(self):
        return {"seq": self.seq + 1 - 2 * self.core}

    @property
    def across(self):
        return {"pos": 1 - self.pos}


def greet_all(ring):
    barrier = pltpu.get_barrier_semaphore()
    for step in range(1, ring.size):
        other = lax.rem(ring.seq + step, ring.size)
        pl.semaphore_signal(barrier, inc=1, device_id={"seq": other}, device_id_type=MESH)
    pl.semaphore_signal(barrier, inc=1, device_id=ring.across, device_id_type=MESH)
    pl.semaphore_wait(barrier, ring.size)


def remote(src, dst, send, recv, device):
    return pltpu.make_async_remote_copy(
        src_ref=src, dst_ref=dst, send_sem=send, recv_sem=recv, device_id=device,
        device_id_type=MESH,
    )


class Reduction:
    def __init__(self, ring, turn, grad, twin, up, down, own, other, sems, block=None):
        self.ring, self.turn = ring, turn
        self.grad, self.twin, self.up, self.down = grad, twin, up, down
        self.own, self.other = own, other
        self.sems = sems
        self.block = block or (lambda chip: self.grad[chip, ring.core])
        self.ups = ring.count // 2
        self.downs = (ring.count - 1) // 2
        self.shifts = [self.ups, -self.downs, *range(1 - self.downs, self.ups)]

    def chip(self, shift):
        return self.ring.chip(shift * self.turn)

    def copies(self):
        ring = self.ring
        made = []
        for shift in self.shifts:
            chip = self.chip(shift)
            made.append((self.grad.at[chip, 1 - ring.core], self.twin.at[chip], ring.sibling))
        for step in range(self.ups):
            block = self.twin.at[self.chip(self.ups - step)]
            made.append((block, self.up.at[step], ring.device(self.turn)))
        for step in range(self.downs):
            block = self.twin.at[self.chip(step - self.downs)]
            made.append((block, self.down.at[step], ring.device(-self.turn)))
        made.append((self.own, self.other, ring.across))
        return made

    def copy(self, index):
        src, dst, device = self.copies()[index]
        return remote(src, dst, self.sems.at[0, index], self.sems.at[1, index], device)

    def begin(self):
        for index in range(self.ring.count):
            self.copy(index).start()

    def step_up(self, step):
        return self.copy(self.ring.count + step)

    def step_down(self, step):
        return self.copy(self.ring.count + self.ups + step)

    def merge(self):
        for index, shift in enumerate(self.shifts):
            self.copy(index).wait_recv()
            chip = self.chip(shift)
            self.twin[chip] = self.twin[chip] + self.block(chip)
            if index == 0:
                self.step_up(0).start()
            if index == 1:
                self.step_down(0).start()

    def advance(self, step):
        self.step_up(step - 1).wait_recv()
        owner = self.chip(self.ups - step)
        self.twin[owner] = self.twin[owner] + self.up[step - 1]
        self.step_up(step).start()
        if step < self.downs:
            self.step_down(step - 1).wait_recv()
            owner = self.chip(step - self.downs)
            self.twin[owner] = self.twin[owner] + self.down[step - 1]
            self.step_down(step).start()

    def collect(self):
        self.step_up(self.ups - 1).wait_recv()
        self.step_down(self.downs - 1).wait_recv()
        mine = self.chip(0)
        total = (
            self.twin[mine].astype(f32)
            + self.up[self.ups - 1].astype(f32)
            + self.down[self.downs - 1].astype(f32)
        )
        self.own[...] = total.astype(bf16)
        self.copy(self.ring.count + self.ups + self.downs).start()

    def result(self):
        self.copy(self.ring.count + self.ups + self.downs).wait_recv()
        return self.own[...].astype(f32) + self.other[...].astype(f32)

    def finish(self):
        for index in range(self.ring.count + 1 + self.ups + self.downs):
            self.copy(index).wait_send()


class SmallSum:
    def __init__(self, ring, values, parts, mine, other, sums, sems):
        self.ring, self.values, self.parts = ring, values, parts
        self.mine, self.other, self.sums = mine, other, sums
        self.sems = sems
        self.rows = parts.shape[1]
        self.waiting = []

    def block(self, index):
        return pl.ds(pl.multiple_of(index * self.rows, 8), self.rows)

    def begin(self):
        ring = self.ring
        self.arriving = []
        for step in range(1, ring.size):
            other = lax.rem(ring.seq + step, ring.size)
            copy = remote(
                self.values.at[self.block(other)], self.parts.at[step],
                self.sems.at[0, step], self.sems.at[1, step], {"seq": other},
            )
            copy.start()
            self.arriving.append(copy)
            self.waiting.append(copy)

    def add_up(self):
        for copy in self.arriving:
            copy.wait_recv()
        total = self.values[self.block(self.ring.seq)]
        for step in range(1, self.ring.size):
            total = total + self.parts[step]
        self.mine[...] = total
        self.crossing = remote(
            self.mine, self.other, self.sems.at[0, 0], self.sems.at[1, 0], self.ring.across
        )
        self.crossing.start()
        self.waiting.append(self.crossing)

    def spread(self):
        self.crossing.wait_recv()
        block = self.block(self.ring.seq)
        self.sums[block] = self.mine[...] + self.other[...]
        self.arriving = []
        for step in range(1, self.ring.size):
            other = lax.rem(self.ring.seq + step, self.ring.size)
            copy = remote(
                self.sums.at[block], self.sums.at[block],
                self.sems.at[2, step], self.sems.at[3, step], {"seq": other},
            )
            copy.start()
            self.waiting.append(copy)
            back = lax.rem(self.ring.seq + (self.ring.size - step), self.ring.size)
            self.arriving.append(
                remote(
                    self.sums.at[self.block(back)], self.sums.at[self.block(back)],
                    self.sems.at[2, step], self.sems.at[3, step], {"seq": other},
                )
            )

    def finish(self):
        for copy in self.arriving:
            copy.wait_recv()
        for copy in self.waiting:
            copy.wait_send()


def small_scratch(size, rows, columns):
    return [
        pltpu.VMEM((size, rows // size, columns), f32),
        pltpu.VMEM((rows // size, columns), f32),
        pltpu.VMEM((rows // size, columns), f32),
        pltpu.SemaphoreType.DMA((4, size)),
    ]


class Gather:
    def __init__(self, ring, turn, mine, full, sems):
        self.ring, self.turn = ring, turn
        self.mine, self.full, self.sems = mine, full, sems
        self.ups = ring.count // 2
        self.downs = (ring.count - 1) // 2
        self.waiting, self.arriving = [], []

    def send(self, src, place, index, device):
        copy = remote(
            src, self.full.at[self.ring.chip(place * self.turn), self.ring.core],
            self.sems.at[0, index], self.sems.at[1, index], device,
        )
        copy.start()
        self.waiting.append(copy)
        return copy

    def share(self, src, place, index):
        index = self.ups + self.downs + index
        self.send(src, place, index, self.ring.sibling)
        block = self.full.at[self.ring.chip(place * self.turn), 1 - self.ring.core]
        self.arriving.append(
            remote(block, block, self.sems.at[0, index], self.sems.at[1, index], self.ring.sibling)
        )

    def wait_block(self, place, index, device):
        block = self.full.at[self.ring.chip(place * self.turn), self.ring.core]
        remote(block, block, self.sems.at[0, index], self.sems.at[1, index], device).wait_recv()
        return block

    def begin(self):
        ring = self.ring
        self.send(self.mine, 0, 0, ring.device(self.turn))
        self.send(self.mine, 0, self.ups, ring.device(-self.turn))
        self.share(self.mine, 0, 0)
        self.local = pltpu.make_async_copy(
            self.mine, self.full.at[ring.chip(0), ring.core], self.sems.at[2, 0]
        )
        self.local.start()

    def advance(self, step):
        ring = self.ring
        block = self.wait_block(-step, step - 1, ring.device(self.turn))
        if step < self.ups:
            self.send(block, -step, step, ring.device(self.turn))
        self.share(block, -step, step)
        if step <= self.downs:
            block = self.wait_block(step, self.ups + step - 1, ring.device(-self.turn))
            if step < self.downs:
                self.send(block, step, self.ups + step, ring.device(-self.turn))
            self.share(block, step, self.ups + step)

    def arrive(self):
        self.local.wait()
        for copy in self.arriving:
            copy.wait_recv()

    def finish(self):
        for copy in self.waiting:
            copy.wait_send()


def gather_sems(size):
    chips = size // 2
    return pltpu.SemaphoreType.DMA((3, 2 * chips))


PI_PARTS = (3.140625, 9.676535897932384e-4)


def sin_cos(x):
    turns = jnp.floor(x * (1.0 / math.pi) + 0.5)
    rest = (x - turns * PI_PARTS[0]) - turns * PI_PARTS[1]
    half = turns * 0.5
    sign = 1.0 - 4.0 * (half - jnp.floor(half))
    square = rest * rest
    odd = 1.0 / 6227020800.0
    for factor in (-1.0 / 39916800.0, 1.0 / 362880.0, -1.0 / 5040.0, 1.0 / 120.0, -1.0 / 6.0):
        odd = odd * square + factor
    even = 1.0 / 479001600.0
    for factor in (-1.0 / 3628800.0, 1.0 / 40320.0, -1.0 / 720.0, 1.0 / 24.0, -0.5):
        even = even * square + factor
    signed = sign * rest
    return signed + signed * square * odd, sign + sign * square * even


def norm_rows(values):
    center = jnp.mean(values, axis=1, keepdims=True)
    centred = values - center
    variance = jnp.mean(centred * centred, axis=1, keepdims=True)
    return centred * lax.rsqrt(variance + 1e-05)


TILE = 256


class Copies:
    def __init__(self, sems):
        self.sems, self.used, self.open = sems, 0, []

    def start(self, src, dst):
        copy = pltpu.make_async_copy(src, dst, self.sems.at[self.used])
        self.used += 1
        copy.start()
        return copy

    def out(self, src, dst):
        copy = self.start(src, dst)
        self.open.append(copy)
        return copy

    def settle(self, copy):
        copy.wait()
        self.open = [other for other in self.open if other is not copy]

    def finish(self):
        for copy in self.open:
            copy.wait()


def valid_rows(length, first, rows, columns):
    at = lax.broadcasted_iota(jnp.int32, (rows, columns), 0) + first
    return jnp.where(at < length, 1.0, 0.0).astype(f32)


def blocks(rows, step):
    return [slice(at, at + step) for at in range(0, rows, step)]


def folded(values):
    return jnp.sum(values.reshape(-1, 8, values.shape[1]), axis=0)


def front_kernel(size, names, *refs):
    ref = types.SimpleNamespace(**dict(zip(names, refs)))
    x, vec, net = ref.x_in, ref.vec, ref.net
    micro, count, width = x.shape
    slot = 2 * count
    tiles = width // TILE
    ring = Ring(size)
    copies = Copies(ref.copy_sems)
    proj_copy = copies.start(ref.proj, ref.proj_in)
    x_copy = copies.start(ref.x, x)
    down_copy = copies.start(ref.down, ref.down_in)
    feature_copy = copies.start(ref.feature, ref.feature_in)
    table_copy = copies.start(ref.table, ref.table_in)
    back_copy = copies.start(ref.back, ref.back_in)
    table, table_back = ref.table_in, ref.back_in
    inside = jnp.where(ring.pos > 0, 1.0, 0.0).astype(f32)

    proj_copy.wait()
    own = ref.in_own
    for j in range(tiles):
        for p in range(3):
            first = p * width + j * TILE
            own[j, :, p * TILE : (p + 1) * TILE] = ref.proj_in[:, first : first + TILE].astype(bf16)
    greet_all(ring)
    gather = [Gather(ring, 1 - 2 * (j % 2), own.at[j], ref.win_in.at[j], ref.win_sem.at[j]) for j in range(tiles)]
    gather_out = Gather(ring, -1, ref.out_own, ref.wout_in, ref.wout_sem)
    gather_up = Gather(ring, 1, ref.up_own, ref.wup, ref.wup_sem)
    gather_down = Gather(ring, -1, ref.down_own, ref.wdown, ref.wdown_sem)
    gather[0].begin()
    x_copy.wait()
    edge = remote(
        x.at[:, pl.ds(count - 16, 16)], ref.halo, ref.halo_sem.at[0],
        ref.halo_sem.at[1], ring.across,
    )
    edge.start()

    gain, shift = vec[0:1], vec[1:2]
    normed_ref, turned_ref = ref.n_in, ref.nt_in

    def first_norm(m):
        for rows in blocks(count, 16):
            normed_ref[m, rows] = (norm_rows(x[m, rows].astype(f32)) * gain + shift).astype(bf16)
        for rows in blocks(count, TILE):
            turned_ref[m, :, rows] = normed_ref[m, rows].T

    first_norm(0)
    gather[0].advance(1)
    gather[1].begin()
    for m in range(1, micro):
        first_norm(m)
    copies.out(turned_ref, ref.nt)
    gather[0].advance(2)
    gather[1].advance(1)
    gather[2].begin()
    feature_copy.wait()

    frequency = net[:, EMB + 3 + 2 * HID : EMB + 4 + 2 * HID]
    pre = ref.pre_in

    def layer(i, weights, values):
        made = jnp.dot(weights, values, precision=highest, preferred_element_type=f32)
        if i > 0:
            first = EMB + 1 + (i - 1) * (HID + 1) + HID
            made = made + net[:, first : first + 1]
        pre[i * HID : (i + 1) * HID] = made
        return jnp.concatenate(
            [sin_cos(frequency[part] * made[part])[0] for part in blocks(HID, 16)], axis=0
        )

    hidden = layer(0, net[:, : ref.feature_in.shape[0]], ref.feature_in[...])
    for i in (1, 2):
        first = EMB + 1 + (i - 1) * (HID + 1)
        hidden = layer(i, net[:, first : first + HID], hidden)
    ref.act_in[...] = hidden.astype(bf16)
    copies.out(pre, ref.pre)
    rates = ref.rate[...].reshape(1, width)

    def filter_rows(at):
        shaped = dot_tn(
            ref.act_in[:, at * TILE : (at + 1) * TILE], ref.final[...].astype(bf16)
        )
        for part in blocks(TILE, 16):
            at_row = lax.broadcasted_iota(jnp.int32, (16, width), 0) + (at * TILE + part.start)
            window = jnp.exp(at_row.astype(f32) * (rates * (-1.0 / slot))) + 0.05
            first = at * TILE + part.start
            ref.filt[first : first + 16] = (shaped[part] * window).astype(bf16)

    row_blocks = slot // TILE
    gather[0].advance(3)
    gather[1].advance(2)
    gather[2].advance(1)
    edge.wait_recv()
    for m in range(micro):
        ref.halo_n[m] = (norm_rows(ref.halo[m].astype(f32)) * gain + shift).astype(bf16)
    ref.out_own[...] = ref.proj_in[:, 3 * width : 4 * width].astype(bf16)
    filter_rows(0)
    gather[0].advance(4)
    gather[1].advance(3)
    gather[2].advance(2)
    gather_out.begin()
    gather[0].arrive()

    z_in, s_in, ulow, urecv = ref.z_in, ref.s_in, ref.ulow, ref.urecv
    zbuf, spec = ref.zbuf, ref.spec
    crossing = []

    def project(j):
        weight = ref.win_in[j].reshape(width, 3 * TILE)
        bias = jnp.concatenate(
            [vec[4 + p : 5 + p, j * TILE : (j + 1) * TILE] for p in range(3)], axis=1
        )
        lane = slice(j * TILE, (j + 1) * TILE)
        taps = [[vec[13 + 3 * k + p : 14 + 3 * k + p, lane] for p in range(3)] for k in range(3)]
        constant = [
            (taps[0][p] + taps[1][p] + taps[2][p]) * vec[4 + p : 5 + p, lane]
            + vec[22 + p : 23 + p, lane]
            for p in range(3)
        ]

        @pl.loop(0, micro)
        def _(m):
            zbuf[16:] = dot(normed_ref[m], weight)
            zbuf[:16] = dot(ref.halo_n[m], weight) * inside + bias * (inside - 1.0)
            ref.zh_in[j, m] = (zbuf[:16] + bias).astype(bf16)
            for rows in blocks(count, 32):
                parts = []
                for p in range(3):
                    cols = slice(p * TILE, (p + 1) * TILE)
                    first = rows.start
                    z = zbuf[first + 16 : first + 48, cols]
                    z_in[j, m, rows, cols] = (z + bias[:, cols]).astype(bf16)
                    short = (
                        taps[0][p] * z
                        + taps[1][p] * zbuf[first + 15 : first + 47, cols]
                        + taps[2][p] * zbuf[first + 14 : first + 46, cols]
                        + constant[p]
                    ).astype(bf16)
                    s_in[j, m, rows, cols] = short
                    parts.append(short.astype(f32))
                ulow[j, m, rows] = (parts[1] * parts[2]).astype(bf16)

        copy = remote(
            ulow.at[j], urecv.at[j], ref.u_sem.at[0, j], ref.u_sem.at[1, j], ring.across
        )
        copy.start()
        crossing.append(copy)
        copies.out(z_in.at[j], ref.z.at[j])
        copies.out(s_in.at[j], ref.s.at[j])

    project(0)
    gather[1].advance(4)
    gather[2].advance(3)
    ref.up_own[...] = ref.proj_in[:, 4 * width :].astype(bf16)
    gather_up.begin()
    gather[1].arrive()
    project(1)
    gather[2].advance(4)
    gather_out.advance(1)
    down_copy.wait()
    ref.down_own[...] = ref.down_in[...].astype(bf16)
    gather_down.begin()
    gather[2].arrive()
    project(2)
    copies.out(ref.zh_in, ref.zh)
    copies.out(ref.win_in, ref.win)
    gather_out.advance(2)
    gather_up.advance(1)
    gather_out.advance(3)
    for at in range(1, row_blocks):
        filter_rows(at)
    gather_down.advance(1)
    gather_out.advance(4)
    gather_out.arrive()
    copies.out(ref.wout_in, ref.wout)
    table_copy.wait()
    back_copy.wait()

    parity = 1.0 - 2.0 * (lax.broadcasted_iota(jnp.int32, (16, TILE), 0) % 2).astype(f32)
    kern, uhat = ref.kern_in, ref.uhat_in
    one, two = ref.one, ref.two

    @pl.loop(0, tiles)
    def _(j):
        cols = pl.ds(pl.multiple_of(j * TILE, TILE), TILE)
        one[...] = dot(table[...], ref.filt[:count, cols])
        two[...] = dot(table[...], ref.filt[count:, cols])
        for re in blocks(count, 16):
            im = slice(re.start + count, re.stop + count)
            kern[j, 0, re] = one[re].astype(bf16)
            kern[j, 0, im] = one[im].astype(bf16)
            kern[j, 1, re] = (two[re] - parity * one[im]).astype(bf16)
            kern[j, 1, im] = (two[im] + parity * one[re]).astype(bf16)
        for m in range(micro):
            uhat[j, m, 0] = dot(table[...], ulow[j, m]).astype(bf16)

    copies.out(kern, ref.kern)
    gather_up.advance(2)

    def mix(j):
        crossing[j].wait_recv()
        lane = slice(j * TILE, (j + 1) * TILE)

        @pl.loop(0, micro)
        def _(m):
            one[...] = dot(table[...], urecv[j, m])
            for re in blocks(count, 16):
                im = slice(re.start + count, re.stop + count)
                k0r, k0i = kern[j, 0, re].astype(f32), kern[j, 0, im].astype(f32)
                k1r, k1i = kern[j, 1, re].astype(f32), kern[j, 1, im].astype(f32)
                ur, ui = uhat[j, m, 0, re].astype(f32), uhat[j, m, 0, im].astype(f32)
                vr, vi = one[re] * inside, one[im] * inside
                uhat[j, m, 1, re] = vr.astype(bf16)
                uhat[j, m, 1, im] = vi.astype(bf16)
                spec[re] = (k0r * ur - k0i * ui + k1r * vr - k1i * vi).astype(bf16)
                spec[im] = (k0r * ui + k0i * ur + k1r * vi + k1i * vr).astype(bf16)
            two[:count] = dot(table_back[...], spec[...])
            length = ref.lens[0, m] - ring.pos * count
            for rows in blocks(count, 32):
                gated = s_in[j, m, rows, TILE : 2 * TILE].astype(f32) * s_in[
                    j, m, rows, 2 * TILE :
                ].astype(f32)
                conv = two[rows] * (1.0 / count) + vec[25:26, lane] * gated
                ref.conv_in[j, m, rows] = conv.astype(bf16)
                mask = valid_rows(length, rows.start, 32, TILE)
                ref.y_in[m, rows, lane] = (
                    mask * s_in[j, m, rows, :TILE].astype(f32) * conv
                ).astype(bf16)

            ref.yt_in[m, lane] = ref.y_in[m, :, lane].T
            part = dot(ref.y_in[m, :, lane], ref.wout_in[...].reshape(width, width)[lane])
            ref.res_in[m] = part if j == 0 else ref.res_in[m] + part

        copies.out(ref.conv_in.at[j], ref.conv.at[j])
        copies.out(uhat.at[j], ref.uhat.at[j])

    for j in range(tiles):
        mix(j)
        if j == 0:
            gather_down.advance(2)
        if j == 1:
            gather_up.advance(3)

    for m in range(micro):
        for rows in blocks(count, 16):
            residual = x[m, rows].astype(f32) + ref.res_in[m, rows] + vec[7:8]
            ref.res_in[m, rows] = residual
            ref.n2_in[m, rows] = (norm_rows(residual) * vec[2:3] + vec[3:4]).astype(bf16)
        for rows in blocks(count, TILE):
            ref.n2t_in[m, :, rows] = ref.n2_in[m, rows].T
        for src, dst in (
            (ref.yt_in, ref.yt), (ref.res_in, ref.res), (ref.n2_in, ref.n2), (ref.n2t_in, ref.n2t)
        ):
            copies.out(src.at[m], dst.at[m])
        if m == 0:
            gather_down.advance(3)
    gather_up.advance(4)
    gather_up.arrive()

    gather_down.advance(4)
    gather_down.arrive()
    for work in gather:
        work.finish()
    for work in (gather_out, gather_up, gather_down):
        work.finish()
    edge.wait_send()
    for copy in crossing:
        copy.wait_send()
    copies.finish()


def front(size, arrays):
    chips = size // 2
    micro, count, width = arrays["x"].shape
    rows, down_rows = arrays["proj"].shape[0], arrays["down"].shape[0]
    wide = down_rows * size
    tiles = width // TILE
    vmem = pl.BlockSpec(memory_space=pltpu.VMEM)
    anywhere = pl.BlockSpec(memory_space=pl.ANY)
    smem = pl.BlockSpec(memory_space=pltpu.SMEM)
    near = ("vec", "net", "final", "rate")
    kinds = dict(
        win=((tiles, chips, 2, rows, 3 * TILE), bf16),
        wout=((chips, 2, rows, width), bf16),
        z=((tiles, micro, count, 3 * TILE), bf16),
        zh=((tiles, micro, 16, 3 * TILE), bf16),
        s=((tiles, micro, count, 3 * TILE), bf16),
        conv=((tiles, micro, count, TILE), bf16),
        uhat=((tiles, micro, 2, 2 * count, TILE), bf16),
        kern=((tiles, 2, 2 * count, TILE), bf16),
        res=((micro, count, width), f32),
        nt=((micro, width, count), bf16),
        n2=((micro, count, width), bf16),
        n2t=((micro, width, count), bf16),
        yt=((micro, width, count), bf16),
        pre=((3 * HID, 2 * count), f32),
    )
    outs = dict(
        kinds,
        wup=((chips, 2, rows, wide), bf16),
        wdown=((chips, 2, down_rows, width), bf16),
    )
    dma = pltpu.SemaphoreType.DMA
    scratch = {
        name + "_in": pltpu.VMEM(*kind) for name, kind in kinds.items()
    }
    for name, array in arrays.items():
        if name not in near and name != "lens":
            scratch[name + "_in"] = pltpu.VMEM(array.shape, array.dtype)
    scratch.update(
        dict(
            n_in=pltpu.VMEM((micro, count, width), bf16),
            one=pltpu.VMEM((2 * count, TILE), f32),
            two=pltpu.VMEM((2 * count, TILE), f32),
            act_in=pltpu.VMEM((HID, 2 * count), bf16),
            y_in=pltpu.VMEM((micro, count, width), bf16),
            in_own=pltpu.VMEM((tiles, rows, 3 * TILE), bf16),
            out_own=pltpu.VMEM((rows, width), bf16),
            up_own=pltpu.VMEM((rows, wide), bf16),
            down_own=pltpu.VMEM((down_rows, width), bf16),
            halo=pltpu.VMEM((micro, 16, width), bf16),
            halo_n=pltpu.VMEM((micro, 16, width), bf16),
            filt=pltpu.VMEM((2 * count, width), bf16),
            zbuf=pltpu.VMEM((16 + count, 3 * TILE), f32),
            ulow=pltpu.VMEM((tiles, micro, count, TILE), bf16),
            urecv=pltpu.VMEM((tiles, micro, count, TILE), bf16),
            spec=pltpu.VMEM((2 * count, TILE), bf16),
            win_sem=dma((tiles, 3, 2 * chips)),
            wout_sem=gather_sems(size),
            wup_sem=gather_sems(size),
            wdown_sem=gather_sems(size),
            halo_sem=dma((2,)),
            u_sem=dma((2, tiles)),
            copy_sems=dma((56,)),
        )
    )
    names = tuple(arrays) + tuple(outs) + tuple(scratch)
    made = pl.pallas_call(
        functools.partial(front_kernel, size, names),
        out_shape=[jax.ShapeDtypeStruct(*kind) for kind in outs.values()],
        in_specs=[
            smem if name == "lens" else vmem if name in near else anywhere for name in arrays
        ],
        out_specs=[anywhere] * len(outs),
        scratch_shapes=list(scratch.values()),
        compiler_params=pltpu.CompilerParams(
            collective_id=0, has_side_effects=True, vmem_limit_bytes=63 * 1024 * 1024
        ),
        name="front",
    )(*arrays.values())
    return dict(zip(outs, made))


GELU_SCALE = math.sqrt(2.0 / math.pi)


def gelu_pair(a):
    square = a * a
    half = 0.5 + 0.5 * jnp.tanh(a * (GELU_SCALE + (GELU_SCALE * 0.044715) * square))
    hidden = a * half
    bend = 2.0 * GELU_SCALE + (2.0 * GELU_SCALE * 0.134145) * square
    return hidden, half + (hidden - hidden * half) * bend


def mlp_kernel(
    n2_ref, n2t_ref, gm_ref, res_ref, vec_ref, wup_ref, wdown_ref,
    out_ref, gb_ref, dup_ref, ddown_ref, small_ref,
    acc_out, acc_gn, hid_ref, ga_ref,
):
    step, last = pl.program_id(0), pl.num_programs(0) - 1
    micro, count, width = n2_ref.shape
    chunk = width
    wup = wup_ref[...].reshape(width, chunk)
    wdown = wdown_ref[...].reshape(chunk, width)
    bias = vec_ref[pl.ds(8 + step, 1)]

    @pl.when(step == 0)
    def _():
        acc_out[...] = jnp.zeros_like(acc_out)
        acc_gn[...] = jnp.zeros_like(acc_gn)
        small_ref[...] = jnp.zeros_like(small_ref)

    bias_sum = jnp.zeros((8, chunk), f32)
    for m in range(micro):
        for rows in blocks(count, TILE):
            hidden, slope = gelu_pair(dot(n2_ref[m, rows], wup) + bias)
            hidden = hidden.astype(bf16)
            ga = (dot_nt(gm_ref[m, rows], wdown) * slope).astype(bf16)
            hid_ref[m, rows] = hidden
            ga_ref[m, rows] = ga
            bias_sum = bias_sum + folded(ga.astype(f32))
            acc_out[m, rows] += dot(hidden, wdown)
            acc_gn[m, rows] += dot_nt(ga, wup)
    small_ref[pl.ds(4 + step, 1)] = jnp.sum(bias_sum, axis=0, keepdims=True)
    down_total = dot_tn(hid_ref[0], gm_ref[0])
    up_total = dot(n2t_ref[0], ga_ref[0])
    for m in range(1, micro):
        down_total = down_total + dot_tn(hid_ref[m], gm_ref[m])
        up_total = up_total + dot(n2t_ref[m], ga_ref[m])
    ddown_ref[...] = down_total.astype(bf16)
    dup_ref[...] = up_total.astype(bf16).reshape(dup_ref.shape)

    @pl.when(step == last)
    def _():
        sums = [jnp.zeros((8, width), f32)] * 4
        for m in range(micro):
            for rows in blocks(count, 16):
                residual = res_ref[m, rows]
                out_ref[m, rows] = (residual + acc_out[m, rows] + vec_ref[12:13]).astype(bf16)
                gx, gain_part, grad = norm_rows_back(acc_gn[m, rows], residual, vec_ref[2:3])
                gm = gm_ref[m, rows].astype(f32)
                low = (gm + gx).astype(bf16)
                gb_ref[m, rows] = low
                parts = (gain_part, grad, low.astype(f32), gm)
                sums = [total + folded(part) for total, part in zip(sums, parts)]
        for k in range(4):
            small_ref[k : k + 1] = jnp.sum(sums[k], axis=0, keepdims=True)


def norm_rows_back(grad, values, gain):
    center = jnp.mean(values, axis=1, keepdims=True)
    centred = values - center
    variance = jnp.mean(centred * centred, axis=1, keepdims=True)
    scale = lax.rsqrt(variance + 1e-05)
    xh = centred * scale
    q = grad * gain
    gx = scale * (
        q - jnp.mean(q, axis=1, keepdims=True) - xh * jnp.mean(q * xh, axis=1, keepdims=True)
    )
    return gx, grad * xh, grad


def mlp(n2, n2t, gm, res, vectors, wup, wdown):
    micro, count, width = gm.shape
    chips, cores, rows, wide = wup.shape
    steps = wide // width
    per = chips // steps

    def whole(array):
        return pl.BlockSpec(array.shape, lambda i: (0,) * array.ndim)

    def shape(dims, kind=bf16):
        return jax.ShapeDtypeStruct(dims, kind)

    tokens = pl.BlockSpec((micro, count, width), lambda i: (0, 0, 0))
    return pl.pallas_call(
        mlp_kernel,
        grid=(steps,),
        in_specs=[
            whole(n2), whole(n2t), whole(gm), whole(res), whole(vectors),
            pl.BlockSpec((chips, cores, rows, width), lambda i: (0, 0, 0, i)),
            pl.BlockSpec((per, cores, wdown.shape[2], width), lambda i: (i, 0, 0, 0)),
        ],
        out_specs=[
            tokens, tokens,
            pl.BlockSpec((chips, cores, 1, rows, width), lambda i: (0, 0, i, 0, 0)),
            pl.BlockSpec((width, width), lambda i: (i, 0)),
            pl.BlockSpec((4 + steps, width), lambda i: (0, 0)),
        ],
        out_shape=[
            shape((micro, count, width)),
            shape((micro, count, width)),
            shape((chips, cores, steps, rows, width)),
            shape((wide, width)),
            shape((4 + steps, width), f32),
        ],
        scratch_shapes=[
            pltpu.VMEM((micro, count, width), f32),
            pltpu.VMEM((micro, count, width), f32),
            pltpu.VMEM((micro, count, width), bf16),
            pltpu.VMEM((micro, count, width), bf16),
        ],
        compiler_params=pltpu.CompilerParams(vmem_limit_bytes=63 * 1024 * 1024),
        name="mlp",
    )(n2, n2t, gm, res, vectors, wup, wdown)


def update_kernel(rates, firsts, *refs):
    count = len(rates)
    kept_in, kept_out, refs = refs[0], refs[4 * count + 1], refs[1 : 4 * count + 1] + refs[4 * count + 2 :]
    kept_out[...] = kept_in[...]
    ins, outs = refs[: 4 * count], refs[4 * count :]
    for i, (rate, first) in enumerate(zip(rates, firsts)):
        grad_ref, weight_ref, moment_ref, average_ref = ins[4 * i : 4 * i + 4]
        rows, columns = weight_ref.shape
        stepped = nesterov(
            weight_ref[...], moment_ref[...], average_ref[...],
            grad_ref[first : first + rows, :columns], rate,
        )
        for out, value in zip(outs[4 * i : 4 * i + 4], stepped):
            out[...] = value


def update(kept, sets):
    steps = 4
    held = pl.BlockSpec(
        (kept.shape[0], kept.shape[1] // steps, kept.shape[2]), lambda i: (0, i, 0)
    )
    arrays, in_specs, out_specs = [kept], [held], [held]
    shapes = [jax.ShapeDtypeStruct(kept.shape, kept.dtype)]

    def spec(shape, cut):
        if cut is None:
            return pl.BlockSpec(shape, lambda i: (0, 0))
        if cut:
            return pl.BlockSpec((shape[0], shape[1] // steps), lambda i: (0, i))
        return pl.BlockSpec((shape[0] // steps, shape[1]), lambda i: (i, 0))

    for grad, weight, moment, average, rate, first, cut in sets:
        arrays += [grad, weight, moment, average]
        in_specs += [spec(grad.shape, cut)] + [spec(weight.shape, cut)] * 3
        out_specs += [spec(weight.shape, cut)] * 4
        shapes += [jax.ShapeDtypeStruct(weight.shape, f32)] * 4
    made = pl.pallas_call(
        functools.partial(update_kernel, [s[4] for s in sets], [s[5] for s in sets]),
        grid=(steps,),
        in_specs=in_specs,
        out_specs=out_specs,
        out_shape=shapes,
        compiler_params=pltpu.CompilerParams(vmem_limit_bytes=63 * 1024 * 1024),
        name="update",
    )(*arrays)
    return made[0], [made[4 * i + 1 : 4 * i + 5] for i in range(len(sets))]


GROUP = 32
HALF = 384


def back_kernel(size, names, *refs):
    ref = types.SimpleNamespace(**dict(zip(names, refs)))
    gb, vec, table, table_back = ref.gb, ref.vec, ref.table, ref.back
    micro, count, width = gb.shape
    slot = 2 * count
    tiles = width // TILE
    ring = Ring(size)
    gw, gc, gcr, gz = ref.gw, ref.gc, ref.gcr, ref.gz
    vsum, nsum, fsum = ref.vsum, ref.nsum, ref.fsum
    one, two = ref.one, ref.two
    gate, turned = ref.gate, ref.turned
    inside = jnp.where(ring.pos < 1, 1.0, 0.0).astype(f32)
    first_half, second_half = ring.pos == 0, ring.pos == 1
    copies = Copies(ref.copy_sems)
    gate_copies = [
        copies.start(ref.s.at[j, :, :, pl.ds(0, TILE)], gate.at[j]) for j in range(tiles)
    ]
    wout = ref.din.at[0]
    wout_copy = copies.start(ref.wout, wout)
    turned_copy = copies.start(ref.yt, turned)
    win_copy = copies.start(ref.win, ref.win_in)

    greet_all(ring)
    red = {}

    def parts_of(name):
        return [getattr(ref, name + str(k)) for k in range(6)]

    deep, blocks_up = ref.ddown.shape[2], ref.dup.shape[2]
    fit = count // deep
    staged = []
    for chip in range(ring.count):
        at, row = chip // fit, chip % fit * deep
        staged.append(
            copies.start(
                ref.ddown.at[chip, ring.core], gz.at[at // micro, at % micro, pl.ds(row, deep)]
            )
        )
    for c in range(blocks_up):
        staged.append(
            copies.start(ref.dup.at[:, ring.core, c], ref.din.at[1 + c // 2, :, c % 2])
        )

    def down_block(chip):
        at, row = chip // fit, pl.multiple_of(lax.rem(chip, fit) * deep, 16)
        return gz[at // micro, lax.rem(at, micro), pl.ds(row, deep)]

    def up_block(chip):
        return jnp.stack([ref.din[1 + c // 2, chip, c % 2] for c in range(blocks_up)])

    down = Reduction(ring, -1, ref.ddown, *parts_of("down"), down_block)
    up = Reduction(ring, 1, ref.dup, *parts_of("up"), up_block)
    out = Reduction(ring, -1, ref.dout, *parts_of("out"))
    inner = [
        Reduction(ring, 1 - 2 * (j % 2), ref.din.at[j], *[part.at[j] for part in parts_of("in")])
        for j in range(tiles)
    ]
    down.begin()
    up.begin()
    vsum[...] = jnp.zeros_like(vsum)
    nsum[...] = jnp.zeros_like(nsum)
    small = ref.small
    for j in range(tiles):
        lane, base = slice(j * TILE, (j + 1) * TILE), j * GROUP
        vsum[base + 2 : base + 4] = small[0:2, lane]
        vsum[base + 7 : base + 8] = small[2:3, lane]
        vsum[base + 12 : base + 13] = small[3:4, lane]
        vsum[base + 8 : base + 12] = small[4:8, lane]

    crossing = []
    wout_copy.wait()
    for j in range(tiles):
        gate_copies[j].wait()
        weight = wout[...].reshape(width, width)[j * TILE : (j + 1) * TILE]

        @pl.loop(0, micro)
        def _(m):
            one[:count] = dot_nt(gb[m], weight)
            length = ref.lens[0, m] - ring.pos * count
            for rows in blocks(count, 32):
                mask = valid_rows(length, rows.start, 32, TILE)
                grad = mask * one[rows].astype(bf16).astype(f32)
                gw[j, m, rows] = grad.astype(bf16)
                gc[j, m, rows] = (grad * gate[j, m, rows].astype(f32)).astype(bf16)

        copy = remote(
            gc.at[j], gcr.at[j], ref.gc_sem.at[0, j], ref.gc_sem.at[1, j], ring.across
        )
        copy.start()
        crossing.append(copy)
    turned_copy.wait()

    @pl.loop(0, tiles)
    def _(j):
        cols = pl.ds(pl.multiple_of(j * TILE, TILE), TILE)
        total = dot(turned[0], gb[0, :, cols])
        for m in range(1, micro):
            total = total + dot(turned[m], gb[m, :, cols])
        dout = ref.dout
        dout[:, :, :, cols] = total.astype(bf16).reshape(dout.shape[:3] + (TILE,))

    turned_copy = copies.start(ref.nt, turned)
    out.begin()
    for copy in staged[: ring.count]:
        copy.wait()
    down.merge()
    for copy in staged[ring.count :]:
        copy.wait()
    up.merge()

    parity = 1.0 - 2.0 * (lax.broadcasted_iota(jnp.int32, (16, TILE), 0) % 2).astype(f32)
    gk = ref.gk
    gbuf, zbuf, spec = ref.gbuf, ref.zbuf, ref.spec
    first_rows, next_rows = ref.first_rows, ref.next_rows

    def loads(j, m, at):
        made = [
            (ref.s.at[j, m, :, pl.ds(TILE, 2 * TILE)], ref.s_buf.at[at]),
            (ref.z.at[j, m], ref.z_buf.at[at]),
            (ref.uhat.at[j, m], ref.u_buf.at[at]),
            (ref.conv.at[j, m], ref.c_buf.at[at]),
        ]
        return [
            pltpu.make_async_copy(src, dst, ref.load_sems.at[at, i])
            for i, (src, dst) in enumerate(made)
        ]

    def load_kernel(j):
        return pltpu.make_async_copy(ref.kern.at[j], ref.k_buf, ref.kernel_sem.at[0])

    def start_loads(j, m, at):
        for copy in loads(j, m, at):
            copy.start()

    start_loads(0, 0, 0)
    load_kernel(0).start()
    gbuf[:, count:] = jnp.zeros_like(gbuf[:, count:])

    def unmix(j):
        crossing[j].wait_recv()
        load_kernel(j).wait()
        lane = slice(j * TILE, (j + 1) * TILE)
        kn = ref.k_buf

        @pl.loop(0, micro)
        def _(m):
            at = lax.rem(j * micro + m, 2)
            for copy in loads(j, m, at):
                copy.wait()

            @pl.when(m + 1 < micro)
            def _():
                start_loads(j, m + 1, 1 - at)

            if j + 1 < tiles:

                @pl.when(m + 1 == micro)
                def _():
                    start_loads(j + 1, 0, 1 - at)

            one[...] = dot(table[...], gc[j, m])
            keep = jnp.where(m > 0, 1.0, 0.0).astype(f32)
            uh = ref.u_buf

            def filter_grad(d, re, im, gr, gi):
                ur, ui = uh[at, d, re].astype(f32), uh[at, d, im].astype(f32)
                gk[d, re] = gk[d, re] * keep + (ur * gr + ui * gi)
                gk[d, im] = gk[d, im] * keep + (ur * gi - ui * gr)

            @pl.when(first_half)
            def _():
                two[...] = dot(table[...], gcr[j, m])
                for re in blocks(count, 16):
                    im = slice(re.start + count, re.stop + count)
                    gr, gi, hr, hi = one[re], one[im], two[re], two[im]
                    k0r, k0i = kn[0, re].astype(f32), kn[0, im].astype(f32)
                    k1r, k1i = kn[1, re].astype(f32), kn[1, im].astype(f32)
                    spec[re] = (k0r * gr + k0i * gi + k1r * hr + k1i * hi).astype(bf16)
                    spec[im] = (k0r * gi - k0i * gr + k1r * hi - k1i * hr).astype(bf16)
                    filter_grad(0, re, im, gr, gi)

            @pl.when(second_half)
            def _():
                for re in blocks(count, 16):
                    im = slice(re.start + count, re.stop + count)
                    gr, gi = one[re], one[im]
                    k0r, k0i = kn[0, re].astype(f32), kn[0, im].astype(f32)
                    spec[re] = (k0r * gr + k0i * gi).astype(bf16)
                    spec[im] = (k0r * gi - k0i * gr).astype(bf16)
                    filter_grad(0, re, im, gr, gi)
                    filter_grad(1, re, im, gr, gi)

            two[:count] = dot(table_back[...], spec[...])
            skip_sum = jnp.zeros((8, TILE), f32)
            for rows in blocks(count, 32):
                x1 = ref.s_buf[at, rows, :TILE].astype(f32)
                v = ref.s_buf[at, rows, TILE:].astype(f32)
                grad_w = gw[j, m, rows].astype(f32)
                gc_full = grad_w * gate[j, m, rows].astype(f32)
                gu = two[rows] * (1.0 / count) + vec[25:26, lane] * gc_full
                skip_sum = skip_sum + folded(gc_full * (x1 * v))
                grads = (grad_w * ref.c_buf[at, rows].astype(f32), gu * v, gu * x1)
                for p in range(3):
                    low = grads[p].astype(bf16)
                    gbuf[p, rows] = low.astype(f32)
                    if rows.start == 0:
                        first_rows[j, m, :, p * TILE : (p + 1) * TILE] = low[:16]
            vsum[j * GROUP + 25 : j * GROUP + 26] += jnp.sum(skip_sum, axis=0, keepdims=True)
            for p in range(3):
                cols = slice(p * TILE, (p + 1) * TILE)
                zbuf[:16] = ref.zh[j, m, :, cols].astype(f32)
                for rows in blocks(count, 32):
                    zbuf[rows.start + 16 : rows.stop + 16] = ref.z_buf[at, rows, cols].astype(f32)
                taps = [vec[13 + 3 * k + p : 14 + 3 * k + p, lane] for k in range(3)]
                sums = [jnp.zeros((8, TILE), f32) for _ in range(4)]
                for rows in blocks(count, 32):
                    first = rows.start
                    grad = gbuf[p, rows]
                    gz[j, m, rows, cols] = (
                        taps[0] * grad
                        + taps[1] * gbuf[p, first + 1 : first + 33]
                        + taps[2] * gbuf[p, first + 2 : first + 34]
                    ).astype(bf16)
                    for k in range(3):
                        sums[k] = sums[k] + folded(grad * zbuf[first + 16 - k : first + 48 - k])
                    sums[3] = sums[3] + folded(grad)
                gz[j, m, count - 16 :, cols] = gbuf[p, count - 16 : count].astype(bf16)
                for k in range(4):
                    row = j * GROUP + 13 + 3 * k + p
                    vsum[row : row + 1] += jnp.sum(sums[k], axis=0, keepdims=True)

        if j + 1 < tiles:
            load_kernel(j + 1).start()
        edge = remote(
            first_rows.at[j], next_rows.at[j], ref.edge_sem.at[0, j],
            ref.edge_sem.at[1, j], ring.across,
        )
        edge.start()
        @pl.when(first_half)
        def _():
            for re in blocks(2 * count, 16):
                spec[re] = gk[0, re].astype(bf16)
            gate[j, 1] = jnp.zeros_like(gate[j, 1])

        @pl.when(second_half)
        def _():
            for re in blocks(2 * count, 16):
                spec[re] = gk[1, re].astype(bf16)
            two[count:] = dot(table_back[...], spec[...])
            for rows in blocks(count, 16):
                second = two[rows.start + count : rows.stop + count]
                gate[j, 1, rows] = (second * (1.0 / count)).astype(bf16)
            for re in blocks(count, 16):
                im = slice(re.start + count, re.stop + count)
                spec[re] = (gk[0, re] + parity * gk[1, im]).astype(bf16)
                spec[im] = (gk[0, im] - parity * gk[1, re]).astype(bf16)

        two[:count] = dot(table_back[...], spec[...])
        for rows in blocks(count, 16):
            gate[j, 0, rows] = (two[rows] * (1.0 / count)).astype(bf16)
        return edge

    def project_back(j, edge):
        edge.wait_recv()
        lane = slice(j * TILE, (j + 1) * TILE)
        ebuf = ref.ebuf
        for m in range(micro):
            for p in range(3):
                cols = slice(p * TILE, (p + 1) * TILE)
                own = gz[j, m, count - 16 :, cols].astype(f32)
                ebuf[:16] = own
                ebuf[16:] = next_rows[j, m, :, cols].astype(f32) * inside
                gz[j, m, count - 16 :, cols] = (
                    vec[13 + p : 14 + p, lane] * own
                    + vec[16 + p : 17 + p, lane] * ebuf[1:17]
                    + vec[19 + p : 20 + p, lane] * ebuf[2:18]
                ).astype(bf16)
        for p in range(3):
            cols = slice(p * TILE, (p + 1) * TILE)
            total = dot(turned[0], gz[j, 0, :, cols])
            for m in range(1, micro):
                total = total + dot(turned[m], gz[j, m, :, cols])
            din = ref.din
            din[j, :, :, :, cols] = total.astype(bf16).reshape(din.shape[1:4] + (TILE,))
            bias = jnp.zeros((8, TILE), f32)
            for m in range(micro):
                for rows in blocks(count, 32):
                    bias = bias + folded(gz[j, m, rows, cols].astype(f32))
            row = j * GROUP + 4 + p
            vsum[row : row + 1] = jnp.sum(bias, axis=0, keepdims=True)
        inner[j].begin()

    edges = [unmix(0)]
    down.advance(1)
    up.advance(1)
    out.merge()
    edges.append(unmix(1))
    turned_copy.wait()
    project_back(0, edges[0])
    down.advance(2)
    up.advance(2)
    out.advance(1)
    inner[0].merge()
    edges.append(unmix(2))
    project_back(1, edges[1])
    x_copies = [
        copies.start(ref.x.at[:, :, pl.ds(j * TILE, TILE)], gcr.at[j]) for j in range(tiles)
    ]
    pre_copies = [
        copies.start(
            ref.pre.at[:, pl.ds(t * TILE, TILE)], one.at[pl.ds(t * 3 * HID, 3 * HID)]
        )
        for t in range(slot // TILE)
    ]
    down.advance(3)
    up.advance(3)
    inner[1].merge()
    project_back(2, edges[2])
    out.advance(2)
    inner[0].advance(1)
    inner[1].advance(1)
    for copy in x_copies:
        copy.wait()
    for copy in crossing:
        copy.wait_send()

    def first_norm(m, part):
        piece = slice(part * TILE, (part + 1) * TILE)
        for t in range(tiles):
            total = 0.0
            for j in range(tiles):
                weight = ref.win_in[j].reshape(width, 3 * TILE)[t * TILE : (t + 1) * TILE]
                total = total + dot_nt(gz[j, m, piece], weight)
            gbuf[t, piece] = total
        sums = [jnp.zeros((8, width), f32)] * 2
        for rows in blocks(count, 16)[part * TILE // 16 : (part + 1) * TILE // 16]:
            tokens = jnp.concatenate([gcr[j, m, rows] for j in range(tiles)], axis=1)
            grad = jnp.concatenate([gbuf[t, rows] for t in range(tiles)], axis=1)
            gx, gain_part, shift_part = norm_rows_back(grad, tokens.astype(f32), vec[0:1])
            sums = [sums[0] + folded(gain_part), sums[1] + folded(shift_part)]
            total = (gb[m, rows].astype(f32) + gx).astype(bf16)
            for j in range(tiles):
                gc[j, m, rows] = total[:, j * TILE : (j + 1) * TILE]
        for k in range(2):
            total = jnp.sum(sums[k], axis=0, keepdims=True)
            for j in range(tiles):
                row = j * GROUP + k
                vsum[row : row + 1] += total[:, j * TILE : (j + 1) * TILE]

    def filter_back():
        ref.net_sum[...] = jnp.zeros_like(ref.net_sum)
        net = ref.net
        for copy in pre_copies:
            copy.wait()

        def pre(first, last):
            return jnp.concatenate(
                [
                    one[t * 3 * HID + first : t * 3 * HID + last]
                    for t in range(slot // TILE)
                ],
                axis=1,
            )

        frequency = net[:, EMB + 3 + 2 * HID : EMB + 4 + 2 * HID]
        rates = ref.rate[...].reshape(1, width)
        final_low = ref.final[...].astype(bf16)
        acts, slopes = [], []
        for i in range(3):
            pairs = [
                sin_cos(frequency[part] * pre(i * HID + part.start, i * HID + part.stop))
                for part in blocks(HID, 16)
            ]
            acts.append(jnp.concatenate([pair[0] for pair in pairs], axis=0))
            slopes.append(jnp.concatenate([pair[1] for pair in pairs], axis=0))
        last = acts[2].astype(bf16)
        grad = jnp.zeros((HID, slot), f32)
        for j in range(tiles):
            lane = slice(j * TILE, (j + 1) * TILE)
            for half in range(2):
                for rows in blocks(count, 32):
                    first = half * count + rows.start
                    at_row = lax.broadcasted_iota(jnp.int32, (32, TILE), 0) + first
                    window = jnp.exp(at_row.astype(f32) * (rates[:, lane] * (-1.0 / slot))) + 0.05
                    spec[first : first + 32] = (gate[j, half, rows].astype(f32) * window).astype(bf16)
            total = dot(last, spec[...])
            for part in blocks(TILE, 128):
                at = j * TILE + part.start
                row, column = at // HALF * HID, at % HALF
                fsum[row : row + HID, column : column + 128] = total[:, part]
            grad = grad + dot_nt(final_low[:, lane], spec[...])
        freq_sum = jnp.zeros((HID, 1), f32)

        def put(first, values):
            ref.net_sum[:, first : first + values.shape[1]] = values

        for i in (2, 1, 0):
            turn = grad * slopes[i]
            freq_sum = freq_sum + jnp.sum(turn * pre(i * HID, (i + 1) * HID), axis=1, keepdims=True)
            grad = turn * frequency
            below = ref.feature[...] if i == 0 else acts[i - 1]
            made = lax.dot_general(
                grad, below, (((1,), (1,)), ((), ())), precision=highest,
                preferred_element_type=f32,
            )
            if i == 0:
                put(0, made[:, : EMB + 1])
            else:
                first = EMB + 1 + (i - 1) * (HID + 1)
                put(first, made)
                put(first + HID, jnp.sum(grad, axis=1, keepdims=True))
                grad = lax.dot_general(
                    net[:, first : first + HID], grad, (((0,), (0,)), ((), ())),
                    precision=highest, preferred_element_type=f32,
                )
        put(EMB + 3 + 2 * HID, freq_sum)
        nsum[:HID] = ref.net_sum[:, :128]
        nsum[HID:] = ref.net_sum[:, 128:]

    smalls = []
    for values, name in ((fsum, "f"), (nsum, "n"), (vsum, "v")):
        parts = [getattr(ref, name + str(k)) for k in range(5)]
        smalls.append(SmallSum(ring, values, *parts))
    win_copy.wait()
    pieces = [(m, part) for m in range(micro) for part in range(count // TILE)]
    quarter = max(1, len(pieces) // 4)

    def norms(at):
        last = len(pieces) if at == 3 else (at + 1) * quarter
        for m, part in pieces[at * quarter : last]:
            first_norm(m, part)

    norms(0)
    inner[2].merge()
    inner[0].advance(2)
    inner[1].advance(2)
    down.collect()
    norms(1)
    inner[2].advance(1)
    up.collect()
    out.advance(3)
    filter_back()
    for work in smalls[:2]:
        work.begin()
    inner[2].advance(2)
    inner[0].advance(3)
    inner[1].advance(3)
    norms(2)
    inner[2].advance(3)
    out.collect()
    inner[0].collect()
    inner[1].collect()
    for work in smalls[:2]:
        work.add_up()
    norms(3)
    smalls[2].begin()
    inner[2].collect()
    for work in smalls[:2]:
        work.spread()
    for j in range(tiles):
        copies.out(gc.at[j], ref.input_grad.at[:, :, pl.ds(j * TILE, TILE)])
    psum = ref.proj_sum
    ref.down_sum[...] = down.result()
    total = up.result()
    for c in range(blocks_up):
        psum[:, (4 + c) * width : (5 + c) * width] = total[c]
    psum[:, 3 * width : 4 * width] = out.result()
    smalls[2].add_up()
    smalls[2].spread()
    for j in range(tiles):
        total = inner[j].result()
        for p in range(3):
            first = p * width + j * TILE
            psum[:, first : first + TILE] = total[:, p * TILE : (p + 1) * TILE]
    for work in smalls:
        work.finish()
    for part in blocks(width, 128):
        row, column = part.start // HALF * HID, part.start % HALF
        ref.final_sum[:, part] = smalls[0].sums[row : row + HID, column : column + 128]
    ref.net_sum[:, :128] = smalls[1].sums[:HID]
    ref.net_sum[:, 128:] = smalls[1].sums[HID:]
    for j in range(tiles):
        ref.vec_sum[:, j * TILE : (j + 1) * TILE] = smalls[2].sums[j * GROUP : (j + 1) * GROUP]
    for work in [down, up, out] + inner:
        work.finish()
    for edge in edges:
        edge.wait_send()
    copies.finish()


def back(size, arrays):
    chips = size // 2
    micro, count, width = arrays["gb"].shape
    blocks_up, rows = arrays["dup"].shape[2:4]
    wide = blocks_up * width
    down_rows = arrays["ddown"].shape[2]
    tiles = width // TILE
    vmem = pl.BlockSpec(memory_space=pltpu.VMEM)
    anywhere = pl.BlockSpec(memory_space=pl.ANY)
    smem = pl.BlockSpec(memory_space=pltpu.SMEM)
    near = ("gb", "vec", "net", "final", "rate", "table", "back", "zh", "small", "feature")
    small_rows = 8 * size
    outs = dict(
        input_grad=((micro, count, width), bf16),
        proj_sum=((rows, 4 * width + wide), f32),
        down_sum=((down_rows, width), f32),
        vec_sum=((GROUP, width), f32),
        final_sum=((HID, width), f32),
        net_sum=((HID, 256), f32),
    )
    dma = pltpu.SemaphoreType.DMA
    tile_tokens = (tiles, micro, count, TILE)
    edge_rows = (tiles, micro, 16, 3 * TILE)
    scratch = dict(
        din=pltpu.VMEM((tiles, chips, 2, rows, 3 * TILE), bf16),
        dout=pltpu.VMEM((chips, 2, rows, width), bf16),
        gw=pltpu.VMEM(tile_tokens, bf16),
        gc=pltpu.VMEM(tile_tokens, bf16),
        gcr=pltpu.VMEM(tile_tokens, bf16),
        gate=pltpu.VMEM(tile_tokens, bf16),
        gz=pltpu.VMEM((tiles, micro, count, 3 * TILE), bf16),
        turned=pltpu.VMEM((micro, width, count), bf16),
        vsum=pltpu.VMEM((small_rows, TILE), f32),
        nsum=pltpu.VMEM((small_rows, 128), f32),
        fsum=pltpu.VMEM((small_rows, HALF), f32),
        gk=pltpu.VMEM((2, 2 * count, TILE), f32),
        gbuf=pltpu.VMEM((3, count + 16, TILE), f32),
        one=pltpu.VMEM((2 * count, TILE), f32),
        two=pltpu.VMEM((2 * count, TILE), f32),
        zbuf=pltpu.VMEM((count + 16, TILE), f32),
        ebuf=pltpu.VMEM((32, TILE), f32),
        spec=pltpu.VMEM((2 * count, TILE), bf16),
        first_rows=pltpu.VMEM(edge_rows, bf16),
        next_rows=pltpu.VMEM(edge_rows, bf16),
        s_buf=pltpu.VMEM((2, count, 2 * TILE), bf16),
        z_buf=pltpu.VMEM((2, count, 3 * TILE), bf16),
        u_buf=pltpu.VMEM((2, 2, 2 * count, TILE), bf16),
        c_buf=pltpu.VMEM((2, count, TILE), bf16),
        k_buf=pltpu.VMEM((2, 2 * count, TILE), bf16),
        load_sems=dma((2, 4)),
        kernel_sem=dma((1,)),
        gc_sem=dma((2, tiles)),
        edge_sem=dma((2, tiles)),
        copy_sems=dma((40,)),
        win_in=pltpu.VMEM(arrays["win"].shape, bf16),
    )
    ups, downs = chips // 2, (chips - 1) // 2
    for name, lead, dims in (
        ("up", (), (blocks_up, rows, width)), ("down", (), (down_rows, width)), ("out", (), (rows, width)),
        ("in", (tiles,), (rows, 3 * TILE)),
    ):
        made = [pltpu.VMEM(lead + (count,) + dims, bf16) for count in (chips, ups, downs)]
        made += [pltpu.VMEM(lead + dims, bf16)] * 2 + [dma(lead + (2, chips + 1 + ups + downs))]
        for k, part in enumerate(made):
            scratch[name + str(k)] = part
    for name, columns in (("v", TILE), ("n", 128), ("f", HALF)):
        made = small_scratch(size, small_rows, columns)
        made.insert(3, pltpu.VMEM((small_rows, columns), f32))
        for k, part in enumerate(made):
            scratch[name + str(k)] = part
    names = tuple(arrays) + tuple(outs) + tuple(scratch)
    return pl.pallas_call(
        functools.partial(back_kernel, size, names),
        out_shape=[jax.ShapeDtypeStruct(*kind) for kind in outs.values()],
        in_specs=[
            smem if name == "lens" else vmem if name in near else anywhere for name in arrays
        ],
        out_specs=[anywhere] + [vmem] * (len(outs) - 1),
        scratch_shapes=list(scratch.values()),
        compiler_params=pltpu.CompilerParams(
            collective_id=1, has_side_effects=True, vmem_limit_bytes=255 * 1024 * 256
        ),
        name="back",
    )(*arrays.values())


def fits(size, groups, tokens, proj_weights, down_weights):
    micro, _, count, width = tokens.shape
    wide = down_weights.shape[0] * size
    return (
        groups == 2
        and size % 4 == 0
        and size == 16
        and proj_weights.shape[0] % 16 == 0
        and down_weights.shape[0] % 16 == 0
        and count % TILE == 0
        and width == 3 * TILE
        and micro >= groups
        and 3 * HID <= TILE
        and down_weights.shape[0] <= count
        and micro * count <= 1024
        and wide == 4 * width
        and proj_weights.shape[1] == 4 * width + wide
    )


def on_device_tuned(
    block_input,
    out_grad,
    lengths,
    decay_rates,
    proj_weights,
    proj_moment,
    proj_average,
    down_weights,
    down_moment,
    down_average,
    vectors,
    vector_moment,
    vector_average,
    filter_net,
    net_moment,
    net_average,
    filter_out,
    final_moment,
    final_average,
):
    micro, _, count, width = block_input.shape
    size = lax.axis_size("seq")
    tokens = block_input.reshape(micro, count, width)
    plain_table = transform_table(count)
    table = jnp.asarray(plain_table, dtype=bf16)
    table_back = jnp.asarray(plain_table.T, dtype=bf16)
    feature = jnp.asarray(feature_table(count * lax.axis_size("pos")))
    shared = dict(
        x=tokens, lens=lengths.T, vec=vectors, net=filter_net.T, final=filter_out,
        rate=decay_rates, table=table, back=table_back, feature=feature,
    )
    made = types.SimpleNamespace(**front(size, dict(shared, proj=proj_weights, down=down_weights)))
    block_output, branch_grad, up_step, down_step, small = mlp(
        made.n2, made.n2t, out_grad.reshape(micro, count, width), made.res, vectors,
        made.wup, made.wdown,
    )
    chips = size // 2
    input_grad, proj_sum, down_sum, vector_sum, final_sum, net_sum = back(
        size,
        dict(
            shared, win=made.win, wout=made.wout, z=made.z, zh=made.zh, s=made.s, conv=made.conv,
            uhat=made.uhat, kern=made.kern, nt=made.nt, yt=made.yt, pre=made.pre,
            gb=branch_grad, small=small,
            dup=up_step,
            ddown=down_step.reshape(chips, 2, -1, width),
        ),
    )
    input_grad, steps = update(
        input_grad,
        [
            (proj_sum, proj_weights, proj_moment, proj_average, 0.0001, 0, 1),
            (down_sum, down_weights, down_moment, down_average, 0.0001, 0, 0),
            (vector_sum, vectors, vector_moment, vector_average, 0.001, 0, None),
            (net_sum, filter_net.T, net_moment.T, net_average.T, 0.0001, 0, None),
            (final_sum, filter_out, final_moment, final_average, 2e-06, 0, None),
        ]
    )
    steps[3] = [array.T for array in steps[3]]
    return (
        block_output.reshape(block_input.shape),
        input_grad.reshape(block_input.shape),
        *steps[0], *steps[1], *steps[2], *steps[3], *steps[4],
    )


def on_device_plain(
    block_input,
    out_grad,
    lengths,
    decay_rates,
    proj_weights,
    proj_moment,
    proj_average,
    down_weights,
    down_moment,
    down_average,
    vectors,
    vector_moment,
    vector_average,
    filter_net,
    net_moment,
    net_average,
    filter_out,
    final_moment,
    final_average,
):
    micro = block_input.shape[0]
    count = block_input.shape[2]
    width = block_input.shape[3]
    groups = lax.axis_size("pos")
    slot_length = count * groups
    tokens_all = micro * count
    group = lax.axis_index("pos")
    tap = vectors[13:22].reshape(3, 3 * width)
    short_bias = vectors[22:25].reshape(-1)
    in_bias = vectors[4:7].reshape(-1)
    up_bias = vectors[8:12].reshape(-1)
    skip = vectors[25]

    low_rows = proj_weights.astype(bf16)
    in_weight = lax.all_gather(low_rows[:, : 3 * width], "seq", axis=0, tiled=True)
    out_weight = lax.all_gather(low_rows[:, 3 * width : 4 * width], "seq", axis=0, tiled=True)
    up_weight = lax.all_gather(low_rows[:, 4 * width :], "seq", axis=0, tiled=True)
    down_weight = lax.all_gather(down_weights.astype(bf16), "seq", axis=0, tiled=True)

    table = jnp.asarray(transform_table(count))
    table_low = table.astype(bf16)
    every = jnp.arange(slot_length, dtype=jnp.int32)

    def make_filter(net_values, final_values):
        return filter_fn(net_values, final_values, decay_rates, every, slot_length)

    filters, filter_back = jax.vjp(make_filter, filter_net, filter_out)
    pieces = filters.reshape(groups, count, width)
    spectra = [
        jnp.dot(table, pieces[d], precision=lax.Precision.HIGH, preferred_element_type=f32)
        for d in range(groups)
    ]
    kernels = [spectra[0]] + [spectra[d] + turned(spectra[d - 1], 1.0) for d in range(1, groups)]

    def transform(values):
        return jnp.stack([dot(table_low, values[m]) for m in range(micro)])

    def transform_back(spectrum):
        low = spectrum.astype(bf16)
        return jnp.stack([dot_tn(table_low, low[m]) for m in range(micro)]) * (1.0 / count)

    tokens_low = block_input[:, 0]
    before = passed_along(tokens_low[:, -2:], "pos", 1)
    tokens = tokens_low.astype(f32).reshape(tokens_all, width)
    xh_one, scale_one = norm_parts(tokens)
    normed = (xh_one * vectors[0] + vectors[1]).astype(bf16)
    xh_before, _ = norm_parts(before.astype(f32).reshape(micro * 2, width))
    normed_before = (xh_before * vectors[0] + vectors[1]).astype(bf16)
    z = (dot(normed, in_weight) + in_bias).reshape(micro, count, 3 * width)
    z_before = (dot(normed_before, in_weight) + in_bias).reshape(micro, 2, 3 * width)
    z_before = jnp.where(group > 0, z_before, 0.0)
    z_long = jnp.concatenate([z_before, z], axis=1)
    short = (
        tap[0] * z_long[:, 2:] + tap[1] * z_long[:, 1:-1] + tap[2] * z_long[:, :-2] + short_bias
    ).astype(bf16)
    x0 = short[:, :, :width].astype(f32)
    x1 = short[:, :, width : 2 * width].astype(f32)
    v = short[:, :, 2 * width :].astype(f32)

    u = x1 * v
    u_low = u.astype(bf16)
    u_hat = [transform(u_low)]
    for d in range(1, groups):
        u_hat.append(transform(passed_along(u_low, "pos", d)))
    total = product(kernels[0], u_hat[0])
    for d in range(1, groups):
        total = total + product(kernels[d], u_hat[d])
    conv = transform_back(total) + skip * u
    here = group * count + jnp.arange(count, dtype=jnp.int32)
    mask = (here[None, :] < lengths[:, 0][:, None]).astype(f32)[:, :, None]
    y = (mask * x0 * conv).astype(bf16).reshape(tokens_all, width)
    residual = tokens + dot(y, out_weight) + vectors[7]
    xh_two, scale_two = norm_parts(residual)
    normed_two = (xh_two * vectors[2] + vectors[3]).astype(bf16)

    cot_low = out_grad[:, 0].reshape(tokens_all, width)
    cot = cot_low.astype(f32)
    pre = dot(normed_two, up_weight) + up_bias
    hidden, gelu_back = jax.vjp(jax.nn.gelu, pre)
    hidden_low = hidden.astype(bf16)
    block_output = (residual + dot(hidden_low, down_weight) + vectors[12]).astype(bf16)
    pre_grad = gelu_back(dot_nt(cot_low, down_weight))[0].astype(bf16)
    down_step = dot_tn(hidden_low, cot_low)
    up_step = dot_tn(normed_two, pre_grad)
    normed_two_grad = dot_nt(pre_grad, up_weight)
    part, gain_two, shift_two = norm_back(normed_two_grad, xh_two, scale_two, vectors[2])
    residual_grad = cot + part
    branch_low = residual_grad.astype(bf16)
    out_step = dot_tn(y, branch_low)
    y_grad = dot_nt(branch_low, out_weight).astype(bf16).astype(f32).reshape(micro, count, width)

    gw = mask * y_grad
    gx0 = gw * conv
    gc = gw * x0
    gc_low = gc.astype(bf16)
    skip_grad = jnp.sum(gc * u, axis=(0, 1))
    gc_hat = [transform(gc_low)]
    for d in range(1, groups):
        gc_hat.append(transform(passed_along(gc_low, "pos", -d)))
    back = product_conj(kernels[0], gc_hat[0])
    for d in range(1, groups):
        back = back + product_conj(kernels[d], gc_hat[d])
    gu = transform_back(back) + skip * gc
    kernel_grads = [jnp.sum(product_conj(u_hat[d], gc_hat[0]), axis=0) for d in range(groups)]
    filter_grads = []
    for d in range(groups):
        got = kernel_grads[d]
        if d + 1 < groups:
            got = got + turned(kernel_grads[d + 1], -1.0)
        filter_grads.append(dot_tn(table_low, got.astype(bf16)) * (1.0 / count))
    net_local, final_local = filter_back(jnp.concatenate(filter_grads, axis=0))
    short_grad = jnp.concatenate([gx0, gu * v, gu * x1], axis=-1).astype(bf16)
    after = passed_along(short_grad[:, :2], "pos", -1)
    short_long = jnp.concatenate([short_grad, after], axis=1).astype(f32)
    z_grad = (
        tap[0] * short_long[:, :-2] + tap[1] * short_long[:, 1:-1] + tap[2] * short_long[:, 2:]
    ).astype(bf16)
    here_grad = short_long[:, :-2]
    tap_grads = [
        jnp.sum(here_grad * z_long[:, 2 - k : 2 - k + count], axis=(0, 1)) for k in range(3)
    ]
    short_bias_grad = jnp.sum(here_grad, axis=(0, 1))
    z_grad = z_grad.reshape(tokens_all, 3 * width)
    in_step = dot_tn(normed, z_grad)
    in_bias_grad = jnp.sum(z_grad.astype(f32), axis=0)
    normed_grad = dot_nt(z_grad, in_weight)
    part, gain_one, shift_one = norm_back(normed_grad, xh_one, scale_one, vectors[0])
    input_grad = (residual_grad + part).astype(bf16)

    vector_local = jnp.concatenate(
        [
            gain_one[None],
            shift_one[None],
            gain_two[None],
            shift_two[None],
            in_bias_grad.reshape(3, width),
            jnp.sum(branch_low.astype(f32), axis=0)[None],
            jnp.sum(pre_grad.astype(f32), axis=0).reshape(4, width),
            jnp.sum(cot, axis=0)[None],
            jnp.stack(tap_grads).reshape(9, width),
            short_bias_grad.reshape(3, width),
            skip_grad[None],
        ],
        axis=0,
    )
    proj_local = jnp.concatenate([in_step, out_step, up_step], axis=1).astype(bf16)
    proj_shard = lax.psum_scatter(proj_local, "seq", scatter_dimension=0, tiled=True)
    down_shard = lax.psum_scatter(down_step.astype(bf16), "seq", scatter_dimension=0, tiled=True)
    proj_sum = lax.psum(proj_shard, "pos").astype(f32)
    down_sum = lax.psum(down_shard, "pos").astype(f32)
    vector_sum, net_sum, final_sum = lax.psum(
        (vector_local, net_local, final_local), ("seq", "pos")
    )
    return (
        block_output.reshape(micro, 1, count, width),
        input_grad.reshape(micro, 1, count, width),
        *nesterov(proj_weights, proj_moment, proj_average, proj_sum, 0.0001),
        *nesterov(down_weights, down_moment, down_average, down_sum, 0.0001),
        *nesterov(vectors, vector_moment, vector_average, vector_sum, 0.001),
        *nesterov(filter_net, net_moment, net_average, net_sum, 0.0001),
        *nesterov(filter_out, final_moment, final_average, final_sum, 2e-06),
    )


def on_device(*arrays):
    tuned = fits(
        lax.axis_size("seq"), lax.axis_size("pos"), arrays[0], arrays[4], arrays[7]
    )
    return (on_device_tuned if tuned else on_device_plain)(*arrays)


def solution(mesh):
    tokens = P(None, "seq", "pos", None)
    rows = P("seq", None)
    whole = P()
    return jax.shard_map(
        on_device,
        mesh=mesh,
        in_specs=(tokens, tokens, P(None, "seq"), whole) + (rows,) * 6 + (whole,) * 9,
        out_specs=(tokens, tokens) + (rows,) * 8 + (whole,) * 12,
        check_vma=False,
    )
```

```python
import functools
import math
import types

import jax
import jax.numpy as jnp
import numpy as np
from jax import lax
from jax.experimental import pallas as pl
from jax.experimental.pallas import tpu as pltpu
from jax.sharding import PartitionSpec as P

HID = 64
EMB = 33

highest = lax.Precision.HIGHEST
f32 = jnp.float32
bf16 = jnp.bfloat16


def passed_along(block, axis, distance):
    devices = range(lax.axis_size(axis))
    route = [(i - distance, i) for i in devices if i - distance in devices]
    return lax.ppermute(block, axis, route)


def dot(a, b):
    return lax.dot_general(a, b, (((1,), (0,)), ((), ())), preferred_element_type=f32)


def dot_tn(a, b):
    return lax.dot_general(a, b, (((0,), (0,)), ((), ())), preferred_element_type=f32)


def dot_nt(a, b):
    return lax.dot_general(a, b, (((1,), (1,)), ((), ())), preferred_element_type=f32)


def features(positions, slot_length):
    band_count = (EMB - 1) // 2
    scaled = positions.astype(f32) / slot_length
    bands = 0.0001 + jnp.arange(band_count, dtype=f32) * (
        (band_count - 1 - 0.0001) / (band_count - 1)
    )
    angles = 2.0 * math.pi * scaled[:, None] * bands[None, :]
    return jnp.concatenate([scaled[:, None], jnp.cos(angles), -jnp.sin(angles)], axis=1)


def filter_fn(net_values, final_values, rates, positions, slot_length):
    embedded = features(positions, slot_length)
    frequency = net_values[EMB + 3 + 2 * HID]
    layer_one = jnp.sin(
        frequency * (jnp.dot(embedded, net_values[:EMB], precision=highest) + net_values[EMB])
    )
    layer_two = jnp.sin(
        frequency
        * (
            jnp.dot(layer_one, net_values[EMB + 1 : EMB + 1 + HID], precision=highest)
            + net_values[EMB + 1 + HID]
        )
    )
    layer_three = jnp.sin(
        frequency
        * (
            jnp.dot(layer_two, net_values[EMB + 2 + HID : EMB + 2 + 2 * HID], precision=highest)
            + net_values[EMB + 2 + 2 * HID]
        )
    )
    shaped = jnp.dot(layer_three, final_values, precision=highest)
    scaled = positions.astype(f32) / slot_length
    window = jnp.exp(-scaled[:, None] * rates[None, :]) + 0.05
    return shaped * window


def transform_table(length):
    product = np.outer(2 * np.arange(length) + 1, np.arange(length)) % (4 * length)
    angle = product.astype(np.float64) * (math.pi / (2 * length))
    return np.concatenate([np.cos(angle), -np.sin(angle)], axis=0).astype(np.float32)


def feature_table(slot_length):
    scaled = np.arange(slot_length, dtype=np.float32) / np.float32(slot_length)
    band_count = (EMB - 1) // 2
    bands = np.float32(0.0001) + np.arange(band_count, dtype=np.float32) * np.float32(
        (band_count - 1 - 0.0001) / (band_count - 1)
    )
    angles = (np.float32(2.0 * math.pi) * scaled[:, None]) * bands[None, :]
    table = np.zeros((40, slot_length), np.float32)
    table[0] = scaled
    table[1 : 1 + band_count] = np.cos(angles).T
    table[1 + band_count : EMB] = -np.sin(angles).T
    table[EMB] = 1.0
    return table


def halves(spectrum):
    half = spectrum.shape[-2] // 2
    return spectrum[..., :half, :], spectrum[..., half:, :]


def turned(spectrum, sign):
    re, im = halves(spectrum)
    parity = (1.0 - 2.0 * (jnp.arange(re.shape[-2]) % 2).astype(f32))[:, None] * sign
    return jnp.concatenate([-parity * im, parity * re], axis=-2)


def product(kernel, signal):
    kr, ki = halves(kernel)
    sr, si = halves(signal)
    return jnp.concatenate([kr * sr - ki * si, kr * si + ki * sr], axis=-2)


def product_conj(kernel, signal):
    kr, ki = halves(kernel)
    sr, si = halves(signal)
    return jnp.concatenate([kr * sr + ki * si, kr * si - ki * sr], axis=-2)


def nesterov(weight, moment, average, gradient, rate):
    moment_next = 0.9 * moment + gradient
    weight_next = weight - rate * (gradient + 0.9 * moment_next)
    average_next = 0.9 * average + 0.1 * weight_next
    return (gradient, weight_next, moment_next, average_next)


def norm_parts(values):
    center = jnp.mean(values, axis=-1, keepdims=True)
    centred = values - center
    variance = jnp.mean(centred * centred, axis=-1, keepdims=True)
    scale = lax.rsqrt(variance + 1e-05)
    return centred * scale, scale


def norm_back(grad, xh, scale, gain):
    q = grad * gain
    return (
        (q - jnp.mean(q, -1, keepdims=True) - xh * jnp.mean(q * xh, -1, keepdims=True)) * scale,
        jnp.sum(grad * xh, axis=0),
        jnp.sum(grad, axis=0),
    )


MESH = pl.DeviceIdType.MESH


class Ring:
    def __init__(self, size):
        self.size = size
        self.count = size // 2
        self.seq = lax.axis_index("seq")
        self.pos = lax.axis_index("pos")
        self.core = lax.rem(self.seq, 2)
        chip = self.seq // 2
        odd = lax.rem(chip, 2)
        self.place = (1 - odd) * (chip // 2) + odd * (self.count - 1 - chip // 2)

    def chip(self, shift):
        place = lax.rem(self.place + (shift + self.count), self.count)
        low = jnp.where(place < self.count // 2, 1, 0)
        return low * (2 * place) + (1 - low) * (2 * (self.count - 1 - place) + 1)

    def device(self, shift):
        return {"seq": 2 * self.chip(shift) + self.core}

    @property
    def sibling(self):
        return {"seq": self.seq + 1 - 2 * self.core}

    @property
    def across(self):
        return {"pos": 1 - self.pos}


def greet_all(ring):
    barrier = pltpu.get_barrier_semaphore()
    for step in range(1, ring.size):
        other = lax.rem(ring.seq + step, ring.size)
        pl.semaphore_signal(barrier, inc=1, device_id={"seq": other}, device_id_type=MESH)
    pl.semaphore_signal(barrier, inc=1, device_id=ring.across, device_id_type=MESH)
    pl.semaphore_wait(barrier, ring.size)


def remote(src, dst, send, recv, device):
    return pltpu.make_async_remote_copy(
        src_ref=src, dst_ref=dst, send_sem=send, recv_sem=recv, device_id=device,
        device_id_type=MESH,
    )


class Reduction:
    def __init__(self, ring, turn, grad, twin, up, down, own, other, sems, block=None):
        self.ring, self.turn = ring, turn
        self.grad, self.twin, self.up, self.down = grad, twin, up, down
        self.own, self.other = own, other
        self.sems = sems
        self.block = block or (lambda chip: self.grad[chip, ring.core])
        self.ups = ring.count // 2
        self.downs = (ring.count - 1) // 2
        self.shifts = [self.ups, -self.downs, *range(1 - self.downs, self.ups)]

    def chip(self, shift):
        return self.ring.chip(shift * self.turn)

    def copies(self):
        ring = self.ring
        made = []
        for shift in self.shifts:
            chip = self.chip(shift)
            made.append((self.grad.at[chip, 1 - ring.core], self.twin.at[chip], ring.sibling))
        for step in range(self.ups):
            block = self.twin.at[self.chip(self.ups - step)]
            made.append((block, self.up.at[step], ring.device(self.turn)))
        for step in range(self.downs):
            block = self.twin.at[self.chip(step - self.downs)]
            made.append((block, self.down.at[step], ring.device(-self.turn)))
        made.append((self.own, self.other, ring.across))
        return made

    def copy(self, index):
        src, dst, device = self.copies()[index]
        return remote(src, dst, self.sems.at[0, index], self.sems.at[1, index], device)

    def begin(self):
        for index in range(self.ring.count):
            self.copy(index).start()

    def step_up(self, step):
        return self.copy(self.ring.count + step)

    def step_down(self, step):
        return self.copy(self.ring.count + self.ups + step)

    def merge(self):
        for index, shift in enumerate(self.shifts):
            self.copy(index).wait_recv()
            chip = self.chip(shift)
            self.twin[chip] = self.twin[chip] + self.block(chip)
            if index == 0:
                self.step_up(0).start()
            if index == 1:
                self.step_down(0).start()

    def advance(self, step):
        self.step_up(step - 1).wait_recv()
        owner = self.chip(self.ups - step)
        self.twin[owner] = self.twin[owner] + self.up[step - 1]
        self.step_up(step).start()
        if step < self.downs:
            self.step_down(step - 1).wait_recv()
            owner = self.chip(step - self.downs)
            self.twin[owner] = self.twin[owner] + self.down[step - 1]
            self.step_down(step).start()

    def collect(self):
        self.step_up(self.ups - 1).wait_recv()
        self.step_down(self.downs - 1).wait_recv()
        mine = self.chip(0)
        total = (
            self.twin[mine].astype(f32)
            + self.up[self.ups - 1].astype(f32)
            + self.down[self.downs - 1].astype(f32)
        )
        self.own[...] = total.astype(bf16)
        self.copy(self.ring.count + self.ups + self.downs).start()

    def result(self):
        self.copy(self.ring.count + self.ups + self.downs).wait_recv()
        return self.own[...].astype(f32) + self.other[...].astype(f32)

    def finish(self):
        for index in range(self.ring.count + 1 + self.ups + self.downs):
            self.copy(index).wait_send()


class SmallSum:
    def __init__(self, ring, values, parts, mine, other, sums, sems):
        self.ring, self.values, self.parts = ring, values, parts
        self.mine, self.other, self.sums = mine, other, sums
        self.sems = sems
        self.rows = parts.shape[1]
        self.waiting = []

    def block(self, index):
        return pl.ds(pl.multiple_of(index * self.rows, 8), self.rows)

    def begin(self):
        ring = self.ring
        self.arriving = []
        for step in range(1, ring.size):
            other = lax.rem(ring.seq + step, ring.size)
            copy = remote(
                self.values.at[self.block(other)], self.parts.at[step],
                self.sems.at[0, step], self.sems.at[1, step], {"seq": other},
            )
            copy.start()
            self.arriving.append(copy)
            self.waiting.append(copy)

    def add_up(self):
        for copy in self.arriving:
            copy.wait_recv()
        total = self.values[self.block(self.ring.seq)]
        for step in range(1, self.ring.size):
            total = total + self.parts[step]
        self.mine[...] = total
        self.crossing = remote(
            self.mine, self.other, self.sems.at[0, 0], self.sems.at[1, 0], self.ring.across
        )
        self.crossing.start()
        self.waiting.append(self.crossing)

    def spread(self):
        self.crossing.wait_recv()
        block = self.block(self.ring.seq)
        self.sums[block] = self.mine[...] + self.other[...]
        self.arriving = []
        for step in range(1, self.ring.size):
            other = lax.rem(self.ring.seq + step, self.ring.size)
            copy = remote(
                self.sums.at[block], self.sums.at[block],
                self.sems.at[2, step], self.sems.at[3, step], {"seq": other},
            )
            copy.start()
            self.waiting.append(copy)
            back = lax.rem(self.ring.seq + (self.ring.size - step), self.ring.size)
            self.arriving.append(
                remote(
                    self.sums.at[self.block(back)], self.sums.at[self.block(back)],
                    self.sems.at[2, step], self.sems.at[3, step], {"seq": other},
                )
            )

    def finish(self):
        for copy in self.arriving:
            copy.wait_recv()
        for copy in self.waiting:
            copy.wait_send()


def small_scratch(size, rows, columns):
    return [
        pltpu.VMEM((size, rows // size, columns), f32),
        pltpu.VMEM((rows // size, columns), f32),
        pltpu.VMEM((rows // size, columns), f32),
        pltpu.SemaphoreType.DMA((4, size)),
    ]


class Gather:
    def __init__(self, ring, turn, mine, full, sems):
        self.ring, self.turn = ring, turn
        self.mine, self.full, self.sems = mine, full, sems
        self.ups = ring.count // 2
        self.downs = (ring.count - 1) // 2
        self.waiting, self.arriving = [], []

    def send(self, src, place, index, device):
        copy = remote(
            src, self.full.at[self.ring.chip(place * self.turn), self.ring.core],
            self.sems.at[0, index], self.sems.at[1, index], device,
        )
        copy.start()
        self.waiting.append(copy)
        return copy

    def share(self, src, place, index):
        index = self.ups + self.downs + index
        self.send(src, place, index, self.ring.sibling)
        block = self.full.at[self.ring.chip(place * self.turn), 1 - self.ring.core]
        self.arriving.append(
            remote(block, block, self.sems.at[0, index], self.sems.at[1, index], self.ring.sibling)
        )

    def wait_block(self, place, index, device):
        block = self.full.at[self.ring.chip(place * self.turn), self.ring.core]
        remote(block, block, self.sems.at[0, index], self.sems.at[1, index], device).wait_recv()
        return block

    def begin(self):
        ring = self.ring
        self.send(self.mine, 0, 0, ring.device(self.turn))
        self.send(self.mine, 0, self.ups, ring.device(-self.turn))
        self.share(self.mine, 0, 0)
        self.local = pltpu.make_async_copy(
            self.mine, self.full.at[ring.chip(0), ring.core], self.sems.at[2, 0]
        )
        self.local.start()

    def advance(self, step):
        ring = self.ring
        block = self.wait_block(-step, step - 1, ring.device(self.turn))
        if step < self.ups:
            self.send(block, -step, step, ring.device(self.turn))
        self.share(block, -step, step)
        if step <= self.downs:
            block = self.wait_block(step, self.ups + step - 1, ring.device(-self.turn))
            if step < self.downs:
                self.send(block, step, self.ups + step, ring.device(-self.turn))
            self.share(block, step, self.ups + step)

    def arrive(self):
        self.local.wait()
        for copy in self.arriving:
            copy.wait_recv()

    def finish(self):
        for copy in self.waiting:
            copy.wait_send()


def gather_sems(size):
    chips = size // 2
    return pltpu.SemaphoreType.DMA((3, 2 * chips))


PI_PARTS = (3.140625, 9.676535897932384e-4)


def sin_cos(x):
    turns = jnp.floor(x * (1.0 / math.pi) + 0.5)
    rest = (x - turns * PI_PARTS[0]) - turns * PI_PARTS[1]
    half = turns * 0.5
    sign = 1.0 - 4.0 * (half - jnp.floor(half))
    square = rest * rest
    odd = 1.0 / 6227020800.0
    for factor in (-1.0 / 39916800.0, 1.0 / 362880.0, -1.0 / 5040.0, 1.0 / 120.0, -1.0 / 6.0):
        odd = odd * square + factor
    even = 1.0 / 479001600.0
    for factor in (-1.0 / 3628800.0, 1.0 / 40320.0, -1.0 / 720.0, 1.0 / 24.0, -0.5):
        even = even * square + factor
    signed = sign * rest
    return signed + signed * square * odd, sign + sign * square * even


def norm_rows(values):
    center = jnp.mean(values, axis=1, keepdims=True)
    centred = values - center
    variance = jnp.mean(centred * centred, axis=1, keepdims=True)
    return centred * lax.rsqrt(variance + 1e-05)


TILE = 256


class Copies:
    def __init__(self, sems):
        self.sems, self.used, self.open = sems, 0, []

    def start(self, src, dst):
        copy = pltpu.make_async_copy(src, dst, self.sems.at[self.used])
        self.used += 1
        copy.start()
        return copy

    def out(self, src, dst):
        copy = self.start(src, dst)
        self.open.append(copy)
        return copy

    def settle(self, copy):
        copy.wait()
        self.open = [other for other in self.open if other is not copy]

    def finish(self):
        for copy in self.open:
            copy.wait()


def valid_rows(length, first, rows, columns):
    at = lax.broadcasted_iota(jnp.int32, (rows, columns), 0) + first
    return jnp.where(at < length, 1.0, 0.0).astype(f32)


def blocks(rows, step):
    return [slice(at, at + step) for at in range(0, rows, step)]


def folded(values):
    return jnp.sum(values.reshape(-1, 8, values.shape[1]), axis=0)


def front_kernel(size, names, *refs):
    ref = types.SimpleNamespace(**dict(zip(names, refs)))
    x, vec, net = ref.x_in, ref.vec, ref.net
    micro, count, width = x.shape
    slot = 2 * count
    tiles = width // TILE
    ring = Ring(size)
    copies = Copies(ref.copy_sems)
    proj_copy = copies.start(ref.proj, ref.proj_in)
    x_copy = copies.start(ref.x, x)
    down_copy = copies.start(ref.down, ref.down_in)
    feature_copy = copies.start(ref.feature, ref.feature_in)
    table_copy = copies.start(ref.table, ref.table_in)
    back_copy = copies.start(ref.back, ref.back_in)
    table, table_back = ref.table_in, ref.back_in
    inside = jnp.where(ring.pos > 0, 1.0, 0.0).astype(f32)

    proj_copy.wait()
    own = ref.in_own
    for j in range(tiles):
        for p in range(3):
            first = p * width + j * TILE
            own[j, :, p * TILE : (p + 1) * TILE] = ref.proj_in[:, first : first + TILE].astype(bf16)
    greet_all(ring)
    gather = [Gather(ring, 1 - 2 * (j % 2), own.at[j], ref.win_in.at[j], ref.win_sem.at[j]) for j in range(tiles)]
    gather_out = Gather(ring, -1, ref.out_own, ref.wout_in, ref.wout_sem)
    gather_up = Gather(ring, 1, ref.up_own, ref.wup, ref.wup_sem)
    gather_down = Gather(ring, -1, ref.down_own, ref.wdown, ref.wdown_sem)
    gather[0].begin()
    x_copy.wait()
    edge = remote(
        x.at[:, pl.ds(count - 16, 16)], ref.halo, ref.halo_sem.at[0],
        ref.halo_sem.at[1], ring.across,
    )
    edge.start()

    gain, shift = vec[0:1], vec[1:2]
    normed_ref, turned_ref = ref.n_in, ref.nt_in

    def first_norm(m):
        for rows in blocks(count, TILE):
            normed_ref[m, rows] = (norm_rows(x[m, rows].astype(f32)) * gain + shift).astype(bf16)
        for rows in blocks(count, TILE):
            turned_ref[m, :, rows] = normed_ref[m, rows].T

    first_norm(0)
    gather[0].advance(1)
    gather[1].begin()
    for m in range(1, micro):
        first_norm(m)
    copies.out(turned_ref, ref.nt)
    gather[0].advance(2)
    gather[1].advance(1)
    gather[2].begin()
    feature_copy.wait()

    frequency = net[:, EMB + 3 + 2 * HID : EMB + 4 + 2 * HID]
    pre = ref.pre_in

    def layer(i, weights, values):
        made = jnp.dot(weights, values, precision=highest, preferred_element_type=f32)
        if i > 0:
            first = EMB + 1 + (i - 1) * (HID + 1) + HID
            made = made + net[:, first : first + 1]
        pre[i * HID : (i + 1) * HID] = made
        return jnp.concatenate(
            [sin_cos(frequency[part] * made[part])[0] for part in blocks(HID, 16)], axis=0
        )

    hidden = layer(0, net[:, : ref.feature_in.shape[0]], ref.feature_in[...])
    for i in (1, 2):
        first = EMB + 1 + (i - 1) * (HID + 1)
        hidden = layer(i, net[:, first : first + HID], hidden)
    ref.act_in[...] = hidden.astype(bf16)
    copies.out(pre, ref.pre)
    rates = ref.rate[...].reshape(1, width)

    def filter_rows(at):
        shaped = dot_tn(
            ref.act_in[:, at * TILE : (at + 1) * TILE], ref.final[...].astype(bf16)
        )
        for part in blocks(TILE, 16):
            at_row = lax.broadcasted_iota(jnp.int32, (16, width), 0) + (at * TILE + part.start)
            window = jnp.exp(at_row.astype(f32) * (rates * (-1.0 / slot))) + 0.05
            first = at * TILE + part.start
            ref.filt[first : first + 16] = (shaped[part] * window).astype(bf16)

    row_blocks = slot // TILE
    gather[0].advance(3)
    gather[1].advance(2)
    gather[2].advance(1)
    edge.wait_recv()
    for m in range(micro):
        ref.halo_n[m] = (norm_rows(ref.halo[m].astype(f32)) * gain + shift).astype(bf16)
    ref.out_own[...] = ref.proj_in[:, 3 * width : 4 * width].astype(bf16)
    filter_rows(0)
    gather[0].advance(4)
    gather[1].advance(3)
    gather[2].advance(2)
    gather_out.begin()
    gather[0].arrive()

    z_in, s_in, ulow, urecv = ref.z_in, ref.s_in, ref.ulow, ref.urecv
    zbuf, spec = ref.zbuf, ref.spec
    crossing = []

    def project(j):
        weight = ref.win_in[j].reshape(width, 3 * TILE)
        bias = jnp.concatenate(
            [vec[4 + p : 5 + p, j * TILE : (j + 1) * TILE] for p in range(3)], axis=1
        )
        lane = slice(j * TILE, (j + 1) * TILE)
        taps = [[vec[13 + 3 * k + p : 14 + 3 * k + p, lane] for p in range(3)] for k in range(3)]
        constant = [
            (taps[0][p] + taps[1][p] + taps[2][p]) * vec[4 + p : 5 + p, lane]
            + vec[22 + p : 23 + p, lane]
            for p in range(3)
        ]

        @pl.loop(0, micro)
        def _(m):
            zbuf[16:] = dot(normed_ref[m], weight)
            zbuf[:16] = dot(ref.halo_n[m], weight) * inside + bias * (inside - 1.0)
            ref.zh_in[j, m] = (zbuf[:16] + bias).astype(bf16)
            for rows in blocks(count, 32):
                parts = []
                for p in range(3):
                    cols = slice(p * TILE, (p + 1) * TILE)
                    first = rows.start
                    z = zbuf[first + 16 : first + 48, cols]
                    z_in[j, m, rows, cols] = (z + bias[:, cols]).astype(bf16)
                    short = (
                        taps[0][p] * z
                        + taps[1][p] * zbuf[first + 15 : first + 47, cols]
                        + taps[2][p] * zbuf[first + 14 : first + 46, cols]
                        + constant[p]
                    ).astype(bf16)
                    s_in[j, m, rows, cols] = short
                    parts.append(short.astype(f32))
                ulow[j, m, rows] = (parts[1] * parts[2]).astype(bf16)

        copy = remote(
            ulow.at[j], urecv.at[j], ref.u_sem.at[0, j], ref.u_sem.at[1, j], ring.across
        )
        copy.start()
        crossing.append(copy)
        copies.out(z_in.at[j], ref.z.at[j])
        copies.out(s_in.at[j], ref.s.at[j])

    project(0)
    gather[1].advance(4)
    gather[2].advance(3)
    ref.up_own[...] = ref.proj_in[:, 4 * width :].astype(bf16)
    gather_up.begin()
    gather[1].arrive()
    project(1)
    gather[2].advance(4)
    gather_out.advance(1)
    down_copy.wait()
    ref.down_own[...] = ref.down_in[...].astype(bf16)
    gather_down.begin()
    gather[2].arrive()
    project(2)
    copies.out(ref.zh_in, ref.zh)
    copies.out(ref.win_in, ref.win)
    gather_out.advance(2)
    gather_up.advance(1)
    gather_out.advance(3)
    for at in range(1, row_blocks):
        filter_rows(at)
    gather_down.advance(1)
    gather_out.advance(4)
    gather_out.arrive()
    copies.out(ref.wout_in, ref.wout)
    table_copy.wait()
    back_copy.wait()

    parity = 1.0 - 2.0 * (lax.broadcasted_iota(jnp.int32, (16, TILE), 0) % 2).astype(f32)
    kern, uhat = ref.kern_in, ref.uhat_in
    one, two = ref.one, ref.two

    @pl.loop(0, tiles)
    def _(j):
        cols = pl.ds(pl.multiple_of(j * TILE, TILE), TILE)
        one[...] = dot(table[...], ref.filt[:count, cols])
        two[...] = dot(table[...], ref.filt[count:, cols])
        for re in blocks(count, 16):
            im = slice(re.start + count, re.stop + count)
            kern[j, 0, re] = one[re].astype(bf16)
            kern[j, 0, im] = one[im].astype(bf16)
            kern[j, 1, re] = (two[re] - parity * one[im]).astype(bf16)
            kern[j, 1, im] = (two[im] + parity * one[re]).astype(bf16)
        for m in range(micro):
            uhat[j, m, 0] = dot(table[...], ulow[j, m]).astype(bf16)

    copies.out(kern, ref.kern)
    gather_up.advance(2)

    def mix(j):
        crossing[j].wait_recv()
        lane = slice(j * TILE, (j + 1) * TILE)

        @pl.loop(0, micro)
        def _(m):
            one[...] = dot(table[...], urecv[j, m])
            for re in blocks(count, 16):
                im = slice(re.start + count, re.stop + count)
                k0r, k0i = kern[j, 0, re].astype(f32), kern[j, 0, im].astype(f32)
                k1r, k1i = kern[j, 1, re].astype(f32), kern[j, 1, im].astype(f32)
                ur, ui = uhat[j, m, 0, re].astype(f32), uhat[j, m, 0, im].astype(f32)
                vr, vi = one[re] * inside, one[im] * inside
                uhat[j, m, 1, re] = vr.astype(bf16)
                uhat[j, m, 1, im] = vi.astype(bf16)
                spec[re] = (k0r * ur - k0i * ui + k1r * vr - k1i * vi).astype(bf16)
                spec[im] = (k0r * ui + k0i * ur + k1r * vi + k1i * vr).astype(bf16)
            two[:count] = dot(table_back[...], spec[...])
            length = ref.lens[0, m] - ring.pos * count
            for rows in blocks(count, 32):
                gated = s_in[j, m, rows, TILE : 2 * TILE].astype(f32) * s_in[
                    j, m, rows, 2 * TILE :
                ].astype(f32)
                conv = two[rows] * (1.0 / count) + vec[25:26, lane] * gated
                ref.conv_in[j, m, rows] = conv.astype(bf16)
                mask = valid_rows(length, rows.start, 32, TILE)
                ref.y_in[m, rows, lane] = (
                    mask * s_in[j, m, rows, :TILE].astype(f32) * conv
                ).astype(bf16)

            ref.yt_in[m, lane] = ref.y_in[m, :, lane].T
            part = dot(ref.y_in[m, :, lane], ref.wout_in[...].reshape(width, width)[lane])
            ref.res_in[m] = part if j == 0 else ref.res_in[m] + part

        copies.out(ref.conv_in.at[j], ref.conv.at[j])
        copies.out(uhat.at[j], ref.uhat.at[j])

    for j in range(tiles):
        mix(j)
        if j == 0:
            gather_down.advance(2)
        if j == 1:
            gather_up.advance(3)

    for m in range(micro):
        for rows in blocks(count, TILE):
            residual = x[m, rows].astype(f32) + ref.res_in[m, rows] + vec[7:8]
            ref.res_in[m, rows] = residual
            ref.n2_in[m, rows] = (norm_rows(residual) * vec[2:3] + vec[3:4]).astype(bf16)
        for rows in blocks(count, TILE):
            ref.n2t_in[m, :, rows] = ref.n2_in[m, rows].T
        for src, dst in (
            (ref.yt_in, ref.yt), (ref.res_in, ref.res), (ref.n2_in, ref.n2), (ref.n2t_in, ref.n2t)
        ):
            copies.out(src.at[m], dst.at[m])
        if m == 0:
            gather_down.advance(3)
    gather_up.advance(4)
    gather_up.arrive()

    gather_down.advance(4)
    gather_down.arrive()
    for work in gather:
        work.finish()
    for work in (gather_out, gather_up, gather_down):
        work.finish()
    edge.wait_send()
    for copy in crossing:
        copy.wait_send()
    copies.finish()


def front(size, arrays):
    chips = size // 2
    micro, count, width = arrays["x"].shape
    rows, down_rows = arrays["proj"].shape[0], arrays["down"].shape[0]
    wide = down_rows * size
    tiles = width // TILE
    vmem = pl.BlockSpec(memory_space=pltpu.VMEM)
    anywhere = pl.BlockSpec(memory_space=pl.ANY)
    smem = pl.BlockSpec(memory_space=pltpu.SMEM)
    near = ("vec", "net", "final", "rate")
    kinds = dict(
        win=((tiles, chips, 2, rows, 3 * TILE), bf16),
        wout=((chips, 2, rows, width), bf16),
        z=((tiles, micro, count, 3 * TILE), bf16),
        zh=((tiles, micro, 16, 3 * TILE), bf16),
        s=((tiles, micro, count, 3 * TILE), bf16),
        conv=((tiles, micro, count, TILE), bf16),
        uhat=((tiles, micro, 2, 2 * count, TILE), bf16),
        kern=((tiles, 2, 2 * count, TILE), bf16),
        res=((micro, count, width), f32),
        nt=((micro, width, count), bf16),
        n2=((micro, count, width), bf16),
        n2t=((micro, width, count), bf16),
        yt=((micro, width, count), bf16),
        pre=((3 * HID, 2 * count), f32),
    )
    outs = dict(
        kinds,
        wup=((chips, 2, rows, wide), bf16),
        wdown=((chips, 2, down_rows, width), bf16),
    )
    dma = pltpu.SemaphoreType.DMA
    scratch = {
        name + "_in": pltpu.VMEM(*kind) for name, kind in kinds.items()
    }
    for name, array in arrays.items():
        if name not in near and name != "lens":
            scratch[name + "_in"] = pltpu.VMEM(array.shape, array.dtype)
    scratch.update(
        dict(
            n_in=pltpu.VMEM((micro, count, width), bf16),
            one=pltpu.VMEM((2 * count, TILE), f32),
            two=pltpu.VMEM((2 * count, TILE), f32),
            act_in=pltpu.VMEM((HID, 2 * count), bf16),
            y_in=pltpu.VMEM((micro, count, width), bf16),
            in_own=pltpu.VMEM((tiles, rows, 3 * TILE), bf16),
            out_own=pltpu.VMEM((rows, width), bf16),
            up_own=pltpu.VMEM((rows, wide), bf16),
            down_own=pltpu.VMEM((down_rows, width), bf16),
            halo=pltpu.VMEM((micro, 16, width), bf16),
            halo_n=pltpu.VMEM((micro, 16, width), bf16),
            filt=pltpu.VMEM((2 * count, width), bf16),
            zbuf=pltpu.VMEM((16 + count, 3 * TILE), f32),
            ulow=pltpu.VMEM((tiles, micro, count, TILE), bf16),
            urecv=pltpu.VMEM((tiles, micro, count, TILE), bf16),
            spec=pltpu.VMEM((2 * count, TILE), bf16),
            win_sem=dma((tiles, 3, 2 * chips)),
            wout_sem=gather_sems(size),
            wup_sem=gather_sems(size),
            wdown_sem=gather_sems(size),
            halo_sem=dma((2,)),
            u_sem=dma((2, tiles)),
            copy_sems=dma((56,)),
        )
    )
    names = tuple(arrays) + tuple(outs) + tuple(scratch)
    made = pl.pallas_call(
        functools.partial(front_kernel, size, names),
        out_shape=[jax.ShapeDtypeStruct(*kind) for kind in outs.values()],
        in_specs=[
            smem if name == "lens" else vmem if name in near else anywhere for name in arrays
        ],
        out_specs=[anywhere] * len(outs),
        scratch_shapes=list(scratch.values()),
        compiler_params=pltpu.CompilerParams(
            collective_id=0, has_side_effects=True, vmem_limit_bytes=63 * 1024 * 1024
        ),
        name="front",
    )(*arrays.values())
    return dict(zip(outs, made))


GELU_SCALE = math.sqrt(2.0 / math.pi)


def gelu_pair(a):
    square = a * a
    half = 0.5 + 0.5 * jnp.tanh(a * (GELU_SCALE + (GELU_SCALE * 0.044715) * square))
    hidden = a * half
    bend = 2.0 * GELU_SCALE + (2.0 * GELU_SCALE * 0.134145) * square
    return hidden, half + (hidden - hidden * half) * bend


def mlp_kernel(
    n2_ref, n2t_ref, gm_ref, res_ref, vec_ref, wup_ref, wdown_ref,
    out_ref, gb_ref, dup_ref, ddown_ref, small_ref,
    acc_out, acc_gn, hid_ref, ga_ref,
):
    step, last = pl.program_id(0), pl.num_programs(0) - 1
    micro, count, width = n2_ref.shape
    chunk = width
    wup = wup_ref[...].reshape(width, chunk)
    wdown = wdown_ref[...].reshape(chunk, width)
    bias = vec_ref[pl.ds(8 + step, 1)]

    @pl.when(step == 0)
    def _():
        acc_out[...] = jnp.zeros_like(acc_out)
        acc_gn[...] = jnp.zeros_like(acc_gn)
        small_ref[...] = jnp.zeros_like(small_ref)

    bias_sum = jnp.zeros((8, chunk), f32)
    for m in range(micro):
        for rows in blocks(count, TILE):
            hidden, slope = gelu_pair(dot(n2_ref[m, rows], wup) + bias)
            hidden = hidden.astype(bf16)
            ga = (dot_nt(gm_ref[m, rows], wdown) * slope).astype(bf16)
            hid_ref[m, rows] = hidden
            ga_ref[m, rows] = ga
            bias_sum = bias_sum + folded(ga.astype(f32))
            acc_out[m, rows] += dot(hidden, wdown)
            acc_gn[m, rows] += dot_nt(ga, wup)
    small_ref[pl.ds(4 + step, 1)] = jnp.sum(bias_sum, axis=0, keepdims=True)
    down_total = dot_tn(hid_ref[0], gm_ref[0])
    up_total = dot(n2t_ref[0], ga_ref[0])
    for m in range(1, micro):
        down_total = down_total + dot_tn(hid_ref[m], gm_ref[m])
        up_total = up_total + dot(n2t_ref[m], ga_ref[m])
    ddown_ref[...] = down_total.astype(bf16)
    dup_ref[...] = up_total.astype(bf16).reshape(dup_ref.shape)

    @pl.when(step == last)
    def _():
        sums = [jnp.zeros((8, width), f32)] * 4
        for m in range(micro):
            for rows in blocks(count, TILE):
                residual = res_ref[m, rows]
                out_ref[m, rows] = (residual + acc_out[m, rows] + vec_ref[12:13]).astype(bf16)
                gx, gain_part, grad = norm_rows_back(acc_gn[m, rows], residual, vec_ref[2:3])
                gm = gm_ref[m, rows].astype(f32)
                low = (gm + gx).astype(bf16)
                gb_ref[m, rows] = low
                parts = (gain_part, grad, low.astype(f32), gm)
                sums = [total + folded(part) for total, part in zip(sums, parts)]
        for k in range(4):
            small_ref[k : k + 1] = jnp.sum(sums[k], axis=0, keepdims=True)


def norm_rows_back(grad, values, gain):
    center = jnp.mean(values, axis=1, keepdims=True)
    centred = values - center
    variance = jnp.mean(centred * centred, axis=1, keepdims=True)
    scale = lax.rsqrt(variance + 1e-05)
    xh = centred * scale
    q = grad * gain
    gx = scale * (
        q - jnp.mean(q, axis=1, keepdims=True) - xh * jnp.mean(q * xh, axis=1, keepdims=True)
    )
    return gx, grad * xh, grad


def mlp(n2, n2t, gm, res, vectors, wup, wdown):
    micro, count, width = gm.shape
    chips, cores, rows, wide = wup.shape
    steps = wide // width
    per = chips // steps

    def whole(array):
        return pl.BlockSpec(array.shape, lambda i: (0,) * array.ndim)

    def shape(dims, kind=bf16):
        return jax.ShapeDtypeStruct(dims, kind)

    tokens = pl.BlockSpec((micro, count, width), lambda i: (0, 0, 0))
    return pl.pallas_call(
        mlp_kernel,
        grid=(steps,),
        in_specs=[
            whole(n2), whole(n2t), whole(gm), whole(res), whole(vectors),
            pl.BlockSpec((chips, cores, rows, width), lambda i: (0, 0, 0, i)),
            pl.BlockSpec((per, cores, wdown.shape[2], width), lambda i: (i, 0, 0, 0)),
        ],
        out_specs=[
            tokens, tokens,
            pl.BlockSpec((chips, cores, 1, rows, width), lambda i: (0, 0, i, 0, 0)),
            pl.BlockSpec((width, width), lambda i: (i, 0)),
            pl.BlockSpec((4 + steps, width), lambda i: (0, 0)),
        ],
        out_shape=[
            shape((micro, count, width)),
            shape((micro, count, width)),
            shape((chips, cores, steps, rows, width)),
            shape((wide, width)),
            shape((4 + steps, width), f32),
        ],
        scratch_shapes=[
            pltpu.VMEM((micro, count, width), f32),
            pltpu.VMEM((micro, count, width), f32),
            pltpu.VMEM((micro, count, width), bf16),
            pltpu.VMEM((micro, count, width), bf16),
        ],
        compiler_params=pltpu.CompilerParams(vmem_limit_bytes=63 * 1024 * 1024),
        name="mlp",
    )(n2, n2t, gm, res, vectors, wup, wdown)


def update_kernel(rates, firsts, *refs):
    count = len(rates)
    kept_in, kept_out, refs = refs[0], refs[4 * count + 1], refs[1 : 4 * count + 1] + refs[4 * count + 2 :]
    kept_out[...] = kept_in[...]
    ins, outs = refs[: 4 * count], refs[4 * count :]
    for i, (rate, first) in enumerate(zip(rates, firsts)):
        grad_ref, weight_ref, moment_ref, average_ref = ins[4 * i : 4 * i + 4]
        rows, columns = weight_ref.shape
        stepped = nesterov(
            weight_ref[...], moment_ref[...], average_ref[...],
            grad_ref[first : first + rows, :columns], rate,
        )
        for out, value in zip(outs[4 * i : 4 * i + 4], stepped):
            out[...] = value


def update(kept, sets):
    steps = 4
    held = pl.BlockSpec(
        (kept.shape[0], kept.shape[1] // steps, kept.shape[2]), lambda i: (0, i, 0)
    )
    arrays, in_specs, out_specs = [kept], [held], [held]
    shapes = [jax.ShapeDtypeStruct(kept.shape, kept.dtype)]

    def spec(shape, cut):
        if cut is None:
            return pl.BlockSpec(shape, lambda i: (0, 0))
        if cut:
            return pl.BlockSpec((shape[0], shape[1] // steps), lambda i: (0, i))
        return pl.BlockSpec((shape[0] // steps, shape[1]), lambda i: (i, 0))

    for grad, weight, moment, average, rate, first, cut in sets:
        arrays += [grad, weight, moment, average]
        in_specs += [spec(grad.shape, cut)] + [spec(weight.shape, cut)] * 3
        out_specs += [spec(weight.shape, cut)] * 4
        shapes += [jax.ShapeDtypeStruct(weight.shape, f32)] * 4
    made = pl.pallas_call(
        functools.partial(update_kernel, [s[4] for s in sets], [s[5] for s in sets]),
        grid=(steps,),
        in_specs=in_specs,
        out_specs=out_specs,
        out_shape=shapes,
        compiler_params=pltpu.CompilerParams(vmem_limit_bytes=63 * 1024 * 1024),
        name="update",
    )(*arrays)
    return made[0], [made[4 * i + 1 : 4 * i + 5] for i in range(len(sets))]


GROUP = 32
HALF = 384


def back_kernel(size, names, *refs):
    ref = types.SimpleNamespace(**dict(zip(names, refs)))
    gb, vec, table, table_back = ref.gb, ref.vec, ref.table, ref.back
    micro, count, width = gb.shape
    slot = 2 * count
    tiles = width // TILE
    ring = Ring(size)
    gw, gc, gcr, gz = ref.gw, ref.gc, ref.gcr, ref.gz
    vsum, nsum, fsum = ref.vsum, ref.nsum, ref.fsum
    one, two = ref.one, ref.two
    gate, turned = ref.gate, ref.turned
    inside = jnp.where(ring.pos < 1, 1.0, 0.0).astype(f32)
    first_half, second_half = ring.pos == 0, ring.pos == 1
    copies = Copies(ref.copy_sems)
    gate_copies = [
        copies.start(ref.s.at[j, :, :, pl.ds(0, TILE)], gate.at[j]) for j in range(tiles)
    ]
    wout = ref.din.at[0]
    wout_copy = copies.start(ref.wout, wout)
    turned_copy = copies.start(ref.yt, turned)
    win_copy = copies.start(ref.win, ref.win_in)

    greet_all(ring)
    red = {}

    def parts_of(name):
        return [getattr(ref, name + str(k)) for k in range(6)]

    deep, blocks_up = ref.ddown.shape[2], ref.dup.shape[2]
    fit = count // deep
    staged = []
    for chip in range(ring.count):
        at, row = chip // fit, chip % fit * deep
        staged.append(
            copies.start(
                ref.ddown.at[chip, ring.core], gz.at[at // micro, at % micro, pl.ds(row, deep)]
            )
        )
    for c in range(blocks_up):
        staged.append(
            copies.start(ref.dup.at[:, ring.core, c], ref.din.at[1 + c // 2, :, c % 2])
        )

    def down_block(chip):
        at, row = chip // fit, pl.multiple_of(lax.rem(chip, fit) * deep, 16)
        return gz[at // micro, lax.rem(at, micro), pl.ds(row, deep)]

    def up_block(chip):
        return jnp.stack([ref.din[1 + c // 2, chip, c % 2] for c in range(blocks_up)])

    down = Reduction(ring, -1, ref.ddown, *parts_of("down"), down_block)
    up = Reduction(ring, 1, ref.dup, *parts_of("up"), up_block)
    out = Reduction(ring, -1, ref.dout, *parts_of("out"))
    inner = [
        Reduction(ring, 1 - 2 * (j % 2), ref.din.at[j], *[part.at[j] for part in parts_of("in")])
        for j in range(tiles)
    ]
    down.begin()
    up.begin()
    vsum[...] = jnp.zeros_like(vsum)
    nsum[...] = jnp.zeros_like(nsum)
    small = ref.small
    for j in range(tiles):
        lane, base = slice(j * TILE, (j + 1) * TILE), j * GROUP
        vsum[base + 2 : base + 4] = small[0:2, lane]
        vsum[base + 7 : base + 8] = small[2:3, lane]
        vsum[base + 12 : base + 13] = small[3:4, lane]
        vsum[base + 8 : base + 12] = small[4:8, lane]

    crossing = []
    wout_copy.wait()
    for j in range(tiles):
        gate_copies[j].wait()
        weight = wout[...].reshape(width, width)[j * TILE : (j + 1) * TILE]

        @pl.loop(0, micro)
        def _(m):
            one[:count] = dot_nt(gb[m], weight)
            length = ref.lens[0, m] - ring.pos * count
            for rows in blocks(count, 32):
                mask = valid_rows(length, rows.start, 32, TILE)
                grad = mask * one[rows].astype(bf16).astype(f32)
                gw[j, m, rows] = grad.astype(bf16)
                gc[j, m, rows] = (grad * gate[j, m, rows].astype(f32)).astype(bf16)

        copy = remote(
            gc.at[j], gcr.at[j], ref.gc_sem.at[0, j], ref.gc_sem.at[1, j], ring.across
        )
        copy.start()
        crossing.append(copy)
    turned_copy.wait()

    @pl.loop(0, tiles)
    def _(j):
        cols = pl.ds(pl.multiple_of(j * TILE, TILE), TILE)
        total = dot(turned[0], gb[0, :, cols])
        for m in range(1, micro):
            total = total + dot(turned[m], gb[m, :, cols])
        dout = ref.dout
        dout[:, :, :, cols] = total.astype(bf16).reshape(dout.shape[:3] + (TILE,))

    turned_copy = copies.start(ref.nt, turned)
    out.begin()
    for copy in staged[: ring.count]:
        copy.wait()
    down.merge()
    for copy in staged[ring.count :]:
        copy.wait()
    up.merge()

    parity = 1.0 - 2.0 * (lax.broadcasted_iota(jnp.int32, (16, TILE), 0) % 2).astype(f32)
    gk = ref.gk
    gbuf, zbuf, spec = ref.gbuf, ref.zbuf, ref.spec
    first_rows, next_rows = ref.first_rows, ref.next_rows

    def loads(j, m, at):
        made = [
            (ref.s.at[j, m, :, pl.ds(TILE, 2 * TILE)], ref.s_buf.at[at]),
            (ref.z.at[j, m], ref.z_buf.at[at]),
            (ref.uhat.at[j, m], ref.u_buf.at[at]),
            (ref.conv.at[j, m], ref.c_buf.at[at]),
        ]
        return [
            pltpu.make_async_copy(src, dst, ref.load_sems.at[at, i])
            for i, (src, dst) in enumerate(made)
        ]

    def load_kernel(j):
        return pltpu.make_async_copy(ref.kern.at[j], ref.k_buf, ref.kernel_sem.at[0])

    def start_loads(j, m, at):
        for copy in loads(j, m, at):
            copy.start()

    start_loads(0, 0, 0)
    load_kernel(0).start()
    gbuf[:, count:] = jnp.zeros_like(gbuf[:, count:])

    def unmix(j):
        crossing[j].wait_recv()
        load_kernel(j).wait()
        lane = slice(j * TILE, (j + 1) * TILE)
        kn = ref.k_buf

        @pl.loop(0, micro)
        def _(m):
            at = lax.rem(j * micro + m, 2)
            for copy in loads(j, m, at):
                copy.wait()

            @pl.when(m + 1 < micro)
            def _():
                start_loads(j, m + 1, 1 - at)

            if j + 1 < tiles:

                @pl.when(m + 1 == micro)
                def _():
                    start_loads(j + 1, 0, 1 - at)

            one[...] = dot(table[...], gc[j, m])
            keep = jnp.where(m > 0, 1.0, 0.0).astype(f32)
            uh = ref.u_buf

            def filter_grad(d, re, im, gr, gi):
                ur, ui = uh[at, d, re].astype(f32), uh[at, d, im].astype(f32)
                gk[d, re] = gk[d, re] * keep + (ur * gr + ui * gi)
                gk[d, im] = gk[d, im] * keep + (ur * gi - ui * gr)

            @pl.when(first_half)
            def _():
                two[...] = dot(table[...], gcr[j, m])
                for re in blocks(count, 16):
                    im = slice(re.start + count, re.stop + count)
                    gr, gi, hr, hi = one[re], one[im], two[re], two[im]
                    k0r, k0i = kn[0, re].astype(f32), kn[0, im].astype(f32)
                    k1r, k1i = kn[1, re].astype(f32), kn[1, im].astype(f32)
                    spec[re] = (k0r * gr + k0i * gi + k1r * hr + k1i * hi).astype(bf16)
                    spec[im] = (k0r * gi - k0i * gr + k1r * hi - k1i * hr).astype(bf16)
                    filter_grad(0, re, im, gr, gi)

            @pl.when(second_half)
            def _():
                for re in blocks(count, 16):
                    im = slice(re.start + count, re.stop + count)
                    gr, gi = one[re], one[im]
                    k0r, k0i = kn[0, re].astype(f32), kn[0, im].astype(f32)
                    spec[re] = (k0r * gr + k0i * gi).astype(bf16)
                    spec[im] = (k0r * gi - k0i * gr).astype(bf16)
                    filter_grad(0, re, im, gr, gi)
                    filter_grad(1, re, im, gr, gi)

            two[:count] = dot(table_back[...], spec[...])
            skip_sum = jnp.zeros((8, TILE), f32)
            for rows in blocks(count, 32):
                x1 = ref.s_buf[at, rows, :TILE].astype(f32)
                v = ref.s_buf[at, rows, TILE:].astype(f32)
                grad_w = gw[j, m, rows].astype(f32)
                gc_full = grad_w * gate[j, m, rows].astype(f32)
                gu = two[rows] * (1.0 / count) + vec[25:26, lane] * gc_full
                skip_sum = skip_sum + folded(gc_full * (x1 * v))
                grads = (grad_w * ref.c_buf[at, rows].astype(f32), gu * v, gu * x1)
                for p in range(3):
                    low = grads[p].astype(bf16)
                    gbuf[p, rows] = low.astype(f32)
                    if rows.start == 0:
                        first_rows[j, m, :, p * TILE : (p + 1) * TILE] = low[:16]
            vsum[j * GROUP + 25 : j * GROUP + 26] += jnp.sum(skip_sum, axis=0, keepdims=True)
            for p in range(3):
                cols = slice(p * TILE, (p + 1) * TILE)
                zbuf[:16] = ref.zh[j, m, :, cols].astype(f32)
                for rows in blocks(count, 32):
                    zbuf[rows.start + 16 : rows.stop + 16] = ref.z_buf[at, rows, cols].astype(f32)
                taps = [vec[13 + 3 * k + p : 14 + 3 * k + p, lane] for k in range(3)]
                sums = [jnp.zeros((8, TILE), f32) for _ in range(4)]
                for rows in blocks(count, 32):
                    first = rows.start
                    grad = gbuf[p, rows]
                    gz[j, m, rows, cols] = (
                        taps[0] * grad
                        + taps[1] * gbuf[p, first + 1 : first + 33]
                        + taps[2] * gbuf[p, first + 2 : first + 34]
                    ).astype(bf16)
                    for k in range(3):
                        sums[k] = sums[k] + folded(grad * zbuf[first + 16 - k : first + 48 - k])
                    sums[3] = sums[3] + folded(grad)
                gz[j, m, count - 16 :, cols] = gbuf[p, count - 16 : count].astype(bf16)
                for k in range(4):
                    row = j * GROUP + 13 + 3 * k + p
                    vsum[row : row + 1] += jnp.sum(sums[k], axis=0, keepdims=True)

        if j + 1 < tiles:
            load_kernel(j + 1).start()
        edge = remote(
            first_rows.at[j], next_rows.at[j], ref.edge_sem.at[0, j],
            ref.edge_sem.at[1, j], ring.across,
        )
        edge.start()
        @pl.when(first_half)
        def _():
            for re in blocks(2 * count, 16):
                spec[re] = gk[0, re].astype(bf16)
            gate[j, 1] = jnp.zeros_like(gate[j, 1])

        @pl.when(second_half)
        def _():
            for re in blocks(2 * count, 16):
                spec[re] = gk[1, re].astype(bf16)
            two[count:] = dot(table_back[...], spec[...])
            for rows in blocks(count, 16):
                second = two[rows.start + count : rows.stop + count]
                gate[j, 1, rows] = (second * (1.0 / count)).astype(bf16)
            for re in blocks(count, 16):
                im = slice(re.start + count, re.stop + count)
                spec[re] = (gk[0, re] + parity * gk[1, im]).astype(bf16)
                spec[im] = (gk[0, im] - parity * gk[1, re]).astype(bf16)

        two[:count] = dot(table_back[...], spec[...])
        for rows in blocks(count, 16):
            gate[j, 0, rows] = (two[rows] * (1.0 / count)).astype(bf16)
        return edge

    def project_back(j, edge):
        edge.wait_recv()
        lane = slice(j * TILE, (j + 1) * TILE)
        ebuf = ref.ebuf
        for m in range(micro):
            for p in range(3):
                cols = slice(p * TILE, (p + 1) * TILE)
                own = gz[j, m, count - 16 :, cols].astype(f32)
                ebuf[:16] = own
                ebuf[16:] = next_rows[j, m, :, cols].astype(f32) * inside
                gz[j, m, count - 16 :, cols] = (
                    vec[13 + p : 14 + p, lane] * own
                    + vec[16 + p : 17 + p, lane] * ebuf[1:17]
                    + vec[19 + p : 20 + p, lane] * ebuf[2:18]
                ).astype(bf16)
        for p in range(3):
            cols = slice(p * TILE, (p + 1) * TILE)
            total = dot(turned[0], gz[j, 0, :, cols])
            for m in range(1, micro):
                total = total + dot(turned[m], gz[j, m, :, cols])
            din = ref.din
            din[j, :, :, :, cols] = total.astype(bf16).reshape(din.shape[1:4] + (TILE,))
            bias = jnp.zeros((8, TILE), f32)
            for m in range(micro):
                for rows in blocks(count, 32):
                    bias = bias + folded(gz[j, m, rows, cols].astype(f32))
            row = j * GROUP + 4 + p
            vsum[row : row + 1] = jnp.sum(bias, axis=0, keepdims=True)
        inner[j].begin()

    edges = [unmix(0)]
    down.advance(1)
    up.advance(1)
    out.merge()
    edges.append(unmix(1))
    turned_copy.wait()
    project_back(0, edges[0])
    down.advance(2)
    up.advance(2)
    out.advance(1)
    inner[0].merge()
    edges.append(unmix(2))
    project_back(1, edges[1])
    x_copies = [
        copies.start(ref.x.at[:, :, pl.ds(j * TILE, TILE)], gcr.at[j]) for j in range(tiles)
    ]
    pre_copies = [
        copies.start(
            ref.pre.at[:, pl.ds(t * TILE, TILE)], one.at[pl.ds(t * 3 * HID, 3 * HID)]
        )
        for t in range(slot // TILE)
    ]
    down.advance(3)
    up.advance(3)
    inner[1].merge()
    project_back(2, edges[2])
    out.advance(2)
    inner[0].advance(1)
    inner[1].advance(1)
    for copy in x_copies:
        copy.wait()
    for copy in crossing:
        copy.wait_send()

    def first_norm(m, part):
        for t in range(tiles if part == 0 else 0):
            total = 0.0
            for j in range(tiles):
                weight = ref.win_in[j].reshape(width, 3 * TILE)[t * TILE : (t + 1) * TILE]
                total = total + dot_nt(gz[j, m], weight)
            gbuf[t, :count] = total
        sums = [jnp.zeros((8, width), f32)] * 2
        for rows in blocks(count, 128)[part * TILE // 128 : (part + 1) * TILE // 128]:
            tokens = jnp.concatenate([gcr[j, m, rows] for j in range(tiles)], axis=1)
            grad = jnp.concatenate([gbuf[t, rows] for t in range(tiles)], axis=1)
            gx, gain_part, shift_part = norm_rows_back(grad, tokens.astype(f32), vec[0:1])
            sums = [sums[0] + folded(gain_part), sums[1] + folded(shift_part)]
            total = (gb[m, rows].astype(f32) + gx).astype(bf16)
            for j in range(tiles):
                gc[j, m, rows] = total[:, j * TILE : (j + 1) * TILE]
        for k in range(2):
            total = jnp.sum(sums[k], axis=0, keepdims=True)
            for j in range(tiles):
                row = j * GROUP + k
                vsum[row : row + 1] += total[:, j * TILE : (j + 1) * TILE]

    def filter_back():
        ref.net_sum[...] = jnp.zeros_like(ref.net_sum)
        net = ref.net
        for copy in pre_copies:
            copy.wait()

        def pre(first, last):
            return jnp.concatenate(
                [
                    one[t * 3 * HID + first : t * 3 * HID + last]
                    for t in range(slot // TILE)
                ],
                axis=1,
            )

        frequency = net[:, EMB + 3 + 2 * HID : EMB + 4 + 2 * HID]
        rates = ref.rate[...].reshape(1, width)
        final_low = ref.final[...].astype(bf16)
        acts, slopes = [], []
        for i in range(3):
            pairs = [
                sin_cos(frequency[part] * pre(i * HID + part.start, i * HID + part.stop))
                for part in blocks(HID, 16)
            ]
            acts.append(jnp.concatenate([pair[0] for pair in pairs], axis=0))
            slopes.append(jnp.concatenate([pair[1] for pair in pairs], axis=0))
        last = acts[2].astype(bf16)
        grad = jnp.zeros((HID, slot), f32)
        for j in range(tiles):
            lane = slice(j * TILE, (j + 1) * TILE)
            for half in range(2):
                for rows in blocks(count, 32):
                    first = half * count + rows.start
                    at_row = lax.broadcasted_iota(jnp.int32, (32, TILE), 0) + first
                    window = jnp.exp(at_row.astype(f32) * (rates[:, lane] * (-1.0 / slot))) + 0.05
                    spec[first : first + 32] = (gate[j, half, rows].astype(f32) * window).astype(bf16)
            total = dot(last, spec[...])
            for part in blocks(TILE, 128):
                at = j * TILE + part.start
                row, column = at // HALF * HID, at % HALF
                fsum[row : row + HID, column : column + 128] = total[:, part]
            grad = grad + dot_nt(final_low[:, lane], spec[...])
        freq_sum = jnp.zeros((HID, 1), f32)

        def put(first, values):
            ref.net_sum[:, first : first + values.shape[1]] = values

        for i in (2, 1, 0):
            turn = grad * slopes[i]
            freq_sum = freq_sum + jnp.sum(turn * pre(i * HID, (i + 1) * HID), axis=1, keepdims=True)
            grad = turn * frequency
            below = ref.feature[...] if i == 0 else acts[i - 1]
            made = lax.dot_general(
                grad, below, (((1,), (1,)), ((), ())), precision=highest,
                preferred_element_type=f32,
            )
            if i == 0:
                put(0, made[:, : EMB + 1])
            else:
                first = EMB + 1 + (i - 1) * (HID + 1)
                put(first, made)
                put(first + HID, jnp.sum(grad, axis=1, keepdims=True))
                grad = lax.dot_general(
                    net[:, first : first + HID], grad, (((0,), (0,)), ((), ())),
                    precision=highest, preferred_element_type=f32,
                )
        put(EMB + 3 + 2 * HID, freq_sum)
        nsum[:HID] = ref.net_sum[:, :128]
        nsum[HID:] = ref.net_sum[:, 128:]

    smalls = []
    for values, name in ((fsum, "f"), (nsum, "n"), (vsum, "v")):
        parts = [getattr(ref, name + str(k)) for k in range(5)]
        smalls.append(SmallSum(ring, values, *parts))
    win_copy.wait()
    pieces = [(m, part) for m in range(micro) for part in range(count // TILE)]
    quarter = max(1, len(pieces) // 4)

    def norms(at):
        last = len(pieces) if at == 3 else (at + 1) * quarter
        for m, part in pieces[at * quarter : last]:
            first_norm(m, part)

    norms(0)
    inner[2].merge()
    inner[0].advance(2)
    inner[1].advance(2)
    down.collect()
    norms(1)
    inner[2].advance(1)
    up.collect()
    out.advance(3)
    filter_back()
    for work in smalls[:2]:
        work.begin()
    inner[2].advance(2)
    inner[0].advance(3)
    inner[1].advance(3)
    norms(2)
    inner[2].advance(3)
    out.collect()
    inner[0].collect()
    inner[1].collect()
    for work in smalls[:2]:
        work.add_up()
    norms(3)
    smalls[2].begin()
    inner[2].collect()
    for work in smalls[:2]:
        work.spread()
    for j in range(tiles):
        copies.out(gc.at[j], ref.input_grad.at[:, :, pl.ds(j * TILE, TILE)])
    psum = ref.proj_sum
    ref.down_sum[...] = down.result()
    total = up.result()
    for c in range(blocks_up):
        psum[:, (4 + c) * width : (5 + c) * width] = total[c]
    psum[:, 3 * width : 4 * width] = out.result()
    smalls[2].add_up()
    smalls[2].spread()
    for j in range(tiles):
        total = inner[j].result()
        for p in range(3):
            first = p * width + j * TILE
            psum[:, first : first + TILE] = total[:, p * TILE : (p + 1) * TILE]
    for work in smalls:
        work.finish()
    for part in blocks(width, 128):
        row, column = part.start // HALF * HID, part.start % HALF
        ref.final_sum[:, part] = smalls[0].sums[row : row + HID, column : column + 128]
    ref.net_sum[:, :128] = smalls[1].sums[:HID]
    ref.net_sum[:, 128:] = smalls[1].sums[HID:]
    for j in range(tiles):
        ref.vec_sum[:, j * TILE : (j + 1) * TILE] = smalls[2].sums[j * GROUP : (j + 1) * GROUP]
    for work in [down, up, out] + inner:
        work.finish()
    for edge in edges:
        edge.wait_send()
    copies.finish()


def back(size, arrays):
    chips = size // 2
    micro, count, width = arrays["gb"].shape
    blocks_up, rows = arrays["dup"].shape[2:4]
    wide = blocks_up * width
    down_rows = arrays["ddown"].shape[2]
    tiles = width // TILE
    vmem = pl.BlockSpec(memory_space=pltpu.VMEM)
    anywhere = pl.BlockSpec(memory_space=pl.ANY)
    smem = pl.BlockSpec(memory_space=pltpu.SMEM)
    near = ("gb", "vec", "net", "final", "rate", "table", "back", "zh", "small", "feature")
    small_rows = 8 * size
    outs = dict(
        input_grad=((micro, count, width), bf16),
        proj_sum=((rows, 4 * width + wide), f32),
        down_sum=((down_rows, width), f32),
        vec_sum=((GROUP, width), f32),
        final_sum=((HID, width), f32),
        net_sum=((HID, 256), f32),
    )
    dma = pltpu.SemaphoreType.DMA
    tile_tokens = (tiles, micro, count, TILE)
    edge_rows = (tiles, micro, 16, 3 * TILE)
    scratch = dict(
        din=pltpu.VMEM((tiles, chips, 2, rows, 3 * TILE), bf16),
        dout=pltpu.VMEM((chips, 2, rows, width), bf16),
        gw=pltpu.VMEM(tile_tokens, bf16),
        gc=pltpu.VMEM(tile_tokens, bf16),
        gcr=pltpu.VMEM(tile_tokens, bf16),
        gate=pltpu.VMEM(tile_tokens, bf16),
        gz=pltpu.VMEM((tiles, micro, count, 3 * TILE), bf16),
        turned=pltpu.VMEM((micro, width, count), bf16),
        vsum=pltpu.VMEM((small_rows, TILE), f32),
        nsum=pltpu.VMEM((small_rows, 128), f32),
        fsum=pltpu.VMEM((small_rows, HALF), f32),
        gk=pltpu.VMEM((2, 2 * count, TILE), f32),
        gbuf=pltpu.VMEM((3, count + 16, TILE), f32),
        one=pltpu.VMEM((2 * count, TILE), f32),
        two=pltpu.VMEM((2 * count, TILE), f32),
        zbuf=pltpu.VMEM((count + 16, TILE), f32),
        ebuf=pltpu.VMEM((32, TILE), f32),
        spec=pltpu.VMEM((2 * count, TILE), bf16),
        first_rows=pltpu.VMEM(edge_rows, bf16),
        next_rows=pltpu.VMEM(edge_rows, bf16),
        s_buf=pltpu.VMEM((2, count, 2 * TILE), bf16),
        z_buf=pltpu.VMEM((2, count, 3 * TILE), bf16),
        u_buf=pltpu.VMEM((2, 2, 2 * count, TILE), bf16),
        c_buf=pltpu.VMEM((2, count, TILE), bf16),
        k_buf=pltpu.VMEM((2, 2 * count, TILE), bf16),
        load_sems=dma((2, 4)),
        kernel_sem=dma((1,)),
        gc_sem=dma((2, tiles)),
        edge_sem=dma((2, tiles)),
        copy_sems=dma((40,)),
        win_in=pltpu.VMEM(arrays["win"].shape, bf16),
    )
    ups, downs = chips // 2, (chips - 1) // 2
    for name, lead, dims in (
        ("up", (), (blocks_up, rows, width)), ("down", (), (down_rows, width)), ("out", (), (rows, width)),
        ("in", (tiles,), (rows, 3 * TILE)),
    ):
        made = [pltpu.VMEM(lead + (count,) + dims, bf16) for count in (chips, ups, downs)]
        made += [pltpu.VMEM(lead + dims, bf16)] * 2 + [dma(lead + (2, chips + 1 + ups + downs))]
        for k, part in enumerate(made):
            scratch[name + str(k)] = part
    for name, columns in (("v", TILE), ("n", 128), ("f", HALF)):
        made = small_scratch(size, small_rows, columns)
        made.insert(3, pltpu.VMEM((small_rows, columns), f32))
        for k, part in enumerate(made):
            scratch[name + str(k)] = part
    names = tuple(arrays) + tuple(outs) + tuple(scratch)
    return pl.pallas_call(
        functools.partial(back_kernel, size, names),
        out_shape=[jax.ShapeDtypeStruct(*kind) for kind in outs.values()],
        in_specs=[
            smem if name == "lens" else vmem if name in near else anywhere for name in arrays
        ],
        out_specs=[anywhere] + [vmem] * (len(outs) - 1),
        scratch_shapes=list(scratch.values()),
        compiler_params=pltpu.CompilerParams(
            collective_id=1, has_side_effects=True, vmem_limit_bytes=255 * 1024 * 256
        ),
        name="back",
    )(*arrays.values())


def fits(size, groups, tokens, proj_weights, down_weights):
    micro, _, count, width = tokens.shape
    wide = down_weights.shape[0] * size
    return (
        groups == 2
        and size % 4 == 0
        and size == 16
        and proj_weights.shape[0] % 16 == 0
        and down_weights.shape[0] % 16 == 0
        and count % TILE == 0
        and width == 3 * TILE
        and micro >= groups
        and 3 * HID <= TILE
        and down_weights.shape[0] <= count
        and micro * count <= 1024
        and wide == 4 * width
        and proj_weights.shape[1] == 4 * width + wide
    )


def on_device_tuned(
    block_input,
    out_grad,
    lengths,
    decay_rates,
    proj_weights,
    proj_moment,
    proj_average,
    down_weights,
    down_moment,
    down_average,
    vectors,
    vector_moment,
    vector_average,
    filter_net,
    net_moment,
    net_average,
    filter_out,
    final_moment,
    final_average,
):
    micro, _, count, width = block_input.shape
    size = lax.axis_size("seq")
    tokens = block_input.reshape(micro, count, width)
    plain_table = transform_table(count)
    table = jnp.asarray(plain_table, dtype=bf16)
    table_back = jnp.asarray(plain_table.T, dtype=bf16)
    feature = jnp.asarray(feature_table(count * lax.axis_size("pos")))
    shared = dict(
        x=tokens, lens=lengths.T, vec=vectors, net=filter_net.T, final=filter_out,
        rate=decay_rates, table=table, back=table_back, feature=feature,
    )
    made = types.SimpleNamespace(**front(size, dict(shared, proj=proj_weights, down=down_weights)))
    block_output, branch_grad, up_step, down_step, small = mlp(
        made.n2, made.n2t, out_grad.reshape(micro, count, width), made.res, vectors,
        made.wup, made.wdown,
    )
    chips = size // 2
    input_grad, proj_sum, down_sum, vector_sum, final_sum, net_sum = back(
        size,
        dict(
            shared, win=made.win, wout=made.wout, z=made.z, zh=made.zh, s=made.s, conv=made.conv,
            uhat=made.uhat, kern=made.kern, nt=made.nt, yt=made.yt, pre=made.pre,
            gb=branch_grad, small=small,
            dup=up_step,
            ddown=down_step.reshape(chips, 2, -1, width),
        ),
    )
    input_grad, steps = update(
        input_grad,
        [
            (proj_sum, proj_weights, proj_moment, proj_average, 0.0001, 0, 1),
            (down_sum, down_weights, down_moment, down_average, 0.0001, 0, 0),
            (vector_sum, vectors, vector_moment, vector_average, 0.001, 0, None),
            (net_sum, filter_net.T, net_moment.T, net_average.T, 0.0001, 0, None),
            (final_sum, filter_out, final_moment, final_average, 2e-06, 0, None),
        ]
    )
    steps[3] = [array.T for array in steps[3]]
    return (
        block_output.reshape(block_input.shape),
        input_grad.reshape(block_input.shape),
        *steps[0], *steps[1], *steps[2], *steps[3], *steps[4],
    )


def on_device_plain(
    block_input,
    out_grad,
    lengths,
    decay_rates,
    proj_weights,
    proj_moment,
    proj_average,
    down_weights,
    down_moment,
    down_average,
    vectors,
    vector_moment,
    vector_average,
    filter_net,
    net_moment,
    net_average,
    filter_out,
    final_moment,
    final_average,
):
    micro = block_input.shape[0]
    count = block_input.shape[2]
    width = block_input.shape[3]
    groups = lax.axis_size("pos")
    slot_length = count * groups
    tokens_all = micro * count
    group = lax.axis_index("pos")
    tap = vectors[13:22].reshape(3, 3 * width)
    short_bias = vectors[22:25].reshape(-1)
    in_bias = vectors[4:7].reshape(-1)
    up_bias = vectors[8:12].reshape(-1)
    skip = vectors[25]

    low_rows = proj_weights.astype(bf16)
    in_weight = lax.all_gather(low_rows[:, : 3 * width], "seq", axis=0, tiled=True)
    out_weight = lax.all_gather(low_rows[:, 3 * width : 4 * width], "seq", axis=0, tiled=True)
    up_weight = lax.all_gather(low_rows[:, 4 * width :], "seq", axis=0, tiled=True)
    down_weight = lax.all_gather(down_weights.astype(bf16), "seq", axis=0, tiled=True)

    table = jnp.asarray(transform_table(count))
    table_low = table.astype(bf16)
    every = jnp.arange(slot_length, dtype=jnp.int32)

    def make_filter(net_values, final_values):
        return filter_fn(net_values, final_values, decay_rates, every, slot_length)

    filters, filter_back = jax.vjp(make_filter, filter_net, filter_out)
    pieces = filters.reshape(groups, count, width)
    spectra = [
        jnp.dot(table, pieces[d], precision=lax.Precision.HIGH, preferred_element_type=f32)
        for d in range(groups)
    ]
    kernels = [spectra[0]] + [spectra[d] + turned(spectra[d - 1], 1.0) for d in range(1, groups)]

    def transform(values):
        return jnp.stack([dot(table_low, values[m]) for m in range(micro)])

    def transform_back(spectrum):
        low = spectrum.astype(bf16)
        return jnp.stack([dot_tn(table_low, low[m]) for m in range(micro)]) * (1.0 / count)

    tokens_low = block_input[:, 0]
    before = passed_along(tokens_low[:, -2:], "pos", 1)
    tokens = tokens_low.astype(f32).reshape(tokens_all, width)
    xh_one, scale_one = norm_parts(tokens)
    normed = (xh_one * vectors[0] + vectors[1]).astype(bf16)
    xh_before, _ = norm_parts(before.astype(f32).reshape(micro * 2, width))
    normed_before = (xh_before * vectors[0] + vectors[1]).astype(bf16)
    z = (dot(normed, in_weight) + in_bias).reshape(micro, count, 3 * width)
    z_before = (dot(normed_before, in_weight) + in_bias).reshape(micro, 2, 3 * width)
    z_before = jnp.where(group > 0, z_before, 0.0)
    z_long = jnp.concatenate([z_before, z], axis=1)
    short = (
        tap[0] * z_long[:, 2:] + tap[1] * z_long[:, 1:-1] + tap[2] * z_long[:, :-2] + short_bias
    ).astype(bf16)
    x0 = short[:, :, :width].astype(f32)
    x1 = short[:, :, width : 2 * width].astype(f32)
    v = short[:, :, 2 * width :].astype(f32)

    u = x1 * v
    u_low = u.astype(bf16)
    u_hat = [transform(u_low)]
    for d in range(1, groups):
        u_hat.append(transform(passed_along(u_low, "pos", d)))
    total = product(kernels[0], u_hat[0])
    for d in range(1, groups):
        total = total + product(kernels[d], u_hat[d])
    conv = transform_back(total) + skip * u
    here = group * count + jnp.arange(count, dtype=jnp.int32)
    mask = (here[None, :] < lengths[:, 0][:, None]).astype(f32)[:, :, None]
    y = (mask * x0 * conv).astype(bf16).reshape(tokens_all, width)
    residual = tokens + dot(y, out_weight) + vectors[7]
    xh_two, scale_two = norm_parts(residual)
    normed_two = (xh_two * vectors[2] + vectors[3]).astype(bf16)

    cot_low = out_grad[:, 0].reshape(tokens_all, width)
    cot = cot_low.astype(f32)
    pre = dot(normed_two, up_weight) + up_bias
    hidden, gelu_back = jax.vjp(jax.nn.gelu, pre)
    hidden_low = hidden.astype(bf16)
    block_output = (residual + dot(hidden_low, down_weight) + vectors[12]).astype(bf16)
    pre_grad = gelu_back(dot_nt(cot_low, down_weight))[0].astype(bf16)
    down_step = dot_tn(hidden_low, cot_low)
    up_step = dot_tn(normed_two, pre_grad)
    normed_two_grad = dot_nt(pre_grad, up_weight)
    part, gain_two, shift_two = norm_back(normed_two_grad, xh_two, scale_two, vectors[2])
    residual_grad = cot + part
    branch_low = residual_grad.astype(bf16)
    out_step = dot_tn(y, branch_low)
    y_grad = dot_nt(branch_low, out_weight).astype(bf16).astype(f32).reshape(micro, count, width)

    gw = mask * y_grad
    gx0 = gw * conv
    gc = gw * x0
    gc_low = gc.astype(bf16)
    skip_grad = jnp.sum(gc * u, axis=(0, 1))
    gc_hat = [transform(gc_low)]
    for d in range(1, groups):
        gc_hat.append(transform(passed_along(gc_low, "pos", -d)))
    back = product_conj(kernels[0], gc_hat[0])
    for d in range(1, groups):
        back = back + product_conj(kernels[d], gc_hat[d])
    gu = transform_back(back) + skip * gc
    kernel_grads = [jnp.sum(product_conj(u_hat[d], gc_hat[0]), axis=0) for d in range(groups)]
    filter_grads = []
    for d in range(groups):
        got = kernel_grads[d]
        if d + 1 < groups:
            got = got + turned(kernel_grads[d + 1], -1.0)
        filter_grads.append(dot_tn(table_low, got.astype(bf16)) * (1.0 / count))
    net_local, final_local = filter_back(jnp.concatenate(filter_grads, axis=0))
    short_grad = jnp.concatenate([gx0, gu * v, gu * x1], axis=-1).astype(bf16)
    after = passed_along(short_grad[:, :2], "pos", -1)
    short_long = jnp.concatenate([short_grad, after], axis=1).astype(f32)
    z_grad = (
        tap[0] * short_long[:, :-2] + tap[1] * short_long[:, 1:-1] + tap[2] * short_long[:, 2:]
    ).astype(bf16)
    here_grad = short_long[:, :-2]
    tap_grads = [
        jnp.sum(here_grad * z_long[:, 2 - k : 2 - k + count], axis=(0, 1)) for k in range(3)
    ]
    short_bias_grad = jnp.sum(here_grad, axis=(0, 1))
    z_grad = z_grad.reshape(tokens_all, 3 * width)
    in_step = dot_tn(normed, z_grad)
    in_bias_grad = jnp.sum(z_grad.astype(f32), axis=0)
    normed_grad = dot_nt(z_grad, in_weight)
    part, gain_one, shift_one = norm_back(normed_grad, xh_one, scale_one, vectors[0])
    input_grad = (residual_grad + part).astype(bf16)

    vector_local = jnp.concatenate(
        [
            gain_one[None],
            shift_one[None],
            gain_two[None],
            shift_two[None],
            in_bias_grad.reshape(3, width),
            jnp.sum(branch_low.astype(f32), axis=0)[None],
            jnp.sum(pre_grad.astype(f32), axis=0).reshape(4, width),
            jnp.sum(cot, axis=0)[None],
            jnp.stack(tap_grads).reshape(9, width),
            short_bias_grad.reshape(3, width),
            skip_grad[None],
        ],
        axis=0,
    )
    proj_local = jnp.concatenate([in_step, out_step, up_step], axis=1).astype(bf16)
    proj_shard = lax.psum_scatter(proj_local, "seq", scatter_dimension=0, tiled=True)
    down_shard = lax.psum_scatter(down_step.astype(bf16), "seq", scatter_dimension=0, tiled=True)
    proj_sum = lax.psum(proj_shard, "pos").astype(f32)
    down_sum = lax.psum(down_shard, "pos").astype(f32)
    vector_sum, net_sum, final_sum = lax.psum(
        (vector_local, net_local, final_local), ("seq", "pos")
    )
    return (
        block_output.reshape(micro, 1, count, width),
        input_grad.reshape(micro, 1, count, width),
        *nesterov(proj_weights, proj_moment, proj_average, proj_sum, 0.0001),
        *nesterov(down_weights, down_moment, down_average, down_sum, 0.0001),
        *nesterov(vectors, vector_moment, vector_average, vector_sum, 0.001),
        *nesterov(filter_net, net_moment, net_average, net_sum, 0.0001),
        *nesterov(filter_out, final_moment, final_average, final_sum, 2e-06),
    )


def on_device(*arrays):
    tuned = fits(
        lax.axis_size("seq"), lax.axis_size("pos"), arrays[0], arrays[4], arrays[7]
    )
    return (on_device_tuned if tuned else on_device_plain)(*arrays)


def solution(mesh):
    tokens = P(None, "seq", "pos", None)
    rows = P("seq", None)
    whole = P()
    return jax.shard_map(
        on_device,
        mesh=mesh,
        in_specs=(tokens, tokens, P(None, "seq"), whole) + (rows,) * 6 + (whole,) * 9,
        out_specs=(tokens, tokens) + (rows,) * 8 + (whole,) * 12,
        check_vma=False,
    )
```
